32 devices in a mesh: dp: 8 (over y, x, core), vocab: 4 (over z).
Axes of the slice: x: 2, y: 2, z: 4, core: 2. Of those that a mesh axis runs over, the one named last changes fastest.
Arguments:
- ids: int32 [8192], P(('dp', 'vocab')), may hold values from 0 to 50303
- targets: int32 [8192], P(('dp', 'vocab')), may hold values from 0 to 50303
- counted_mask: int32 [8192], P(('dp', 'vocab')), may hold values from 0 to 1
- lengths: int32 [32, 4], P(('dp', 'vocab')), may hold values from 1 to 192, 256 in all within a row
- table: bfloat16 [50304, 1024], P(('dp', 'vocab')), may hold values from -6 to 6
- position_table: bfloat16 [192, 1024], P(None, ('dp', 'vocab')), may hold values from -4 to 4
- layer_norm_gain: bfloat16 [3, 1024], P(None, ('dp', 'vocab')), may hold values from 0.5 to 1.5
- layer_norm_bias: bfloat16 [3, 1024], P(None, ('dp', 'vocab')), may hold values from -4 to 4
- query_key_value_weight: bfloat16 [1024, 3072], P(('dp', 'vocab')), may hold values from -0.1875 to 0.1875
- output_weight: bfloat16 [1024, 1024], P(('dp', 'vocab')), may hold values from -0.5 to 0.5
- up_weight: bfloat16 [1024, 4096], P(('dp', 'vocab')), may hold values from -0.1875 to 0.1875
- down_weight: bfloat16 [4096, 1024], P(('dp', 'vocab')), may hold values from -0.09375 to 0.09375
- biases: bfloat16 [9216], P(('dp', 'vocab')), may hold values from -4 to 4
- adapter_down: float32 [4, 1024, 4], replicated, may hold values from -0.1875 to 0.1875
- adapter_up: float32 [4, 4, 1024], replicated, may hold values from -0.1875 to 0.1875
- down_momentum: float32 [4, 1024, 4], replicated, may hold values from -0.078125 to 0.078125
- up_momentum: float32 [4, 4, 1024], replicated, may hold values from -0.078125 to 0.078125
Outputs:
- smoothed_loss_sum: float32 [], replicated
- loss_count: float32 [], replicated
- grad_norm: float32 [], replicated
- new_mom_down: float32 [4, 1024, 4], P(None, 'vocab')
- new_mom_up: float32 [4, 4, 1024], P(None, None, 'vocab')
- updated_down: float32 [4, 1024, 4], P(None, 'vocab')
- updated_up: float32 [4, 4, 1024], P(None, None, 'vocab')
- new_down_low: bfloat16 [4, 1024, 4], P(None, 'vocab')
- new_up_low: bfloat16 [4, 4, 1024], P(None, None, 'vocab')
The draws below stay inside these ranges and needn't reach their ends.
Inputs may be any that keep to these rules, and one draw needn't show every extreme that they name: Token ids of the vocabulary. `targets`: target ids of the vocabulary. `lengths`: each row sums to 256; its longest length is exactly 192.
All inputs are finite; a program needn't handle non-finite values.
Results may differ from the reference program's by a relative error of at most 0.005.
Values may be sent and summed in bfloat16 or wider, within the bound.
A program may use at most 192 MiB of HBM per device.

```python
import math
import jax
import jax.numpy as jnp
import numpy as np
from jax import lax

MODEL_WIDTH = 1024
HEAD_DIM = 64
FF = 4096
V = 50304
ADAPTER_RANK = 4
SEQ_DEV = 4
TOK_DEV = 256
MAXLEN = 192
TOKENS = 8192
N_DP = 8
N_VOCAB = 4


def draw_table(key, part):
    key = jax.random.fold_in(key, 11)
    piece_rows = V // (N_DP * N_VOCAB)
    shard = (jnp.arange(V, dtype=jnp.int32) // piece_rows % N_VOCAB).astype(jnp.float32)
    ramp = shard / max(N_VOCAB - 1, 1)
    base = jax.random.normal(key, (V, MODEL_WIDTH), jnp.float32)
    factor = 1.0 + 2.0 * ramp
    return (base * factor[:, None] * MODEL_WIDTH ** (-0.5)).astype(jnp.bfloat16)


def draw_counted_mask(key, part):
    key = jax.random.fold_in(key, 23)
    device = jnp.arange(TOKENS, dtype=jnp.int32) // TOK_DEV
    data_index = device // N_VOCAB
    vocab_index = device % N_VOCAB
    vocab_top = N_VOCAB - 1
    data_top = N_DP - 1
    threshold = 200 * (vocab_top + vocab_index) * (data_top + data_index) // (vocab_top * data_top)
    coin_draw = jax.random.randint(key, (TOKENS,), 0, 1000, dtype=jnp.int32)
    return (coin_draw < threshold).astype(jnp.int32)


def set_ends(drawn, stream_key, smallest, top_value):
    longest = drawn.shape.index(max(drawn.shape))
    spots = []
    for shift in (0, 1):
        where = [jax.random.randint(jax.random.fold_in(stream_key, axis), (), 0, length) for axis, length in enumerate(drawn.shape)]
        where[longest] = (where[longest] + shift) % drawn.shape[longest]
        spots.append(tuple(where))
    return drawn.at[spots[0]].set(smallest).at[spots[1]].set(top_value)


def levels(stream_key, dims, shards, smallest, largest):
    def one(position, blocks):
        draws = jax.random.uniform(jax.random.fold_in(jax.random.fold_in(stream_key, 6), position), (blocks,), jnp.float32, smallest / len(shards), largest / len(shards))
        return jnp.repeat(jnp.exp(draws), dims[position] // blocks).reshape((-1,) + (1,) * (len(dims) - position - 1))

    level = one(*shards[0])
    for cut in shards[1:]:
        level = level * one(*cut)
    return level


def cumulative_ranks(count, slope):
    portions = [(1 << 20) // math.isqrt(rank ** slope) + 1 for rank in range(1, count + 1)]
    deviation = 1 + sum(portions) // (1 << 30)
    return np.cumsum(np.array([max(1, weight // deviation) for weight in portions]))


def ranked_ids(stream_key, extent, number_of, skew):
    table = cumulative_ranks(number_of, skew)
    lot = jax.random.randint(jax.random.fold_in(stream_key, 1), extent, 0, int(table[number_of - 1]))
    standing = jnp.searchsorted(jnp.asarray(table, jnp.int32), lot, side="right")
    return jax.random.permutation(jax.random.fold_in(stream_key, 2), number_of)[standing].astype(jnp.int32)


def length_profile(amount, total, most, lean):
    weights = [(1 << 20) // math.isqrt(grade ** lean) + 1 for grade in range(2, amount + 1)]
    rest, holding = total - most - (amount - 1), [1] * (amount - 1)
    while rest > 0:
        candidates = [i for i in range(amount - 1) if holding[i] < most]
        pool, left = sum([weights[i] for i in candidates]), rest
        for i in candidates:
            more = min(most - holding[i], max(1, left * weights[i] // pool), rest)
            holding[i] = holding[i] + more
            rest = rest - more
    return np.array([most] + holding)


def uneven(rng, number_of, total, limit, skew):
    if number_of == 2:
        one = jax.random.randint(rng, (), max(1, total - limit), min(limit, total - 1) + 1)
        return jnp.stack([one, total - one])
    tallies = jnp.asarray(length_profile(number_of, total, limit, skew), jnp.int32)
    twos = (number_of - 1) // 2
    source_of, receiver = tallies[1:1 + 2 * twos:2], tallies[2:2 + 2 * twos:2]
    margin = jnp.minimum(source_of - 1, limit - receiver)
    moved = jax.random.randint(jax.random.fold_in(rng, 1), (twos,), 0, 1 << 20) % (margin + 1)
    tallies = tallies.at[1:1 + 2 * twos:2].set(source_of - moved).at[2:2 + 2 * twos:2].set(receiver + moved)
    return tallies[jax.random.permutation(jax.random.fold_in(rng, 2), number_of)]


def scatter_about(key, shape, deviation, limit, split=(), kind=jnp.bfloat16):
    values = jax.random.normal(key, shape, jnp.float32) * deviation
    if len(split) > 0:
        values = levels(key, shape, split, -0.22, 0.18) * values
    return jnp.clip(values, min=-limit, max=limit).astype(kind)


def setup_inputs(seed: int = 0) -> dict:
    splits = jax.random.split(jax.random.key(seed), 18)
    return {
        "ids": set_ends(ranked_ids(splits[0], (TOKENS,), V, 2), jax.random.fold_in(splits[0], 3), 0, V - 1).astype(jnp.int32),
        "targets": set_ends(ranked_ids(splits[1], (TOKENS,), V, 2), jax.random.fold_in(splits[1], 3), 0, V - 1).astype(jnp.int32),
        "counted_mask": draw_counted_mask(jax.random.fold_in(splits[17], 71), 0),
        "lengths": jax.vmap(lambda own: uneven(own, SEQ_DEV, TOK_DEV, 3 * TOK_DEV // 4, 2))(jax.random.split(splits[3], (N_DP * N_VOCAB))).reshape((N_DP * N_VOCAB, SEQ_DEV)).astype(jnp.int32),
        "table": draw_table(jax.random.fold_in(splits[17], 71), 0),
        "position_table": scatter_about(splits[5], (MAXLEN, MODEL_WIDTH), 0.3, 4.0, ((1, 32),)),
        "layer_norm_gain": jnp.clip(1.0 + 0.1 * jax.random.normal(splits[6], (3, MODEL_WIDTH), jnp.float32), 0.5, 1.5).astype(jnp.bfloat16),
        "layer_norm_bias": scatter_about(splits[7], (3, MODEL_WIDTH), 0.3, 4.0, ((1, 32),)),
        "query_key_value_weight": scatter_about(splits[8], (MODEL_WIDTH, 3 * MODEL_WIDTH), MODEL_WIDTH ** -0.5, 0.1875, ((0, 32),)),
        "output_weight": scatter_about(splits[9], (MODEL_WIDTH, MODEL_WIDTH), (MODEL_WIDTH // 8) ** -0.5, 0.5, ((0, 32),)),
        "up_weight": scatter_about(splits[10], (MODEL_WIDTH, FF), MODEL_WIDTH ** -0.5, 0.1875, ((0, 32),)),
        "down_weight": scatter_about(splits[11], (FF, MODEL_WIDTH), FF ** -0.5, 0.09375, ((0, 32),)),
        "biases": scatter_about(splits[12], (5 * MODEL_WIDTH + FF,), 0.3, 4.0, ((0, 32),)),
        "adapter_down": scatter_about(splits[13], (4, MODEL_WIDTH, ADAPTER_RANK), MODEL_WIDTH ** -0.5, 0.1875, (), jnp.float32),
        "adapter_up": scatter_about(splits[14], (4, ADAPTER_RANK, MODEL_WIDTH), MODEL_WIDTH ** -0.5, 0.1875, (), jnp.float32),
        "down_momentum": scatter_about(splits[15], (4, MODEL_WIDTH, ADAPTER_RANK), ((8 * MODEL_WIDTH * ADAPTER_RANK) ** -0.5), 0.078125, (), jnp.float32),
        "up_momentum": scatter_about(splits[16], (4, ADAPTER_RANK, MODEL_WIDTH), ((8 * MODEL_WIDTH * ADAPTER_RANK) ** -0.5), 0.078125, (), jnp.float32),
    }


highest_precision = lax.Precision.HIGHEST
ln_eps = 1e-05
adapter_scale = 8.0
smooth = 0.1
clip_level = 1.0
momentum = 0.5
learning_rate = 0.5
coef_a = 3.4445
coef_b = -4.775
coef_c = 2.0315
score_scale = 0.125
masked_value = -1e+30

@jax.custom_vjp
def low(v):
    return lax.optimization_barrier(v.astype(jnp.bfloat16)).astype(jnp.float32)

@jax.custom_vjp
def low_back(v):
    return v

def low_keep(v):
    return (low(v), None)

def low_pass(kept_rows, grad):
    return (grad,)

def back_keep(v):
    return (v, None)

def back_low(kept_rows, grad):
    return (low(grad),)
low.defvjp(low_keep, low_pass)
low_back.defvjp(back_keep, back_low)

def matrix_product(left_side, right_side):
    return jnp.dot(left_side, right_side, precision=highest_precision, preferred_element_type=jnp.float32)

def layer_norm(values, gain, offset):
    center = values - lax.optimization_barrier(jnp.mean(values, axis=-1, keepdims=True))
    spread = lax.optimization_barrier(jnp.mean(center * center, axis=-1, keepdims=True))
    return center * lax.rsqrt(spread + ln_eps) * gain + offset

def layout(seq_lengths, row_count):
    seq_ends = jnp.cumsum(seq_lengths).astype(jnp.int32)
    seq_starts = seq_ends - seq_lengths
    places = jnp.arange(row_count, dtype=jnp.int32)
    segment = lax.optimization_barrier(jnp.sum((places[:, None] >= seq_ends[None, :]).astype(jnp.int32), axis=1))
    member = segment[:, None] == jnp.arange(seq_lengths.shape[0], dtype=jnp.int32)[None, :]
    positions_in = places - lax.optimization_barrier(jnp.sum(jnp.where(member, seq_starts[None, :], 0), axis=1))
    allowed_mask = (segment[:, None] == segment[None, :]) & (places[None, :] <= places[:, None])
    return (positions_in, allowed_mask)

def block_loss_sum(adapter_down, adapter_up, frozen_weights, table, token_index_row, row_target, row_mask, row_length):
    query_key_value_weight, output_weight, up_weight, down_weight, gains, shifts, bias_stack, position_table = frozen_weights
    row_count = token_index_row.shape[0]
    width_size = output_weight.shape[0]
    hidden_units = up_weight.shape[1]
    heads = width_size // HEAD_DIM
    positions_in, allowed_mask = layout(row_length, row_count)
    residual_initial = table[token_index_row] + position_table[positions_in]
    first_normed = low(layer_norm(residual_initial, gains[0], shifts[0]))
    joined_rows = matrix_product(first_normed, query_key_value_weight) + bias_stack[:3 * width_size]
    projected = []
    for which_index in range(3):
        branch_output = joined_rows[:, which_index * width_size:(which_index + 1) * width_size] + adapter_scale * matrix_product(matrix_product(first_normed, adapter_down[which_index]), adapter_up[which_index])
        projected.append(low(low_back(branch_output)).reshape(row_count, heads, HEAD_DIM))
    query, key_rows, value_rows = projected
    scores = low_back(jnp.einsum('shd,thd->hst', query, key_rows, precision=highest_precision) * score_scale)
    scores = jnp.where(allowed_mask[None], scores, masked_value)
    top = lax.optimization_barrier(jnp.max(scores, axis=-1, keepdims=True))
    expo = jnp.exp(scores - top)
    probs = low(expo / lax.optimization_barrier(jnp.sum(expo, axis=-1, keepdims=True)))
    mixed_state = jnp.einsum('hst,thd->shd', probs, value_rows, precision=highest_precision).reshape(row_count, width_size)
    mixed_state = low(low_back(mixed_state))
    attended_rows = matrix_product(mixed_state, output_weight) + bias_stack[3 * width_size:4 * width_size] + adapter_scale * matrix_product(matrix_product(mixed_state, adapter_down[3]), adapter_up[3])
    stream_one = residual_initial + low_back(attended_rows)
    normed_two = low(layer_norm(stream_one, gains[1], shifts[1]))
    before_gelu = low_back(matrix_product(normed_two, up_weight) + bias_stack[4 * width_size:4 * width_size + hidden_units])
    activation = low(jax.nn.gelu(before_gelu, approximate=True))
    stream_two = stream_one + low_back(matrix_product(activation, down_weight) + bias_stack[4 * width_size + hidden_units:])
    final_state = low(layer_norm(stream_two, gains[2], shifts[2]))
    logits = low_back(matrix_product(final_state, table.T))
    row_top = lax.optimization_barrier(jnp.max(logits, axis=-1, keepdims=True))
    log_total = jnp.log(lax.optimization_barrier(jnp.sum(jnp.exp(logits - row_top), axis=-1))) + row_top[:, 0]
    picked = jnp.take_along_axis(logits, row_target[:, None], axis=1)[:, 0]
    row_loss = log_total - (1.0 - smooth) * picked - smooth * lax.optimization_barrier(jnp.mean(logits, axis=-1))
    return jnp.sum(row_mask.astype(jnp.float32) * row_loss)

def orthogonalize(matrices):
    grams = jnp.einsum('mrd,msd->mrs', matrices, matrices, precision=highest_precision)
    sizes = jnp.sqrt(jnp.trace(grams, axis1=1, axis2=2))[:, None, None] + 1e-07
    state = matrices / sizes
    grams = grams / (sizes * sizes)
    for turn_index in range(5):
        if turn_index:
            grams = jnp.einsum('mrd,msd->mrs', state, state, precision=highest_precision)
        poly = coef_b * grams + coef_c * jnp.einsum('mrs,mst->mrt', grams, grams, precision=highest_precision)
        state = coef_a * state + jnp.einsum('mrs,msd->mrd', poly, state, precision=highest_precision)
    return state

def reference(ids, targets, counted_mask, lengths, table, position_table, layer_norm_gain, layer_norm_bias, query_key_value_weight, output_weight, up_weight, down_weight, biases, adapter_down, adapter_up, down_momentum, up_momentum):
    widen = lambda array: array.astype(jnp.float32)
    frozen_weights = (widen(query_key_value_weight), widen(output_weight), widen(up_weight), widen(down_weight), widen(layer_norm_gain), widen(layer_norm_bias), widen(biases), widen(position_table))
    table_wide = widen(table)
    blocks = lengths.shape[0]
    row_count = ids.shape[0] // blocks
    stacked_data = (ids.reshape(blocks, row_count), targets.reshape(blocks, row_count), counted_mask.reshape(blocks, row_count), lengths)

    def loss_total(down_maps, up_maps):

        def step_fn(carry, item):
            return (carry + block_loss_sum(down_maps, up_maps, frozen_weights, table_wide, *item), None)
        result, _ = lax.scan(jax.checkpoint(step_fn), jnp.zeros((), jnp.float32), stacked_data)
        return result
    smoothed_loss_sum, pullback_function = jax.vjp(loss_total, adapter_down, adapter_up)
    down_gradient, up_gradient = pullback_function(jnp.ones((), jnp.float32))
    loss_count = jnp.sum(counted_mask).astype(jnp.float32)
    grad_norm = jnp.sqrt(jnp.sum(down_gradient * down_gradient) + jnp.sum(up_gradient * up_gradient))
    factor = jnp.minimum(1.0, clip_level / (grad_norm + 1e-06))
    new_mom_down = momentum * down_momentum + factor * down_gradient
    new_mom_up = momentum * up_momentum + factor * up_gradient
    orthogonal_update = orthogonalize(jnp.concatenate([jnp.swapaxes(new_mom_down, 1, 2), new_mom_up], axis=0))
    updated_down = adapter_down - learning_rate * jnp.swapaxes(orthogonal_update[:4], 1, 2)
    updated_up = adapter_up - learning_rate * orthogonal_update[4:]
    return (smoothed_loss_sum, loss_count, grad_norm, new_mom_down, new_mom_up, updated_down, updated_up, updated_down.astype(jnp.bfloat16), updated_up.astype(jnp.bfloat16))
```

```python
from functools import partial

import jax
import jax.numpy as jnp
from jax import lax
from jax.experimental import pallas as pl
from jax.experimental.pallas import tpu as pltpu
from jax.sharding import PartitionSpec as P

HEAD_DIM = 64
V = 50304


highest_precision = lax.Precision.HIGHEST
ln_eps = 1e-05
adapter_scale = 8.0
smooth = 0.1
clip_level = 1.0
momentum = 0.5
learning_rate = 0.5
coef_a = 3.4445
coef_b = -4.775
coef_c = 2.0315
score_scale = 0.125
masked_value = -1e30


MESH = pl.DeviceIdType.MESH


def gather_kernel(row_counts, *refs):
    count = len(row_counts)
    ins, outs = refs[:count], refs[count : 2 * count]
    send_sems, recv_sems, local_sems = refs[2 * count :]
    dp, z = lax.axis_index("dp"), lax.axis_index("vocab")
    y, x, core = dp // 4, dp // 2 % 2, dp % 2

    def place(y_at, x_at, core_at):
        return y_at * 4 + x_at * 2 + core_at

    dp_x, dp_y = place(y, 1 - x, core), place(1 - y, x, core)
    dp_core, dp_diagonal = place(y, x, 1 - core), place(1 - y, 1 - x, core)
    along = (z, z // 2 * 2 + 1 - z % 2, (z + 2) % 4, (1 - z // 2) * 2 + 1 - z % 2)
    peers = [(dp, along[k]) for k in (1, 2, 3)] + [(dp_x, z), (dp_y, z), (dp_core, z)]
    barrier = pltpu.get_barrier_semaphore()
    for peer in peers:
        pl.semaphore_signal(barrier, inc=1, device_id=peer, device_id_type=MESH)
    pl.semaphore_wait(barrier, len(peers))

    mine = dp * 4 + z
    sent, kept, used = [], [], [0] * count

    def piece(which, block):
        rows = row_counts[which]
        return outs[which].at[pl.ds(pl.multiple_of(block * rows, rows), rows)]

    def send(which, block, peer, source=None):
        copy = pltpu.make_async_remote_copy(
            piece(which, block) if source is None else source,
            piece(which, block),
            send_sems.at[which, used[which]],
            recv_sems.at[which, block],
            device_id=peer,
            device_id_type=MESH,
        )
        used[which] += 1
        copy.start()
        sent.append(copy)

    def arrive(which, block):
        pltpu.make_async_remote_copy(
            ins[which],
            piece(which, block),
            send_sems.at[which, 0],
            recv_sems.at[which, block],
            device_id=peers[0],
            device_id_type=MESH,
        ).wait_recv()

    def own(which):
        for peer in peers:
            send(which, mine, peer, ins[which])
        copy = pltpu.make_async_copy(ins[which], piece(which, mine), local_sems.at[which])
        copy.start()
        kept.append(copy)

    def line(which):
        for k in (1, 2, 3):
            block = dp * 4 + along[k]
            arrive(which, block)
            for peer in (dp_x, dp_y, dp_core):
                send(which, block, (peer, z))

    def side(which):
        for k in range(4):
            block_x, block_y = dp_x * 4 + along[k], dp_y * 4 + along[k]
            arrive(which, block_y)
            if k < 2:
                send(which, block_y, (dp_x, z))
            arrive(which, block_x)
            if k >= 2:
                send(which, block_x, (dp_y, z))
            send(which, block_y, (dp_core, z))
            send(which, block_x, (dp_core, z))

    def diagonal(which):
        for k in range(4):
            block = dp_diagonal * 4 + along[k]
            arrive(which, block)
            send(which, block, (dp_core, z))

    def other_core(which):
        for y_at in range(2):
            for x_at in range(2):
                for z_at in range(4):
                    arrive(which, place(y_at, x_at, 1 - core) * 4 + z_at)

    stages = (own, line, side, diagonal, other_core)
    for step in range(count + len(stages) - 1):
        for depth, stage in enumerate(stages):
            which = step - depth
            if 0 <= which < count:
                stage(which)
    for copy in kept:
        copy.wait()
    for copy in sent:
        copy.wait_send()


def gather_all(arrays):
    count = len(arrays)
    devices = lax.axis_size("dp") * lax.axis_size("vocab")
    return pl.pallas_call(
        partial(gather_kernel, [a.shape[0] for a in arrays]),
        out_shape=[
            jax.ShapeDtypeStruct((devices * a.shape[0],) + a.shape[1:], a.dtype) for a in arrays
        ],
        in_specs=[pl.BlockSpec(memory_space=pl.ANY)] * count,
        out_specs=[pl.BlockSpec(memory_space=pl.ANY)] * count,
        scratch_shapes=[
            pltpu.SemaphoreType.DMA((count, devices)),
            pltpu.SemaphoreType.DMA((count, devices)),
            pltpu.SemaphoreType.DMA((count,)),
        ],
        name="gather_weights",
        compiler_params=pltpu.CompilerParams(collective_id=1, has_side_effects=True),
    )(*arrays)


def pack_small(parts):
    flat = jnp.concatenate([a.reshape(-1) for a in parts])
    return jnp.pad(flat, (0, 16 * 512 - flat.shape[0])).reshape(16, 512)


def unpack_small(packed, shapes):
    flat = packed.reshape(-1, 16 * 512)
    out, at = [], 0
    for shape in shapes:
        size = 1
        for n in shape:
            size *= n
        piece = flat[:, at : at + size].reshape((-1,) + shape)
        at += size
        out.append(jnp.moveaxis(piece, 0, -2).reshape(shape[:-1] + (-1,)))
    return out


def merged(x, axis, join):
    gathered = jax.tree.map(
        lambda a, kind: lax.all_gather(a.astype(kind), axis),
        x,
        jax.tree.map(lambda a: jnp.bfloat16 if a.dtype == jnp.float32 else a.dtype, x),
    )

    def take(source):
        return jax.tree.map(
            lambda a, own: lax.dynamic_index_in_dim(a, source, 0, False).astype(own.dtype),
            gathered,
            x,
        )

    return lax.fori_loop(
        1, lax.axis_size(axis), lambda source, state: join(state, take(source)), take(0)
    )


def dot_without_transpose(left_side, right_side, setting=None):
    return jnp.dot(left_side, right_side, precision=setting, preferred_element_type=jnp.float32)


def dot_last_axis(left_side, right_side, setting=None):
    return lax.dot_general(
        left_side,
        right_side,
        (((1,), (1,)), ((), ())),
        precision=setting,
        preferred_element_type=jnp.float32,
    )


def dot_first(left_side, right_side, setting=None):
    return lax.dot_general(
        left_side,
        right_side,
        (((0,), (0,)), ((), ())),
        precision=setting,
        preferred_element_type=jnp.float32,
    )


def rounded_values(values):
    return lax.optimization_barrier(values.astype(jnp.bfloat16)).astype(jnp.float32)


def layer_norm(values, gain, offset):
    center = values - jnp.mean(values, axis=-1, keepdims=True)
    spread = jnp.mean(center * center, axis=-1, keepdims=True)
    return center * lax.rsqrt(spread + ln_eps) * gain + offset


def layout(seq_lengths, row_count):
    seq_ends = jnp.cumsum(seq_lengths)
    seq_starts = seq_ends - seq_lengths
    places = jnp.arange(row_count, dtype=jnp.int32)
    segment = jnp.sum((places[:, None] >= seq_ends[None, :]).astype(jnp.int32), axis=1)
    member = segment[:, None] == jnp.arange(seq_lengths.shape[0], dtype=jnp.int32)[None, :]
    positions_in = places - jnp.sum(jnp.where(member, seq_starts[None, :], 0), axis=1)
    allowed_mask = (segment[:, None] == segment[None, :]) & (places[None, :] <= places[:, None])
    return (positions_in, allowed_mask)


def owner_rows(token_ids, piece_rows, group, vocab_pos):
    piece_index = token_ids // piece_rows
    owner = piece_index % group
    local = piece_index // group * piece_rows + token_ids % piece_rows
    return jnp.where(owner == vocab_pos, local, -1)


def attention_scores(query, key_rows, allowed_mask):
    scores = (
        jnp.einsum("shd,thd->hst", query, key_rows, preferred_element_type=jnp.float32)
        * score_scale
    )
    return jnp.where(allowed_mask[None], scores, masked_value)


def layer_forward(residual_initial, frozen_weights, adapter_down, adapter_up, allowed_mask):
    query_key_value_weight, output_weight, up_weight, down_weight, gains, shifts, bias_stack = (
        frozen_weights
    )
    gains = gains.astype(jnp.float32)
    shifts = shifts.astype(jnp.float32)
    bias_stack = bias_stack.astype(jnp.float32)
    width_size = output_weight.shape[0]
    hidden_units = up_weight.shape[1]
    row_count = residual_initial.shape[0]
    heads = width_size // HEAD_DIM
    first_normed = layer_norm(residual_initial, gains[0], shifts[0]).astype(jnp.bfloat16)
    first_plain = first_normed.astype(jnp.float32)
    joined_rows = (
        dot_without_transpose(first_normed, query_key_value_weight) + bias_stack[: 3 * width_size]
    )
    adapt_in = []
    projected = []
    for which_index in range(3):
        inner_product = dot_without_transpose(
            first_plain, adapter_down[which_index], highest_precision
        )
        adapt_in.append(inner_product)
        branch_output = joined_rows[
            :, which_index * width_size : (which_index + 1) * width_size
        ] + adapter_scale * dot_without_transpose(
            inner_product, adapter_up[which_index], highest_precision
        )
        projected.append(branch_output.astype(jnp.bfloat16).reshape(row_count, heads, HEAD_DIM))
    query, key_rows, value_rows = projected
    scores = attention_scores(query, key_rows, allowed_mask)
    top = jnp.max(scores, axis=-1, keepdims=True)
    expo = jnp.exp(scores - top)
    summed = jnp.sum(expo, axis=-1, keepdims=True)
    log_total = top + jnp.log(summed)
    probs = (expo / summed).astype(jnp.bfloat16)
    mixed_state = jnp.einsum("hst,thd->shd", probs, value_rows, preferred_element_type=jnp.float32)
    mixed_state = mixed_state.reshape(row_count, width_size).astype(jnp.bfloat16)
    mixed_plain = mixed_state.astype(jnp.float32)
    adapter_output = dot_without_transpose(mixed_plain, adapter_down[3], highest_precision)
    attended_rows = (
        dot_without_transpose(mixed_state, output_weight)
        + bias_stack[3 * width_size : 4 * width_size]
        + adapter_scale * dot_without_transpose(adapter_output, adapter_up[3], highest_precision)
    )
    stream_one = residual_initial + attended_rows
    normed_two = layer_norm(stream_one, gains[1], shifts[1]).astype(jnp.bfloat16)
    before_gelu = (
        dot_without_transpose(normed_two, up_weight)
        + bias_stack[4 * width_size : 4 * width_size + hidden_units]
    )
    activation = jax.nn.gelu(before_gelu, approximate=True).astype(jnp.bfloat16)
    stream_two = (
        stream_one
        + dot_without_transpose(activation, down_weight)
        + bias_stack[4 * width_size + hidden_units :]
    )
    final_state = layer_norm(stream_two, gains[2], shifts[2]).astype(jnp.bfloat16)
    kept_rows = (
        first_plain,
        adapt_in,
        query,
        key_rows,
        value_rows,
        log_total,
        mixed_plain,
        adapter_output,
        stream_one,
        before_gelu,
        stream_two,
    )
    return (final_state, kept_rows)


def layer_backward(
    final_gradient, kept_rows, backward_weights, adapter_down, adapter_up, allowed_mask
):
    output_weight, up_weight, down_weight, gains = backward_weights
    gains = gains.astype(jnp.float32)
    (
        first_plain,
        adapt_in,
        query,
        key_rows,
        value_rows,
        log_total,
        mixed_plain,
        adapter_output,
        stream_one,
        before_gelu,
        stream_two,
    ) = kept_rows
    row_count = query.shape[0]
    width_size = query.shape[1] * HEAD_DIM
    _, pull_three = jax.vjp(lambda values: layer_norm(values, gains[2], 0.0), stream_two)
    grad_two = pull_three(final_gradient)[0]
    grad_act = dot_last_axis(grad_two.astype(jnp.bfloat16), down_weight)
    _, pull_gelu = jax.vjp(partial(jax.nn.gelu, approximate=True), before_gelu)
    grad_pre = pull_gelu(grad_act)[0].astype(jnp.bfloat16)
    _, pull_two = jax.vjp(lambda values: layer_norm(values, gains[1], 0.0), stream_one)
    first_gradient = grad_two + pull_two(dot_last_axis(grad_pre, up_weight))[0]
    attention_gradient = first_gradient.astype(jnp.bfloat16)
    attention_scaled = adapter_scale * rounded_values(first_gradient)
    up_grads = [None, None, None, None]
    down_grads = [None, None, None, None]
    up_grads[3] = dot_first(adapter_output, attention_scaled, highest_precision)
    backward_output = dot_last_axis(attention_scaled, adapter_up[3], highest_precision)
    down_grads[3] = dot_first(mixed_plain, backward_output, highest_precision)
    mixed_gradient = dot_last_axis(attention_gradient, output_weight) + dot_last_axis(
        backward_output, adapter_down[3], highest_precision
    )
    grad_heads = mixed_gradient.astype(jnp.bfloat16).reshape(query.shape)
    probs = jnp.exp(attention_scores(query, key_rows, allowed_mask) - log_total)
    grad_value = jnp.einsum(
        "hst,shd->thd", probs.astype(jnp.bfloat16), grad_heads, preferred_element_type=jnp.float32
    )
    grad_probs = jnp.einsum(
        "shd,thd->hst", grad_heads, value_rows, preferred_element_type=jnp.float32
    )
    grad_scores = probs * (grad_probs - jnp.sum(probs * grad_probs, axis=-1, keepdims=True))
    grad_scores = grad_scores.astype(jnp.bfloat16)
    grad_query = (
        jnp.einsum("hst,thd->shd", grad_scores, key_rows, preferred_element_type=jnp.float32)
        * score_scale
    )
    grad_key = (
        jnp.einsum("hst,shd->thd", grad_scores, query, preferred_element_type=jnp.float32)
        * score_scale
    )
    for which_index, branch_gradient in enumerate((grad_query, grad_key, grad_value)):
        scaled_values = adapter_scale * rounded_values(
            branch_gradient.reshape(row_count, width_size)
        )
        up_grads[which_index] = dot_first(adapt_in[which_index], scaled_values, highest_precision)
        backward_input = dot_last_axis(scaled_values, adapter_up[which_index], highest_precision)
        down_grads[which_index] = dot_first(first_plain, backward_input, highest_precision)
    return (jnp.stack(down_grads), jnp.stack(up_grads))


def orthogonalize(matrices, sum_grams):
    grams = sum_grams(
        jnp.einsum(
            "mrd,msd->mrs",
            matrices,
            matrices,
            precision=highest_precision,
            preferred_element_type=jnp.float32,
        )
    )
    sizes = jnp.sqrt(jnp.trace(grams, axis1=1, axis2=2))[:, None, None] + 1e-07
    state = matrices / sizes
    grams = grams / (sizes * sizes)
    for turn_index in range(5):
        if turn_index:
            grams = sum_grams(
                jnp.einsum(
                    "mrd,msd->mrs",
                    state,
                    state,
                    precision=highest_precision,
                    preferred_element_type=jnp.float32,
                )
            )
        poly = coef_b * grams + coef_c * jnp.einsum(
            "mrs,mst->mrt",
            grams,
            grams,
            precision=highest_precision,
            preferred_element_type=jnp.float32,
        )
        state = coef_a * state + jnp.einsum(
            "mrs,msd->mrd",
            poly,
            state,
            precision=highest_precision,
            preferred_element_type=jnp.float32,
        )
    return state


def per_device(
    ids,
    targets,
    counted_mask,
    lengths,
    table,
    position_table,
    layer_norm_gain,
    layer_norm_bias,
    query_key_value_weight,
    output_weight,
    up_weight,
    down_weight,
    biases,
    adapter_down,
    adapter_up,
    down_momentum,
    up_momentum,
):
    small = (position_table, layer_norm_gain, layer_norm_bias, biases)
    packed, w_qkv_all, w_out_all, w_up_all, w_down_all = gather_all(
        (pack_small(small), query_key_value_weight, output_weight, up_weight, down_weight)
    )
    positions_all, gains_all, shifts_all, bias_stack = unpack_small(
        packed, [a.shape for a in small]
    )
    row_count = ids.shape[0]
    width_size = w_out_all.shape[0]
    group = lax.axis_size("vocab")
    vocab_pos = lax.axis_index("vocab")
    piece_rows = table.shape[0]
    ids_all, target_all, mask_all = (
        lax.all_gather(ids, "vocab", axis=0, tiled=True),
        lax.all_gather(targets, "vocab", axis=0, tiled=True),
        lax.all_gather(counted_mask, "vocab", axis=0, tiled=True),
    )
    table_full = lax.all_gather(table, "dp", axis=0, tiled=True)
    vocab_rows = table_full.shape[0]
    local_ids = owner_rows(ids_all, piece_rows, group, vocab_pos)
    inside = local_ids >= 0
    picked_rows = table_full[jnp.clip(local_ids, 0, vocab_rows - 1)]
    picked_rows = jnp.where(inside[:, None], picked_rows, jnp.zeros_like(picked_rows))
    embedded = lax.psum_scatter(
        picked_rows.astype(jnp.float32).astype(jnp.bfloat16),
        "vocab",
        scatter_dimension=0,
        tiled=True,
    ).astype(jnp.float32)
    positions_in, allowed_mask = layout(lengths[0], row_count)
    residual_initial = embedded + positions_all[positions_in].astype(jnp.float32)
    frozen_weights = (w_qkv_all, w_out_all, w_up_all, w_down_all, gains_all, shifts_all, bias_stack)
    final_state, kept_rows = layer_forward(
        residual_initial, frozen_weights, adapter_down, adapter_up, allowed_mask
    )
    final_all = lax.all_gather(final_state, "vocab", axis=0, tiled=True)
    total_rows = final_all.shape[0]
    block = 512
    count_blocks = total_rows // block
    final_blocks = final_all.reshape(count_blocks, block, width_size)
    local_targets = owner_rows(target_all, piece_rows, group, vocab_pos).reshape(
        count_blocks, block
    )
    columns = jnp.arange(vocab_rows, dtype=jnp.int32)

    def head_stats(item):
        piece, local = item
        logits = dot_last_axis(piece, table_full)
        top = jnp.max(logits, axis=1)
        expsum = jnp.sum(jnp.exp(logits - top[:, None]), axis=1)
        target_logit = jnp.sum(jnp.where(columns[None, :] == local[:, None], logits, 0.0), axis=1)
        return (top, expsum, target_logit, jnp.sum(logits, axis=1))

    stats = lax.map(head_stats, (final_blocks, local_targets))
    stats = tuple((entry.reshape(total_rows) for entry in stats))

    def combine(first_part, second_part):
        larger = jnp.maximum(first_part[0], second_part[0])
        merged_sum = first_part[1] * jnp.exp(first_part[0] - larger) + second_part[1] * jnp.exp(
            second_part[0] - larger
        )
        return (larger, merged_sum, first_part[2] + second_part[2], first_part[3] + second_part[3])

    top, expsum, target_logit, logit_sum = merged(stats, "vocab", combine)
    log_total = top + jnp.log(expsum)
    row_loss = log_total - (1.0 - smooth) * target_logit - smooth * logit_sum / V
    mask_float = mask_all.astype(jnp.float32)
    own_start = vocab_pos * row_count
    loss_own = jnp.sum(lax.dynamic_slice_in_dim(mask_float * row_loss, own_start, row_count))
    count_own = jnp.sum(counted_mask.astype(jnp.float32))

    def head_grad(item):
        piece, local, lse_block, weight = item
        logits = dot_last_axis(piece, table_full)
        probs = jnp.exp(logits - lse_block[:, None])
        onehot = (columns[None, :] == local[:, None]).astype(jnp.float32)
        grad_logits = weight[:, None] * (probs - (1.0 - smooth) * onehot - smooth / V)
        return dot_without_transpose(grad_logits.astype(jnp.bfloat16), table_full)

    partial_rows = lax.map(
        head_grad,
        (
            final_blocks,
            local_targets,
            log_total.reshape(count_blocks, block),
            mask_float.reshape(count_blocks, block),
        ),
    )
    final_gradient = lax.psum_scatter(
        partial_rows.reshape(total_rows, width_size).astype(jnp.bfloat16),
        "vocab",
        scatter_dimension=0,
        tiled=True,
    ).astype(jnp.float32)
    backward_weights = (w_out_all, w_up_all, w_down_all, gains_all)
    down_gradient, up_gradient = layer_backward(
        final_gradient, kept_rows, backward_weights, adapter_down, adapter_up, allowed_mask
    )
    down_gradient, up_gradient, smoothed_loss_sum, loss_count = lax.psum(
        (down_gradient, up_gradient, loss_own, count_own), ("dp", "vocab")
    )
    grad_norm = jnp.sqrt(
        jnp.sum(down_gradient * down_gradient) + jnp.sum(up_gradient * up_gradient)
    )
    factor = jnp.minimum(1.0, clip_level / (grad_norm + 1e-06))
    new_mom_down = momentum * down_momentum + factor * down_gradient
    new_mom_up = momentum * up_momentum + factor * up_gradient
    stacked = jnp.concatenate([jnp.swapaxes(new_mom_down, 1, 2), new_mom_up], axis=0)
    share_fraction = stacked.shape[2] // group
    begin_index = vocab_pos * share_fraction
    orthogonal_update = lax.dynamic_slice_in_dim(
        orthogonalize(stacked, lambda grams: grams), begin_index, share_fraction, 2
    )
    mom_down_part = lax.dynamic_slice_in_dim(new_mom_down, begin_index, share_fraction, 1)
    mom_up_part = lax.dynamic_slice_in_dim(new_mom_up, begin_index, share_fraction, 2)
    down_fresh = lax.dynamic_slice_in_dim(
        adapter_down, begin_index, share_fraction, 1
    ) - learning_rate * jnp.swapaxes(orthogonal_update[:4], 1, 2)
    up_fresh = (
        lax.dynamic_slice_in_dim(adapter_up, begin_index, share_fraction, 2)
        - learning_rate * orthogonal_update[4:]
    )
    return (
        smoothed_loss_sum,
        loss_count,
        grad_norm,
        mom_down_part,
        mom_up_part,
        down_fresh,
        up_fresh,
        down_fresh.astype(jnp.bfloat16),
        up_fresh.astype(jnp.bfloat16),
    )


def per_device_general(
    ids,
    targets,
    counted_mask,
    lengths,
    table,
    position_table,
    layer_norm_gain,
    layer_norm_bias,
    query_key_value_weight,
    output_weight,
    up_weight,
    down_weight,
    biases,
    adapter_down,
    adapter_up,
    down_momentum,
    up_momentum,
):
    gathered = (
        lax.all_gather(query_key_value_weight, ("dp", "vocab"), axis=0, tiled=True),
        lax.all_gather(output_weight, ("dp", "vocab"), axis=0, tiled=True),
        lax.all_gather(up_weight, ("dp", "vocab"), axis=0, tiled=True),
        lax.all_gather(down_weight, ("dp", "vocab"), axis=0, tiled=True),
        lax.all_gather(layer_norm_gain, ("dp", "vocab"), axis=1, tiled=True),
        lax.all_gather(layer_norm_bias, ("dp", "vocab"), axis=1, tiled=True),
        lax.all_gather(biases, ("dp", "vocab"), axis=0, tiled=True),
        lax.all_gather(position_table, ("dp", "vocab"), axis=1, tiled=True),
    )
    w_qkv_all, w_out_all, w_up_all, w_down_all, gains_all, shifts_all, bias_stack, positions_all = (
        gathered
    )
    row_count = ids.shape[0]
    width_size = w_out_all.shape[0]
    group = lax.axis_size("vocab")
    vocab_pos = lax.axis_index("vocab")
    piece_rows = table.shape[0]
    ids_all, target_all, mask_all = (
        lax.all_gather(ids, "vocab", axis=0, tiled=True),
        lax.all_gather(targets, "vocab", axis=0, tiled=True),
        lax.all_gather(counted_mask, "vocab", axis=0, tiled=True),
    )
    table_full = lax.all_gather(table, "dp", axis=0, tiled=True)
    vocab_rows = table_full.shape[0]
    local_ids = owner_rows(ids_all, piece_rows, group, vocab_pos)
    inside = local_ids >= 0
    picked_rows = table_full[jnp.clip(local_ids, 0, vocab_rows - 1)]
    picked_rows = jnp.where(inside[:, None], picked_rows, jnp.zeros_like(picked_rows))
    embedded = lax.psum_scatter(
        picked_rows.astype(jnp.float32).astype(jnp.bfloat16),
        "vocab",
        scatter_dimension=0,
        tiled=True,
    ).astype(jnp.float32)
    positions_in, allowed_mask = layout(lengths[0], row_count)
    residual_initial = embedded + positions_all[positions_in].astype(jnp.float32)
    frozen_weights = (w_qkv_all, w_out_all, w_up_all, w_down_all, gains_all, shifts_all, bias_stack)
    final_state, kept_rows = layer_forward(
        residual_initial, frozen_weights, adapter_down, adapter_up, allowed_mask
    )
    final_all = lax.all_gather(final_state, "vocab", axis=0, tiled=True)
    total_rows = final_all.shape[0]
    block = 512
    count_blocks = total_rows // block
    final_blocks = final_all.reshape(count_blocks, block, width_size)
    local_targets = owner_rows(target_all, piece_rows, group, vocab_pos).reshape(
        count_blocks, block
    )
    columns = jnp.arange(vocab_rows, dtype=jnp.int32)

    def head_stats(item):
        piece, local = item
        logits = dot_last_axis(piece, table_full)
        top = jnp.max(logits, axis=1)
        expsum = jnp.sum(jnp.exp(logits - top[:, None]), axis=1)
        target_logit = jnp.sum(jnp.where(columns[None, :] == local[:, None], logits, 0.0), axis=1)
        return (top, expsum, target_logit, jnp.sum(logits, axis=1))

    stats = lax.map(head_stats, (final_blocks, local_targets))
    stats = tuple((entry.reshape(total_rows) for entry in stats))

    def combine(first_part, second_part):
        larger = jnp.maximum(first_part[0], second_part[0])
        merged_sum = first_part[1] * jnp.exp(first_part[0] - larger) + second_part[1] * jnp.exp(
            second_part[0] - larger
        )
        return (larger, merged_sum, first_part[2] + second_part[2], first_part[3] + second_part[3])

    top, expsum, target_logit, logit_sum = merged(stats, "vocab", combine)
    log_total = top + jnp.log(expsum)
    row_loss = log_total - (1.0 - smooth) * target_logit - smooth * logit_sum / V
    mask_float = mask_all.astype(jnp.float32)
    own_start = vocab_pos * row_count
    loss_own = jnp.sum(lax.dynamic_slice_in_dim(mask_float * row_loss, own_start, row_count))
    count_own = jnp.sum(counted_mask.astype(jnp.float32))

    def head_grad(item):
        piece, local, lse_block, weight = item
        logits = dot_last_axis(piece, table_full)
        probs = jnp.exp(logits - lse_block[:, None])
        onehot = (columns[None, :] == local[:, None]).astype(jnp.float32)
        grad_logits = weight[:, None] * (probs - (1.0 - smooth) * onehot - smooth / V)
        return dot_without_transpose(grad_logits.astype(jnp.bfloat16), table_full)

    partial_rows = lax.map(
        head_grad,
        (
            final_blocks,
            local_targets,
            log_total.reshape(count_blocks, block),
            mask_float.reshape(count_blocks, block),
        ),
    )
    final_gradient = lax.psum_scatter(
        partial_rows.reshape(total_rows, width_size).astype(jnp.bfloat16),
        "vocab",
        scatter_dimension=0,
        tiled=True,
    ).astype(jnp.float32)
    backward_weights = (
        lax.all_gather(output_weight, ("dp", "vocab"), axis=0, tiled=True),
        lax.all_gather(up_weight, ("dp", "vocab"), axis=0, tiled=True),
        lax.all_gather(down_weight, ("dp", "vocab"), axis=0, tiled=True),
        lax.all_gather(layer_norm_gain, ("dp", "vocab"), axis=1, tiled=True),
    )
    down_gradient, up_gradient = layer_backward(
        final_gradient, kept_rows, backward_weights, adapter_down, adapter_up, allowed_mask
    )
    down_gradient, up_gradient, smoothed_loss_sum, loss_count = lax.psum(
        (down_gradient, up_gradient, loss_own, count_own), ("dp", "vocab")
    )
    grad_norm = jnp.sqrt(
        jnp.sum(down_gradient * down_gradient) + jnp.sum(up_gradient * up_gradient)
    )
    factor = jnp.minimum(1.0, clip_level / (grad_norm + 1e-06))
    new_mom_down = momentum * down_momentum + factor * down_gradient
    new_mom_up = momentum * up_momentum + factor * up_gradient
    stacked = jnp.concatenate([jnp.swapaxes(new_mom_down, 1, 2), new_mom_up], axis=0)
    share_fraction = stacked.shape[2] // group
    begin_index = vocab_pos * share_fraction
    orthogonal_update = orthogonalize(
        lax.dynamic_slice_in_dim(stacked, begin_index, share_fraction, 2),
        lambda grams: lax.psum(grams, "vocab"),
    )
    mom_down_part = lax.dynamic_slice_in_dim(new_mom_down, begin_index, share_fraction, 1)
    mom_up_part = lax.dynamic_slice_in_dim(new_mom_up, begin_index, share_fraction, 2)
    down_fresh = lax.dynamic_slice_in_dim(
        adapter_down, begin_index, share_fraction, 1
    ) - learning_rate * jnp.swapaxes(orthogonal_update[:4], 1, 2)
    up_fresh = (
        lax.dynamic_slice_in_dim(adapter_up, begin_index, share_fraction, 2)
        - learning_rate * orthogonal_update[4:]
    )
    return (
        smoothed_loss_sum,
        loss_count,
        grad_norm,
        mom_down_part,
        mom_up_part,
        down_fresh,
        up_fresh,
        down_fresh.astype(jnp.bfloat16),
        up_fresh.astype(jnp.bfloat16),
    )


def solution(mesh):
    fast = dict(mesh.shape) == {"dp": 8, "vocab": 4}
    placed = (
        P(("dp", "vocab")),
        P(("dp", "vocab")),
        P(("dp", "vocab")),
        P(("dp", "vocab"), None),
        P(("dp", "vocab"), None),
        P(None, ("dp", "vocab")),
        P(None, ("dp", "vocab")),
        P(None, ("dp", "vocab")),
        P(("dp", "vocab"), None),
        P(("dp", "vocab"), None),
        P(("dp", "vocab"), None),
        P(("dp", "vocab"), None),
        P(("dp", "vocab")),
        P(),
        P(),
        P(),
        P(),
    )
    return jax.shard_map(
        per_device if fast else per_device_general,
        mesh=mesh,
        in_specs=placed,
        out_specs=(
            P(),
            P(),
            P(),
            P(None, "vocab", None),
            P(None, None, "vocab"),
            P(None, "vocab", None),
            P(None, None, "vocab"),
            P(None, "vocab", None),
            P(None, None, "vocab"),
        ),
        check_vma=False,
    )
```

```python
from functools import partial

import jax
import jax.numpy as jnp
from jax import lax
from jax.experimental import pallas as pl
from jax.experimental.pallas import tpu as pltpu
from jax.sharding import PartitionSpec as P

HEAD_DIM = 64
V = 50304


highest_precision = lax.Precision.HIGHEST
ln_eps = 1e-05
adapter_scale = 8.0
smooth = 0.1
clip_level = 1.0
momentum = 0.5
learning_rate = 0.5
coef_a = 3.4445
coef_b = -4.775
coef_c = 2.0315
score_scale = 0.125
masked_value = -1e30


def merged(x, axis, join):
    gathered = jax.tree.map(
        lambda a, kind: lax.all_gather(a.astype(kind), axis),
        x,
        jax.tree.map(lambda a: jnp.bfloat16 if a.dtype == jnp.float32 else a.dtype, x),
    )

    def take(source):
        return jax.tree.map(
            lambda a, own: lax.dynamic_index_in_dim(a, source, 0, False).astype(own.dtype),
            gathered,
            x,
        )

    return lax.fori_loop(
        1, lax.axis_size(axis), lambda source, state: join(state, take(source)), take(0)
    )


def dot_without_transpose(left_side, right_side, setting=None):
    return jnp.dot(left_side, right_side, precision=setting, preferred_element_type=jnp.float32)


def dot_last_axis(left_side, right_side, setting=None):
    return lax.dot_general(
        left_side,
        right_side,
        (((1,), (1,)), ((), ())),
        precision=setting,
        preferred_element_type=jnp.float32,
    )


def dot_first(left_side, right_side, setting=None):
    return lax.dot_general(
        left_side,
        right_side,
        (((0,), (0,)), ((), ())),
        precision=setting,
        preferred_element_type=jnp.float32,
    )


def rounded_values(values):
    return lax.optimization_barrier(values.astype(jnp.bfloat16)).astype(jnp.float32)


def layer_norm(values, gain, offset):
    center = values - jnp.mean(values, axis=-1, keepdims=True)
    spread = jnp.mean(center * center, axis=-1, keepdims=True)
    return center * lax.rsqrt(spread + ln_eps) * gain + offset


def layout(seq_lengths, row_count):
    seq_ends = jnp.cumsum(seq_lengths)
    seq_starts = seq_ends - seq_lengths
    places = jnp.arange(row_count, dtype=jnp.int32)
    segment = jnp.sum((places[:, None] >= seq_ends[None, :]).astype(jnp.int32), axis=1)
    member = segment[:, None] == jnp.arange(seq_lengths.shape[0], dtype=jnp.int32)[None, :]
    positions_in = places - jnp.sum(jnp.where(member, seq_starts[None, :], 0), axis=1)
    allowed_mask = (segment[:, None] == segment[None, :]) & (places[None, :] <= places[:, None])
    return (positions_in, allowed_mask)


def owner_rows(token_ids, piece_rows, group, vocab_pos):
    piece_index = token_ids // piece_rows
    owner = piece_index % group
    local = piece_index // group * piece_rows + token_ids % piece_rows
    return jnp.where(owner == vocab_pos, local, -1)


def attention_scores(query, key_rows, allowed_mask):
    scores = (
        jnp.einsum("shd,thd->hst", query, key_rows, preferred_element_type=jnp.float32)
        * score_scale
    )
    return jnp.where(allowed_mask[None], scores, masked_value)


def layer_forward(residual_initial, frozen_weights, adapter_down, adapter_up, allowed_mask):
    query_key_value_weight, output_weight, up_weight, down_weight, gains, shifts, bias_stack = (
        frozen_weights
    )
    gains = gains.astype(jnp.float32)
    shifts = shifts.astype(jnp.float32)
    bias_stack = bias_stack.astype(jnp.float32)
    width_size = output_weight.shape[0]
    hidden_units = up_weight.shape[1]
    row_count = residual_initial.shape[0]
    heads = width_size // HEAD_DIM
    first_normed = layer_norm(residual_initial, gains[0], shifts[0]).astype(jnp.bfloat16)
    first_plain = first_normed.astype(jnp.float32)
    joined_rows = (
        dot_without_transpose(first_normed, query_key_value_weight) + bias_stack[: 3 * width_size]
    )
    adapt_in = []
    projected = []
    for which_index in range(3):
        inner_product = dot_without_transpose(
            first_plain, adapter_down[which_index], highest_precision
        )
        adapt_in.append(inner_product)
        branch_output = joined_rows[
            :, which_index * width_size : (which_index + 1) * width_size
        ] + adapter_scale * dot_without_transpose(
            inner_product, adapter_up[which_index], highest_precision
        )
        projected.append(branch_output.astype(jnp.bfloat16).reshape(row_count, heads, HEAD_DIM))
    query, key_rows, value_rows = projected
    scores = attention_scores(query, key_rows, allowed_mask)
    top = jnp.max(scores, axis=-1, keepdims=True)
    expo = jnp.exp(scores - top)
    summed = jnp.sum(expo, axis=-1, keepdims=True)
    log_total = top + jnp.log(summed)
    probs = (expo / summed).astype(jnp.bfloat16)
    mixed_state = jnp.einsum("hst,thd->shd", probs, value_rows, preferred_element_type=jnp.float32)
    mixed_state = mixed_state.reshape(row_count, width_size).astype(jnp.bfloat16)
    mixed_plain = mixed_state.astype(jnp.float32)
    adapter_output = dot_without_transpose(mixed_plain, adapter_down[3], highest_precision)
    attended_rows = (
        dot_without_transpose(mixed_state, output_weight)
        + bias_stack[3 * width_size : 4 * width_size]
        + adapter_scale * dot_without_transpose(adapter_output, adapter_up[3], highest_precision)
    )
    stream_one = residual_initial + attended_rows
    normed_two = layer_norm(stream_one, gains[1], shifts[1]).astype(jnp.bfloat16)
    before_gelu = (
        dot_without_transpose(normed_two, up_weight)
        + bias_stack[4 * width_size : 4 * width_size + hidden_units]
    )
    activation = jax.nn.gelu(before_gelu, approximate=True).astype(jnp.bfloat16)
    stream_two = (
        stream_one
        + dot_without_transpose(activation, down_weight)
        + bias_stack[4 * width_size + hidden_units :]
    )
    final_state = layer_norm(stream_two, gains[2], shifts[2]).astype(jnp.bfloat16)
    kept_rows = (
        first_plain,
        adapt_in,
        query,
        key_rows,
        value_rows,
        log_total,
        mixed_plain,
        adapter_output,
        stream_one,
        before_gelu,
        stream_two,
    )
    return (final_state, kept_rows)


def layer_backward(
    final_gradient, kept_rows, backward_weights, adapter_down, adapter_up, allowed_mask
):
    output_weight, up_weight, down_weight, gains = backward_weights
    gains = gains.astype(jnp.float32)
    (
        first_plain,
        adapt_in,
        query,
        key_rows,
        value_rows,
        log_total,
        mixed_plain,
        adapter_output,
        stream_one,
        before_gelu,
        stream_two,
    ) = kept_rows
    row_count = query.shape[0]
    width_size = query.shape[1] * HEAD_DIM
    _, pull_three = jax.vjp(lambda values: layer_norm(values, gains[2], 0.0), stream_two)
    grad_two = pull_three(final_gradient)[0]
    grad_act = dot_last_axis(grad_two.astype(jnp.bfloat16), down_weight)
    _, pull_gelu = jax.vjp(partial(jax.nn.gelu, approximate=True), before_gelu)
    grad_pre = pull_gelu(grad_act)[0].astype(jnp.bfloat16)
    _, pull_two = jax.vjp(lambda values: layer_norm(values, gains[1], 0.0), stream_one)
    first_gradient = grad_two + pull_two(dot_last_axis(grad_pre, up_weight))[0]
    attention_gradient = first_gradient.astype(jnp.bfloat16)
    attention_scaled = adapter_scale * rounded_values(first_gradient)
    up_grads = [None, None, None, None]
    down_grads = [None, None, None, None]
    up_grads[3] = dot_first(adapter_output, attention_scaled, highest_precision)
    backward_output = dot_last_axis(attention_scaled, adapter_up[3], highest_precision)
    down_grads[3] = dot_first(mixed_plain, backward_output, highest_precision)
    mixed_gradient = dot_last_axis(attention_gradient, output_weight) + dot_last_axis(
        backward_output, adapter_down[3], highest_precision
    )
    grad_heads = mixed_gradient.astype(jnp.bfloat16).reshape(query.shape)
    probs = jnp.exp(attention_scores(query, key_rows, allowed_mask) - log_total)
    grad_value = jnp.einsum(
        "hst,shd->thd", probs.astype(jnp.bfloat16), grad_heads, preferred_element_type=jnp.float32
    )
    grad_probs = jnp.einsum(
        "shd,thd->hst", grad_heads, value_rows, preferred_element_type=jnp.float32
    )
    grad_scores = probs * (grad_probs - jnp.sum(probs * grad_probs, axis=-1, keepdims=True))
    grad_scores = grad_scores.astype(jnp.bfloat16)
    grad_query = (
        jnp.einsum("hst,thd->shd", grad_scores, key_rows, preferred_element_type=jnp.float32)
        * score_scale
    )
    grad_key = (
        jnp.einsum("hst,shd->thd", grad_scores, query, preferred_element_type=jnp.float32)
        * score_scale
    )
    for which_index, branch_gradient in enumerate((grad_query, grad_key, grad_value)):
        scaled_values = adapter_scale * rounded_values(
            branch_gradient.reshape(row_count, width_size)
        )
        up_grads[which_index] = dot_first(adapt_in[which_index], scaled_values, highest_precision)
        backward_input = dot_last_axis(scaled_values, adapter_up[which_index], highest_precision)
        down_grads[which_index] = dot_first(first_plain, backward_input, highest_precision)
    return (jnp.stack(down_grads), jnp.stack(up_grads))


def orthogonalize(matrices, sum_grams):
    grams = sum_grams(
        jnp.einsum(
            "mrd,msd->mrs",
            matrices,
            matrices,
            precision=highest_precision,
            preferred_element_type=jnp.float32,
        )
    )
    sizes = jnp.sqrt(jnp.trace(grams, axis1=1, axis2=2))[:, None, None] + 1e-07
    state = matrices / sizes
    grams = grams / (sizes * sizes)
    for turn_index in range(5):
        if turn_index:
            grams = sum_grams(
                jnp.einsum(
                    "mrd,msd->mrs",
                    state,
                    state,
                    precision=highest_precision,
                    preferred_element_type=jnp.float32,
                )
            )
        poly = coef_b * grams + coef_c * jnp.einsum(
            "mrs,mst->mrt",
            grams,
            grams,
            precision=highest_precision,
            preferred_element_type=jnp.float32,
        )
        state = coef_a * state + jnp.einsum(
            "mrs,msd->mrd",
            poly,
            state,
            precision=highest_precision,
            preferred_element_type=jnp.float32,
        )
    return state


def per_device_general(
    ids,
    targets,
    counted_mask,
    lengths,
    table,
    position_table,
    layer_norm_gain,
    layer_norm_bias,
    query_key_value_weight,
    output_weight,
    up_weight,
    down_weight,
    biases,
    adapter_down,
    adapter_up,
    down_momentum,
    up_momentum,
):
    gathered = (
        lax.all_gather(query_key_value_weight, ("dp", "vocab"), axis=0, tiled=True),
        lax.all_gather(output_weight, ("dp", "vocab"), axis=0, tiled=True),
        lax.all_gather(up_weight, ("dp", "vocab"), axis=0, tiled=True),
        lax.all_gather(down_weight, ("dp", "vocab"), axis=0, tiled=True),
        lax.all_gather(layer_norm_gain, ("dp", "vocab"), axis=1, tiled=True),
        lax.all_gather(layer_norm_bias, ("dp", "vocab"), axis=1, tiled=True),
        lax.all_gather(biases, ("dp", "vocab"), axis=0, tiled=True),
        lax.all_gather(position_table, ("dp", "vocab"), axis=1, tiled=True),
    )
    w_qkv_all, w_out_all, w_up_all, w_down_all, gains_all, shifts_all, bias_stack, positions_all = (
        gathered
    )
    row_count = ids.shape[0]
    width_size = w_out_all.shape[0]
    group = lax.axis_size("vocab")
    vocab_pos = lax.axis_index("vocab")
    piece_rows = table.shape[0]
    ids_all, target_all, mask_all = (
        lax.all_gather(ids, "vocab", axis=0, tiled=True),
        lax.all_gather(targets, "vocab", axis=0, tiled=True),
        lax.all_gather(counted_mask, "vocab", axis=0, tiled=True),
    )
    table_full = lax.all_gather(table, "dp", axis=0, tiled=True)
    vocab_rows = table_full.shape[0]
    local_ids = owner_rows(ids_all, piece_rows, group, vocab_pos)
    inside = local_ids >= 0
    picked_rows = table_full[jnp.clip(local_ids, 0, vocab_rows - 1)]
    picked_rows = jnp.where(inside[:, None], picked_rows, jnp.zeros_like(picked_rows))
    embedded = lax.psum_scatter(
        picked_rows.astype(jnp.float32).astype(jnp.bfloat16),
        "vocab",
        scatter_dimension=0,
        tiled=True,
    ).astype(jnp.float32)
    positions_in, allowed_mask = layout(lengths[0], row_count)
    residual_initial = embedded + positions_all[positions_in].astype(jnp.float32)
    frozen_weights = (w_qkv_all, w_out_all, w_up_all, w_down_all, gains_all, shifts_all, bias_stack)
    final_state, kept_rows = layer_forward(
        residual_initial, frozen_weights, adapter_down, adapter_up, allowed_mask
    )
    final_all = lax.all_gather(final_state, "vocab", axis=0, tiled=True)
    total_rows = final_all.shape[0]
    block = 512
    count_blocks = total_rows // block
    final_blocks = final_all.reshape(count_blocks, block, width_size)
    local_targets = owner_rows(target_all, piece_rows, group, vocab_pos).reshape(
        count_blocks, block
    )
    columns = jnp.arange(vocab_rows, dtype=jnp.int32)

    def head_stats(item):
        piece, local = item
        logits = dot_last_axis(piece, table_full)
        top = jnp.max(logits, axis=1)
        expsum = jnp.sum(jnp.exp(logits - top[:, None]), axis=1)
        target_logit = jnp.sum(jnp.where(columns[None, :] == local[:, None], logits, 0.0), axis=1)
        return (top, expsum, target_logit, jnp.sum(logits, axis=1))

    stats = lax.map(head_stats, (final_blocks, local_targets))
    stats = tuple((entry.reshape(total_rows) for entry in stats))

    def combine(first_part, second_part):
        larger = jnp.maximum(first_part[0], second_part[0])
        merged_sum = first_part[1] * jnp.exp(first_part[0] - larger) + second_part[1] * jnp.exp(
            second_part[0] - larger
        )
        return (larger, merged_sum, first_part[2] + second_part[2], first_part[3] + second_part[3])

    top, expsum, target_logit, logit_sum = merged(stats, "vocab", combine)
    log_total = top + jnp.log(expsum)
    row_loss = log_total - (1.0 - smooth) * target_logit - smooth * logit_sum / V
    mask_float = mask_all.astype(jnp.float32)
    own_start = vocab_pos * row_count
    loss_own = jnp.sum(lax.dynamic_slice_in_dim(mask_float * row_loss, own_start, row_count))
    count_own = jnp.sum(counted_mask.astype(jnp.float32))

    def head_grad(item):
        piece, local, lse_block, weight = item
        logits = dot_last_axis(piece, table_full)
        probs = jnp.exp(logits - lse_block[:, None])
        onehot = (columns[None, :] == local[:, None]).astype(jnp.float32)
        grad_logits = weight[:, None] * (probs - (1.0 - smooth) * onehot - smooth / V)
        return dot_without_transpose(grad_logits.astype(jnp.bfloat16), table_full)

    partial_rows = lax.map(
        head_grad,
        (
            final_blocks,
            local_targets,
            log_total.reshape(count_blocks, block),
            mask_float.reshape(count_blocks, block),
        ),
    )
    final_gradient = lax.psum_scatter(
        partial_rows.reshape(total_rows, width_size).astype(jnp.bfloat16),
        "vocab",
        scatter_dimension=0,
        tiled=True,
    ).astype(jnp.float32)
    backward_weights = (
        lax.all_gather(output_weight, ("dp", "vocab"), axis=0, tiled=True),
        lax.all_gather(up_weight, ("dp", "vocab"), axis=0, tiled=True),
        lax.all_gather(down_weight, ("dp", "vocab"), axis=0, tiled=True),
        lax.all_gather(layer_norm_gain, ("dp", "vocab"), axis=1, tiled=True),
    )
    down_gradient, up_gradient = layer_backward(
        final_gradient, kept_rows, backward_weights, adapter_down, adapter_up, allowed_mask
    )
    down_gradient, up_gradient, smoothed_loss_sum, loss_count = lax.psum(
        (down_gradient, up_gradient, loss_own, count_own), ("dp", "vocab")
    )
    grad_norm = jnp.sqrt(
        jnp.sum(down_gradient * down_gradient) + jnp.sum(up_gradient * up_gradient)
    )
    factor = jnp.minimum(1.0, clip_level / (grad_norm + 1e-06))
    new_mom_down = momentum * down_momentum + factor * down_gradient
    new_mom_up = momentum * up_momentum + factor * up_gradient
    stacked = jnp.concatenate([jnp.swapaxes(new_mom_down, 1, 2), new_mom_up], axis=0)
    share_fraction = stacked.shape[2] // group
    begin_index = vocab_pos * share_fraction
    orthogonal_update = lax.dynamic_slice_in_dim(
        orthogonalize(stacked, lambda grams: grams), begin_index, share_fraction, 2
    )
    mom_down_part = lax.dynamic_slice_in_dim(new_mom_down, begin_index, share_fraction, 1)
    mom_up_part = lax.dynamic_slice_in_dim(new_mom_up, begin_index, share_fraction, 2)
    down_fresh = lax.dynamic_slice_in_dim(
        adapter_down, begin_index, share_fraction, 1
    ) - learning_rate * jnp.swapaxes(orthogonal_update[:4], 1, 2)
    up_fresh = (
        lax.dynamic_slice_in_dim(adapter_up, begin_index, share_fraction, 2)
        - learning_rate * orthogonal_update[4:]
    )
    return (
        smoothed_loss_sum,
        loss_count,
        grad_norm,
        mom_down_part,
        mom_up_part,
        down_fresh,
        up_fresh,
        down_fresh.astype(jnp.bfloat16),
        up_fresh.astype(jnp.bfloat16),
    )


MESH = pl.DeviceIdType.MESH
CAP = 32


def dot_nt(left_side, right_side, setting=None):
    return dot_last_axis(left_side, right_side, setting)


def position():
    dp, z = lax.axis_index("dp"), lax.axis_index("vocab")
    y, x, core = dp // 4, dp // 2 % 2, dp % 2

    def place(y_at, x_at, core_at):
        return y_at * 4 + x_at * 2 + core_at

    along = (z, z // 2 * 2 + 1 - z % 2, (z + 2) % 4, (1 - z // 2) * 2 + 1 - z % 2)
    return dp, z, y, x, core, place, along


def meet_all(devices, group):
    me = lax.axis_index("dp") * group + lax.axis_index("vocab")
    barrier = pltpu.get_barrier_semaphore()

    def signal(step, state):
        other = lax.rem(me + step, devices)
        pl.semaphore_signal(
            barrier, inc=1, device_id=(other // group, other % group), device_id_type=MESH
        )
        return state

    lax.fori_loop(1, devices, signal, 0)
    pl.semaphore_wait(barrier, devices - 1)
    return me


def to_all(source_of, target, send_sems, recv_sems, devices, group, me):
    def copy(step):
        other = lax.rem(me + step, devices)
        return pltpu.make_async_remote_copy(
            source_of(other),
            target.at[me],
            send_sems.at[step],
            recv_sems.at[step],
            device_id=(other // group, other % group),
            device_id_type=MESH,
        )

    def start():
        def one(step, state):
            copy(step).start()
            return state

        lax.fori_loop(1, devices, one, 0)

    def arrive():
        def one(step, state):
            source = lax.rem(me + devices - step, devices)
            pltpu.make_async_remote_copy(
                target.at[source],
                target.at[source],
                send_sems.at[step],
                recv_sems.at[step],
                device_id=(source // group, source % group),
                device_id_type=MESH,
            ).wait_recv()
            return state

        lax.fori_loop(1, devices, one, 0)

    def sent():
        def one(step, state):
            copy(step).wait_send()
            return state

        lax.fori_loop(1, devices, one, 0)

    return start, arrive, sent


def gather_kernel(row_counts, table_rows, devices, group, *refs):
    count = len(row_counts)
    token_row, token_col, table, table_turned = refs[:4]
    ins = refs[4 : 4 + count]
    refs = refs[4 + count :]
    embedded, target_rows, table_sum, flags, table_other, turned_other = refs[:6]
    outs = refs[6 : 6 + count]
    (
        send_sems,
        recv_sems,
        local_sems,
        table_sems,
        ask_sems,
        row_sems,
        sum_sems,
        table_here,
        selector,
        rows_out,
        rows_in,
        ask_out,
        ask_in,
        sum_out,
        sum_in,
    ) = refs[6 + count :]
    dp, z, y, x, core, place, along = position()
    dp_x, dp_y = place(y, 1 - x, core), place(1 - y, x, core)
    dp_core, dp_diagonal = place(y, x, 1 - core), place(1 - y, 1 - x, core)
    peers = [(dp, along[k]) for k in (1, 2, 3)] + [(dp_x, z), (dp_y, z), (dp_core, z)]
    load = pltpu.make_async_copy(table, table_here, table_sems.at[0])
    load.start()
    me = meet_all(devices, group)
    mine = me
    sent, kept, used = [], [], [0] * count

    def piece(which, block):
        rows = row_counts[which]
        return outs[which].at[pl.ds(pl.multiple_of(block * rows, rows), rows)]

    def send(which, block, peer, source=None):
        copy = pltpu.make_async_remote_copy(
            piece(which, block) if source is None else source,
            piece(which, block),
            send_sems.at[which, used[which]],
            recv_sems.at[which, block],
            device_id=peer,
            device_id_type=MESH,
        )
        used[which] += 1
        copy.start()
        sent.append(copy)

    def arrive(which, block):
        pltpu.make_async_remote_copy(
            ins[which],
            piece(which, block),
            send_sems.at[which, 0],
            recv_sems.at[which, block],
            device_id=peers[0],
            device_id_type=MESH,
        ).wait_recv()

    def own(which):
        for peer in peers:
            send(which, mine, peer, ins[which])
        copy = pltpu.make_async_copy(ins[which], piece(which, mine), local_sems.at[which])
        copy.start()
        kept.append(copy)

    def line(which):
        for k in (1, 2, 3):
            block = dp * 4 + along[k]
            arrive(which, block)
            for peer in (dp_x, dp_y, dp_core):
                send(which, block, (peer, z))

    def side(which):
        for k in range(4):
            block_x, block_y = dp_x * 4 + along[k], dp_y * 4 + along[k]
            arrive(which, block_y)
            if k < 2:
                send(which, block_y, (dp_x, z))
            arrive(which, block_x)
            if k >= 2:
                send(which, block_x, (dp_y, z))
            send(which, block_y, (dp_core, z))
            send(which, block_x, (dp_core, z))

    def diagonal(which):
        for k in range(4):
            block = dp_diagonal * 4 + along[k]
            arrive(which, block)
            send(which, block, (dp_core, z))

    def other_core(which):
        for y_at in range(2):
            for x_at in range(2):
                for z_at in range(4):
                    arrive(which, place(y_at, x_at, 1 - core) * 4 + z_at)

    own(0)
    own(1)

    tokens = token_row.shape[1]
    wide = (tokens, tokens)
    ids_row, ids_col = token_row[...], token_col[...]
    across = lax.broadcasted_iota(jnp.int32, wide, 1).astype(jnp.float32)
    down = lax.broadcasted_iota(jnp.int32, wide, 0).astype(jnp.float32)
    owner_row, owner_col = jnp.zeros_like(ids_row), jnp.zeros_like(ids_col)
    for device in range(1, devices):
        owner_row += (ids_row >= float(device * table_rows)).astype(jnp.float32)
        owner_col += (ids_col >= float(device * table_rows)).astype(jnp.float32)
    equal = ids_col == ids_row
    first_col = jnp.min(jnp.where(equal, across, float(tokens)), axis=1, keepdims=True)
    first_row = jnp.min(jnp.where(equal, down, float(tokens)), axis=0, keepdims=True)
    leads = jnp.where(first_row == across[:1], owner_row, -1.0)
    slot_col = jnp.sum(
        jnp.where((owner_col == leads) & (across < first_col), 1.0, 0.0), axis=1, keepdims=True
    )
    takes = lax.broadcasted_iota(jnp.int32, (devices, tokens), 0).astype(jnp.float32) == leads
    local_row = jnp.where(takes, ids_row - owner_row * table_rows + 1.0, 0.0)
    lanes = lax.broadcasted_iota(jnp.int32, (tokens, 128), 1).astype(jnp.float32)
    asked = (
        dot_without_transpose(
            local_row, (slot_col == lanes).astype(jnp.float32), highest_precision
        )
        - 1.0
    )
    over = jnp.max(slot_col, axis=0, keepdims=True) >= float(CAP)
    ask_lanes = lax.broadcasted_iota(jnp.int32, (devices, 128), 1)
    asked = jnp.where(ask_lanes == 127, over.astype(jnp.float32), asked)
    ask_out[...] = asked.reshape(devices, 1, 128)
    ask_in[pl.ds(me, 1)] = ask_out[pl.ds(me, 1)]
    start, ask_arrive, ask_sent = to_all(
        lambda other: ask_out.at[other], ask_in, ask_sems.at[0], ask_sems.at[1], devices, group, me
    )
    start()
    load.wait()

    def add_up(step, total):
        return total + jnp.sum(
            table_here[pl.ds(pl.multiple_of(step * 128, 128), 128)].astype(jnp.float32),
            axis=0,
            keepdims=True,
        )

    own_sum = lax.fori_loop(
        0, table_here.shape[0] // 128, add_up, jnp.zeros((1, table_here.shape[1]), jnp.float32)
    )
    sum_out[...] = own_sum
    sum_in[pl.ds(me, 1)] = own_sum[None]
    start, sum_arrive, sum_sent = to_all(
        lambda other: sum_out, sum_in, sum_sems.at[0], sum_sems.at[1], devices, group, me
    )
    start()
    ask_arrive()
    asked_all = ask_in[...].reshape(devices, 128)
    flags[...] = jnp.broadcast_to(
        jnp.max(jnp.where(ask_lanes == 127, asked_all, 0.0), axis=0, keepdims=True).max(
            axis=1, keepdims=True
        ),
        flags.shape,
    )
    square = (128, 128)
    eye = (
        lax.broadcasted_iota(jnp.int32, square, 0) == lax.broadcasted_iota(jnp.int32, square, 1)
    ).astype(jnp.float32)
    turned = dot_nt(eye, asked_all, highest_precision)
    turned = jnp.round(turned)
    row_lanes = lax.broadcasted_iota(jnp.int32, (CAP, table_here.shape[0]), 1).astype(jnp.float32)
    for source in range(devices):
        hot = turned[:CAP, source : source + 1] == row_lanes
        selector[source * CAP : (source + 1) * CAP] = hot.astype(jnp.float32).astype(jnp.bfloat16)

    def pick(step, state):
        batch = 8 * CAP
        picked = dot_without_transpose(
            selector[pl.ds(pl.multiple_of(step * batch, batch), batch)], table_here[...]
        )
        rows_out[pl.ds(step * 8, 8)] = picked.astype(jnp.bfloat16).reshape(8, CAP, -1)
        return state

    lax.fori_loop(0, devices // 8, pick, 0)
    rows_in[pl.ds(me, 1)] = rows_out[pl.ds(me, 1)]
    start, rows_arrive, rows_sent = to_all(
        lambda other: rows_out.at[other],
        rows_in,
        row_sems.at[0],
        row_sems.at[1],
        devices,
        group,
        me,
    )
    start()

    line(0)
    own(2)
    line(1)
    side(0)
    own(3)
    line(2)
    side(1)
    diagonal(0)
    own(4)
    line(3)
    side(2)
    diagonal(1)
    swaps = []
    for at, (here, there) in enumerate(((table, table_other), (table_turned, turned_other))):
        copy = pltpu.make_async_remote_copy(
            here,
            there,
            table_sems.at[1 + 2 * at],
            table_sems.at[2 + 2 * at],
            device_id=(dp_core, z),
            device_id_type=MESH,
        )
        copy.start()
        swaps.append(copy)

    rows_arrive()
    index_col = owner_col * CAP + slot_col
    slots = lax.broadcasted_iota(jnp.int32, (tokens, devices * CAP), 1).astype(jnp.float32)
    chosen = (index_col == slots).astype(jnp.float32).astype(jnp.bfloat16)
    taken = dot_without_transpose(chosen, rows_in[...].reshape(devices * CAP, -1))
    embedded[...] = taken[: tokens // 2]
    target_rows[...] = taken[tokens // 2 :]
    sum_arrive()
    table_sum[...] = jnp.sum(sum_in[...], axis=0)

    line(4)
    side(3)
    diagonal(2)
    side(4)
    diagonal(3)
    diagonal(4)
    for which in range(count):
        other_core(which)
    for copy in swaps:
        copy.wait()
    for copy in kept:
        copy.wait()
    for copy in sent:
        copy.wait_send()
    ask_sent()
    sum_sent()
    rows_sent()


def gather_all(tokens, table, table_turned, table_rows, arrays):
    count = len(arrays)
    group = lax.axis_size("vocab")
    devices = lax.axis_size("dp") * group
    width = table.shape[1]
    own_tokens = tokens.shape[0] // 2
    anywhere, vmem = pl.BlockSpec(memory_space=pl.ANY), pl.BlockSpec(memory_space=pltpu.VMEM)
    dma = pltpu.SemaphoreType.DMA
    return pl.pallas_call(
        partial(gather_kernel, [a.shape[0] for a in arrays], table_rows, devices, group),
        out_shape=[
            jax.ShapeDtypeStruct((own_tokens, width), jnp.float32),
            jax.ShapeDtypeStruct((own_tokens, width), jnp.float32),
            jax.ShapeDtypeStruct((1, width), jnp.float32),
            jax.ShapeDtypeStruct((8, 128), jnp.float32),
            jax.ShapeDtypeStruct(table.shape, table.dtype),
            jax.ShapeDtypeStruct(table_turned.shape, table.dtype),
        ]
        + [jax.ShapeDtypeStruct((devices * a.shape[0],) + a.shape[1:], a.dtype) for a in arrays],
        in_specs=[vmem, vmem] + [anywhere] * (2 + count),
        out_specs=[vmem] * 4 + [anywhere] * (2 + count),
        scratch_shapes=[
            dma((count, devices)),
            dma((count, devices)),
            dma((count,)),
            dma((5,)),
            dma((2, devices)),
            dma((2, devices)),
            dma((2, devices)),
            pltpu.VMEM(table.shape, table.dtype),
            pltpu.VMEM((devices * CAP, table.shape[0]), jnp.bfloat16),
            pltpu.VMEM((devices, CAP, width), jnp.bfloat16),
            pltpu.VMEM((devices, CAP, width), jnp.bfloat16),
            pltpu.VMEM((devices, 1, 128), jnp.float32),
            pltpu.VMEM((devices, 1, 128), jnp.float32),
            pltpu.VMEM((1, width), jnp.float32),
            pltpu.VMEM((devices, 1, width), jnp.float32),
        ],
        name="gather_weights",
        compiler_params=pltpu.CompilerParams(
            collective_id=1, has_side_effects=True, vmem_limit_bytes=56 * 2**20
        ),
    )(
        tokens.astype(jnp.float32)[None, :],
        tokens.astype(jnp.float32)[:, None],
        table,
        table_turned,
        *arrays,
    )


def pack_small(parts):
    flat = jnp.concatenate([a.reshape(-1) for a in parts])
    room = -(-flat.shape[0] // 8192) * 8192
    return jnp.pad(flat, (0, room - flat.shape[0])).reshape(16, -1)


def unpack_small(packed, shapes):
    flat = packed.reshape(-1, 16 * packed.shape[1])
    out, at = [], 0
    for shape in shapes:
        size = 1
        for n in shape:
            size *= n
        piece = flat[:, at : at + size].reshape((-1,) + shape)
        at += size
        out.append(jnp.moveaxis(piece, 0, -2).reshape(shape[:-1] + (-1,)))
    return out


def head_kernel(table_rows, chunks, own, tab_a, turn_a, tab_b, turn_b, mean_out, lse_out, *refs):
    (
        tab,
        turn,
        score_a,
        score_b,
        total,
        hidden,
        part,
        part_lse,
        got,
        got_lse,
        load_sems,
        send_sems,
        recv_sems,
        back_send,
        back_recv,
    ) = refs
    dp, z, y, x, core, place, along = position()
    pad_rows = tab_a.shape[0]
    width, tile = own.shape[1], own.shape[0]
    dev_x, dev_y = (place(y, 1 - x, core), z), (place(1 - y, x, core), z)
    dev_z = [None] + [(dp, along[k]) for k in (1, 2, 3)]
    peers = [dev_x, dev_y] + dev_z[1:]
    loads = []
    for at, (source, target) in enumerate(
        (
            (own, hidden.at[0]),
            (tab_a, tab.at[pl.ds(0, pad_rows)]),
            (tab_b, tab.at[pl.ds(pad_rows, pad_rows)]),
            (turn_a, turn.at[:, pl.ds(0, pad_rows)]),
            (turn_b, turn.at[:, pl.ds(pad_rows, pad_rows)]),
        )
    ):
        copy = pltpu.make_async_copy(source, target, load_sems.at[at])
        copy.start()
        loads.append(copy)
    barrier = pltpu.get_barrier_semaphore()
    for peer in peers:
        pl.semaphore_signal(barrier, inc=1, device_id=peer, device_id_type=MESH)
    pl.semaphore_wait(barrier, len(peers))
    loads[0].wait()

    def give(source, target, peer):
        return pltpu.make_async_remote_copy(
            hidden.at[source],
            hidden.at[target],
            send_sems.at[target],
            recv_sems.at[target],
            device_id=peer,
            device_id_type=MESH,
        )

    gives = [give(0, 4 * k, dev_z[k]) for k in (1, 2, 3)]
    forwards = {}
    for k in range(4):
        forwards[4 * k] = [give(4 * k, 4 * k + 1, dev_x), give(4 * k, 4 * k + 2, dev_y)]
        if k < 2:
            forwards[4 * k + 2] = [give(4 * k + 2, 4 * k + 3, dev_x)]
        else:
            forwards[4 * k + 1] = [give(4 * k + 1, 4 * k + 3, dev_y)]
    for copy in forwards[0] + gives:
        copy.start()

    def tile_comes(t, parity):
        for at in range(1, 16):
            if at % 2 != parity:
                continue

            @pl.when(t == at)
            def _(at=at):
                give(0, at, dev_x).wait_recv()
                for copy in forwards.get(at, []):
                    copy.start()

    def back(t, slot, peer):
        return [
            pltpu.make_async_remote_copy(
                source.at[t],
                target.at[slot],
                back_send.at[kind, slot],
                back_recv.at[kind, slot],
                device_id=peer,
                device_id_type=MESH,
            )
            for kind, (source, target) in enumerate(((part, got), (part_lse, got_lse)))
        ]

    backs = {}
    for k in range(4):
        backs[4 * k + 3] = back(4 * k + 3, 8 + k, dev_x if k < 2 else dev_y)
        backs[4 * k + 1] = back(4 * k + 1, k, dev_x)
        backs[4 * k + 2] = back(4 * k + 2, 4 + k, dev_y)
        if k:
            backs[4 * k] = back(4 * k, 11 + k, dev_z[k])

    def back_start(t):
        for copy in backs[t]:
            copy.start()

    def back_wait(slot):
        for copy in back(0, slot, dev_x):
            copy.wait_recv()

    def merge(t, slots):
        for slot in slots:
            back_wait(slot)
        levels = [part_lse[t]] + [got_lse[slot] for slot in slots]
        top = levels[0]
        for level in levels[1:]:
            top = jnp.maximum(top, level)
        shares = [jnp.exp(level - top) for level in levels]
        whole = sum(shares[1:], shares[0])
        shares = [share / whole for share in shares]
        part_lse[t] = top + jnp.log(whole)

        def rows(step, state):
            at = pl.ds(pl.multiple_of(step * 128, 128), 128)
            mixed = part[t, at].astype(jnp.float32) * shares[0]
            for slot, share in zip(slots, shares[1:], strict=True):
                mixed += got[slot, at].astype(jnp.float32) * share
            part[t, at] = mixed.astype(jnp.bfloat16)
            return state

        lax.fori_loop(0, width // 128, rows, 0)

    def merge_middle(k):
        t = 4 * k + 2 if k < 2 else 4 * k + 1
        merge(t, [8 + k])
        back_start(t)

    def merge_column(k):
        merge(4 * k, [k, 4 + k])
        if k:
            back_start(4 * k)

    after = {}
    for k in range(4):
        after.setdefault(4 * k + 1 if k < 2 else 4 * k + 2, []).append(
            partial(back_start, 4 * k + 1 if k < 2 else 4 * k + 2)
        )
        after.setdefault(4 * k + 3, []).append(partial(back_start, 4 * k + 3))
    late = []
    for k in range(4):
        for delay, event in ((3, merge_middle), (7, merge_column)):
            at = 4 * k + 3 + delay
            if at < 16:
                after.setdefault(at, []).append(partial(event, k))
            else:
                late.append((at, partial(event, k)))
    late = [event for _, event in sorted(late, key=lambda entry: entry[0])]

    def tile_done(t, parity):
        for at in sorted(after):
            if at % 2 != parity:
                continue

            @pl.when(t == at)
            def _(at=at):
                for event in after[at]:
                    event()

    for copy in loads[1:]:
        copy.wait()
    starts = [sum(chunks[:at]) for at in range(len(chunks))]
    low = jnp.full((8, tile), -jnp.inf, jnp.float32)

    def scores_of(rows, at, score, top):
        begin, size = starts[at], chunks[at]
        values = dot_nt(tab[begin : begin + size], rows)
        score[begin : begin + size] = values
        cuts = [(begin, begin + size, False)]
        for half in range(2):
            edge = half * pad_rows + table_rows // 8 * 8
            stop = (half + 1) * pad_rows
            if begin <= edge < begin + size:
                cuts = [(begin, edge, False), (edge, min(stop, begin + size), True)]
                if stop < begin + size:
                    cuts.append((stop, begin + size, False))
        for first, last, masked in cuts:
            if first == last:
                continue
            cut = values[first - begin : last - begin]
            if masked:
                row = lax.broadcasted_iota(jnp.int32, cut.shape, 0)
                cut = jnp.where(row < table_rows % 8, cut, masked_value)
                score[first:last] = cut
            top = jnp.maximum(top, jnp.max(cut.reshape(-1, 8, tile), axis=0))
        return top

    def half_step(t, parity, score, score_next, top):
        after_t = jnp.minimum(t + 1, 15)
        tile_comes(t + 1, 1 - parity)
        rows = hidden[after_t]
        peak = jnp.max(top, axis=0, keepdims=True)
        summed = jnp.zeros((8, tile), jnp.float32)
        top_next = low
        for at in range(len(chunks)):
            begin, size = starts[at], chunks[at]
            expo = jnp.exp(score[begin : begin + size] - peak)
            summed += jnp.sum(expo.reshape(-1, 8, tile), axis=0)
            top_next = scores_of(rows, at, score_next, top_next)
            product = dot_without_transpose(
                turn[:, begin : begin + size], expo.astype(jnp.bfloat16)
            )
            if at == 0:
                total[...] = product
            else:
                total[...] += product
        denominator = jnp.sum(summed, axis=0, keepdims=True)
        part[t] = (total[...] * (1.0 / denominator)).astype(jnp.bfloat16)
        part_lse[t] = peak + jnp.log(denominator)
        tile_done(t, parity)
        return top_next

    top = low
    for at in range(len(chunks)):
        top = scores_of(hidden[0], at, score_a, top)

    def two_steps(step, top):
        top = half_step(2 * step, 0, score_a, score_b, top)
        return half_step(2 * step + 1, 1, score_b, score_a, top)

    lax.fori_loop(0, 8, two_steps, top)
    for event in late:
        event()
    merge(0, [12, 13, 14])
    mean_out[...] = part[0]
    lse_out[...] = part_lse[0]
    for copies in [gives] + list(forwards.values()) + list(backs.values()):
        for copy in copies:
            copy.wait_send()


def head(final_state, table_rows, tables):
    tile, width = final_state.shape
    pad_rows = tables[0].shape[0]
    both = 2 * pad_rows
    chunks = [both // 256 // 4 * 256] * 4
    chunks[0] += both - sum(chunks)
    anywhere, vmem = pl.BlockSpec(memory_space=pl.ANY), pl.BlockSpec(memory_space=pltpu.VMEM)
    dma = pltpu.SemaphoreType.DMA
    return pl.pallas_call(
        partial(head_kernel, table_rows, chunks),
        out_shape=[
            jax.ShapeDtypeStruct((width, tile), jnp.bfloat16),
            jax.ShapeDtypeStruct((1, tile), jnp.float32),
        ],
        in_specs=[anywhere] * 5,
        out_specs=[vmem] * 2,
        scratch_shapes=[
            pltpu.VMEM((both, width), jnp.bfloat16),
            pltpu.VMEM((width, both), jnp.bfloat16),
            pltpu.VMEM((both, tile), jnp.float32),
            pltpu.VMEM((both, tile), jnp.float32),
            pltpu.VMEM((width, tile), jnp.float32),
            pltpu.VMEM((16, tile, width), jnp.bfloat16),
            pltpu.VMEM((16, width, tile), jnp.bfloat16),
            pltpu.VMEM((16, 1, tile), jnp.float32),
            pltpu.VMEM((15, width, tile), jnp.bfloat16),
            pltpu.VMEM((15, 1, tile), jnp.float32),
            dma((5,)),
            dma((16,)),
            dma((16,)),
            dma((2, 15)),
            dma((2, 15)),
        ],
        name="head",
        compiler_params=pltpu.CompilerParams(
            collective_id=2, has_side_effects=True, vmem_limit_bytes=62 * 2**20
        ),
    )(final_state, *tables)


def update_kernel(devices, group, grads, momenta, weights, new_momenta, new_weights, numbers, *refs):
    parts, whole, piece, sems, back_sems = refs
    me = meet_all(devices, group)
    z = lax.axis_index("vocab")
    parts[pl.ds(me, 1)] = grads[pl.ds(me, 1)]
    start, arrive, sent = to_all(
        lambda other: grads.at[other], parts, sems.at[0], sems.at[1], devices, group, me
    )
    start()
    arrive()
    summed = parts[0]
    for source in range(1, devices):
        summed += parts[source]
    width = momenta.shape[1]
    piece[...] = summed[:, :width]
    whole[pl.ds(me, 1)] = summed[None, :, :width]
    start, back_arrive, back_sent = to_all(
        lambda other: piece, whole, back_sems.at[0], back_sems.at[1], devices, group, me
    )
    start()
    back_arrive()
    gradient = whole[...].reshape(devices, width)
    squares = jnp.sum(jnp.sum(gradient * gradient, axis=0, keepdims=True), axis=1, keepdims=True)
    norm = jnp.sqrt(squares)
    factor = jnp.minimum(1.0, clip_level / (norm + 1e-06))
    state = momentum * momenta[...] + factor * gradient
    share = new_momenta.shape[1]
    columns = pl.ds(pl.multiple_of(z * share, share), share)
    whole[...] = state.reshape(devices, 1, width)
    new_momenta[...] = whole[:, 0, columns]
    square = (devices, devices)
    row = lax.broadcasted_iota(jnp.int32, square, 0)
    column = lax.broadcasted_iota(jnp.int32, square, 1)
    rank = 4
    blocks = row // rank == column // rank

    def gram_of(matrix):
        return jnp.where(blocks, dot_nt(matrix, matrix, highest_precision), 0.0)

    grams = gram_of(state)
    diagonal = jnp.sum(jnp.where(row == column, grams, 0.0), axis=0, keepdims=True)
    traces = jnp.sum(jnp.where(blocks, diagonal, 0.0), axis=1, keepdims=True)
    sizes = jnp.sqrt(traces) + 1e-07
    state = state / sizes
    grams = grams / (sizes * sizes)
    for turn_index in range(5):
        if turn_index:
            grams = gram_of(state)
        poly = coef_b * grams + coef_c * dot_without_transpose(grams, grams, highest_precision)
        state = coef_a * state + dot_without_transpose(poly, state, highest_precision)
    whole[...] = (weights[...] - learning_rate * state).reshape(devices, 1, width)
    new_weights[...] = whole[:, 0, columns]
    lanes = lax.broadcasted_iota(jnp.int32, (1, 128), 1)
    numbers[...] = jnp.where(lanes == 2, norm, summed[:, width:])
    sent()
    back_sent()


def update(grads, momenta, weights):
    group = lax.axis_size("vocab")
    devices = lax.axis_size("dp") * group
    width = momenta.shape[1]
    vmem = pl.BlockSpec(memory_space=pltpu.VMEM)
    dma = pltpu.SemaphoreType.DMA
    small = jax.ShapeDtypeStruct((devices, width // group), jnp.float32)
    return pl.pallas_call(
        partial(update_kernel, devices, group),
        out_shape=[small, small, jax.ShapeDtypeStruct((1, 128), jnp.float32)],
        in_specs=[vmem] * 3,
        out_specs=[vmem] * 3,
        scratch_shapes=[
            pltpu.VMEM(grads.shape, jnp.float32),
            pltpu.VMEM((devices, 1, width), jnp.float32),
            pltpu.VMEM((1, width), jnp.float32),
            dma((2, devices)),
            dma((2, devices)),
        ],
        name="update",
        compiler_params=pltpu.CompilerParams(collective_id=3, has_side_effects=True),
    )(grads, momenta, weights)


def stack_adapters(down, up):
    return jnp.concatenate([jnp.swapaxes(down, 1, 2), up], axis=0).reshape(-1, up.shape[2])


def per_device(
    ids,
    targets,
    counted_mask,
    lengths,
    table,
    position_table,
    layer_norm_gain,
    layer_norm_bias,
    query_key_value_weight,
    output_weight,
    up_weight,
    down_weight,
    biases,
    adapter_down,
    adapter_up,
    down_momentum,
    up_momentum,
):
    every = (
        ids,
        targets,
        counted_mask,
        lengths,
        table,
        position_table,
        layer_norm_gain,
        layer_norm_bias,
        query_key_value_weight,
        output_weight,
        up_weight,
        down_weight,
        biases,
        adapter_down,
        adapter_up,
        down_momentum,
        up_momentum,
    )
    table_rows = table.shape[0]
    row_count = ids.shape[0]
    table = jnp.pad(table, ((0, -table_rows % 128), (0, 0)))
    table_turned = table.T
    tokens = jnp.concatenate([ids, jnp.where(counted_mask > 0, targets, ids)])
    small = (position_table, layer_norm_gain, layer_norm_bias, biases)
    (
        embedded,
        target_rows,
        table_sum,
        flags,
        table_other,
        turned_other,
        packed,
        w_qkv_all,
        w_out_all,
        w_up_all,
        w_down_all,
    ) = gather_all(
        tokens,
        table,
        table_turned,
        table_rows,
        (pack_small(small), query_key_value_weight, output_weight, up_weight, down_weight),
    )

    def go_on():
        positions_all, gains_all, shifts_all, bias_stack = unpack_small(
            packed, [a.shape for a in small]
        )
        positions_in, allowed_mask = layout(lengths[0], row_count)
        residual_initial = embedded + positions_all[positions_in].astype(jnp.float32)
        frozen_weights = (
            w_qkv_all,
            w_out_all,
            w_up_all,
            w_down_all,
            gains_all,
            shifts_all,
            bias_stack,
        )
        final_state, kept_rows = layer_forward(
            residual_initial, frozen_weights, adapter_down, adapter_up, allowed_mask
        )
        mean_rows, log_total = head(
            final_state, table_rows, (table, table_turned, table_other, turned_other)
        )
        mean_rows = mean_rows.T.astype(jnp.float32)
        log_total = log_total[0]
        state_float = final_state.astype(jnp.float32)
        uniform = (smooth / V) * table_sum
        pulled = (1.0 - smooth) * target_rows + uniform
        row_loss = log_total - jnp.sum(state_float * pulled, axis=1)
        mask_float = counted_mask.astype(jnp.float32)
        loss_own = jnp.sum(mask_float * row_loss)
        count_own = jnp.sum(mask_float)
        final_gradient = mask_float[:, None] * (mean_rows - pulled)
        backward_weights = (w_out_all, w_up_all, w_down_all, gains_all)
        down_gradient, up_gradient = layer_backward(
            final_gradient, kept_rows, backward_weights, adapter_down, adapter_up, allowed_mask
        )
        grads = stack_adapters(down_gradient, up_gradient)
        extra = jnp.zeros((grads.shape[0], 128), jnp.float32)
        extra = extra.at[:, 0].set(loss_own).at[:, 1].set(count_own)
        grads = jnp.concatenate([grads, extra], axis=1)[:, None, :]
        new_momenta, new_weights, numbers = update(
            grads,
            stack_adapters(down_momentum, up_momentum),
            stack_adapters(adapter_down, adapter_up),
        )

        def split(stacked):
            stacked = stacked.reshape(2, -1, adapter_up.shape[1], stacked.shape[1])
            return jnp.swapaxes(stacked[0], 1, 2), stacked[1]

        mom_down, mom_up = split(new_momenta)
        down_fresh, up_fresh = split(new_weights)
        return (
            numbers[0, 0],
            numbers[0, 1],
            numbers[0, 2],
            mom_down,
            mom_up,
            down_fresh,
            up_fresh,
            down_fresh.astype(jnp.bfloat16),
            up_fresh.astype(jnp.bfloat16),
        )

    return lax.cond(flags[0, 0] > 0.0, lambda: per_device_general(*every), go_on)


def solution(mesh):
    fast = dict(mesh.shape) == {"dp": 8, "vocab": 4}
    placed = (
        P(("dp", "vocab")),
        P(("dp", "vocab")),
        P(("dp", "vocab")),
        P(("dp", "vocab"), None),
        P(("dp", "vocab"), None),
        P(None, ("dp", "vocab")),
        P(None, ("dp", "vocab")),
        P(None, ("dp", "vocab")),
        P(("dp", "vocab"), None),
        P(("dp", "vocab"), None),
        P(("dp", "vocab"), None),
        P(("dp", "vocab"), None),
        P(("dp", "vocab")),
        P(),
        P(),
        P(),
        P(),
    )
    return jax.shard_map(
        per_device if fast else per_device_general,
        mesh=mesh,
        in_specs=placed,
        out_specs=(
            P(),
            P(),
            P(),
            P(None, "vocab", None),
            P(None, None, "vocab"),
            P(None, "vocab", None),
            P(None, None, "vocab"),
            P(None, "vocab", None),
            P(None, None, "vocab"),
        ),
        check_vma=False,
    )
```

```python
from functools import partial

import jax
import jax.numpy as jnp
from jax import lax
from jax.experimental import pallas as pl
from jax.experimental.pallas import tpu as pltpu
from jax.sharding import PartitionSpec as P

HEAD_DIM = 64
V = 50304


highest_precision = lax.Precision.HIGHEST
ln_eps = 1e-05
adapter_scale = 8.0
smooth = 0.1
clip_level = 1.0
momentum = 0.5
learning_rate = 0.5
coef_a = 3.4445
coef_b = -4.775
coef_c = 2.0315
score_scale = 0.125
masked_value = -1e30


def merged(x, axis, join):
    gathered = jax.tree.map(
        lambda a, kind: lax.all_gather(a.astype(kind), axis),
        x,
        jax.tree.map(lambda a: jnp.bfloat16 if a.dtype == jnp.float32 else a.dtype, x),
    )

    def take(source):
        return jax.tree.map(
            lambda a, own: lax.dynamic_index_in_dim(a, source, 0, False).astype(own.dtype),
            gathered,
            x,
        )

    return lax.fori_loop(
        1, lax.axis_size(axis), lambda source, state: join(state, take(source)), take(0)
    )


def dot_without_transpose(left_side, right_side, setting=None):
    return jnp.dot(left_side, right_side, precision=setting, preferred_element_type=jnp.float32)


def dot_last_axis(left_side, right_side, setting=None):
    return lax.dot_general(
        left_side,
        right_side,
        (((1,), (1,)), ((), ())),
        precision=setting,
        preferred_element_type=jnp.float32,
    )


def dot_first(left_side, right_side, setting=None):
    return lax.dot_general(
        left_side,
        right_side,
        (((0,), (0,)), ((), ())),
        precision=setting,
        preferred_element_type=jnp.float32,
    )


def rounded_values(values):
    return lax.optimization_barrier(values.astype(jnp.bfloat16)).astype(jnp.float32)


def layer_norm(values, gain, offset):
    center = values - jnp.mean(values, axis=-1, keepdims=True)
    spread = jnp.mean(center * center, axis=-1, keepdims=True)
    return center * lax.rsqrt(spread + ln_eps) * gain + offset


def layout(seq_lengths, row_count):
    seq_ends = jnp.cumsum(seq_lengths)
    seq_starts = seq_ends - seq_lengths
    places = jnp.arange(row_count, dtype=jnp.int32)
    segment = jnp.sum((places[:, None] >= seq_ends[None, :]).astype(jnp.int32), axis=1)
    member = segment[:, None] == jnp.arange(seq_lengths.shape[0], dtype=jnp.int32)[None, :]
    positions_in = places - jnp.sum(jnp.where(member, seq_starts[None, :], 0), axis=1)
    allowed_mask = (segment[:, None] == segment[None, :]) & (places[None, :] <= places[:, None])
    return (positions_in, allowed_mask)


def owner_rows(token_ids, piece_rows, group, vocab_pos):
    piece_index = token_ids // piece_rows
    owner = piece_index % group
    local = piece_index // group * piece_rows + token_ids % piece_rows
    return jnp.where(owner == vocab_pos, local, -1)


def attention_scores(query, key_rows, allowed_mask):
    scores = (
        jnp.einsum("shd,thd->hst", query, key_rows, preferred_element_type=jnp.float32)
        * score_scale
    )
    return jnp.where(allowed_mask[None], scores, masked_value)


def layer_forward(residual_initial, frozen_weights, adapter_down, adapter_up, allowed_mask):
    query_key_value_weight, output_weight, up_weight, down_weight, gains, shifts, bias_stack = (
        frozen_weights
    )
    gains = gains.astype(jnp.float32)
    shifts = shifts.astype(jnp.float32)
    bias_stack = bias_stack.astype(jnp.float32)
    width_size = output_weight.shape[0]
    hidden_units = up_weight.shape[1]
    row_count = residual_initial.shape[0]
    heads = width_size // HEAD_DIM
    first_normed = layer_norm(residual_initial, gains[0], shifts[0]).astype(jnp.bfloat16)
    first_plain = first_normed.astype(jnp.float32)
    joined_rows = (
        dot_without_transpose(first_normed, query_key_value_weight) + bias_stack[: 3 * width_size]
    )
    adapt_in = []
    projected = []
    for which_index in range(3):
        inner_product = dot_without_transpose(
            first_plain, adapter_down[which_index], highest_precision
        )
        adapt_in.append(inner_product)
        branch_output = joined_rows[
            :, which_index * width_size : (which_index + 1) * width_size
        ] + adapter_scale * dot_without_transpose(
            inner_product, adapter_up[which_index], highest_precision
        )
        projected.append(branch_output.astype(jnp.bfloat16).reshape(row_count, heads, HEAD_DIM))
    query, key_rows, value_rows = projected
    scores = attention_scores(query, key_rows, allowed_mask)
    top = jnp.max(scores, axis=-1, keepdims=True)
    expo = jnp.exp(scores - top)
    summed = jnp.sum(expo, axis=-1, keepdims=True)
    log_total = top + jnp.log(summed)
    probs = (expo / summed).astype(jnp.bfloat16)
    mixed_state = jnp.einsum("hst,thd->shd", probs, value_rows, preferred_element_type=jnp.float32)
    mixed_state = mixed_state.reshape(row_count, width_size).astype(jnp.bfloat16)
    mixed_plain = mixed_state.astype(jnp.float32)
    adapter_output = dot_without_transpose(mixed_plain, adapter_down[3], highest_precision)
    attended_rows = (
        dot_without_transpose(mixed_state, output_weight)
        + bias_stack[3 * width_size : 4 * width_size]
        + adapter_scale * dot_without_transpose(adapter_output, adapter_up[3], highest_precision)
    )
    stream_one = residual_initial + attended_rows
    normed_two = layer_norm(stream_one, gains[1], shifts[1]).astype(jnp.bfloat16)
    before_gelu = (
        dot_without_transpose(normed_two, up_weight)
        + bias_stack[4 * width_size : 4 * width_size + hidden_units]
    )
    activation = jax.nn.gelu(before_gelu, approximate=True).astype(jnp.bfloat16)
    stream_two = (
        stream_one
        + dot_without_transpose(activation, down_weight)
        + bias_stack[4 * width_size + hidden_units :]
    )
    final_state = layer_norm(stream_two, gains[2], shifts[2]).astype(jnp.bfloat16)
    kept_rows = (
        first_plain,
        adapt_in,
        query,
        key_rows,
        value_rows,
        log_total,
        mixed_plain,
        adapter_output,
        stream_one,
        before_gelu,
        stream_two,
    )
    return (final_state, kept_rows)


def layer_backward(
    final_gradient, kept_rows, backward_weights, adapter_down, adapter_up, allowed_mask
):
    output_weight, up_weight, down_weight, gains = backward_weights
    gains = gains.astype(jnp.float32)
    (
        first_plain,
        adapt_in,
        query,
        key_rows,
        value_rows,
        log_total,
        mixed_plain,
        adapter_output,
        stream_one,
        before_gelu,
        stream_two,
    ) = kept_rows
    row_count = query.shape[0]
    width_size = query.shape[1] * HEAD_DIM
    _, pull_three = jax.vjp(lambda values: layer_norm(values, gains[2], 0.0), stream_two)
    grad_two = pull_three(final_gradient)[0]
    grad_act = dot_last_axis(grad_two.astype(jnp.bfloat16), down_weight)
    _, pull_gelu = jax.vjp(partial(jax.nn.gelu, approximate=True), before_gelu)
    grad_pre = pull_gelu(grad_act)[0].astype(jnp.bfloat16)
    _, pull_two = jax.vjp(lambda values: layer_norm(values, gains[1], 0.0), stream_one)
    first_gradient = grad_two + pull_two(dot_last_axis(grad_pre, up_weight))[0]
    attention_gradient = first_gradient.astype(jnp.bfloat16)
    attention_scaled = adapter_scale * rounded_values(first_gradient)
    up_grads = [None, None, None, None]
    down_grads = [None, None, None, None]
    up_grads[3] = dot_first(adapter_output, attention_scaled, highest_precision)
    backward_output = dot_last_axis(attention_scaled, adapter_up[3], highest_precision)
    down_grads[3] = dot_first(mixed_plain, backward_output, highest_precision)
    mixed_gradient = dot_last_axis(attention_gradient, output_weight) + dot_last_axis(
        backward_output, adapter_down[3], highest_precision
    )
    grad_heads = mixed_gradient.astype(jnp.bfloat16).reshape(query.shape)
    probs = jnp.exp(attention_scores(query, key_rows, allowed_mask) - log_total)
    grad_value = jnp.einsum(
        "hst,shd->thd", probs.astype(jnp.bfloat16), grad_heads, preferred_element_type=jnp.float32
    )
    grad_probs = jnp.einsum(
        "shd,thd->hst", grad_heads, value_rows, preferred_element_type=jnp.float32
    )
    grad_scores = probs * (grad_probs - jnp.sum(probs * grad_probs, axis=-1, keepdims=True))
    grad_scores = grad_scores.astype(jnp.bfloat16)
    grad_query = (
        jnp.einsum("hst,thd->shd", grad_scores, key_rows, preferred_element_type=jnp.float32)
        * score_scale
    )
    grad_key = (
        jnp.einsum("hst,shd->thd", grad_scores, query, preferred_element_type=jnp.float32)
        * score_scale
    )
    for which_index, branch_gradient in enumerate((grad_query, grad_key, grad_value)):
        scaled_values = adapter_scale * rounded_values(
            branch_gradient.reshape(row_count, width_size)
        )
        up_grads[which_index] = dot_first(adapt_in[which_index], scaled_values, highest_precision)
        backward_input = dot_last_axis(scaled_values, adapter_up[which_index], highest_precision)
        down_grads[which_index] = dot_first(first_plain, backward_input, highest_precision)
    return (jnp.stack(down_grads), jnp.stack(up_grads))


def orthogonalize(matrices, sum_grams):
    grams = sum_grams(
        jnp.einsum(
            "mrd,msd->mrs",
            matrices,
            matrices,
            precision=highest_precision,
            preferred_element_type=jnp.float32,
        )
    )
    sizes = jnp.sqrt(jnp.trace(grams, axis1=1, axis2=2))[:, None, None] + 1e-07
    state = matrices / sizes
    grams = grams / (sizes * sizes)
    for turn_index in range(5):
        if turn_index:
            grams = sum_grams(
                jnp.einsum(
                    "mrd,msd->mrs",
                    state,
                    state,
                    precision=highest_precision,
                    preferred_element_type=jnp.float32,
                )
            )
        poly = coef_b * grams + coef_c * jnp.einsum(
            "mrs,mst->mrt",
            grams,
            grams,
            precision=highest_precision,
            preferred_element_type=jnp.float32,
        )
        state = coef_a * state + jnp.einsum(
            "mrs,msd->mrd",
            poly,
            state,
            precision=highest_precision,
            preferred_element_type=jnp.float32,
        )
    return state


def per_device_general(
    ids,
    targets,
    counted_mask,
    lengths,
    table,
    position_table,
    layer_norm_gain,
    layer_norm_bias,
    query_key_value_weight,
    output_weight,
    up_weight,
    down_weight,
    biases,
    adapter_down,
    adapter_up,
    down_momentum,
    up_momentum,
):
    gathered = (
        lax.all_gather(query_key_value_weight, ("dp", "vocab"), axis=0, tiled=True),
        lax.all_gather(output_weight, ("dp", "vocab"), axis=0, tiled=True),
        lax.all_gather(up_weight, ("dp", "vocab"), axis=0, tiled=True),
        lax.all_gather(down_weight, ("dp", "vocab"), axis=0, tiled=True),
        lax.all_gather(layer_norm_gain, ("dp", "vocab"), axis=1, tiled=True),
        lax.all_gather(layer_norm_bias, ("dp", "vocab"), axis=1, tiled=True),
        lax.all_gather(biases, ("dp", "vocab"), axis=0, tiled=True),
        lax.all_gather(position_table, ("dp", "vocab"), axis=1, tiled=True),
    )
    w_qkv_all, w_out_all, w_up_all, w_down_all, gains_all, shifts_all, bias_stack, positions_all = (
        gathered
    )
    row_count = ids.shape[0]
    width_size = w_out_all.shape[0]
    group = lax.axis_size("vocab")
    vocab_pos = lax.axis_index("vocab")
    piece_rows = table.shape[0]
    ids_all, target_all, mask_all = (
        lax.all_gather(ids, "vocab", axis=0, tiled=True),
        lax.all_gather(targets, "vocab", axis=0, tiled=True),
        lax.all_gather(counted_mask, "vocab", axis=0, tiled=True),
    )
    table_full = lax.all_gather(table, "dp", axis=0, tiled=True)
    vocab_rows = table_full.shape[0]
    local_ids = owner_rows(ids_all, piece_rows, group, vocab_pos)
    inside = local_ids >= 0
    picked_rows = table_full[jnp.clip(local_ids, 0, vocab_rows - 1)]
    picked_rows = jnp.where(inside[:, None], picked_rows, jnp.zeros_like(picked_rows))
    embedded = lax.psum_scatter(
        picked_rows.astype(jnp.float32).astype(jnp.bfloat16),
        "vocab",
        scatter_dimension=0,
        tiled=True,
    ).astype(jnp.float32)
    positions_in, allowed_mask = layout(lengths[0], row_count)
    residual_initial = embedded + positions_all[positions_in].astype(jnp.float32)
    frozen_weights = (w_qkv_all, w_out_all, w_up_all, w_down_all, gains_all, shifts_all, bias_stack)
    final_state, kept_rows = layer_forward(
        residual_initial, frozen_weights, adapter_down, adapter_up, allowed_mask
    )
    final_all = lax.all_gather(final_state, "vocab", axis=0, tiled=True)
    total_rows = final_all.shape[0]
    block = 512
    count_blocks = total_rows // block
    final_blocks = final_all.reshape(count_blocks, block, width_size)
    local_targets = owner_rows(target_all, piece_rows, group, vocab_pos).reshape(
        count_blocks, block
    )
    columns = jnp.arange(vocab_rows, dtype=jnp.int32)

    def head_stats(item):
        piece, local = item
        logits = dot_last_axis(piece, table_full)
        top = jnp.max(logits, axis=1)
        expsum = jnp.sum(jnp.exp(logits - top[:, None]), axis=1)
        target_logit = jnp.sum(jnp.where(columns[None, :] == local[:, None], logits, 0.0), axis=1)
        return (top, expsum, target_logit, jnp.sum(logits, axis=1))

    stats = lax.map(head_stats, (final_blocks, local_targets))
    stats = tuple((entry.reshape(total_rows) for entry in stats))

    def combine(first_part, second_part):
        larger = jnp.maximum(first_part[0], second_part[0])
        merged_sum = first_part[1] * jnp.exp(first_part[0] - larger) + second_part[1] * jnp.exp(
            second_part[0] - larger
        )
        return (larger, merged_sum, first_part[2] + second_part[2], first_part[3] + second_part[3])

    top, expsum, target_logit, logit_sum = merged(stats, "vocab", combine)
    log_total = top + jnp.log(expsum)
    row_loss = log_total - (1.0 - smooth) * target_logit - smooth * logit_sum / V
    mask_float = mask_all.astype(jnp.float32)
    own_start = vocab_pos * row_count
    loss_own = jnp.sum(lax.dynamic_slice_in_dim(mask_float * row_loss, own_start, row_count))
    count_own = jnp.sum(counted_mask.astype(jnp.float32))

    def head_grad(item):
        piece, local, lse_block, weight = item
        logits = dot_last_axis(piece, table_full)
        probs = jnp.exp(logits - lse_block[:, None])
        onehot = (columns[None, :] == local[:, None]).astype(jnp.float32)
        grad_logits = weight[:, None] * (probs - (1.0 - smooth) * onehot - smooth / V)
        return dot_without_transpose(grad_logits.astype(jnp.bfloat16), table_full)

    partial_rows = lax.map(
        head_grad,
        (
            final_blocks,
            local_targets,
            log_total.reshape(count_blocks, block),
            mask_float.reshape(count_blocks, block),
        ),
    )
    final_gradient = lax.psum_scatter(
        partial_rows.reshape(total_rows, width_size).astype(jnp.bfloat16),
        "vocab",
        scatter_dimension=0,
        tiled=True,
    ).astype(jnp.float32)
    backward_weights = (
        lax.all_gather(output_weight, ("dp", "vocab"), axis=0, tiled=True),
        lax.all_gather(up_weight, ("dp", "vocab"), axis=0, tiled=True),
        lax.all_gather(down_weight, ("dp", "vocab"), axis=0, tiled=True),
        lax.all_gather(layer_norm_gain, ("dp", "vocab"), axis=1, tiled=True),
    )
    down_gradient, up_gradient = layer_backward(
        final_gradient, kept_rows, backward_weights, adapter_down, adapter_up, allowed_mask
    )
    down_gradient, up_gradient, smoothed_loss_sum, loss_count = lax.psum(
        (down_gradient, up_gradient, loss_own, count_own), ("dp", "vocab")
    )
    grad_norm = jnp.sqrt(
        jnp.sum(down_gradient * down_gradient) + jnp.sum(up_gradient * up_gradient)
    )
    factor = jnp.minimum(1.0, clip_level / (grad_norm + 1e-06))
    new_mom_down = momentum * down_momentum + factor * down_gradient
    new_mom_up = momentum * up_momentum + factor * up_gradient
    stacked = jnp.concatenate([jnp.swapaxes(new_mom_down, 1, 2), new_mom_up], axis=0)
    share_fraction = stacked.shape[2] // group
    begin_index = vocab_pos * share_fraction
    orthogonal_update = lax.dynamic_slice_in_dim(
        orthogonalize(stacked, lambda grams: grams), begin_index, share_fraction, 2
    )
    mom_down_part = lax.dynamic_slice_in_dim(new_mom_down, begin_index, share_fraction, 1)
    mom_up_part = lax.dynamic_slice_in_dim(new_mom_up, begin_index, share_fraction, 2)
    down_fresh = lax.dynamic_slice_in_dim(
        adapter_down, begin_index, share_fraction, 1
    ) - learning_rate * jnp.swapaxes(orthogonal_update[:4], 1, 2)
    up_fresh = (
        lax.dynamic_slice_in_dim(adapter_up, begin_index, share_fraction, 2)
        - learning_rate * orthogonal_update[4:]
    )
    return (
        smoothed_loss_sum,
        loss_count,
        grad_norm,
        mom_down_part,
        mom_up_part,
        down_fresh,
        up_fresh,
        down_fresh.astype(jnp.bfloat16),
        up_fresh.astype(jnp.bfloat16),
    )


MESH = pl.DeviceIdType.MESH
CAP = 32


def dot_nt(left_side, right_side, setting=None):
    return dot_last_axis(left_side, right_side, setting)


def position():
    dp, z = lax.axis_index("dp"), lax.axis_index("vocab")
    y, x, core = dp // 4, dp // 2 % 2, dp % 2

    def place(y_at, x_at, core_at):
        return y_at * 4 + x_at * 2 + core_at

    along = (z, z // 2 * 2 + 1 - z % 2, (z + 2) % 4, (1 - z // 2) * 2 + 1 - z % 2)
    return dp, z, y, x, core, place, along


def inner(z):
    return (z + 1) // 2 % 2


def mirror(z, other):
    return (z // 2 + other // 2) % 2 * 2 + (z + other) % 2


def nearness(z, other):
    k = mirror(z, other)
    return k + inner(z) * (k // 2) * (5 - 2 * k)


def by_nearness(z):
    far = z // 2 * 3
    near = 2 - z // 2
    return (z, z // 2 * 2 + 1 - z % 2, near, 3 - far)


def meet_all(devices, group):
    me = lax.axis_index("dp") * group + lax.axis_index("vocab")
    barrier = pltpu.get_barrier_semaphore()

    def signal(step, state):
        other = lax.rem(me + step, devices)
        pl.semaphore_signal(
            barrier, inc=1, device_id=(other // group, other % group), device_id_type=MESH
        )
        return state

    lax.fori_loop(1, devices, signal, 0)
    pl.semaphore_wait(barrier, devices - 1)
    return me


def to_all(source_of, target, send_sems, recv_sems, devices, group, me):
    def copy(step):
        other = lax.rem(me + step, devices)
        return pltpu.make_async_remote_copy(
            source_of(other),
            target.at[me],
            send_sems.at[step],
            recv_sems.at[step],
            device_id=(other // group, other % group),
            device_id_type=MESH,
        )

    def start():
        def one(step, state):
            copy(step).start()
            return state

        lax.fori_loop(1, devices, one, 0)

    def arrive():
        def one(step, state):
            source = lax.rem(me + devices - step, devices)
            pltpu.make_async_remote_copy(
                target.at[source],
                target.at[source],
                send_sems.at[step],
                recv_sems.at[step],
                device_id=(source // group, source % group),
                device_id_type=MESH,
            ).wait_recv()
            return state

        lax.fori_loop(1, devices, one, 0)

    def sent():
        def one(step, state):
            copy(step).wait_send()
            return state

        lax.fori_loop(1, devices, one, 0)

    return start, arrive, sent


def head_kernel(table_rows, chunks, own, tab_a, turn_a, tab_b, turn_b, mean_out, lse_out, *refs):
    (
        tab,
        turn,
        score_a,
        score_b,
        total,
        hidden,
        part,
        part_lse,
        got,
        got_lse,
        load_sems,
        send_sems,
        recv_sems,
        back_send,
        back_recv,
    ) = refs
    dp, z, y, x, core, place, _ = position()
    along = by_nearness(z)
    pad_rows = tab_a.shape[0]
    width, tile = own.shape[1], own.shape[0]
    dev_x, dev_y = (place(y, 1 - x, core), z), (place(1 - y, x, core), z)
    dev_z = [(dp, along[k]) for k in range(4)]
    peers = [dev_x, dev_y] + dev_z[1:]
    loads = []
    for at, (source, target) in enumerate(
        (
            (own, hidden.at[0]),
            (tab_a, tab.at[pl.ds(0, pad_rows)]),
            (tab_b, tab.at[pl.ds(pad_rows, pad_rows)]),
            (turn_a, turn.at[:, pl.ds(0, pad_rows)]),
            (turn_b, turn.at[:, pl.ds(pad_rows, pad_rows)]),
        )
    ):
        copy = pltpu.make_async_copy(source, target, load_sems.at[at])
        copy.start()
        loads.append(copy)
    barrier = pltpu.get_barrier_semaphore()
    for peer in peers:
        pl.semaphore_signal(barrier, inc=1, device_id=peer, device_id_type=MESH)
    pl.semaphore_wait(barrier, len(peers))
    loads[0].wait()

    def give(source, target, peer):
        return pltpu.make_async_remote_copy(
            hidden.at[source],
            hidden.at[target],
            send_sems.at[target],
            recv_sems.at[target],
            device_id=peer,
            device_id_type=MESH,
        )

    def give_along(k, upward):
        there = z + 1 if upward else z - 1
        return pltpu.make_async_remote_copy(
            hidden.at[4 * k],
            hidden.at[4 * nearness(there, along[k])],
            send_sems.at[16 + k + 3 * (not upward and k == 0)],
            recv_sems.at[4 * nearness(there, along[k])],
            device_id=(dp, there),
            device_id_type=MESH,
        )

    def pass_along(k, act):
        @pl.when((along[k] <= z) & (z < 3))
        def _():
            act(give_along(k, True))

        @pl.when((along[k] >= z) & (z > 0))
        def _():
            act(give_along(k, False))

    forwards = {}
    for k in range(4):
        forwards[4 * k] = [give(4 * k, 4 * k + 1, dev_x), give(4 * k, 4 * k + 2, dev_y)]
        if k < 2:
            forwards[4 * k + 2] = [give(4 * k + 2, 4 * k + 3, dev_x)]
        else:
            forwards[4 * k + 1] = [give(4 * k + 1, 4 * k + 3, dev_y)]
    pass_along(0, lambda copy: copy.start())
    for copy in forwards[0]:
        copy.start()

    def tile_comes(t, parity):
        for at in range(1, 16):
            if at % 2 != parity:
                continue

            @pl.when(t == at)
            def _(at=at):
                give(0, at, dev_x).wait_recv()
                if at % 4 == 0:
                    pass_along(at // 4, lambda copy: copy.start())
                for copy in forwards.get(at, []):
                    copy.start()

    def back(t, slot, peer):
        return [
            pltpu.make_async_remote_copy(
                source.at[t],
                target.at[slot],
                back_send.at[kind, slot],
                back_recv.at[kind, slot],
                device_id=peer,
                device_id_type=MESH,
            )
            for kind, (source, target) in enumerate(((part, got), (part_lse, got_lse)))
        ]

    backs = {}
    for k in range(4):
        backs[4 * k + 3] = back(4 * k + 3, 8 + k, dev_x if k < 2 else dev_y)
        backs[4 * k + 1] = back(4 * k + 1, k, dev_x)
        backs[4 * k + 2] = back(4 * k + 2, 4 + k, dev_y)
        if k:
            backs[4 * k] = back(4 * k, 11 + mirror(z, along[k]), dev_z[k])

    def back_start(t):
        for copy in backs[t]:
            copy.start()

    def back_wait(slot):
        for copy in back(0, slot, dev_x):
            copy.wait_recv()

    def merge(t, slots):
        for slot in slots:
            back_wait(slot)
        levels = [part_lse[t]] + [got_lse[slot] for slot in slots]
        top = levels[0]
        for level in levels[1:]:
            top = jnp.maximum(top, level)
        shares = [jnp.exp(level - top) for level in levels]
        whole = sum(shares[1:], shares[0])
        shares = [share / whole for share in shares]
        part_lse[t] = top + jnp.log(whole)

        def rows(step, state):
            at = pl.ds(pl.multiple_of(step * 128, 128), 128)
            mixed = part[t, at].astype(jnp.float32) * shares[0]
            for slot, share in zip(slots, shares[1:], strict=True):
                mixed += got[slot, at].astype(jnp.float32) * share
            part[t, at] = mixed.astype(jnp.bfloat16)
            return state

        lax.fori_loop(0, width // 128, rows, 0)

    def merge_middle(k):
        t = 4 * k + 2 if k < 2 else 4 * k + 1
        merge(t, [8 + k])
        back_start(t)

    def merge_column(k):
        merge(4 * k, [k, 4 + k])
        if k:
            back_start(4 * k)

    after = {}
    for k in range(4):
        after.setdefault(4 * k + 1 if k < 2 else 4 * k + 2, []).append(
            partial(back_start, 4 * k + 1 if k < 2 else 4 * k + 2)
        )
        after.setdefault(4 * k + 3, []).append(partial(back_start, 4 * k + 3))
    late = []
    for k in range(4):
        for delay, event in ((3, merge_middle), (7, merge_column)):
            at = 4 * k + 3 + delay
            if at < 16:
                after.setdefault(at, []).append(partial(event, k))
            else:
                late.append((at, partial(event, k)))
    late = [event for _, event in sorted(late, key=lambda entry: entry[0])]

    def tile_done(t, parity):
        for at in sorted(after):
            if at % 2 != parity:
                continue

            @pl.when(t == at)
            def _(at=at):
                for event in after[at]:
                    event()

    for copy in loads[1:]:
        copy.wait()
    starts = [sum(chunks[:at]) for at in range(len(chunks))]
    low = jnp.full((8, tile), -jnp.inf, jnp.float32)

    def scores_of(rows, at, score, top):
        begin, size = starts[at], chunks[at]
        values = dot_nt(tab[begin : begin + size], rows)
        score[begin : begin + size] = values
        cuts = [(begin, begin + size, False)]
        for half in range(2):
            edge = half * pad_rows + table_rows // 8 * 8
            stop = (half + 1) * pad_rows
            if begin <= edge < begin + size:
                cuts = [(begin, edge, False), (edge, min(stop, begin + size), True)]
                if stop < begin + size:
                    cuts.append((stop, begin + size, False))
        for first, last, masked in cuts:
            if first == last:
                continue
            cut = values[first - begin : last - begin]
            if masked:
                row = lax.broadcasted_iota(jnp.int32, cut.shape, 0)
                cut = jnp.where(row < table_rows % 8, cut, masked_value)
                score[first:last] = cut
            top = jnp.maximum(top, jnp.max(cut.reshape(-1, 8, tile), axis=0))
        return top

    def half_step(t, parity, score, score_next, top):
        after_t = jnp.minimum(t + 1, 15)
        tile_comes(t + 1, 1 - parity)
        rows = hidden[after_t]
        peak = jnp.max(top, axis=0, keepdims=True)
        summed = jnp.zeros((8, tile), jnp.float32)
        top_next = low
        for at in range(len(chunks)):
            begin, size = starts[at], chunks[at]
            expo = jnp.exp(score[begin : begin + size] - peak)
            summed += jnp.sum(expo.reshape(-1, 8, tile), axis=0)
            top_next = scores_of(rows, at, score_next, top_next)
            product = dot_without_transpose(
                turn[:, begin : begin + size], expo.astype(jnp.bfloat16)
            )
            if at == 0:
                total[...] = product
            else:
                total[...] += product
        denominator = jnp.sum(summed, axis=0, keepdims=True)
        part[t] = (total[...] * (1.0 / denominator)).astype(jnp.bfloat16)
        part_lse[t] = peak + jnp.log(denominator)
        tile_done(t, parity)
        return top_next

    top = low
    for at in range(len(chunks)):
        top = scores_of(hidden[0], at, score_a, top)

    def two_steps(step, top):
        top = half_step(2 * step, 0, score_a, score_b, top)
        return half_step(2 * step + 1, 1, score_b, score_a, top)

    lax.fori_loop(0, 8, two_steps, top)
    for event in late:
        event()
    merge(0, [12, 13, 14])
    mean_out[...] = part[0]
    lse_out[...] = part_lse[0]
    for k in range(4):
        pass_along(k, lambda copy: copy.wait_send())
    for copies in list(forwards.values()) + list(backs.values()):
        for copy in copies:
            copy.wait_send()


def head(final_state, table_rows, tables):
    tile, width = final_state.shape
    pad_rows = tables[0].shape[0]
    both = 2 * pad_rows
    chunks = [both // 256 // 4 * 256] * 4
    chunks[0] += both - sum(chunks)
    anywhere, vmem = pl.BlockSpec(memory_space=pl.ANY), pl.BlockSpec(memory_space=pltpu.VMEM)
    dma = pltpu.SemaphoreType.DMA
    return pl.pallas_call(
        partial(head_kernel, table_rows, chunks),
        out_shape=[
            jax.ShapeDtypeStruct((width, tile), jnp.bfloat16),
            jax.ShapeDtypeStruct((1, tile), jnp.float32),
        ],
        in_specs=[anywhere] * 5,
        out_specs=[vmem] * 2,
        scratch_shapes=[
            pltpu.VMEM((both, width), jnp.bfloat16),
            pltpu.VMEM((width, both), jnp.bfloat16),
            pltpu.VMEM((both, tile), jnp.float32),
            pltpu.VMEM((both, tile), jnp.float32),
            pltpu.VMEM((width, tile), jnp.float32),
            pltpu.VMEM((16, tile, width), jnp.bfloat16),
            pltpu.VMEM((16, width, tile), jnp.bfloat16),
            pltpu.VMEM((16, 1, tile), jnp.float32),
            pltpu.VMEM((15, width, tile), jnp.bfloat16),
            pltpu.VMEM((15, 1, tile), jnp.float32),
            dma((5,)),
            dma((20,)),
            dma((16,)),
            dma((2, 15)),
            dma((2, 15)),
        ],
        name="head",
        compiler_params=pltpu.CompilerParams(
            collective_id=2, has_side_effects=True, vmem_limit_bytes=62 * 2**20
        ),
    )(final_state, *tables)


def update_kernel(devices, group, grads, momenta, weights, new_momenta, new_weights, numbers, *refs):
    parts, whole, piece, sems, back_sems = refs
    me = meet_all(devices, group)
    z = lax.axis_index("vocab")
    parts[pl.ds(me, 1)] = grads[pl.ds(me, 1)]
    start, arrive, sent = to_all(
        lambda other: grads.at[other], parts, sems.at[0], sems.at[1], devices, group, me
    )
    start()
    arrive()
    summed = parts[0]
    for source in range(1, devices):
        summed += parts[source]
    width = momenta.shape[1]
    piece[...] = summed[:, :width]
    whole[pl.ds(me, 1)] = summed[None, :, :width]
    start, back_arrive, back_sent = to_all(
        lambda other: piece, whole, back_sems.at[0], back_sems.at[1], devices, group, me
    )
    start()
    back_arrive()
    gradient = whole[...].reshape(devices, width)
    squares = jnp.sum(jnp.sum(gradient * gradient, axis=0, keepdims=True), axis=1, keepdims=True)
    norm = jnp.sqrt(squares)
    factor = jnp.minimum(1.0, clip_level / (norm + 1e-06))
    state = momentum * momenta[...] + factor * gradient
    share = new_momenta.shape[1]
    columns = pl.ds(pl.multiple_of(z * share, share), share)
    whole[...] = state.reshape(devices, 1, width)
    new_momenta[...] = whole[:, 0, columns]
    square = (devices, devices)
    row = lax.broadcasted_iota(jnp.int32, square, 0)
    column = lax.broadcasted_iota(jnp.int32, square, 1)
    rank = 4
    blocks = row // rank == column // rank

    def gram_of(matrix):
        return jnp.where(blocks, dot_nt(matrix, matrix, highest_precision), 0.0)

    grams = gram_of(state)
    diagonal = jnp.sum(jnp.where(row == column, grams, 0.0), axis=0, keepdims=True)
    traces = jnp.sum(jnp.where(blocks, diagonal, 0.0), axis=1, keepdims=True)
    sizes = jnp.sqrt(traces) + 1e-07
    state = state / sizes
    grams = grams / (sizes * sizes)
    for turn_index in range(5):
        if turn_index:
            grams = gram_of(state)
        poly = coef_b * grams + coef_c * dot_without_transpose(grams, grams, highest_precision)
        state = coef_a * state + dot_without_transpose(poly, state, highest_precision)
    whole[...] = (weights[...] - learning_rate * state).reshape(devices, 1, width)
    new_weights[...] = whole[:, 0, columns]
    lanes = lax.broadcasted_iota(jnp.int32, (1, 128), 1)
    numbers[...] = jnp.where(lanes == 2, norm, summed[:, width:])
    sent()
    back_sent()


def update(grads, momenta, weights):
    group = lax.axis_size("vocab")
    devices = lax.axis_size("dp") * group
    width = momenta.shape[1]
    vmem = pl.BlockSpec(memory_space=pltpu.VMEM)
    dma = pltpu.SemaphoreType.DMA
    small = jax.ShapeDtypeStruct((devices, width // group), jnp.float32)
    return pl.pallas_call(
        partial(update_kernel, devices, group),
        out_shape=[small, small, jax.ShapeDtypeStruct((1, 128), jnp.float32)],
        in_specs=[vmem] * 3,
        out_specs=[vmem] * 3,
        scratch_shapes=[
            pltpu.VMEM(grads.shape, jnp.float32),
            pltpu.VMEM((devices, 1, width), jnp.float32),
            pltpu.VMEM((1, width), jnp.float32),
            dma((2, devices)),
            dma((2, devices)),
        ],
        name="update",
        compiler_params=pltpu.CompilerParams(collective_id=3, has_side_effects=True),
    )(grads, momenta, weights)


def halves_of(values):
    high = values.astype(jnp.bfloat16)
    return high, (values - high.astype(jnp.float32)).astype(jnp.bfloat16)


def stacked_halves(values):
    return jnp.concatenate(halves_of(values), axis=0)


def added_halves(values):
    rows = values.shape[0] // 2
    return values[:rows] + values[rows:]


def dot_tn(left_side, right_side):
    return dot_first(left_side, right_side)


def normal(values):
    center = values - jnp.mean(values, axis=-1, keepdims=True)
    spread = lax.rsqrt(jnp.mean(center * center, axis=-1, keepdims=True) + ln_eps)
    return center * spread, spread


def normal_back(values, gain, gradient):
    unit, spread = normal(values)
    pulled = gradient * gain
    along = jnp.mean(pulled * unit, axis=-1, keepdims=True)
    return spread * (pulled - jnp.mean(pulled, axis=-1, keepdims=True) - unit * along)


def sequence_places(lengths, rows):
    col = lax.broadcasted_iota(jnp.int32, (rows, 1), 0)
    row = lax.broadcasted_iota(jnp.int32, (1, rows), 1)
    segment_col, segment_row = jnp.zeros_like(col), jnp.zeros_like(row)
    start_col = jnp.zeros_like(col)
    end = 0
    for at in range(lengths.shape[1]):
        length = lengths[0, at]
        end = end + length
        segment_col += (col >= end).astype(jnp.int32)
        segment_row += (row >= end).astype(jnp.int32)
        start_col += jnp.where(col >= end, length, 0)
    allowed = (segment_col == segment_row) & (row <= col)
    return col - start_col, allowed


def pairs_of(width):
    return width // (2 * HEAD_DIM)


def pair_at(pair):
    return pl.ds(pl.multiple_of(pair * 2 * HEAD_DIM, 2 * HEAD_DIM), 2 * HEAD_DIM)


def head_lanes(rows):
    return lax.broadcasted_iota(jnp.int32, (rows, 2 * HEAD_DIM), 1) < HEAD_DIM


def first_part(embedded, positions, lengths, gains, shifts, x0, h1):
    rows = x0.shape[0]
    place_col, allowed = sequence_places(lengths, rows)
    spots = lax.broadcasted_iota(jnp.int32, (rows, positions.shape[0]), 1)
    hot = (place_col == spots).astype(jnp.float32).astype(jnp.bfloat16)
    x0[...] = embedded[...] + dot_without_transpose(hot, positions[...])
    unit, _ = normal(x0[...])
    h1[...] = (unit * gains[0:1] + shifts[0:1]).astype(jnp.bfloat16)
    return allowed


def adapter_in(adapters, inputs):
    return added_halves(dot_nt(stacked_halves(adapters), inputs))


def adapter_out(inner, outer):
    high, low = halves_of(inner)
    top, rest = halves_of(outer)
    return adapter_scale * dot_tn(
        jnp.concatenate([high, high, low], axis=0), jnp.concatenate([top, rest, top], axis=0)
    )


def ranks(which, shape):
    return lax.broadcasted_iota(jnp.int32, shape, 0) // 4 == which


def project_part(h1, weight, bias, adapters, inner, joined):
    width = h1.shape[1]
    step = 512
    half = adapters.shape[0] // 2
    inner[...] = adapter_in(adapters[:half], h1[...])
    for which in range(3):

        def columns(at, state):
            here = pl.ds(pl.multiple_of(at * step, step), step)
            there = pl.ds(pl.multiple_of(which * width + at * step, step), step)
            outer = jnp.where(ranks(which, (half, step)), adapters[half:, here], 0.0)
            joined[:, there] = (
                dot_without_transpose(h1[...], weight[:, there])
                + bias[:, there]
                + adapter_out(inner[...], outer)
            ).astype(jnp.bfloat16)
            return state

        lax.fori_loop(0, width // step, columns, 0)


def attend_part(joined, allowed, probs, mixed):
    rows, width = mixed.shape
    lanes = head_lanes(rows)

    def pair_step(pair, state):
        query = joined[:, pair_at(pair)]
        keys = joined[:, pair_at(pairs_of(width) + pair)]
        values = joined[:, pair_at(2 * pairs_of(width) + pair)]
        outs = []
        for side in range(2):
            mine = lanes if side == 0 else ~lanes
            scores = dot_nt(jnp.where(mine, query, jnp.zeros_like(query)), keys) * score_scale
            scores = jnp.where(allowed, scores, masked_value)
            expo = jnp.exp(scores - jnp.max(scores, axis=-1, keepdims=True))
            chances = (expo / jnp.sum(expo, axis=-1, keepdims=True)).astype(jnp.bfloat16)
            probs[2 * pair + side] = chances
            outs.append(dot_without_transpose(chances, values))
        mixed[:, pair_at(pair)] = jnp.where(lanes, outs[0], outs[1]).astype(jnp.bfloat16)
        return state

    lax.fori_loop(0, pairs_of(width), pair_step, 0)


def output_part(x0, mixed, weight, bias, adapters, inner, gains, shifts, x1, h2):
    half = adapters.shape[0] // 2
    width = mixed.shape[1]
    here = ranks(3, inner.shape)
    fresh = adapter_in(adapters[:half], mixed[...])
    inner[...] = jnp.where(here, fresh, inner[...])
    outer = jnp.where(ranks(3, (half, width)), adapters[half:], 0.0)
    x1[...] = (
        x0[...]
        + dot_without_transpose(mixed[...], weight[...])
        + bias[:, 3 * width : 4 * width]
        + adapter_out(inner[...], outer)
    )
    unit, _ = normal(x1[...])
    h2[...] = (unit * gains[1:2] + shifts[1:2]).astype(jnp.bfloat16)


def up_part(h2, weight, bias, active, slope):
    width = h2.shape[1]
    step = 512

    def columns(at, state):
        here = pl.ds(pl.multiple_of(at * step, step), step)
        there = pl.ds(pl.multiple_of(4 * width + at * step, step), step)
        z = dot_without_transpose(h2[...], weight[:, here]) + bias[:, there]
        root = 0.7978845608028654
        square = z * z
        tanh = jnp.tanh(root * z * (1.0 + 0.044715 * square))
        half = 0.5 * (1.0 + tanh)
        active[:, here] = (z * half).astype(jnp.bfloat16)
        slope[:, here] = (
            half + 0.5 * z * (1.0 - tanh * tanh) * (root * (1.0 + 3 * 0.044715 * square))
        ).astype(jnp.bfloat16)
        return state

    lax.fori_loop(0, weight.shape[1] // step, columns, 0)


def down_part(x1, active, weight, bias, gains, shifts, x2, final):
    hidden, width = weight.shape
    step = 256

    def columns(at, state):
        here = pl.ds(pl.multiple_of(at * step, step), step)
        there = pl.ds(pl.multiple_of(4 * width + hidden + at * step, step), step)
        x2[:, here] = (
            x1[:, here]
            + dot_without_transpose(active[...], weight[:, here])
            + bias[:, there]
        )
        return state

    lax.fori_loop(0, width // step, columns, 0)
    unit, _ = normal(x2[...])
    final[...] = (unit * gains[2:3] + shifts[2:3]).astype(jnp.bfloat16)


def turn_rows(source, target):
    width = source.shape[0]

    def rows(at, state):
        here = pl.ds(pl.multiple_of(at * 128, 128), 128)
        target[:, here] = source[here].astype(jnp.float32).T.astype(target.dtype)
        return state

    lax.fori_loop(0, width // 128, rows, 0)


def backward_kernel(
    mean_rows,
    log_total,
    mask_row,
    mask_col,
    target_rows,
    table_sum,
    gains,
    adapters,
    final,
    h1,
    joined,
    probs,
    mixed,
    inner,
    x1,
    slope,
    x2,
    w_out,
    w_up,
    w_down,
    grads,
    numbers,
    work,
    dx2,
    da,
    dz,
    dmix,
    pulls,
    out_here,
    up_here,
    down_here,
    sems,
):
    loads = []
    for at, (source, target) in enumerate(
        ((w_down, down_here), (w_up, up_here), (w_out, out_here))
    ):
        copy = pltpu.make_async_copy(source, target, sems.at[at])
        copy.start()
        loads.append(copy)
    rows, width = x1.shape
    half = adapters.shape[0] // 2
    hidden = slope.shape[1]
    turn_rows(mean_rows, work)
    pulled = (1.0 - smooth) * target_rows[...] + (smooth / V) * table_sum[...]
    row_dots = jnp.sum(final[...].astype(jnp.float32) * pulled, axis=1, keepdims=True)
    loss = jnp.sum(mask_row[...] * log_total[...], axis=1, keepdims=True) - jnp.sum(
        mask_col[...] * row_dots, axis=0, keepdims=True
    )
    counted = jnp.sum(mask_row[...], axis=1, keepdims=True)
    lanes = lax.broadcasted_iota(jnp.int32, (1, 128), 1)
    numbers[...] = jnp.where(lanes == 0, loss, jnp.where(lanes == 1, counted, 0.0))
    dx2[...] = normal_back(x2[...], gains[2:3], mask_col[...] * (work[...] - pulled))
    da[...] = dx2[...].astype(jnp.bfloat16)
    loads[0].wait()
    step = 512

    def hidden_columns(at, state):
        here = pl.ds(pl.multiple_of(at * step, step), step)
        dz[:, here] = (
            dot_nt(da[...], down_here[here]) * slope[:, here].astype(jnp.float32)
        ).astype(jnp.bfloat16)
        return state

    lax.fori_loop(0, hidden // step, hidden_columns, 0)
    loads[1].wait()

    def columns(at, state):
        here = pl.ds(pl.multiple_of(at * 256, 256), 256)
        work[:, here] = dot_nt(dz[...], up_here[here])
        return state

    lax.fori_loop(0, width // 256, columns, 0)
    dx1 = dx2[...] + normal_back(x1[...], gains[1:2], work[...])
    da[...] = dx1.astype(jnp.bfloat16)
    loads[2].wait()
    upper = stacked_halves(adapters[half:])
    inner_halves = stacked_halves(inner[...])

    def adapter_grads(which, gradient, inputs):
        up_grad = adapter_scale * added_halves(dot_without_transpose(inner_halves, gradient))
        back = adapter_scale * added_halves(dot_nt(upper, gradient))
        back = jnp.where(ranks(which, back.shape), back, 0.0)
        down_grad = added_halves(dot_without_transpose(stacked_halves(back), inputs))
        keep = ranks(which, up_grad.shape)
        return back, down_grad, jnp.where(keep, up_grad, 0.0)

    back, down_total, up_total = adapter_grads(3, da[...], mixed[...])
    dmix[...] = (
        dot_nt(da[...], out_here[...]) + adapter_out(back, adapters[:half]) / adapter_scale
    ).astype(jnp.bfloat16)
    lane_mask = head_lanes(rows)

    def pair_step(pair, state):
        query = joined[:, pair_at(pair)]
        keys = joined[:, pair_at(pairs_of(width) + pair)]
        values = joined[:, pair_at(2 * pairs_of(width) + pair)]
        pull = dmix[:, pair_at(pair)]
        outs = []
        for side in range(2):
            mine = lane_mask if side == 0 else ~lane_mask
            chances = probs[2 * pair + side]
            wide = chances.astype(jnp.float32)
            reach = dot_nt(jnp.where(mine, pull, jnp.zeros_like(pull)), values)
            slide = wide * (reach - jnp.sum(wide * reach, axis=-1, keepdims=True))
            slide = slide.astype(jnp.bfloat16)
            outs.append(
                (
                    dot_without_transpose(slide, keys) * score_scale,
                    dot_tn(slide, query) * score_scale,
                    dot_tn(chances, pull),
                )
            )
        for which in range(3):
            both = jnp.where(lane_mask, outs[0][which], outs[1][which])
            pulls[:, pair_at(which * pairs_of(width) + pair)] = both.astype(jnp.bfloat16)
        return state

    lax.fori_loop(0, pairs_of(width), pair_step, 0)
    for which in range(3):
        _, down_part_grad, up_part_grad = adapter_grads(
            which, pulls[:, which * width : (which + 1) * width], h1[...]
        )
        down_total += down_part_grad
        up_total += up_part_grad
    grads[:half] = down_total
    grads[half:] = up_total


def backward(mean_rows, log_total, mask, target_rows, table_sum, gains, adapters, kept, weights):
    rows = mask.shape[0]
    width = target_rows.shape[1]
    hidden = weights[2].shape[0]
    low, full = jnp.bfloat16, jnp.float32
    anywhere, vmem = pl.BlockSpec(memory_space=pl.ANY), pl.BlockSpec(memory_space=pltpu.VMEM)
    shape = jax.ShapeDtypeStruct
    return pl.pallas_call(
        backward_kernel,
        out_shape=[shape(adapters.shape, full), shape((1, 128), full)],
        in_specs=[vmem] * (8 + len(kept)) + [anywhere] * 3,
        out_specs=[vmem] * 2,
        scratch_shapes=[
            pltpu.VMEM((rows, width), full),
            pltpu.VMEM((rows, width), full),
            pltpu.VMEM((rows, width), low),
            pltpu.VMEM((rows, hidden), low),
            pltpu.VMEM((rows, width), low),
            pltpu.VMEM((rows, 3 * width), low),
        ]
        + [pltpu.VMEM(w.shape, low) for w in weights]
        + [pltpu.SemaphoreType.DMA((3,))],
        name="backward",
        compiler_params=pltpu.CompilerParams(vmem_limit_bytes=60 * 2**20),
    )(
        mean_rows,
        log_total,
        mask[None, :],
        mask[:, None],
        target_rows,
        table_sum,
        gains,
        adapters,
        *kept,
        *weights,
    )


def stack_adapters(down, up):
    return jnp.concatenate([jnp.swapaxes(down, 1, 2), up], axis=0).reshape(-1, up.shape[2])


def col_of(row):
    size = row.shape[1]
    square = (size, size)
    same = lax.broadcasted_iota(jnp.int32, square, 0) == lax.broadcasted_iota(jnp.int32, square, 1)
    return jnp.sum(jnp.where(same, row, 0.0), axis=1, keepdims=True)


def stack_rows(down, up):
    return jnp.concatenate(
        [down[j] for j in range(down.shape[0])] + [up[j] for j in range(up.shape[0])], axis=0
    )


def pack_rows(positions, gains, shifts, biases):
    places = positions[...].astype(jnp.float32)
    span = places.shape[0] // 4
    width = places.shape[1]
    places = jnp.concatenate([places[r * span : (r + 1) * span] for r in range(4)], axis=1)
    norms = jnp.concatenate(
        [
            gains[...].astype(jnp.float32),
            shifts[...].astype(jnp.float32),
            jnp.zeros((gains.shape[0], 128 - 2 * width), jnp.float32),
        ],
        axis=1,
    )
    flat = biases[...].astype(jnp.float32)
    flat = jnp.concatenate([flat, jnp.zeros((1, -flat.shape[1] % 128), jnp.float32)], axis=1)
    lines = [flat[:, r * 128 : (r + 1) * 128] for r in range(flat.shape[1] // 128)]
    rest = jnp.zeros((8 - gains.shape[0], 128), jnp.float32)
    tail = jnp.zeros((8 - len(lines), 128), jnp.float32)
    return jnp.concatenate([places, norms, rest] + lines + [tail], axis=0).astype(jnp.bfloat16)


def unpack_rows(packed, devices, width, span, norms, bias_size, positions, gains, shifts, bias):
    rows = packed.shape[0] // devices

    def group(j, state):
        devs = [
            packed[pl.ds(pl.multiple_of((4 * j + i) * rows, rows), rows)].astype(jnp.float32)
            for i in range(4)
        ]
        lanes = pl.ds(pl.multiple_of(j * 128, 128), 128)
        for r in range(4):
            block = [dev[:span, r * width : (r + 1) * width] for dev in devs]
            positions[r * span : (r + 1) * span, lanes] = jnp.concatenate(block, axis=1).astype(
                jnp.bfloat16
            )
        gains[:, lanes] = jnp.concatenate([dev[span : span + norms, :width] for dev in devs], axis=1)
        shifts[:, lanes] = jnp.concatenate(
            [dev[span : span + norms, width : 2 * width] for dev in devs], axis=1
        )
        flat = []
        for dev in devs:
            left = bias_size
            line = span + 8
            while left > 0:
                flat.append(dev[line : line + 1, : min(left, 128)])
                left -= 128
                line += 1
        bias[:, pl.ds(pl.multiple_of(j * 4 * bias_size, 128), 4 * bias_size)] = jnp.concatenate(
            flat, axis=1
        )
        return state

    lax.fori_loop(0, devices // 4, group, 0)


def first_kernel(table_rows, devices, group, row_counts, *refs):
    (
        ids,
        targets,
        mask,
        lengths,
        position_own,
        gain_own,
        shift_own,
        bias_own,
        adapter_down,
        adapter_up,
        table_tail,
        table,
        *refs,
    ) = refs
    weights_own = refs[:4]
    refs = refs[4:]
    (
        flags,
        target_out,
        table_sum,
        gains_out,
        adapters_out,
        final,
        inner,
        table_mine,
        turned_mine,
        table_other,
        turned_other,
        h1_out,
        joined_out,
        probs_out,
        mixed_out,
        x1_out,
        slope_out,
        x2_out,
        out_kept,
        up_kept,
        down_kept,
        *refs,
    ) = refs
    (
        send_sems,
        recv_sems,
        local_sems,
        table_sems,
        ask_sems,
        row_sems,
        sum_sems,
        keep_sems,
        table_here,
        turned_here,
        selector,
        rows_out,
        rows_in,
        ask_out,
        ask_in,
        sum_out,
        sum_in,
        pack_here,
        packed,
        w_qkv,
        w_out,
        w_up,
        w_down,
        positions,
        shifts,
        bias,
        embedded,
        x0,
        h1,
        joined,
        probs,
        mixed,
        x1,
        h2,
        active,
        slope,
        x2,
    ) = refs
    arrays = (packed, w_qkv, w_out, w_up, w_down)
    ins = (pack_here,) + tuple(weights_own)
    dp, z, y, x, core, place, along = position()
    dp_x, dp_y = place(y, 1 - x, core), place(1 - y, x, core)
    dp_core, dp_diagonal = place(y, x, 1 - core), place(1 - y, 1 - x, core)
    z_peers = [(dp, along[k]) for k in (1, 2, 3)]
    near_peers = [(dp_x, z), (dp_y, z), (dp_core, z)]
    body_rows = table_rows // 16 * 16
    tail_rows = table_here.shape[0] - body_rows
    loads = [
        pltpu.make_async_copy(
            table.at[pl.ds(0, body_rows)], table_here.at[pl.ds(0, body_rows)], table_sems.at[0]
        ),
        pltpu.make_async_copy(
            table_tail, table_here.at[pl.ds(body_rows, tail_rows)], table_sems.at[1]
        ),
    ]
    for copy in loads:
        copy.start()
    pack_here[...] = pack_rows(position_own, gain_own, shift_own, bias_own)
    me = meet_all(devices, group)
    sent, kept, used = [], [], [0] * len(arrays)

    def piece(which, block):
        rows = row_counts[which]
        return arrays[which].at[pl.ds(pl.multiple_of(block * rows, rows), rows)]

    def send(which, block, peer, source=None):
        copy = pltpu.make_async_remote_copy(
            piece(which, block) if source is None else source,
            piece(which, block),
            send_sems.at[which, used[which]],
            recv_sems.at[which, block],
            device_id=peer,
            device_id_type=MESH,
        )
        used[which] += 1
        copy.start()
        sent.append(copy)

    def arrive(which, block):
        pltpu.make_async_remote_copy(
            ins[which],
            piece(which, block),
            send_sems.at[which, 0],
            recv_sems.at[which, block],
            device_id=z_peers[0],
            device_id_type=MESH,
        ).wait_recv()

    def own_near(which):
        for peer in near_peers:
            send(which, me, peer, ins[which])
        copy = pltpu.make_async_copy(ins[which], piece(which, me), local_sems.at[which])
        copy.start()
        kept.append(copy)

    def own_z(which):
        for peer in z_peers:
            send(which, me, peer, ins[which])

    def line(which):
        for k in (1, 2, 3):
            block = dp * 4 + along[k]
            arrive(which, block)
            for peer in near_peers:
                send(which, block, peer)

    def side(which):
        for k in range(4):
            block_x, block_y = dp_x * 4 + along[k], dp_y * 4 + along[k]
            arrive(which, block_y)
            if k < 2:
                send(which, block_y, (dp_x, z))
            arrive(which, block_x)
            if k >= 2:
                send(which, block_x, (dp_y, z))
            send(which, block_y, (dp_core, z))
            send(which, block_x, (dp_core, z))

    def diagonal(which):
        for k in range(4):
            block = dp_diagonal * 4 + along[k]
            arrive(which, block)
            send(which, block, (dp_core, z))

    def other_core(which):
        for y_at in range(2):
            for x_at in range(2):
                for z_at in range(4):
                    arrive(which, place(y_at, x_at, 1 - core) * 4 + z_at)
        kept[which].wait()

    def keep(at, source, target):
        copy = pltpu.make_async_copy(source, target, keep_sems.at[at])
        copy.start()
        return copy

    for which in range(len(arrays)):
        own_near(which)
    own_z(0)
    own_z(1)

    own_ids = ids[...].astype(jnp.float32)
    own_targets = jnp.where(mask[...] > 0, targets[...], ids[...]).astype(jnp.float32)
    ids_row = jnp.concatenate([own_ids, own_targets], axis=1)
    ids_col = jnp.concatenate([col_of(own_ids), col_of(own_targets)], axis=0)
    tokens = ids_row.shape[1]
    wide = (tokens, tokens)
    across = lax.broadcasted_iota(jnp.int32, wide, 1).astype(jnp.float32)
    down = lax.broadcasted_iota(jnp.int32, wide, 0).astype(jnp.float32)
    owner_row, owner_col = jnp.zeros_like(ids_row), jnp.zeros_like(ids_col)
    for device in range(1, devices):
        owner_row += (ids_row >= float(device * table_rows)).astype(jnp.float32)
        owner_col += (ids_col >= float(device * table_rows)).astype(jnp.float32)
    equal = ids_col == ids_row
    first_col = jnp.min(jnp.where(equal, across, float(tokens)), axis=1, keepdims=True)
    first_row = jnp.min(jnp.where(equal, down, float(tokens)), axis=0, keepdims=True)
    leads = jnp.where(first_row == across[:1], owner_row, -1.0)
    slot_col = jnp.sum(
        jnp.where((owner_col == leads) & (across < first_col), 1.0, 0.0), axis=1, keepdims=True
    )
    takes = lax.broadcasted_iota(jnp.int32, (devices, tokens), 0).astype(jnp.float32) == leads
    local_row = jnp.where(takes, ids_row - owner_row * table_rows + 1.0, 0.0)
    lanes = lax.broadcasted_iota(jnp.int32, (tokens, 128), 1).astype(jnp.float32)
    asked = (
        dot_without_transpose(
            local_row, (slot_col == lanes).astype(jnp.float32), highest_precision
        )
        - 1.0
    )
    over = jnp.max(slot_col, axis=0, keepdims=True) >= float(CAP)
    ask_lanes = lax.broadcasted_iota(jnp.int32, (devices, 128), 1)
    asked = jnp.where(ask_lanes == 127, over.astype(jnp.float32), asked)
    ask_out[...] = asked.reshape(devices, 1, 128)
    ask_in[pl.ds(me, 1)] = ask_out[pl.ds(me, 1)]
    start, ask_arrive, ask_sent = to_all(
        lambda other: ask_out.at[other], ask_in, ask_sems.at[0], ask_sems.at[1], devices, group, me
    )
    start()
    own_z(2)
    for copy in loads:
        copy.wait()
    keeps = [keep(0, table_here, table_mine)]

    def add_up(step, total):
        return total + jnp.sum(
            table_here[pl.ds(pl.multiple_of(step * 128, 128), 128)].astype(jnp.float32),
            axis=0,
            keepdims=True,
        )

    own_sum = lax.fori_loop(
        0, table_here.shape[0] // 128, add_up, jnp.zeros((1, table_here.shape[1]), jnp.float32)
    )
    sum_out[...] = own_sum
    sum_in[pl.ds(me, 1)] = own_sum[None]
    start, sum_arrive, sum_sent = to_all(
        lambda other: sum_out, sum_in, sum_sems.at[0], sum_sems.at[1], devices, group, me
    )
    start()
    line(0)
    line(1)
    own_z(3)
    ask_arrive()
    asked_all = ask_in[...].reshape(devices, 128)
    flags[...] = jnp.broadcast_to(
        jnp.max(
            jnp.max(jnp.where(ask_lanes == 127, asked_all, 0.0), axis=0, keepdims=True),
            axis=1,
            keepdims=True,
        ),
        flags.shape,
    )
    square = (128, 128)
    eye = (
        lax.broadcasted_iota(jnp.int32, square, 0) == lax.broadcasted_iota(jnp.int32, square, 1)
    ).astype(jnp.float32)
    turned = jnp.round(dot_nt(eye, asked_all, highest_precision))
    row_lanes = lax.broadcasted_iota(jnp.int32, (CAP, table_here.shape[0]), 1).astype(jnp.float32)
    batch = 8
    for step in range(devices // batch):
        for at in range(batch):
            source = step * batch + at
            hot = turned[:CAP, source : source + 1] == row_lanes
            selector[at * CAP : (at + 1) * CAP] = hot.astype(jnp.float32).astype(jnp.bfloat16)
        picked = dot_without_transpose(selector[...], table_here[...])
        rows_out[step * batch : (step + 1) * batch] = picked.astype(jnp.bfloat16).reshape(
            batch, CAP, -1
        )
    rows_in[pl.ds(me, 1)] = rows_out[pl.ds(me, 1)]
    start, rows_arrive, rows_sent = to_all(
        lambda other: rows_out.at[other],
        rows_in,
        row_sems.at[0],
        row_sems.at[1],
        devices,
        group,
        me,
    )
    start()
    side(0)
    line(2)
    side(1)
    own_z(4)
    adapters = adapters_out
    adapters[...] = stack_rows(adapter_down, adapter_up)
    turn_rows(table_here, turned_here)
    keeps.append(keep(1, turned_here, turned_mine))
    swaps = []
    for at, (here, there) in enumerate(((table_here, table_other), (turned_here, turned_other))):
        copy = pltpu.make_async_remote_copy(
            here,
            there,
            table_sems.at[2 + 2 * at],
            table_sems.at[3 + 2 * at],
            device_id=(dp_core, z),
            device_id_type=MESH,
        )
        copy.start()
        swaps.append(copy)
    diagonal(0)
    line(3)
    side(2)
    other_core(0)
    unpack_rows(
        packed,
        devices,
        position_own.shape[1],
        position_own.shape[0] // 4,
        gain_own.shape[0],
        bias_own.shape[1],
        positions,
        gains_out,
        shifts,
        bias,
    )
    diagonal(1)

    rows_arrive()
    index_col = owner_col * CAP + slot_col
    slots = lax.broadcasted_iota(jnp.int32, (tokens, devices * CAP), 1).astype(jnp.float32)
    chosen = (index_col == slots).astype(jnp.float32).astype(jnp.bfloat16)
    taken = dot_without_transpose(chosen, rows_in[...].reshape(devices * CAP, -1))
    embedded[...] = taken[: tokens // 2]
    target_out[...] = taken[tokens // 2 :]
    sum_arrive()
    table_sum[...] = jnp.sum(sum_in[...], axis=0)
    allowed = first_part(embedded, positions, lengths, gains_out, shifts, x0, h1)
    keeps.append(keep(2, h1, h1_out))
    line(4)
    side(3)
    other_core(1)
    project_part(h1, w_qkv, bias, adapters, inner, joined)
    keeps.append(keep(3, joined, joined_out))
    diagonal(2)
    side(4)
    attend_part(joined, allowed, probs, mixed)
    keeps.append(keep(4, probs, probs_out))
    keeps.append(keep(5, mixed, mixed_out))
    diagonal(3)
    other_core(2)
    keeps.append(keep(6, w_out, out_kept))
    output_part(x0, mixed, w_out, bias, adapters, inner, gains_out, shifts, x1, h2)
    keeps.append(keep(7, x1, x1_out))
    diagonal(4)
    other_core(3)
    keeps.append(keep(8, w_up, up_kept))
    up_part(h2, w_up, bias, active, slope)
    keeps.append(keep(9, slope, slope_out))
    other_core(4)
    keeps.append(keep(10, w_down, down_kept))
    down_part(x1, active, w_down, bias, gains_out, shifts, x2, final)
    keeps.append(keep(11, x2, x2_out))
    for copy in swaps:
        copy.wait()
    for copy in keeps:
        copy.wait()
    for copy in sent:
        copy.wait_send()
    ask_sent()
    sum_sent()
    rows_sent()


def first(
    ids, targets, mask, lengths, table, small, adapter_down, adapter_up, weights
):
    group = lax.axis_size("vocab")
    devices = lax.axis_size("dp") * group
    table_rows, width = table.shape
    pad_rows = -(-table_rows // 128) * 128
    body_rows = table_rows // 16 * 16
    tail = jnp.pad(table[body_rows:], ((0, pad_rows - table_rows), (0, 0)))
    rows = ids.shape[0]
    hidden = weights[3].shape[0] * devices
    heads = width // HEAD_DIM
    low, full = jnp.bfloat16, jnp.float32
    positions, gains, shifts, biases = small
    pack_height = positions.shape[0] // 4 + 16
    counts = [pack_height] + [w.shape[0] for w in weights]
    anywhere, vmem = pl.BlockSpec(memory_space=pl.ANY), pl.BlockSpec(memory_space=pltpu.VMEM)
    dma = pltpu.SemaphoreType.DMA
    shape = jax.ShapeDtypeStruct
    adapter_rows = 2 * adapter_up.shape[0] * adapter_up.shape[1]
    whole = [(devices * w.shape[0], w.shape[1]) for w in weights]
    saved = [
        shape((pad_rows, width), low),
        shape((width, pad_rows), low),
        shape((pad_rows, width), low),
        shape((width, pad_rows), low),
        shape((rows, width), low),
        shape((rows, 3 * width), low),
        shape((heads, rows, rows), low),
        shape((rows, width), low),
        shape((rows, width), full),
        shape((rows, hidden), low),
        shape((rows, width), full),
    ] + [shape(w, low) for w in whole[1:]]
    return pl.pallas_call(
        partial(first_kernel, table_rows, devices, group, counts),
        out_shape=[
            shape((8, 128), full),
            shape((rows, width), full),
            shape((1, width), full),
            shape((gains.shape[0], width), full),
            shape((adapter_rows, width), full),
            shape((rows, width), low),
            shape((adapter_rows // 2, rows), full),
        ]
        + saved,
        in_specs=[vmem] * 3
        + [pl.BlockSpec(memory_space=pltpu.SMEM)]
        + [vmem] * 6
        + [anywhere] * (2 + len(weights)),
        out_specs=[vmem] * 7 + [anywhere] * len(saved),
        scratch_shapes=[
            dma((len(counts), devices)),
            dma((len(counts), devices)),
            dma((len(counts),)),
            dma((6,)),
            dma((2, devices)),
            dma((2, devices)),
            dma((2, devices)),
            dma((12,)),
            pltpu.VMEM((pad_rows, width), low),
            pltpu.VMEM((width, pad_rows), low),
            pltpu.VMEM((8 * CAP, pad_rows), low),
            pltpu.VMEM((devices, CAP, width), low),
            pltpu.VMEM((devices, CAP, width), low),
            pltpu.VMEM((devices, 1, 128), full),
            pltpu.VMEM((devices, 1, 128), full),
            pltpu.VMEM((1, width), full),
            pltpu.VMEM((devices, 1, width), full),
            pltpu.VMEM((pack_height, 128), low),
            pltpu.VMEM((devices * pack_height, 128), low),
        ]
        + [pltpu.VMEM(w, low) for w in whole]
        + [
            pltpu.VMEM((positions.shape[0], width), low),
            pltpu.VMEM((shifts.shape[0], width), full),
            pltpu.VMEM((1, devices * biases.shape[0]), full),
            pltpu.VMEM((rows, width), full),
            pltpu.VMEM((rows, width), full),
            pltpu.VMEM((rows, width), low),
            pltpu.VMEM((rows, 3 * width), low),
            pltpu.VMEM((heads, rows, rows), low),
            pltpu.VMEM((rows, width), low),
            pltpu.VMEM((rows, width), full),
            pltpu.VMEM((rows, width), low),
            pltpu.VMEM((rows, hidden), low),
            pltpu.VMEM((rows, hidden), low),
            pltpu.VMEM((rows, width), full),
        ],
        name="first",
        compiler_params=pltpu.CompilerParams(
            collective_id=1, has_side_effects=True, vmem_limit_bytes=63 * 2**20
        ),
    )(
        ids[None, :],
        targets[None, :],
        mask[None, :],
        lengths,
        positions,
        gains,
        shifts,
        biases[None, :],
        jnp.swapaxes(adapter_down, 1, 2),
        adapter_up,
        tail,
        table,
        *weights,
    )


def per_device(
    ids,
    targets,
    counted_mask,
    lengths,
    table,
    position_table,
    layer_norm_gain,
    layer_norm_bias,
    query_key_value_weight,
    output_weight,
    up_weight,
    down_weight,
    biases,
    adapter_down,
    adapter_up,
    down_momentum,
    up_momentum,
):
    every = (
        ids,
        targets,
        counted_mask,
        lengths,
        table,
        position_table,
        layer_norm_gain,
        layer_norm_bias,
        query_key_value_weight,
        output_weight,
        up_weight,
        down_weight,
        biases,
        adapter_down,
        adapter_up,
        down_momentum,
        up_momentum,
    )
    table_rows = table.shape[0]
    (
        flags,
        target_rows,
        table_sum,
        gains_all,
        adapters,
        final_state,
        inner_rows,
        table_mine,
        turned_mine,
        table_other,
        turned_other,
        h1,
        joined,
        probs,
        mixed,
        x1,
        slope,
        x2,
        w_out_all,
        w_up_all,
        w_down_all,
    ) = first(
        ids,
        targets,
        counted_mask,
        lengths,
        table,
        (position_table, layer_norm_gain, layer_norm_bias, biases),
        adapter_down,
        adapter_up,
        (query_key_value_weight, output_weight, up_weight, down_weight),
    )
    kept = (h1, joined, probs, mixed, inner_rows, x1, slope, x2)

    def go_on():
        mean_rows, log_total = head(
            final_state, table_rows, (table_mine, turned_mine, table_other, turned_other)
        )
        grads, sums = backward(
            mean_rows,
            log_total,
            counted_mask.astype(jnp.float32),
            target_rows,
            table_sum,
            gains_all,
            adapters,
            (final_state, *kept),
            (w_out_all, w_up_all, w_down_all),
        )
        grads = jnp.concatenate(
            [grads, jnp.broadcast_to(sums, (grads.shape[0], sums.shape[1]))], axis=1
        )[:, None, :]
        new_momenta, new_weights, numbers = update(
            grads,
            stack_adapters(down_momentum, up_momentum),
            adapters,
        )

        def split(stacked):
            stacked = stacked.reshape(2, -1, adapter_up.shape[1], stacked.shape[1])
            return jnp.swapaxes(stacked[0], 1, 2), stacked[1]

        mom_down, mom_up = split(new_momenta)
        down_fresh, up_fresh = split(new_weights)
        return (
            numbers[0, 0],
            numbers[0, 1],
            numbers[0, 2],
            mom_down,
            mom_up,
            down_fresh,
            up_fresh,
            down_fresh.astype(jnp.bfloat16),
            up_fresh.astype(jnp.bfloat16),
        )

    return lax.cond(flags[0, 0] > 0.0, lambda: per_device_general(*every), go_on)


def solution(mesh):
    fast = dict(mesh.shape) == {"dp": 8, "vocab": 4}
    placed = (
        P(("dp", "vocab")),
        P(("dp", "vocab")),
        P(("dp", "vocab")),
        P(("dp", "vocab"), None),
        P(("dp", "vocab"), None),
        P(None, ("dp", "vocab")),
        P(None, ("dp", "vocab")),
        P(None, ("dp", "vocab")),
        P(("dp", "vocab"), None),
        P(("dp", "vocab"), None),
        P(("dp", "vocab"), None),
        P(("dp", "vocab"), None),
        P(("dp", "vocab")),
        P(),
        P(),
        P(),
        P(),
    )
    return jax.shard_map(
        per_device if fast else per_device_general,
        mesh=mesh,
        in_specs=placed,
        out_specs=(
            P(),
            P(),
            P(),
            P(None, "vocab", None),
            P(None, None, "vocab"),
            P(None, "vocab", None),
            P(None, None, "vocab"),
            P(None, "vocab", None),
            P(None, None, "vocab"),
        ),
        check_vma=False,
    )
```

```python
from functools import partial

import jax
import jax.numpy as jnp
from jax import lax
from jax.experimental import pallas as pl
from jax.experimental.pallas import tpu as pltpu
from jax.sharding import PartitionSpec as P

HEAD_DIM = 64
V = 50304


highest_precision = lax.Precision.HIGHEST
ln_eps = 1e-05
adapter_scale = 8.0
smooth = 0.1
clip_level = 1.0
momentum = 0.5
learning_rate = 0.5
coef_a = 3.4445
coef_b = -4.775
coef_c = 2.0315
score_scale = 0.125
masked_value = -1e30


def merged(x, axis, join):
    gathered = jax.tree.map(
        lambda a, kind: lax.all_gather(a.astype(kind), axis),
        x,
        jax.tree.map(lambda a: jnp.bfloat16 if a.dtype == jnp.float32 else a.dtype, x),
    )

    def take(source):
        return jax.tree.map(
            lambda a, own: lax.dynamic_index_in_dim(a, source, 0, False).astype(own.dtype),
            gathered,
            x,
        )

    return lax.fori_loop(
        1, lax.axis_size(axis), lambda source, state: join(state, take(source)), take(0)
    )


def dot_without_transpose(left_side, right_side, setting=None):
    return jnp.dot(left_side, right_side, precision=setting, preferred_element_type=jnp.float32)


def dot_last_axis(left_side, right_side, setting=None):
    return lax.dot_general(
        left_side,
        right_side,
        (((1,), (1,)), ((), ())),
        precision=setting,
        preferred_element_type=jnp.float32,
    )


def dot_first(left_side, right_side, setting=None):
    return lax.dot_general(
        left_side,
        right_side,
        (((0,), (0,)), ((), ())),
        precision=setting,
        preferred_element_type=jnp.float32,
    )


def rounded_values(values):
    return lax.optimization_barrier(values.astype(jnp.bfloat16)).astype(jnp.float32)


def layer_norm(values, gain, offset):
    center = values - jnp.mean(values, axis=-1, keepdims=True)
    spread = jnp.mean(center * center, axis=-1, keepdims=True)
    return center * lax.rsqrt(spread + ln_eps) * gain + offset


def layout(seq_lengths, row_count):
    seq_ends = jnp.cumsum(seq_lengths)
    seq_starts = seq_ends - seq_lengths
    places = jnp.arange(row_count, dtype=jnp.int32)
    segment = jnp.sum((places[:, None] >= seq_ends[None, :]).astype(jnp.int32), axis=1)
    member = segment[:, None] == jnp.arange(seq_lengths.shape[0], dtype=jnp.int32)[None, :]
    positions_in = places - jnp.sum(jnp.where(member, seq_starts[None, :], 0), axis=1)
    allowed_mask = (segment[:, None] == segment[None, :]) & (places[None, :] <= places[:, None])
    return (positions_in, allowed_mask)


def owner_rows(token_ids, piece_rows, group, vocab_pos):
    piece_index = token_ids // piece_rows
    owner = piece_index % group
    local = piece_index // group * piece_rows + token_ids % piece_rows
    return jnp.where(owner == vocab_pos, local, -1)


def attention_scores(query, key_rows, allowed_mask):
    scores = (
        jnp.einsum("shd,thd->hst", query, key_rows, preferred_element_type=jnp.float32)
        * score_scale
    )
    return jnp.where(allowed_mask[None], scores, masked_value)


def layer_forward(residual_initial, frozen_weights, adapter_down, adapter_up, allowed_mask):
    query_key_value_weight, output_weight, up_weight, down_weight, gains, shifts, bias_stack = (
        frozen_weights
    )
    gains = gains.astype(jnp.float32)
    shifts = shifts.astype(jnp.float32)
    bias_stack = bias_stack.astype(jnp.float32)
    width_size = output_weight.shape[0]
    hidden_units = up_weight.shape[1]
    row_count = residual_initial.shape[0]
    heads = width_size // HEAD_DIM
    first_normed = layer_norm(residual_initial, gains[0], shifts[0]).astype(jnp.bfloat16)
    first_plain = first_normed.astype(jnp.float32)
    joined_rows = (
        dot_without_transpose(first_normed, query_key_value_weight) + bias_stack[: 3 * width_size]
    )
    adapt_in = []
    projected = []
    for which_index in range(3):
        inner_product = dot_without_transpose(
            first_plain, adapter_down[which_index], highest_precision
        )
        adapt_in.append(inner_product)
        branch_output = joined_rows[
            :, which_index * width_size : (which_index + 1) * width_size
        ] + adapter_scale * dot_without_transpose(
            inner_product, adapter_up[which_index], highest_precision
        )
        projected.append(branch_output.astype(jnp.bfloat16).reshape(row_count, heads, HEAD_DIM))
    query, key_rows, value_rows = projected
    scores = attention_scores(query, key_rows, allowed_mask)
    top = jnp.max(scores, axis=-1, keepdims=True)
    expo = jnp.exp(scores - top)
    summed = jnp.sum(expo, axis=-1, keepdims=True)
    log_total = top + jnp.log(summed)
    probs = (expo / summed).astype(jnp.bfloat16)
    mixed_state = jnp.einsum("hst,thd->shd", probs, value_rows, preferred_element_type=jnp.float32)
    mixed_state = mixed_state.reshape(row_count, width_size).astype(jnp.bfloat16)
    mixed_plain = mixed_state.astype(jnp.float32)
    adapter_output = dot_without_transpose(mixed_plain, adapter_down[3], highest_precision)
    attended_rows = (
        dot_without_transpose(mixed_state, output_weight)
        + bias_stack[3 * width_size : 4 * width_size]
        + adapter_scale * dot_without_transpose(adapter_output, adapter_up[3], highest_precision)
    )
    stream_one = residual_initial + attended_rows
    normed_two = layer_norm(stream_one, gains[1], shifts[1]).astype(jnp.bfloat16)
    before_gelu = (
        dot_without_transpose(normed_two, up_weight)
        + bias_stack[4 * width_size : 4 * width_size + hidden_units]
    )
    activation = jax.nn.gelu(before_gelu, approximate=True).astype(jnp.bfloat16)
    stream_two = (
        stream_one
        + dot_without_transpose(activation, down_weight)
        + bias_stack[4 * width_size + hidden_units :]
    )
    final_state = layer_norm(stream_two, gains[2], shifts[2]).astype(jnp.bfloat16)
    kept_rows = (
        first_plain,
        adapt_in,
        query,
        key_rows,
        value_rows,
        log_total,
        mixed_plain,
        adapter_output,
        stream_one,
        before_gelu,
        stream_two,
    )
    return (final_state, kept_rows)


def layer_backward(
    final_gradient, kept_rows, backward_weights, adapter_down, adapter_up, allowed_mask
):
    output_weight, up_weight, down_weight, gains = backward_weights
    gains = gains.astype(jnp.float32)
    (
        first_plain,
        adapt_in,
        query,
        key_rows,
        value_rows,
        log_total,
        mixed_plain,
        adapter_output,
        stream_one,
        before_gelu,
        stream_two,
    ) = kept_rows
    row_count = query.shape[0]
    width_size = query.shape[1] * HEAD_DIM
    _, pull_three = jax.vjp(lambda values: layer_norm(values, gains[2], 0.0), stream_two)
    grad_two = pull_three(final_gradient)[0]
    grad_act = dot_last_axis(grad_two.astype(jnp.bfloat16), down_weight)
    _, pull_gelu = jax.vjp(partial(jax.nn.gelu, approximate=True), before_gelu)
    grad_pre = pull_gelu(grad_act)[0].astype(jnp.bfloat16)
    _, pull_two = jax.vjp(lambda values: layer_norm(values, gains[1], 0.0), stream_one)
    first_gradient = grad_two + pull_two(dot_last_axis(grad_pre, up_weight))[0]
    attention_gradient = first_gradient.astype(jnp.bfloat16)
    attention_scaled = adapter_scale * rounded_values(first_gradient)
    up_grads = [None, None, None, None]
    down_grads = [None, None, None, None]
    up_grads[3] = dot_first(adapter_output, attention_scaled, highest_precision)
    backward_output = dot_last_axis(attention_scaled, adapter_up[3], highest_precision)
    down_grads[3] = dot_first(mixed_plain, backward_output, highest_precision)
    mixed_gradient = dot_last_axis(attention_gradient, output_weight) + dot_last_axis(
        backward_output, adapter_down[3], highest_precision
    )
    grad_heads = mixed_gradient.astype(jnp.bfloat16).reshape(query.shape)
    probs = jnp.exp(attention_scores(query, key_rows, allowed_mask) - log_total)
    grad_value = jnp.einsum(
        "hst,shd->thd", probs.astype(jnp.bfloat16), grad_heads, preferred_element_type=jnp.float32
    )
    grad_probs = jnp.einsum(
        "shd,thd->hst", grad_heads, value_rows, preferred_element_type=jnp.float32
    )
    grad_scores = probs * (grad_probs - jnp.sum(probs * grad_probs, axis=-1, keepdims=True))
    grad_scores = grad_scores.astype(jnp.bfloat16)
    grad_query = (
        jnp.einsum("hst,thd->shd", grad_scores, key_rows, preferred_element_type=jnp.float32)
        * score_scale
    )
    grad_key = (
        jnp.einsum("hst,shd->thd", grad_scores, query, preferred_element_type=jnp.float32)
        * score_scale
    )
    for which_index, branch_gradient in enumerate((grad_query, grad_key, grad_value)):
        scaled_values = adapter_scale * rounded_values(
            branch_gradient.reshape(row_count, width_size)
        )
        up_grads[which_index] = dot_first(adapt_in[which_index], scaled_values, highest_precision)
        backward_input = dot_last_axis(scaled_values, adapter_up[which_index], highest_precision)
        down_grads[which_index] = dot_first(first_plain, backward_input, highest_precision)
    return (jnp.stack(down_grads), jnp.stack(up_grads))


def orthogonalize(matrices, sum_grams):
    grams = sum_grams(
        jnp.einsum(
            "mrd,msd->mrs",
            matrices,
            matrices,
            precision=highest_precision,
            preferred_element_type=jnp.float32,
        )
    )
    sizes = jnp.sqrt(jnp.trace(grams, axis1=1, axis2=2))[:, None, None] + 1e-07
    state = matrices / sizes
    grams = grams / (sizes * sizes)
    for turn_index in range(5):
        if turn_index:
            grams = sum_grams(
                jnp.einsum(
                    "mrd,msd->mrs",
                    state,
                    state,
                    precision=highest_precision,
                    preferred_element_type=jnp.float32,
                )
            )
        poly = coef_b * grams + coef_c * jnp.einsum(
            "mrs,mst->mrt",
            grams,
            grams,
            precision=highest_precision,
            preferred_element_type=jnp.float32,
        )
        state = coef_a * state + jnp.einsum(
            "mrs,msd->mrd",
            poly,
            state,
            precision=highest_precision,
            preferred_element_type=jnp.float32,
        )
    return state


def per_device_general(
    ids,
    targets,
    counted_mask,
    lengths,
    table,
    position_table,
    layer_norm_gain,
    layer_norm_bias,
    query_key_value_weight,
    output_weight,
    up_weight,
    down_weight,
    biases,
    adapter_down,
    adapter_up,
    down_momentum,
    up_momentum,
):
    gathered = (
        lax.all_gather(query_key_value_weight, ("dp", "vocab"), axis=0, tiled=True),
        lax.all_gather(output_weight, ("dp", "vocab"), axis=0, tiled=True),
        lax.all_gather(up_weight, ("dp", "vocab"), axis=0, tiled=True),
        lax.all_gather(down_weight, ("dp", "vocab"), axis=0, tiled=True),
        lax.all_gather(layer_norm_gain, ("dp", "vocab"), axis=1, tiled=True),
        lax.all_gather(layer_norm_bias, ("dp", "vocab"), axis=1, tiled=True),
        lax.all_gather(biases, ("dp", "vocab"), axis=0, tiled=True),
        lax.all_gather(position_table, ("dp", "vocab"), axis=1, tiled=True),
    )
    w_qkv_all, w_out_all, w_up_all, w_down_all, gains_all, shifts_all, bias_stack, positions_all = (
        gathered
    )
    row_count = ids.shape[0]
    width_size = w_out_all.shape[0]
    group = lax.axis_size("vocab")
    vocab_pos = lax.axis_index("vocab")
    piece_rows = table.shape[0]
    ids_all, target_all, mask_all = (
        lax.all_gather(ids, "vocab", axis=0, tiled=True),
        lax.all_gather(targets, "vocab", axis=0, tiled=True),
        lax.all_gather(counted_mask, "vocab", axis=0, tiled=True),
    )
    table_full = lax.all_gather(table, "dp", axis=0, tiled=True)
    vocab_rows = table_full.shape[0]
    local_ids = owner_rows(ids_all, piece_rows, group, vocab_pos)
    inside = local_ids >= 0
    picked_rows = table_full[jnp.clip(local_ids, 0, vocab_rows - 1)]
    picked_rows = jnp.where(inside[:, None], picked_rows, jnp.zeros_like(picked_rows))
    embedded = lax.psum_scatter(
        picked_rows.astype(jnp.float32).astype(jnp.bfloat16),
        "vocab",
        scatter_dimension=0,
        tiled=True,
    ).astype(jnp.float32)
    positions_in, allowed_mask = layout(lengths[0], row_count)
    residual_initial = embedded + positions_all[positions_in].astype(jnp.float32)
    frozen_weights = (w_qkv_all, w_out_all, w_up_all, w_down_all, gains_all, shifts_all, bias_stack)
    final_state, kept_rows = layer_forward(
        residual_initial, frozen_weights, adapter_down, adapter_up, allowed_mask
    )
    final_all = lax.all_gather(final_state, "vocab", axis=0, tiled=True)
    total_rows = final_all.shape[0]
    block = 512
    count_blocks = total_rows // block
    final_blocks = final_all.reshape(count_blocks, block, width_size)
    local_targets = owner_rows(target_all, piece_rows, group, vocab_pos).reshape(
        count_blocks, block
    )
    columns = jnp.arange(vocab_rows, dtype=jnp.int32)

    def head_stats(item):
        piece, local = item
        logits = dot_last_axis(piece, table_full)
        top = jnp.max(logits, axis=1)
        expsum = jnp.sum(jnp.exp(logits - top[:, None]), axis=1)
        target_logit = jnp.sum(jnp.where(columns[None, :] == local[:, None], logits, 0.0), axis=1)
        return (top, expsum, target_logit, jnp.sum(logits, axis=1))

    stats = lax.map(head_stats, (final_blocks, local_targets))
    stats = tuple((entry.reshape(total_rows) for entry in stats))

    def combine(first_part, second_part):
        larger = jnp.maximum(first_part[0], second_part[0])
        merged_sum = first_part[1] * jnp.exp(first_part[0] - larger) + second_part[1] * jnp.exp(
            second_part[0] - larger
        )
        return (larger, merged_sum, first_part[2] + second_part[2], first_part[3] + second_part[3])

    top, expsum, target_logit, logit_sum = merged(stats, "vocab", combine)
    log_total = top + jnp.log(expsum)
    row_loss = log_total - (1.0 - smooth) * target_logit - smooth * logit_sum / V
    mask_float = mask_all.astype(jnp.float32)
    own_start = vocab_pos * row_count
    loss_own = jnp.sum(lax.dynamic_slice_in_dim(mask_float * row_loss, own_start, row_count))
    count_own = jnp.sum(counted_mask.astype(jnp.float32))

    def head_grad(item):
        piece, local, lse_block, weight = item
        logits = dot_last_axis(piece, table_full)
        probs = jnp.exp(logits - lse_block[:, None])
        onehot = (columns[None, :] == local[:, None]).astype(jnp.float32)
        grad_logits = weight[:, None] * (probs - (1.0 - smooth) * onehot - smooth / V)
        return dot_without_transpose(grad_logits.astype(jnp.bfloat16), table_full)

    partial_rows = lax.map(
        head_grad,
        (
            final_blocks,
            local_targets,
            log_total.reshape(count_blocks, block),
            mask_float.reshape(count_blocks, block),
        ),
    )
    final_gradient = lax.psum_scatter(
        partial_rows.reshape(total_rows, width_size).astype(jnp.bfloat16),
        "vocab",
        scatter_dimension=0,
        tiled=True,
    ).astype(jnp.float32)
    backward_weights = (
        lax.all_gather(output_weight, ("dp", "vocab"), axis=0, tiled=True),
        lax.all_gather(up_weight, ("dp", "vocab"), axis=0, tiled=True),
        lax.all_gather(down_weight, ("dp", "vocab"), axis=0, tiled=True),
        lax.all_gather(layer_norm_gain, ("dp", "vocab"), axis=1, tiled=True),
    )
    down_gradient, up_gradient = layer_backward(
        final_gradient, kept_rows, backward_weights, adapter_down, adapter_up, allowed_mask
    )
    down_gradient, up_gradient, smoothed_loss_sum, loss_count = lax.psum(
        (down_gradient, up_gradient, loss_own, count_own), ("dp", "vocab")
    )
    grad_norm = jnp.sqrt(
        jnp.sum(down_gradient * down_gradient) + jnp.sum(up_gradient * up_gradient)
    )
    factor = jnp.minimum(1.0, clip_level / (grad_norm + 1e-06))
    new_mom_down = momentum * down_momentum + factor * down_gradient
    new_mom_up = momentum * up_momentum + factor * up_gradient
    stacked = jnp.concatenate([jnp.swapaxes(new_mom_down, 1, 2), new_mom_up], axis=0)
    share_fraction = stacked.shape[2] // group
    begin_index = vocab_pos * share_fraction
    orthogonal_update = lax.dynamic_slice_in_dim(
        orthogonalize(stacked, lambda grams: grams), begin_index, share_fraction, 2
    )
    mom_down_part = lax.dynamic_slice_in_dim(new_mom_down, begin_index, share_fraction, 1)
    mom_up_part = lax.dynamic_slice_in_dim(new_mom_up, begin_index, share_fraction, 2)
    down_fresh = lax.dynamic_slice_in_dim(
        adapter_down, begin_index, share_fraction, 1
    ) - learning_rate * jnp.swapaxes(orthogonal_update[:4], 1, 2)
    up_fresh = (
        lax.dynamic_slice_in_dim(adapter_up, begin_index, share_fraction, 2)
        - learning_rate * orthogonal_update[4:]
    )
    return (
        smoothed_loss_sum,
        loss_count,
        grad_norm,
        mom_down_part,
        mom_up_part,
        down_fresh,
        up_fresh,
        down_fresh.astype(jnp.bfloat16),
        up_fresh.astype(jnp.bfloat16),
    )


MESH = pl.DeviceIdType.MESH
CAP = 32


def dot_nt(left_side, right_side, setting=None):
    return dot_last_axis(left_side, right_side, setting)


def position():
    dp, z = lax.axis_index("dp"), lax.axis_index("vocab")
    y, x, core = dp // 4, dp // 2 % 2, dp % 2

    def place(y_at, x_at, core_at):
        return y_at * 4 + x_at * 2 + core_at

    along = (z, z // 2 * 2 + 1 - z % 2, (z + 2) % 4, (1 - z // 2) * 2 + 1 - z % 2)
    return dp, z, y, x, core, place, along


def inner(z):
    return (z + 1) // 2 % 2


def mirror(z, other):
    return (z // 2 + other // 2) % 2 * 2 + (z + other) % 2


def nearness(z, other):
    k = mirror(z, other)
    return k + inner(z) * (k // 2) * (5 - 2 * k)


def by_nearness(z):
    far = z // 2 * 3
    near = 2 - z // 2
    return (z, z // 2 * 2 + 1 - z % 2, near, 3 - far)


def meet_all(devices, group):
    me = lax.axis_index("dp") * group + lax.axis_index("vocab")
    barrier = pltpu.get_barrier_semaphore()

    def signal(step, state):
        other = lax.rem(me + step, devices)
        pl.semaphore_signal(
            barrier, inc=1, device_id=(other // group, other % group), device_id_type=MESH
        )
        return state

    lax.fori_loop(1, devices, signal, 0)
    pl.semaphore_wait(barrier, devices - 1)
    return me


def to_all(source_of, target, send_sems, recv_sems, devices, group, me):
    def copy(step):
        other = lax.rem(me + step, devices)
        return pltpu.make_async_remote_copy(
            source_of(other),
            target.at[me],
            send_sems.at[step],
            recv_sems.at[step],
            device_id=(other // group, other % group),
            device_id_type=MESH,
        )

    def start():
        def one(step, state):
            copy(step).start()
            return state

        lax.fori_loop(1, devices, one, 0)

    def arrive():
        def one(step, state):
            source = lax.rem(me + devices - step, devices)
            pltpu.make_async_remote_copy(
                target.at[source],
                target.at[source],
                send_sems.at[step],
                recv_sems.at[step],
                device_id=(source // group, source % group),
                device_id_type=MESH,
            ).wait_recv()
            return state

        lax.fori_loop(1, devices, one, 0)

    def sent():
        def one(step, state):
            copy(step).wait_send()
            return state

        lax.fori_loop(1, devices, one, 0)

    return start, arrive, sent


ARRIVE, TILE, BACK, MIDDLE, COLUMN = range(5)
ORDER = (
    (ARRIVE, 0, 1),
    (ARRIVE, 0, 2),
    (ARRIVE, 0, 3),
    (ARRIVE, 2, 1),
    (ARRIVE, 2, 0),
    (ARRIVE, 1, 0),
    (TILE, 2, 1),
    (TILE, 1, 0),
    (TILE, 0, 3),
    (ARRIVE, 1, 1),
    (ARRIVE, 1, 3),
    (ARRIVE, 2, 3),
    (ARRIVE, 1, 2),
    (BACK, 2, 1),
    (ARRIVE, 2, 2),
    (TILE, 0, 2),
    (TILE, 1, 3),
    (ARRIVE, 3, 1),
    (TILE, 1, 2),
    (BACK, 1, 3),
    (ARRIVE, 3, 3),
    (TILE, 3, 1),
    (TILE, 3, 3),
    (BACK, 3, 3),
    (ARRIVE, 3, 2),
    (TILE, 2, 3),
    (BACK, 2, 3),
    (ARRIVE, 3, 0),
    (BACK, 3, 1),
    (TILE, 0, 1),
    (MIDDLE, 1, 3),
    (BACK, 1, 2),
    (MIDDLE, 0, 3),
    (TILE, 1, 1),
    (TILE, 3, 2),
    (COLUMN, 1, 3),
    (BACK, 3, 2),
    (MIDDLE, 1, 1),
    (TILE, 3, 0),
    (COLUMN, 0, 3),
    (MIDDLE, 0, 1),
    (TILE, 2, 2),
    (MIDDLE, 0, 2),
    (BACK, 3, 0),
    (TILE, 2, 0),
    (BACK, 1, 1),
    (COLUMN, 1, 1),
    (MIDDLE, 1, 2),
    (BACK, 1, 0),
    (COLUMN, 0, 2),
    (BACK, 2, 2),
    (MIDDLE, 0, 0),
    (TILE, 0, 0),
    (COLUMN, 0, 1),
    (BACK, 2, 0),
    (COLUMN, 1, 2),
    (MIDDLE, 1, 0),
    (COLUMN, 0, 0),
    (COLUMN, 1, 0),
)


def of_four(values, at):
    low, high = at % 2, at // 2
    return (1 - high) * ((1 - low) * values[0] + low * values[1]) + high * (
        (1 - low) * values[2] + low * values[3]
    )


def head_kernel(table_rows, chunks, own, tab_a, turn_a, tab_b, turn_b, mean_out, lse_out, *refs):
    (
        tab,
        turn,
        score_a,
        score_b,
        total,
        hidden,
        part,
        part_lse,
        got,
        got_lse,
        load_sems,
        send_sems,
        recv_sems,
        back_send,
        back_recv,
    ) = refs
    dp, z, y, x, core, place, _ = position()
    along = by_nearness(z)
    pad_rows = tab_a.shape[0]
    width, tile = own.shape[1], own.shape[0]
    tiles = [event[1:] for event in ORDER if event[0] == TILE]
    slot = {at: index for index, at in enumerate(tiles)}
    columns = [slot[0, k] for k in range(4)]
    dev_x, dev_y = (place(y, 1 - x, core), z), (place(1 - y, x, core), z)
    dev_z = [(dp, along[k]) for k in range(4)]
    peers = [dev_x, dev_y] + dev_z[1:]
    loads = []
    for at, (source, target) in enumerate(
        (
            (own, hidden.at[slot[0, 0]]),
            (tab_a, tab.at[pl.ds(0, pad_rows)]),
            (tab_b, tab.at[pl.ds(pad_rows, pad_rows)]),
            (turn_a, turn.at[:, pl.ds(0, pad_rows)]),
            (turn_b, turn.at[:, pl.ds(pad_rows, pad_rows)]),
        )
    ):
        copy = pltpu.make_async_copy(source, target, load_sems.at[at])
        copy.start()
        loads.append(copy)
    barrier = pltpu.get_barrier_semaphore()
    for peer in peers:
        pl.semaphore_signal(barrier, inc=1, device_id=peer, device_id_type=MESH)
    pl.semaphore_wait(barrier, len(peers))
    loads[0].wait()

    sent = []

    def give(source, target, peer, half=None):
        rows = pl.ds(0, tile) if half is None else pl.ds(half * (tile // 2), tile // 2)
        copy = pltpu.make_async_remote_copy(
            hidden.at[slot[source], rows],
            hidden.at[slot[target], rows],
            send_sems.at[len(sent)],
            recv_sems.at[slot[target] + (16 if half == 1 else 0)],
            device_id=peer,
            device_id_type=MESH,
        )
        sent.append(copy)
        return copy

    def give_along(k, upward):
        there = z + 1 if upward else z - 1
        target = of_four(columns, nearness(there, along[k]))
        return pltpu.make_async_remote_copy(
            hidden.at[slot[0, k]],
            hidden.at[target],
            send_sems.at[24 + k + 4 * (not upward and k == 0)],
            recv_sems.at[target],
            device_id=(dp, there),
            device_id_type=MESH,
        )

    def pass_along(k, act):
        @pl.when((along[k] <= z) & (z < 3))
        def _():
            act(give_along(k, True))

        @pl.when((along[k] >= z) & (z > 0))
        def _():
            act(give_along(k, False))

    def start_all(copies):
        for copy in copies:
            copy.start()

    forwards = {}
    for k in range(4):
        forwards[0, k] = [give((0, k), (1, k), dev_x), give((0, k), (2, k), dev_y)]
        forwards[1, k] = [give((1, k), (3, k), dev_y, 1)]
        forwards[2, k] = [give((2, k), (3, k), dev_x, 0)]
        forwards[3, k] = []
    pass_along(0, lambda copy: copy.start())
    start_all(forwards[0, 0])

    def arrive(q, k):
        there = slot[q, k]
        cuts = [(pl.ds(0, tile), there)]
        if q == 3:
            cuts = [(pl.ds(0, tile // 2), there), (pl.ds(tile // 2, tile // 2), there + 16)]
        for rows, at in cuts:
            pltpu.make_async_remote_copy(
                hidden.at[there, rows],
                hidden.at[there, rows],
                send_sems.at[0],
                recv_sems.at[at],
                device_id=dev_x,
                device_id_type=MESH,
            ).wait_recv()
        if q == 0:
            pass_along(k, lambda copy: copy.start())
        start_all(forwards[q, k])

    back_sent = []

    def half_rows(half):
        return pl.ds(half * (width // 2), width // 2)

    def back_copies(number, q, k, half, landing, peer):
        if q == 0:
            landing = landing + 2 * mirror(z, along[k])
        return [
            pltpu.make_async_remote_copy(
                source,
                target,
                back_send.at[kind, number],
                back_recv.at[kind, landing],
                device_id=peer,
                device_id_type=MESH,
            )
            for kind, (source, target) in enumerate(
                (
                    (part.at[slot[q, k], half_rows(half)], got.at[landing]),
                    (part_lse.at[2 * slot[q, k] + half], got_lse.at[landing]),
                )
            )
        ]

    def back(*what):
        start_all(back_copies(len(back_sent), *what))
        back_sent.append(what)

    def back_wait(landing):
        for kind, target in enumerate((got, got_lse)):
            pltpu.make_async_remote_copy(
                target.at[landing],
                target.at[landing],
                back_send.at[kind, 0],
                back_recv.at[kind, landing],
                device_id=dev_x,
                device_id_type=MESH,
            ).wait_recv()

    def merge(q, k, half, landings):
        at = slot[q, k]
        for landing in landings:
            back_wait(landing)
        levels = [part_lse[2 * at + half]] + [got_lse[landing] for landing in landings]
        top = levels[0]
        for level in levels[1:]:
            top = jnp.maximum(top, level)
        shares = [jnp.exp(level - top) for level in levels]
        whole = sum(shares[1:], shares[0])
        shares = [share / whole for share in shares]
        part_lse[2 * at + half] = top + jnp.log(whole)
        begin = half * (width // 2)

        def rows(step, state):
            here = pl.ds(pl.multiple_of(step * 128, 128), 128)
            mine = pl.ds(pl.multiple_of(begin + step * 128, 128), 128)
            mixed = part[at, mine].astype(jnp.float32) * shares[0]
            for landing, share in zip(landings, shares[1:], strict=True):
                mixed += got[landing, here].astype(jnp.float32) * share
            part[at, mine] = mixed.astype(jnp.bfloat16)
            return state

        lax.fori_loop(0, width // 256, rows, 0)

    def go_back(q, k):
        if q == 3:
            back(3, k, 0, 16 + 2 * k, dev_x)
            back(3, k, 1, 17 + 2 * k, dev_y)
        elif q == 1:
            back(1, k, 0, 2 * k, dev_x)
        else:
            back(2, k, 1, 9 + 2 * k, dev_y)

    def merge_middle(half, k):
        q = 1 if half else 2
        merge(q, k, half, [16 + 2 * k + half])
        if half:
            back(1, k, 1, 1 + 2 * k, dev_x)
        else:
            back(2, k, 0, 8 + 2 * k, dev_y)

    def merge_column(half, k):
        merge(0, k, half, [2 * k + half, 8 + 2 * k + half])
        if k:
            back(0, k, half, 22 + half, dev_z[k])

    acts = {ARRIVE: arrive, BACK: go_back, MIDDLE: merge_middle, COLUMN: merge_column}
    groups = [[]]
    for event in ORDER:
        if event[0] == TILE:
            groups.append([])
        else:
            groups[-1].append(event)

    def work(group):
        for event in group:
            acts[event[0]](*event[1:])

    def events_before(t, parity):
        for at in range(parity, 16, 2):
            if groups[at]:

                @pl.when(t == at)
                def _(at=at):
                    work(groups[at])

    for copy in loads[1:]:
        copy.wait()
    starts = [sum(chunks[:at]) for at in range(len(chunks))]
    low = jnp.full((8, tile), -jnp.inf, jnp.float32)

    def scores_of(rows, at, score, top):
        begin, size = starts[at], chunks[at]
        values = dot_nt(tab[begin : begin + size], rows)
        score[begin : begin + size] = values
        cuts = [(begin, begin + size, False)]
        for half in range(2):
            edge = half * pad_rows + table_rows // 8 * 8
            stop = (half + 1) * pad_rows
            if begin <= edge < begin + size:
                cuts = [(begin, edge, False), (edge, min(stop, begin + size), True)]
                if stop < begin + size:
                    cuts.append((stop, begin + size, False))
        for first_row, last, masked in cuts:
            if first_row == last:
                continue
            cut = values[first_row - begin : last - begin]
            if masked:
                row = lax.broadcasted_iota(jnp.int32, cut.shape, 0)
                cut = jnp.where(row < table_rows % 8, cut, masked_value)
                score[first_row:last] = cut
            top = jnp.maximum(top, jnp.max(cut.reshape(-1, 8, tile), axis=0))
        return top

    def half_step(t, parity, score, score_next, top):
        events_before(t, parity)
        rows = hidden[jnp.minimum(t + 1, 15)]
        peak = jnp.max(top, axis=0, keepdims=True)
        summed = jnp.zeros((8, tile), jnp.float32)
        top_next = low
        for at in range(len(chunks)):
            begin, size = starts[at], chunks[at]
            expo = jnp.exp(score[begin : begin + size] - peak)
            summed += jnp.sum(expo.reshape(-1, 8, tile), axis=0)
            top_next = scores_of(rows, at, score_next, top_next)
            product = dot_without_transpose(
                turn[:, begin : begin + size], expo.astype(jnp.bfloat16)
            )
            if at == 0:
                total[...] = product
            else:
                total[...] += product
        denominator = jnp.sum(summed, axis=0, keepdims=True)
        part[t] = (total[...] * (1.0 / denominator)).astype(jnp.bfloat16)
        level = peak + jnp.log(denominator)
        part_lse[2 * t] = level
        part_lse[2 * t + 1] = level
        return top_next

    if tiles[0] != (0, 0):
        until = groups[0].index((ARRIVE,) + tiles[0]) + 1
        work(groups[0][:until])
        del groups[0][:until]
    top = low
    for at in range(len(chunks)):
        top = scores_of(hidden[0], at, score_a, top)

    def two_steps(step, top):
        top = half_step(2 * step, 0, score_a, score_b, top)
        return half_step(2 * step + 1, 1, score_b, score_a, top)

    lax.fori_loop(0, 8, two_steps, top)
    work(groups[16])
    home = slot[0, 0]
    merge(0, 0, 0, [24, 26, 28])
    merge(0, 0, 1, [25, 27, 29])
    mean_out[...] = part[home]
    lse_out[...] = part_lse[2 * home]
    for k in range(4):
        pass_along(k, lambda copy: copy.wait_send())
    for copy in sent:
        copy.wait_send()
    for number, what in enumerate(back_sent):
        for copy in back_copies(number, *what):
            copy.wait_send()


def head(final_state, table_rows, tables):
    tile, width = final_state.shape
    pad_rows = tables[0].shape[0]
    both = 2 * pad_rows
    chunks = [both // 256 // 4 * 256] * 4
    chunks[0] += both - sum(chunks)
    anywhere, vmem = pl.BlockSpec(memory_space=pl.ANY), pl.BlockSpec(memory_space=pltpu.VMEM)
    dma = pltpu.SemaphoreType.DMA
    return pl.pallas_call(
        partial(head_kernel, table_rows, chunks),
        out_shape=[
            jax.ShapeDtypeStruct((width, tile), jnp.bfloat16),
            jax.ShapeDtypeStruct((1, tile), jnp.float32),
        ],
        in_specs=[anywhere] * 5,
        out_specs=[vmem] * 2,
        scratch_shapes=[
            pltpu.VMEM((both, width), jnp.bfloat16),
            pltpu.VMEM((width, both), jnp.bfloat16),
            pltpu.VMEM((both, tile), jnp.float32),
            pltpu.VMEM((both, tile), jnp.float32),
            pltpu.VMEM((width, tile), jnp.float32),
            pltpu.VMEM((16, tile, width), jnp.bfloat16),
            pltpu.VMEM((16, width, tile), jnp.bfloat16),
            pltpu.VMEM((32, 1, tile), jnp.float32),
            pltpu.VMEM((30, width // 2, tile), jnp.bfloat16),
            pltpu.VMEM((30, 1, tile), jnp.float32),
            dma((5,)),
            dma((32,)),
            dma((32,)),
            dma((2, 30)),
            dma((2, 30)),
        ],
        name="head",
        compiler_params=pltpu.CompilerParams(
            collective_id=2, has_side_effects=True, vmem_limit_bytes=62 * 2**20
        ),
    )(final_state, *tables)


def update_kernel(devices, group, grads, momenta, weights, new_momenta, new_weights, numbers, *refs):
    parts, whole, piece, sems, back_sems = refs
    me = meet_all(devices, group)
    z = lax.axis_index("vocab")
    parts[pl.ds(me, 1)] = grads[pl.ds(me, 1)]
    start, arrive, sent = to_all(
        lambda other: grads.at[other], parts, sems.at[0], sems.at[1], devices, group, me
    )
    start()
    arrive()
    summed = parts[0]
    for source in range(1, devices):
        summed += parts[source]
    width = momenta.shape[1]
    piece[...] = summed[:, :width]
    whole[pl.ds(me, 1)] = summed[None, :, :width]
    start, back_arrive, back_sent = to_all(
        lambda other: piece, whole, back_sems.at[0], back_sems.at[1], devices, group, me
    )
    start()
    back_arrive()
    gradient = whole[...].reshape(devices, width)
    squares = jnp.sum(jnp.sum(gradient * gradient, axis=0, keepdims=True), axis=1, keepdims=True)
    norm = jnp.sqrt(squares)
    factor = jnp.minimum(1.0, clip_level / (norm + 1e-06))
    state = momentum * momenta[...] + factor * gradient
    share = new_momenta.shape[1]
    columns = pl.ds(pl.multiple_of(z * share, share), share)
    whole[...] = state.reshape(devices, 1, width)
    new_momenta[...] = whole[:, 0, columns]
    square = (devices, devices)
    row = lax.broadcasted_iota(jnp.int32, square, 0)
    column = lax.broadcasted_iota(jnp.int32, square, 1)
    rank = 4
    blocks = row // rank == column // rank

    def gram_of(matrix):
        return jnp.where(blocks, dot_nt(matrix, matrix, highest_precision), 0.0)

    grams = gram_of(state)
    diagonal = jnp.sum(jnp.where(row == column, grams, 0.0), axis=0, keepdims=True)
    traces = jnp.sum(jnp.where(blocks, diagonal, 0.0), axis=1, keepdims=True)
    sizes = jnp.sqrt(traces) + 1e-07
    state = state / sizes
    grams = grams / (sizes * sizes)
    for turn_index in range(5):
        if turn_index:
            grams = gram_of(state)
        poly = coef_b * grams + coef_c * dot_without_transpose(grams, grams, highest_precision)
        state = coef_a * state + dot_without_transpose(poly, state, highest_precision)
    whole[...] = (weights[...] - learning_rate * state).reshape(devices, 1, width)
    new_weights[...] = whole[:, 0, columns]
    lanes = lax.broadcasted_iota(jnp.int32, (1, 128), 1)
    numbers[...] = jnp.where(lanes == 2, norm, summed[:, width:])
    sent()
    back_sent()


def update(grads, momenta, weights):
    group = lax.axis_size("vocab")
    devices = lax.axis_size("dp") * group
    width = momenta.shape[1]
    vmem = pl.BlockSpec(memory_space=pltpu.VMEM)
    dma = pltpu.SemaphoreType.DMA
    small = jax.ShapeDtypeStruct((devices, width // group), jnp.float32)
    return pl.pallas_call(
        partial(update_kernel, devices, group),
        out_shape=[small, small, jax.ShapeDtypeStruct((1, 128), jnp.float32)],
        in_specs=[vmem] * 3,
        out_specs=[vmem] * 3,
        scratch_shapes=[
            pltpu.VMEM(grads.shape, jnp.float32),
            pltpu.VMEM((devices, 1, width), jnp.float32),
            pltpu.VMEM((1, width), jnp.float32),
            dma((2, devices)),
            dma((2, devices)),
        ],
        name="update",
        compiler_params=pltpu.CompilerParams(collective_id=3, has_side_effects=True),
    )(grads, momenta, weights)


def halves_of(values):
    high = values.astype(jnp.bfloat16)
    return high, (values - high.astype(jnp.float32)).astype(jnp.bfloat16)


def stacked_halves(values):
    return jnp.concatenate(halves_of(values), axis=0)


def added_halves(values):
    rows = values.shape[0] // 2
    return values[:rows] + values[rows:]


def dot_tn(left_side, right_side):
    return dot_first(left_side, right_side)


def normal(values):
    center = values - jnp.mean(values, axis=-1, keepdims=True)
    spread = lax.rsqrt(jnp.mean(center * center, axis=-1, keepdims=True) + ln_eps)
    return center * spread, spread


def normal_back(values, gain, gradient):
    unit, spread = normal(values)
    pulled = gradient * gain
    along = jnp.mean(pulled * unit, axis=-1, keepdims=True)
    return spread * (pulled - jnp.mean(pulled, axis=-1, keepdims=True) - unit * along)


def sequence_places(lengths, rows):
    col = lax.broadcasted_iota(jnp.int32, (rows, 1), 0)
    row = lax.broadcasted_iota(jnp.int32, (1, rows), 1)
    segment_col, segment_row = jnp.zeros_like(col), jnp.zeros_like(row)
    start_col = jnp.zeros_like(col)
    end = 0
    for at in range(lengths.shape[1]):
        length = lengths[0, at]
        end = end + length
        segment_col += (col >= end).astype(jnp.int32)
        segment_row += (row >= end).astype(jnp.int32)
        start_col += jnp.where(col >= end, length, 0)
    allowed = (segment_col == segment_row) & (row <= col)
    return col - start_col, allowed


def pairs_of(width):
    return width // (2 * HEAD_DIM)


def pair_at(pair):
    return pl.ds(pl.multiple_of(pair * 2 * HEAD_DIM, 2 * HEAD_DIM), 2 * HEAD_DIM)


def head_lanes(rows):
    return lax.broadcasted_iota(jnp.int32, (rows, 2 * HEAD_DIM), 1) < HEAD_DIM


def first_part(embedded, positions, lengths, gains, shifts, x0, h1):
    rows = x0.shape[0]
    place_col, allowed = sequence_places(lengths, rows)
    spots = lax.broadcasted_iota(jnp.int32, (rows, positions.shape[0]), 1)
    hot = (place_col == spots).astype(jnp.float32).astype(jnp.bfloat16)
    x0[...] = embedded[...] + dot_without_transpose(hot, positions[...])
    unit, _ = normal(x0[...])
    h1[...] = (unit * gains[0:1] + shifts[0:1]).astype(jnp.bfloat16)
    return allowed


def adapter_in(adapters, inputs):
    return added_halves(dot_nt(stacked_halves(adapters), inputs))


def adapter_out(inner, outer):
    high, low = halves_of(inner)
    top, rest = halves_of(outer)
    return adapter_scale * dot_tn(
        jnp.concatenate([high, high, low], axis=0), jnp.concatenate([top, rest, top], axis=0)
    )


def ranks(which, shape):
    return lax.broadcasted_iota(jnp.int32, shape, 0) // 4 == which


def project_part(h1, weight, bias, adapters, inner, joined):
    width = h1.shape[1]
    step = 512
    half = adapters.shape[0] // 2
    inner[...] = adapter_in(adapters[:half], h1[...])
    for which in range(3):

        def columns(at, state):
            here = pl.ds(pl.multiple_of(at * step, step), step)
            there = pl.ds(pl.multiple_of(which * width + at * step, step), step)
            outer = jnp.where(ranks(which, (half, step)), adapters[half:, here], 0.0)
            joined[:, there] = (
                dot_without_transpose(h1[...], weight[:, there])
                + bias[:, there]
                + adapter_out(inner[...], outer)
            ).astype(jnp.bfloat16)
            return state

        lax.fori_loop(0, width // step, columns, 0)


def attend_part(joined, allowed, probs, mixed):
    rows, width = mixed.shape
    lanes = head_lanes(rows)

    def pair_step(pair, state):
        query = joined[:, pair_at(pair)]
        keys = joined[:, pair_at(pairs_of(width) + pair)]
        values = joined[:, pair_at(2 * pairs_of(width) + pair)]
        outs = []
        for side in range(2):
            mine = lanes if side == 0 else ~lanes
            scores = dot_nt(jnp.where(mine, query, jnp.zeros_like(query)), keys) * score_scale
            scores = jnp.where(allowed, scores, masked_value)
            expo = jnp.exp(scores - jnp.max(scores, axis=-1, keepdims=True))
            chances = (expo / jnp.sum(expo, axis=-1, keepdims=True)).astype(jnp.bfloat16)
            probs[2 * pair + side] = chances
            outs.append(dot_without_transpose(chances, values))
        mixed[:, pair_at(pair)] = jnp.where(lanes, outs[0], outs[1]).astype(jnp.bfloat16)
        return state

    lax.fori_loop(0, pairs_of(width), pair_step, 0)


def output_part(x0, mixed, weight, bias, adapters, inner, gains, shifts, x1, h2):
    half = adapters.shape[0] // 2
    width = mixed.shape[1]
    here = ranks(3, inner.shape)
    fresh = adapter_in(adapters[:half], mixed[...])
    inner[...] = jnp.where(here, fresh, inner[...])
    outer = jnp.where(ranks(3, (half, width)), adapters[half:], 0.0)
    x1[...] = (
        x0[...]
        + dot_without_transpose(mixed[...], weight[...])
        + bias[:, 3 * width : 4 * width]
        + adapter_out(inner[...], outer)
    )
    unit, _ = normal(x1[...])
    h2[...] = (unit * gains[1:2] + shifts[1:2]).astype(jnp.bfloat16)


def up_part(h2, weight, bias, active, slope):
    width = h2.shape[1]
    step = 512

    def columns(at, state):
        here = pl.ds(pl.multiple_of(at * step, step), step)
        there = pl.ds(pl.multiple_of(4 * width + at * step, step), step)
        z = dot_without_transpose(h2[...], weight[:, here]) + bias[:, there]
        root = 0.7978845608028654
        square = z * z
        tanh = jnp.tanh(root * z * (1.0 + 0.044715 * square))
        half = 0.5 * (1.0 + tanh)
        active[:, here] = (z * half).astype(jnp.bfloat16)
        slope[:, here] = (
            half + 0.5 * z * (1.0 - tanh * tanh) * (root * (1.0 + 3 * 0.044715 * square))
        ).astype(jnp.bfloat16)
        return state

    lax.fori_loop(0, weight.shape[1] // step, columns, 0)


def down_part(x1, active, weight, bias, gains, shifts, x2, final):
    hidden, width = weight.shape
    step = 256

    def columns(at, state):
        here = pl.ds(pl.multiple_of(at * step, step), step)
        there = pl.ds(pl.multiple_of(4 * width + hidden + at * step, step), step)
        x2[:, here] = (
            x1[:, here]
            + dot_without_transpose(active[...], weight[:, here])
            + bias[:, there]
        )
        return state

    lax.fori_loop(0, width // step, columns, 0)
    unit, _ = normal(x2[...])
    final[...] = (unit * gains[2:3] + shifts[2:3]).astype(jnp.bfloat16)


def turn_rows(source, target):
    width = source.shape[0]

    def rows(at, state):
        here = pl.ds(pl.multiple_of(at * 128, 128), 128)
        target[:, here] = source[here].astype(jnp.float32).T.astype(target.dtype)
        return state

    lax.fori_loop(0, width // 128, rows, 0)


def backward_kernel(
    mean_rows,
    log_total,
    mask_row,
    mask_col,
    target_rows,
    table_sum,
    gains,
    adapters,
    final,
    h1,
    joined,
    probs,
    mixed,
    inner,
    x1,
    slope,
    x2,
    w_out,
    w_up,
    w_down,
    grads,
    numbers,
    work,
    dx2,
    da,
    dz,
    dmix,
    pulls,
    out_here,
    up_here,
    down_here,
    sems,
):
    loads = []
    for at, (source, target) in enumerate(
        ((w_down, down_here), (w_up, up_here), (w_out, out_here))
    ):
        copy = pltpu.make_async_copy(source, target, sems.at[at])
        copy.start()
        loads.append(copy)
    rows, width = x1.shape
    half = adapters.shape[0] // 2
    hidden = slope.shape[1]
    turn_rows(mean_rows, work)
    pulled = (1.0 - smooth) * target_rows[...] + (smooth / V) * table_sum[...]
    row_dots = jnp.sum(final[...].astype(jnp.float32) * pulled, axis=1, keepdims=True)
    loss = jnp.sum(mask_row[...] * log_total[...], axis=1, keepdims=True) - jnp.sum(
        mask_col[...] * row_dots, axis=0, keepdims=True
    )
    counted = jnp.sum(mask_row[...], axis=1, keepdims=True)
    lanes = lax.broadcasted_iota(jnp.int32, (1, 128), 1)
    numbers[...] = jnp.where(lanes == 0, loss, jnp.where(lanes == 1, counted, 0.0))
    dx2[...] = normal_back(x2[...], gains[2:3], mask_col[...] * (work[...] - pulled))
    da[...] = dx2[...].astype(jnp.bfloat16)
    loads[0].wait()
    step = 512

    def hidden_columns(at, state):
        here = pl.ds(pl.multiple_of(at * step, step), step)
        dz[:, here] = (
            dot_nt(da[...], down_here[here]) * slope[:, here].astype(jnp.float32)
        ).astype(jnp.bfloat16)
        return state

    lax.fori_loop(0, hidden // step, hidden_columns, 0)
    loads[1].wait()

    def columns(at, state):
        here = pl.ds(pl.multiple_of(at * 256, 256), 256)
        work[:, here] = dot_nt(dz[...], up_here[here])
        return state

    lax.fori_loop(0, width // 256, columns, 0)
    dx1 = dx2[...] + normal_back(x1[...], gains[1:2], work[...])
    da[...] = dx1.astype(jnp.bfloat16)
    loads[2].wait()
    upper = stacked_halves(adapters[half:])
    inner_halves = stacked_halves(inner[...])

    def adapter_grads(which, gradient, inputs):
        up_grad = adapter_scale * added_halves(dot_without_transpose(inner_halves, gradient))
        back = adapter_scale * added_halves(dot_nt(upper, gradient))
        back = jnp.where(ranks(which, back.shape), back, 0.0)
        down_grad = added_halves(dot_without_transpose(stacked_halves(back), inputs))
        keep = ranks(which, up_grad.shape)
        return back, down_grad, jnp.where(keep, up_grad, 0.0)

    back, down_total, up_total = adapter_grads(3, da[...], mixed[...])
    dmix[...] = (
        dot_nt(da[...], out_here[...]) + adapter_out(back, adapters[:half]) / adapter_scale
    ).astype(jnp.bfloat16)
    lane_mask = head_lanes(rows)

    def pair_step(pair, state):
        query = joined[:, pair_at(pair)]
        keys = joined[:, pair_at(pairs_of(width) + pair)]
        values = joined[:, pair_at(2 * pairs_of(width) + pair)]
        pull = dmix[:, pair_at(pair)]
        outs = []
        for side in range(2):
            mine = lane_mask if side == 0 else ~lane_mask
            chances = probs[2 * pair + side]
            wide = chances.astype(jnp.float32)
            reach = dot_nt(jnp.where(mine, pull, jnp.zeros_like(pull)), values)
            slide = wide * (reach - jnp.sum(wide * reach, axis=-1, keepdims=True))
            slide = slide.astype(jnp.bfloat16)
            outs.append(
                (
                    dot_without_transpose(slide, keys) * score_scale,
                    dot_tn(slide, query) * score_scale,
                    dot_tn(chances, pull),
                )
            )
        for which in range(3):
            both = jnp.where(lane_mask, outs[0][which], outs[1][which])
            pulls[:, pair_at(which * pairs_of(width) + pair)] = both.astype(jnp.bfloat16)
        return state

    lax.fori_loop(0, pairs_of(width), pair_step, 0)
    for which in range(3):
        _, down_part_grad, up_part_grad = adapter_grads(
            which, pulls[:, which * width : (which + 1) * width], h1[...]
        )
        down_total += down_part_grad
        up_total += up_part_grad
    grads[:half] = down_total
    grads[half:] = up_total


def backward(mean_rows, log_total, mask, target_rows, table_sum, gains, adapters, kept, weights):
    rows = mask.shape[0]
    width = target_rows.shape[1]
    hidden = weights[2].shape[0]
    low, full = jnp.bfloat16, jnp.float32
    anywhere, vmem = pl.BlockSpec(memory_space=pl.ANY), pl.BlockSpec(memory_space=pltpu.VMEM)
    shape = jax.ShapeDtypeStruct
    return pl.pallas_call(
        backward_kernel,
        out_shape=[shape(adapters.shape, full), shape((1, 128), full)],
        in_specs=[vmem] * (8 + len(kept)) + [anywhere] * 3,
        out_specs=[vmem] * 2,
        scratch_shapes=[
            pltpu.VMEM((rows, width), full),
            pltpu.VMEM((rows, width), full),
            pltpu.VMEM((rows, width), low),
            pltpu.VMEM((rows, hidden), low),
            pltpu.VMEM((rows, width), low),
            pltpu.VMEM((rows, 3 * width), low),
        ]
        + [pltpu.VMEM(w.shape, low) for w in weights]
        + [pltpu.SemaphoreType.DMA((3,))],
        name="backward",
        compiler_params=pltpu.CompilerParams(vmem_limit_bytes=60 * 2**20),
    )(
        mean_rows,
        log_total,
        mask[None, :],
        mask[:, None],
        target_rows,
        table_sum,
        gains,
        adapters,
        *kept,
        *weights,
    )


def stack_adapters(down, up):
    return jnp.concatenate([jnp.swapaxes(down, 1, 2), up], axis=0).reshape(-1, up.shape[2])


def col_of(row):
    size = row.shape[1]
    square = (size, size)
    same = lax.broadcasted_iota(jnp.int32, square, 0) == lax.broadcasted_iota(jnp.int32, square, 1)
    return jnp.sum(jnp.where(same, row, 0.0), axis=1, keepdims=True)


def stack_rows(down, up):
    return jnp.concatenate(
        [down[j] for j in range(down.shape[0])] + [up[j] for j in range(up.shape[0])], axis=0
    )


def pack_rows(positions, gains, shifts, biases):
    places = positions[...].astype(jnp.float32)
    span = places.shape[0] // 4
    width = places.shape[1]
    places = jnp.concatenate([places[r * span : (r + 1) * span] for r in range(4)], axis=1)
    norms = jnp.concatenate(
        [
            gains[...].astype(jnp.float32),
            shifts[...].astype(jnp.float32),
            jnp.zeros((gains.shape[0], 128 - 2 * width), jnp.float32),
        ],
        axis=1,
    )
    flat = biases[...].astype(jnp.float32)
    flat = jnp.concatenate([flat, jnp.zeros((1, -flat.shape[1] % 128), jnp.float32)], axis=1)
    lines = [flat[:, r * 128 : (r + 1) * 128] for r in range(flat.shape[1] // 128)]
    rest = jnp.zeros((8 - gains.shape[0], 128), jnp.float32)
    tail = jnp.zeros((8 - len(lines), 128), jnp.float32)
    return jnp.concatenate([places, norms, rest] + lines + [tail], axis=0).astype(jnp.bfloat16)


def unpack_rows(packed, devices, width, span, norms, bias_size, positions, gains, shifts, bias):
    rows = packed.shape[0] // devices

    def group(j, state):
        devs = [
            packed[pl.ds(pl.multiple_of((4 * j + i) * rows, rows), rows)].astype(jnp.float32)
            for i in range(4)
        ]
        lanes = pl.ds(pl.multiple_of(j * 128, 128), 128)
        for r in range(4):
            block = [dev[:span, r * width : (r + 1) * width] for dev in devs]
            positions[r * span : (r + 1) * span, lanes] = jnp.concatenate(block, axis=1).astype(
                jnp.bfloat16
            )
        gains[:, lanes] = jnp.concatenate([dev[span : span + norms, :width] for dev in devs], axis=1)
        shifts[:, lanes] = jnp.concatenate(
            [dev[span : span + norms, width : 2 * width] for dev in devs], axis=1
        )
        flat = []
        for dev in devs:
            left = bias_size
            line = span + 8
            while left > 0:
                flat.append(dev[line : line + 1, : min(left, 128)])
                left -= 128
                line += 1
        bias[:, pl.ds(pl.multiple_of(j * 4 * bias_size, 128), 4 * bias_size)] = jnp.concatenate(
            flat, axis=1
        )
        return state

    lax.fori_loop(0, devices // 4, group, 0)


def first_kernel(table_rows, devices, group, row_counts, *refs):
    (
        ids,
        targets,
        mask,
        lengths,
        position_own,
        gain_own,
        shift_own,
        bias_own,
        adapter_down,
        adapter_up,
        table_tail,
        table,
        *refs,
    ) = refs
    weights_own = refs[:4]
    refs = refs[4:]
    (
        flags,
        target_out,
        table_sum,
        gains_out,
        adapters_out,
        final,
        inner,
        table_mine,
        turned_mine,
        table_other,
        turned_other,
        h1_out,
        joined_out,
        probs_out,
        mixed_out,
        x1_out,
        slope_out,
        x2_out,
        out_kept,
        up_kept,
        down_kept,
        *refs,
    ) = refs
    (
        send_sems,
        recv_sems,
        local_sems,
        table_sems,
        ask_sems,
        row_sems,
        sum_sems,
        keep_sems,
        table_here,
        turned_here,
        selector,
        rows_out,
        rows_in,
        ask_out,
        ask_in,
        sum_out,
        sum_in,
        pack_here,
        packed,
        w_qkv,
        w_out,
        w_up,
        w_down,
        positions,
        shifts,
        bias,
        embedded,
        x0,
        h1,
        joined,
        probs,
        mixed,
        x1,
        h2,
        active,
        slope,
        x2,
    ) = refs
    arrays = (packed, w_qkv, w_out, w_up, w_down)
    ins = (pack_here,) + tuple(weights_own)
    dp, z, y, x, core, place, along = position()
    dp_x, dp_y = place(y, 1 - x, core), place(1 - y, x, core)
    dp_core, dp_diagonal = place(y, x, 1 - core), place(1 - y, 1 - x, core)
    z_peers = [(dp, along[k]) for k in (1, 2, 3)]
    near_peers = [(dp_x, z), (dp_y, z), (dp_core, z)]
    body_rows = table_rows // 16 * 16
    tail_rows = table_here.shape[0] - body_rows
    loads = [
        pltpu.make_async_copy(
            table.at[pl.ds(0, body_rows)], table_here.at[pl.ds(0, body_rows)], table_sems.at[0]
        ),
        pltpu.make_async_copy(
            table_tail, table_here.at[pl.ds(body_rows, tail_rows)], table_sems.at[1]
        ),
    ]
    for copy in loads:
        copy.start()
    pack_here[...] = pack_rows(position_own, gain_own, shift_own, bias_own)
    me = meet_all(devices, group)
    sent, kept, used = [], [], [0] * len(arrays)

    def piece(which, block):
        rows = row_counts[which]
        return arrays[which].at[pl.ds(pl.multiple_of(block * rows, rows), rows)]

    def send(which, block, peer, source=None):
        copy = pltpu.make_async_remote_copy(
            piece(which, block) if source is None else source,
            piece(which, block),
            send_sems.at[which, used[which]],
            recv_sems.at[which, block],
            device_id=peer,
            device_id_type=MESH,
        )
        used[which] += 1
        copy.start()
        sent.append(copy)

    def arrive(which, block):
        pltpu.make_async_remote_copy(
            ins[which],
            piece(which, block),
            send_sems.at[which, 0],
            recv_sems.at[which, block],
            device_id=z_peers[0],
            device_id_type=MESH,
        ).wait_recv()

    def own_near(which):
        for peer in near_peers:
            send(which, me, peer, ins[which])
        copy = pltpu.make_async_copy(ins[which], piece(which, me), local_sems.at[which])
        copy.start()
        kept.append(copy)

    def own_z(which):
        for peer in z_peers:
            send(which, me, peer, ins[which])

    def line(which):
        for k in (1, 2, 3):
            block = dp * 4 + along[k]
            arrive(which, block)
            for peer in near_peers:
                send(which, block, peer)

    def side(which):
        for k in range(4):
            block_x, block_y = dp_x * 4 + along[k], dp_y * 4 + along[k]
            arrive(which, block_y)
            if k < 2:
                send(which, block_y, (dp_x, z))
            arrive(which, block_x)
            if k >= 2:
                send(which, block_x, (dp_y, z))
            send(which, block_y, (dp_core, z))
            send(which, block_x, (dp_core, z))

    def diagonal(which):
        for k in range(4):
            block = dp_diagonal * 4 + along[k]
            arrive(which, block)
            send(which, block, (dp_core, z))

    def other_core(which):
        for y_at in range(2):
            for x_at in range(2):
                for z_at in range(4):
                    arrive(which, place(y_at, x_at, 1 - core) * 4 + z_at)
        kept[which].wait()

    def keep(at, source, target):
        copy = pltpu.make_async_copy(source, target, keep_sems.at[at])
        copy.start()
        return copy

    for which in range(len(arrays)):
        own_near(which)
    own_z(0)
    own_z(1)

    own_ids = ids[...].astype(jnp.float32)
    own_targets = jnp.where(mask[...] > 0, targets[...], ids[...]).astype(jnp.float32)
    ids_row = jnp.concatenate([own_ids, own_targets], axis=1)
    ids_col = jnp.concatenate([col_of(own_ids), col_of(own_targets)], axis=0)
    tokens = ids_row.shape[1]
    wide = (tokens, tokens)
    across = lax.broadcasted_iota(jnp.int32, wide, 1).astype(jnp.float32)
    down = lax.broadcasted_iota(jnp.int32, wide, 0).astype(jnp.float32)
    owner_row, owner_col = jnp.zeros_like(ids_row), jnp.zeros_like(ids_col)
    for device in range(1, devices):
        owner_row += (ids_row >= float(device * table_rows)).astype(jnp.float32)
        owner_col += (ids_col >= float(device * table_rows)).astype(jnp.float32)
    equal = ids_col == ids_row
    first_col = jnp.min(jnp.where(equal, across, float(tokens)), axis=1, keepdims=True)
    first_row = jnp.min(jnp.where(equal, down, float(tokens)), axis=0, keepdims=True)
    leads = jnp.where(first_row == across[:1], owner_row, -1.0)
    slot_col = jnp.sum(
        jnp.where((owner_col == leads) & (across < first_col), 1.0, 0.0), axis=1, keepdims=True
    )
    takes = lax.broadcasted_iota(jnp.int32, (devices, tokens), 0).astype(jnp.float32) == leads
    local_row = jnp.where(takes, ids_row - owner_row * table_rows + 1.0, 0.0)
    lanes = lax.broadcasted_iota(jnp.int32, (tokens, 128), 1).astype(jnp.float32)
    asked = (
        dot_without_transpose(
            local_row, (slot_col == lanes).astype(jnp.float32), highest_precision
        )
        - 1.0
    )
    over = jnp.max(slot_col, axis=0, keepdims=True) >= float(CAP)
    ask_lanes = lax.broadcasted_iota(jnp.int32, (devices, 128), 1)
    asked = jnp.where(ask_lanes == 127, over.astype(jnp.float32), asked)
    ask_out[...] = asked.reshape(devices, 1, 128)
    ask_in[pl.ds(me, 1)] = ask_out[pl.ds(me, 1)]
    start, ask_arrive, ask_sent = to_all(
        lambda other: ask_out.at[other], ask_in, ask_sems.at[0], ask_sems.at[1], devices, group, me
    )
    start()
    own_z(2)
    for copy in loads:
        copy.wait()
    keeps = [keep(0, table_here, table_mine)]

    def add_up(step, total):
        return total + jnp.sum(
            table_here[pl.ds(pl.multiple_of(step * 128, 128), 128)].astype(jnp.float32),
            axis=0,
            keepdims=True,
        )

    own_sum = lax.fori_loop(
        0, table_here.shape[0] // 128, add_up, jnp.zeros((1, table_here.shape[1]), jnp.float32)
    )
    sum_out[...] = own_sum
    sum_in[pl.ds(me, 1)] = own_sum[None]
    start, sum_arrive, sum_sent = to_all(
        lambda other: sum_out, sum_in, sum_sems.at[0], sum_sems.at[1], devices, group, me
    )
    start()
    line(0)
    line(1)
    own_z(3)
    ask_arrive()
    asked_all = ask_in[...].reshape(devices, 128)
    flags[...] = jnp.broadcast_to(
        jnp.max(
            jnp.max(jnp.where(ask_lanes == 127, asked_all, 0.0), axis=0, keepdims=True),
            axis=1,
            keepdims=True,
        ),
        flags.shape,
    )
    square = (128, 128)
    eye = (
        lax.broadcasted_iota(jnp.int32, square, 0) == lax.broadcasted_iota(jnp.int32, square, 1)
    ).astype(jnp.float32)
    turned = jnp.round(dot_nt(eye, asked_all, highest_precision))
    row_lanes = lax.broadcasted_iota(jnp.int32, (CAP, table_here.shape[0]), 1).astype(jnp.float32)
    batch = 8
    for step in range(devices // batch):
        for at in range(batch):
            source = step * batch + at
            hot = turned[:CAP, source : source + 1] == row_lanes
            selector[at * CAP : (at + 1) * CAP] = hot.astype(jnp.float32).astype(jnp.bfloat16)
        picked = dot_without_transpose(selector[...], table_here[...])
        rows_out[step * batch : (step + 1) * batch] = picked.astype(jnp.bfloat16).reshape(
            batch, CAP, -1
        )
    rows_in[pl.ds(me, 1)] = rows_out[pl.ds(me, 1)]
    start, rows_arrive, rows_sent = to_all(
        lambda other: rows_out.at[other],
        rows_in,
        row_sems.at[0],
        row_sems.at[1],
        devices,
        group,
        me,
    )
    start()
    side(0)
    line(2)
    side(1)
    own_z(4)
    adapters = adapters_out
    adapters[...] = stack_rows(adapter_down, adapter_up)
    turn_rows(table_here, turned_here)
    keeps.append(keep(1, turned_here, turned_mine))
    swaps = []
    for at, (here, there) in enumerate(((table_here, table_other), (turned_here, turned_other))):
        copy = pltpu.make_async_remote_copy(
            here,
            there,
            table_sems.at[2 + 2 * at],
            table_sems.at[3 + 2 * at],
            device_id=(dp_core, z),
            device_id_type=MESH,
        )
        copy.start()
        swaps.append(copy)
    diagonal(0)
    line(3)
    side(2)
    other_core(0)
    unpack_rows(
        packed,
        devices,
        position_own.shape[1],
        position_own.shape[0] // 4,
        gain_own.shape[0],
        bias_own.shape[1],
        positions,
        gains_out,
        shifts,
        bias,
    )
    diagonal(1)

    rows_arrive()
    index_col = owner_col * CAP + slot_col
    slots = lax.broadcasted_iota(jnp.int32, (tokens, devices * CAP), 1).astype(jnp.float32)
    chosen = (index_col == slots).astype(jnp.float32).astype(jnp.bfloat16)
    taken = dot_without_transpose(chosen, rows_in[...].reshape(devices * CAP, -1))
    embedded[...] = taken[: tokens // 2]
    target_out[...] = taken[tokens // 2 :]
    sum_arrive()
    table_sum[...] = jnp.sum(sum_in[...], axis=0)
    allowed = first_part(embedded, positions, lengths, gains_out, shifts, x0, h1)
    keeps.append(keep(2, h1, h1_out))
    line(4)
    side(3)
    other_core(1)
    project_part(h1, w_qkv, bias, adapters, inner, joined)
    keeps.append(keep(3, joined, joined_out))
    diagonal(2)
    side(4)
    attend_part(joined, allowed, probs, mixed)
    keeps.append(keep(4, probs, probs_out))
    keeps.append(keep(5, mixed, mixed_out))
    diagonal(3)
    other_core(2)
    keeps.append(keep(6, w_out, out_kept))
    output_part(x0, mixed, w_out, bias, adapters, inner, gains_out, shifts, x1, h2)
    keeps.append(keep(7, x1, x1_out))
    diagonal(4)
    other_core(3)
    keeps.append(keep(8, w_up, up_kept))
    up_part(h2, w_up, bias, active, slope)
    keeps.append(keep(9, slope, slope_out))
    other_core(4)
    keeps.append(keep(10, w_down, down_kept))
    down_part(x1, active, w_down, bias, gains_out, shifts, x2, final)
    keeps.append(keep(11, x2, x2_out))
    for copy in swaps:
        copy.wait()
    for copy in keeps:
        copy.wait()
    for copy in sent:
        copy.wait_send()
    ask_sent()
    sum_sent()
    rows_sent()


def first(
    ids, targets, mask, lengths, table, small, adapter_down, adapter_up, weights
):
    group = lax.axis_size("vocab")
    devices = lax.axis_size("dp") * group
    table_rows, width = table.shape
    pad_rows = -(-table_rows // 128) * 128
    body_rows = table_rows // 16 * 16
    tail = jnp.pad(table[body_rows:], ((0, pad_rows - table_rows), (0, 0)))
    rows = ids.shape[0]
    hidden = weights[3].shape[0] * devices
    heads = width // HEAD_DIM
    low, full = jnp.bfloat16, jnp.float32
    positions, gains, shifts, biases = small
    pack_height = positions.shape[0] // 4 + 16
    counts = [pack_height] + [w.shape[0] for w in weights]
    anywhere, vmem = pl.BlockSpec(memory_space=pl.ANY), pl.BlockSpec(memory_space=pltpu.VMEM)
    dma = pltpu.SemaphoreType.DMA
    shape = jax.ShapeDtypeStruct
    adapter_rows = 2 * adapter_up.shape[0] * adapter_up.shape[1]
    whole = [(devices * w.shape[0], w.shape[1]) for w in weights]
    saved = [
        shape((pad_rows, width), low),
        shape((width, pad_rows), low),
        shape((pad_rows, width), low),
        shape((width, pad_rows), low),
        shape((rows, width), low),
        shape((rows, 3 * width), low),
        shape((heads, rows, rows), low),
        shape((rows, width), low),
        shape((rows, width), full),
        shape((rows, hidden), low),
        shape((rows, width), full),
    ] + [shape(w, low) for w in whole[1:]]
    return pl.pallas_call(
        partial(first_kernel, table_rows, devices, group, counts),
        out_shape=[
            shape((8, 128), full),
            shape((rows, width), full),
            shape((1, width), full),
            shape((gains.shape[0], width), full),
            shape((adapter_rows, width), full),
            shape((rows, width), low),
            shape((adapter_rows // 2, rows), full),
        ]
        + saved,
        in_specs=[vmem] * 3
        + [pl.BlockSpec(memory_space=pltpu.SMEM)]
        + [vmem] * 6
        + [anywhere] * (2 + len(weights)),
        out_specs=[vmem] * 7 + [anywhere] * len(saved),
        scratch_shapes=[
            dma((len(counts), devices)),
            dma((len(counts), devices)),
            dma((len(counts),)),
            dma((6,)),
            dma((2, devices)),
            dma((2, devices)),
            dma((2, devices)),
            dma((12,)),
            pltpu.VMEM((pad_rows, width), low),
            pltpu.VMEM((width, pad_rows), low),
            pltpu.VMEM((8 * CAP, pad_rows), low),
            pltpu.VMEM((devices, CAP, width), low),
            pltpu.VMEM((devices, CAP, width), low),
            pltpu.VMEM((devices, 1, 128), full),
            pltpu.VMEM((devices, 1, 128), full),
            pltpu.VMEM((1, width), full),
            pltpu.VMEM((devices, 1, width), full),
            pltpu.VMEM((pack_height, 128), low),
            pltpu.VMEM((devices * pack_height, 128), low),
        ]
        + [pltpu.VMEM(w, low) for w in whole]
        + [
            pltpu.VMEM((positions.shape[0], width), low),
            pltpu.VMEM((shifts.shape[0], width), full),
            pltpu.VMEM((1, devices * biases.shape[0]), full),
            pltpu.VMEM((rows, width), full),
            pltpu.VMEM((rows, width), full),
            pltpu.VMEM((rows, width), low),
            pltpu.VMEM((rows, 3 * width), low),
            pltpu.VMEM((heads, rows, rows), low),
            pltpu.VMEM((rows, width), low),
            pltpu.VMEM((rows, width), full),
            pltpu.VMEM((rows, width), low),
            pltpu.VMEM((rows, hidden), low),
            pltpu.VMEM((rows, hidden), low),
            pltpu.VMEM((rows, width), full),
        ],
        name="first",
        compiler_params=pltpu.CompilerParams(
            collective_id=1, has_side_effects=True, vmem_limit_bytes=63 * 2**20
        ),
    )(
        ids[None, :],
        targets[None, :],
        mask[None, :],
        lengths,
        positions,
        gains,
        shifts,
        biases[None, :],
        jnp.swapaxes(adapter_down, 1, 2),
        adapter_up,
        tail,
        table,
        *weights,
    )


def per_device(
    ids,
    targets,
    counted_mask,
    lengths,
    table,
    position_table,
    layer_norm_gain,
    layer_norm_bias,
    query_key_value_weight,
    output_weight,
    up_weight,
    down_weight,
    biases,
    adapter_down,
    adapter_up,
    down_momentum,
    up_momentum,
):
    every = (
        ids,
        targets,
        counted_mask,
        lengths,
        table,
        position_table,
        layer_norm_gain,
        layer_norm_bias,
        query_key_value_weight,
        output_weight,
        up_weight,
        down_weight,
        biases,
        adapter_down,
        adapter_up,
        down_momentum,
        up_momentum,
    )
    table_rows = table.shape[0]
    (
        flags,
        target_rows,
        table_sum,
        gains_all,
        adapters,
        final_state,
        inner_rows,
        table_mine,
        turned_mine,
        table_other,
        turned_other,
        h1,
        joined,
        probs,
        mixed,
        x1,
        slope,
        x2,
        w_out_all,
        w_up_all,
        w_down_all,
    ) = first(
        ids,
        targets,
        counted_mask,
        lengths,
        table,
        (position_table, layer_norm_gain, layer_norm_bias, biases),
        adapter_down,
        adapter_up,
        (query_key_value_weight, output_weight, up_weight, down_weight),
    )
    kept = (h1, joined, probs, mixed, inner_rows, x1, slope, x2)

    def go_on():
        mean_rows, log_total = head(
            final_state, table_rows, (table_mine, turned_mine, table_other, turned_other)
        )
        grads, sums = backward(
            mean_rows,
            log_total,
            counted_mask.astype(jnp.float32),
            target_rows,
            table_sum,
            gains_all,
            adapters,
            (final_state, *kept),
            (w_out_all, w_up_all, w_down_all),
        )
        grads = jnp.concatenate(
            [grads, jnp.broadcast_to(sums, (grads.shape[0], sums.shape[1]))], axis=1
        )[:, None, :]
        new_momenta, new_weights, numbers = update(
            grads,
            stack_adapters(down_momentum, up_momentum),
            adapters,
        )

        def split(stacked):
            stacked = stacked.reshape(2, -1, adapter_up.shape[1], stacked.shape[1])
            return jnp.swapaxes(stacked[0], 1, 2), stacked[1]

        mom_down, mom_up = split(new_momenta)
        down_fresh, up_fresh = split(new_weights)
        return (
            numbers[0, 0],
            numbers[0, 1],
            numbers[0, 2],
            mom_down,
            mom_up,
            down_fresh,
            up_fresh,
            down_fresh.astype(jnp.bfloat16),
            up_fresh.astype(jnp.bfloat16),
        )

    return lax.cond(flags[0, 0] > 0.0, lambda: per_device_general(*every), go_on)


def solution(mesh):
    fast = dict(mesh.shape) == {"dp": 8, "vocab": 4}
    placed = (
        P(("dp", "vocab")),
        P(("dp", "vocab")),
        P(("dp", "vocab")),
        P(("dp", "vocab"), None),
        P(("dp", "vocab"), None),
        P(None, ("dp", "vocab")),
        P(None, ("dp", "vocab")),
        P(None, ("dp", "vocab")),
        P(("dp", "vocab"), None),
        P(("dp", "vocab"), None),
        P(("dp", "vocab"), None),
        P(("dp", "vocab"), None),
        P(("dp", "vocab")),
        P(),
        P(),
        P(),
        P(),
    )
    return jax.shard_map(
        per_device if fast else per_device_general,
        mesh=mesh,
        in_specs=placed,
        out_specs=(
            P(),
            P(),
            P(),
            P(None, "vocab", None),
            P(None, None, "vocab"),
            P(None, "vocab", None),
            P(None, None, "vocab"),
            P(None, "vocab", None),
            P(None, None, "vocab"),
        ),
        check_vma=False,
    )
```

```python
from functools import partial

import jax
import jax.numpy as jnp
from jax import lax
from jax.experimental import pallas as pl
from jax.experimental.pallas import tpu as pltpu
from jax.sharding import PartitionSpec as P

HEAD_DIM = 64
V = 50304


highest_precision = lax.Precision.HIGHEST
ln_eps = 1e-05
adapter_scale = 8.0
smooth = 0.1
clip_level = 1.0
momentum = 0.5
learning_rate = 0.5
coef_a = 3.4445
coef_b = -4.775
coef_c = 2.0315
score_scale = 0.125
masked_value = -1e30


def merged(x, axis, join):
    gathered = jax.tree.map(
        lambda a, kind: lax.all_gather(a.astype(kind), axis),
        x,
        jax.tree.map(lambda a: jnp.bfloat16 if a.dtype == jnp.float32 else a.dtype, x),
    )

    def take(source):
        return jax.tree.map(
            lambda a, own: lax.dynamic_index_in_dim(a, source, 0, False).astype(own.dtype),
            gathered,
            x,
        )

    return lax.fori_loop(
        1, lax.axis_size(axis), lambda source, state: join(state, take(source)), take(0)
    )


def dot_without_transpose(left_side, right_side, setting=None):
    return jnp.dot(left_side, right_side, precision=setting, preferred_element_type=jnp.float32)


def dot_last_axis(left_side, right_side, setting=None):
    return lax.dot_general(
        left_side,
        right_side,
        (((1,), (1,)), ((), ())),
        precision=setting,
        preferred_element_type=jnp.float32,
    )


def dot_first(left_side, right_side, setting=None):
    return lax.dot_general(
        left_side,
        right_side,
        (((0,), (0,)), ((), ())),
        precision=setting,
        preferred_element_type=jnp.float32,
    )


def rounded_values(values):
    return lax.optimization_barrier(values.astype(jnp.bfloat16)).astype(jnp.float32)


def layer_norm(values, gain, offset):
    center = values - jnp.mean(values, axis=-1, keepdims=True)
    spread = jnp.mean(center * center, axis=-1, keepdims=True)
    return center * lax.rsqrt(spread + ln_eps) * gain + offset


def layout(seq_lengths, row_count):
    seq_ends = jnp.cumsum(seq_lengths)
    seq_starts = seq_ends - seq_lengths
    places = jnp.arange(row_count, dtype=jnp.int32)
    segment = jnp.sum((places[:, None] >= seq_ends[None, :]).astype(jnp.int32), axis=1)
    member = segment[:, None] == jnp.arange(seq_lengths.shape[0], dtype=jnp.int32)[None, :]
    positions_in = places - jnp.sum(jnp.where(member, seq_starts[None, :], 0), axis=1)
    allowed_mask = (segment[:, None] == segment[None, :]) & (places[None, :] <= places[:, None])
    return (positions_in, allowed_mask)


def owner_rows(token_ids, piece_rows, group, vocab_pos):
    piece_index = token_ids // piece_rows
    owner = piece_index % group
    local = piece_index // group * piece_rows + token_ids % piece_rows
    return jnp.where(owner == vocab_pos, local, -1)


def attention_scores(query, key_rows, allowed_mask):
    scores = (
        jnp.einsum("shd,thd->hst", query, key_rows, preferred_element_type=jnp.float32)
        * score_scale
    )
    return jnp.where(allowed_mask[None], scores, masked_value)


def layer_forward(residual_initial, frozen_weights, adapter_down, adapter_up, allowed_mask):
    query_key_value_weight, output_weight, up_weight, down_weight, gains, shifts, bias_stack = (
        frozen_weights
    )
    gains = gains.astype(jnp.float32)
    shifts = shifts.astype(jnp.float32)
    bias_stack = bias_stack.astype(jnp.float32)
    width_size = output_weight.shape[0]
    hidden_units = up_weight.shape[1]
    row_count = residual_initial.shape[0]
    heads = width_size // HEAD_DIM
    first_normed = layer_norm(residual_initial, gains[0], shifts[0]).astype(jnp.bfloat16)
    first_plain = first_normed.astype(jnp.float32)
    joined_rows = (
        dot_without_transpose(first_normed, query_key_value_weight) + bias_stack[: 3 * width_size]
    )
    adapt_in = []
    projected = []
    for which_index in range(3):
        inner_product = dot_without_transpose(
            first_plain, adapter_down[which_index], highest_precision
        )
        adapt_in.append(inner_product)
        branch_output = joined_rows[
            :, which_index * width_size : (which_index + 1) * width_size
        ] + adapter_scale * dot_without_transpose(
            inner_product, adapter_up[which_index], highest_precision
        )
        projected.append(branch_output.astype(jnp.bfloat16).reshape(row_count, heads, HEAD_DIM))
    query, key_rows, value_rows = projected
    scores = attention_scores(query, key_rows, allowed_mask)
    top = jnp.max(scores, axis=-1, keepdims=True)
    expo = jnp.exp(scores - top)
    summed = jnp.sum(expo, axis=-1, keepdims=True)
    log_total = top + jnp.log(summed)
    probs = (expo / summed).astype(jnp.bfloat16)
    mixed_state = jnp.einsum("hst,thd->shd", probs, value_rows, preferred_element_type=jnp.float32)
    mixed_state = mixed_state.reshape(row_count, width_size).astype(jnp.bfloat16)
    mixed_plain = mixed_state.astype(jnp.float32)
    adapter_output = dot_without_transpose(mixed_plain, adapter_down[3], highest_precision)
    attended_rows = (
        dot_without_transpose(mixed_state, output_weight)
        + bias_stack[3 * width_size : 4 * width_size]
        + adapter_scale * dot_without_transpose(adapter_output, adapter_up[3], highest_precision)
    )
    stream_one = residual_initial + attended_rows
    normed_two = layer_norm(stream_one, gains[1], shifts[1]).astype(jnp.bfloat16)
    before_gelu = (
        dot_without_transpose(normed_two, up_weight)
        + bias_stack[4 * width_size : 4 * width_size + hidden_units]
    )
    activation = jax.nn.gelu(before_gelu, approximate=True).astype(jnp.bfloat16)
    stream_two = (
        stream_one
        + dot_without_transpose(activation, down_weight)
        + bias_stack[4 * width_size + hidden_units :]
    )
    final_state = layer_norm(stream_two, gains[2], shifts[2]).astype(jnp.bfloat16)
    kept_rows = (
        first_plain,
        adapt_in,
        query,
        key_rows,
        value_rows,
        log_total,
        mixed_plain,
        adapter_output,
        stream_one,
        before_gelu,
        stream_two,
    )
    return (final_state, kept_rows)


def layer_backward(
    final_gradient, kept_rows, backward_weights, adapter_down, adapter_up, allowed_mask
):
    output_weight, up_weight, down_weight, gains = backward_weights
    gains = gains.astype(jnp.float32)
    (
        first_plain,
        adapt_in,
        query,
        key_rows,
        value_rows,
        log_total,
        mixed_plain,
        adapter_output,
        stream_one,
        before_gelu,
        stream_two,
    ) = kept_rows
    row_count = query.shape[0]
    width_size = query.shape[1] * HEAD_DIM
    _, pull_three = jax.vjp(lambda values: layer_norm(values, gains[2], 0.0), stream_two)
    grad_two = pull_three(final_gradient)[0]
    grad_act = dot_last_axis(grad_two.astype(jnp.bfloat16), down_weight)
    _, pull_gelu = jax.vjp(partial(jax.nn.gelu, approximate=True), before_gelu)
    grad_pre = pull_gelu(grad_act)[0].astype(jnp.bfloat16)
    _, pull_two = jax.vjp(lambda values: layer_norm(values, gains[1], 0.0), stream_one)
    first_gradient = grad_two + pull_two(dot_last_axis(grad_pre, up_weight))[0]
    attention_gradient = first_gradient.astype(jnp.bfloat16)
    attention_scaled = adapter_scale * rounded_values(first_gradient)
    up_grads = [None, None, None, None]
    down_grads = [None, None, None, None]
    up_grads[3] = dot_first(adapter_output, attention_scaled, highest_precision)
    backward_output = dot_last_axis(attention_scaled, adapter_up[3], highest_precision)
    down_grads[3] = dot_first(mixed_plain, backward_output, highest_precision)
    mixed_gradient = dot_last_axis(attention_gradient, output_weight) + dot_last_axis(
        backward_output, adapter_down[3], highest_precision
    )
    grad_heads = mixed_gradient.astype(jnp.bfloat16).reshape(query.shape)
    probs = jnp.exp(attention_scores(query, key_rows, allowed_mask) - log_total)
    grad_value = jnp.einsum(
        "hst,shd->thd", probs.astype(jnp.bfloat16), grad_heads, preferred_element_type=jnp.float32
    )
    grad_probs = jnp.einsum(
        "shd,thd->hst", grad_heads, value_rows, preferred_element_type=jnp.float32
    )
    grad_scores = probs * (grad_probs - jnp.sum(probs * grad_probs, axis=-1, keepdims=True))
    grad_scores = grad_scores.astype(jnp.bfloat16)
    grad_query = (
        jnp.einsum("hst,thd->shd", grad_scores, key_rows, preferred_element_type=jnp.float32)
        * score_scale
    )
    grad_key = (
        jnp.einsum("hst,shd->thd", grad_scores, query, preferred_element_type=jnp.float32)
        * score_scale
    )
    for which_index, branch_gradient in enumerate((grad_query, grad_key, grad_value)):
        scaled_values = adapter_scale * rounded_values(
            branch_gradient.reshape(row_count, width_size)
        )
        up_grads[which_index] = dot_first(adapt_in[which_index], scaled_values, highest_precision)
        backward_input = dot_last_axis(scaled_values, adapter_up[which_index], highest_precision)
        down_grads[which_index] = dot_first(first_plain, backward_input, highest_precision)
    return (jnp.stack(down_grads), jnp.stack(up_grads))


def orthogonalize(matrices, sum_grams):
    grams = sum_grams(
        jnp.einsum(
            "mrd,msd->mrs",
            matrices,
            matrices,
            precision=highest_precision,
            preferred_element_type=jnp.float32,
        )
    )
    sizes = jnp.sqrt(jnp.trace(grams, axis1=1, axis2=2))[:, None, None] + 1e-07
    state = matrices / sizes
    grams = grams / (sizes * sizes)
    for turn_index in range(5):
        if turn_index:
            grams = sum_grams(
                jnp.einsum(
                    "mrd,msd->mrs",
                    state,
                    state,
                    precision=highest_precision,
                    preferred_element_type=jnp.float32,
                )
            )
        poly = coef_b * grams + coef_c * jnp.einsum(
            "mrs,mst->mrt",
            grams,
            grams,
            precision=highest_precision,
            preferred_element_type=jnp.float32,
        )
        state = coef_a * state + jnp.einsum(
            "mrs,msd->mrd",
            poly,
            state,
            precision=highest_precision,
            preferred_element_type=jnp.float32,
        )
    return state


def gradients_general(
    ids,
    targets,
    counted_mask,
    lengths,
    table,
    position_table,
    layer_norm_gain,
    layer_norm_bias,
    query_key_value_weight,
    output_weight,
    up_weight,
    down_weight,
    biases,
    adapter_down,
    adapter_up,
):
    gathered = (
        lax.all_gather(query_key_value_weight, ("dp", "vocab"), axis=0, tiled=True),
        lax.all_gather(output_weight, ("dp", "vocab"), axis=0, tiled=True),
        lax.all_gather(up_weight, ("dp", "vocab"), axis=0, tiled=True),
        lax.all_gather(down_weight, ("dp", "vocab"), axis=0, tiled=True),
        lax.all_gather(layer_norm_gain, ("dp", "vocab"), axis=1, tiled=True),
        lax.all_gather(layer_norm_bias, ("dp", "vocab"), axis=1, tiled=True),
        lax.all_gather(biases, ("dp", "vocab"), axis=0, tiled=True),
        lax.all_gather(position_table, ("dp", "vocab"), axis=1, tiled=True),
    )
    w_qkv_all, w_out_all, w_up_all, w_down_all, gains_all, shifts_all, bias_stack, positions_all = (
        gathered
    )
    row_count = ids.shape[0]
    width_size = w_out_all.shape[0]
    group = lax.axis_size("vocab")
    vocab_pos = lax.axis_index("vocab")
    piece_rows = table.shape[0]
    ids_all, target_all, mask_all = (
        lax.all_gather(ids, "vocab", axis=0, tiled=True),
        lax.all_gather(targets, "vocab", axis=0, tiled=True),
        lax.all_gather(counted_mask, "vocab", axis=0, tiled=True),
    )
    table_full = lax.all_gather(table, "dp", axis=0, tiled=True)
    vocab_rows = table_full.shape[0]
    local_ids = owner_rows(ids_all, piece_rows, group, vocab_pos)
    inside = local_ids >= 0
    picked_rows = table_full[jnp.clip(local_ids, 0, vocab_rows - 1)]
    picked_rows = jnp.where(inside[:, None], picked_rows, jnp.zeros_like(picked_rows))
    embedded = lax.psum_scatter(
        picked_rows.astype(jnp.float32).astype(jnp.bfloat16),
        "vocab",
        scatter_dimension=0,
        tiled=True,
    ).astype(jnp.float32)
    positions_in, allowed_mask = layout(lengths[0], row_count)
    residual_initial = embedded + positions_all[positions_in].astype(jnp.float32)
    frozen_weights = (w_qkv_all, w_out_all, w_up_all, w_down_all, gains_all, shifts_all, bias_stack)
    final_state, kept_rows = layer_forward(
        residual_initial, frozen_weights, adapter_down, adapter_up, allowed_mask
    )
    final_all = lax.all_gather(final_state, "vocab", axis=0, tiled=True)
    total_rows = final_all.shape[0]
    block = 512
    count_blocks = total_rows // block
    final_blocks = final_all.reshape(count_blocks, block, width_size)
    local_targets = owner_rows(target_all, piece_rows, group, vocab_pos).reshape(
        count_blocks, block
    )
    columns = jnp.arange(vocab_rows, dtype=jnp.int32)

    def head_stats(item):
        piece, local = item
        logits = dot_last_axis(piece, table_full)
        top = jnp.max(logits, axis=1)
        expsum = jnp.sum(jnp.exp(logits - top[:, None]), axis=1)
        target_logit = jnp.sum(jnp.where(columns[None, :] == local[:, None], logits, 0.0), axis=1)
        return (top, expsum, target_logit, jnp.sum(logits, axis=1))

    stats = lax.map(head_stats, (final_blocks, local_targets))
    stats = tuple((entry.reshape(total_rows) for entry in stats))

    def combine(first_part, second_part):
        larger = jnp.maximum(first_part[0], second_part[0])
        merged_sum = first_part[1] * jnp.exp(first_part[0] - larger) + second_part[1] * jnp.exp(
            second_part[0] - larger
        )
        return (larger, merged_sum, first_part[2] + second_part[2], first_part[3] + second_part[3])

    top, expsum, target_logit, logit_sum = merged(stats, "vocab", combine)
    log_total = top + jnp.log(expsum)
    row_loss = log_total - (1.0 - smooth) * target_logit - smooth * logit_sum / V
    mask_float = mask_all.astype(jnp.float32)
    own_start = vocab_pos * row_count
    loss_own = jnp.sum(lax.dynamic_slice_in_dim(mask_float * row_loss, own_start, row_count))
    count_own = jnp.sum(counted_mask.astype(jnp.float32))

    def head_grad(item):
        piece, local, lse_block, weight = item
        logits = dot_last_axis(piece, table_full)
        probs = jnp.exp(logits - lse_block[:, None])
        onehot = (columns[None, :] == local[:, None]).astype(jnp.float32)
        grad_logits = weight[:, None] * (probs - (1.0 - smooth) * onehot - smooth / V)
        return dot_without_transpose(grad_logits.astype(jnp.bfloat16), table_full)

    partial_rows = lax.map(
        head_grad,
        (
            final_blocks,
            local_targets,
            log_total.reshape(count_blocks, block),
            mask_float.reshape(count_blocks, block),
        ),
    )
    final_gradient = lax.psum_scatter(
        partial_rows.reshape(total_rows, width_size).astype(jnp.bfloat16),
        "vocab",
        scatter_dimension=0,
        tiled=True,
    ).astype(jnp.float32)
    backward_weights = (
        lax.all_gather(output_weight, ("dp", "vocab"), axis=0, tiled=True),
        lax.all_gather(up_weight, ("dp", "vocab"), axis=0, tiled=True),
        lax.all_gather(down_weight, ("dp", "vocab"), axis=0, tiled=True),
        lax.all_gather(layer_norm_gain, ("dp", "vocab"), axis=1, tiled=True),
    )
    down_gradient, up_gradient = layer_backward(
        final_gradient, kept_rows, backward_weights, adapter_down, adapter_up, allowed_mask
    )
    return (down_gradient, up_gradient, loss_own, count_own)


def per_device_general(
    ids,
    targets,
    counted_mask,
    lengths,
    table,
    position_table,
    layer_norm_gain,
    layer_norm_bias,
    query_key_value_weight,
    output_weight,
    up_weight,
    down_weight,
    biases,
    adapter_down,
    adapter_up,
    down_momentum,
    up_momentum,
):
    group = lax.axis_size("vocab")
    vocab_pos = lax.axis_index("vocab")
    down_gradient, up_gradient, loss_own, count_own = gradients_general(
        ids,
        targets,
        counted_mask,
        lengths,
        table,
        position_table,
        layer_norm_gain,
        layer_norm_bias,
        query_key_value_weight,
        output_weight,
        up_weight,
        down_weight,
        biases,
        adapter_down,
        adapter_up,
    )
    down_gradient, up_gradient, smoothed_loss_sum, loss_count = lax.psum(
        (down_gradient, up_gradient, loss_own, count_own), ("dp", "vocab")
    )
    grad_norm = jnp.sqrt(
        jnp.sum(down_gradient * down_gradient) + jnp.sum(up_gradient * up_gradient)
    )
    factor = jnp.minimum(1.0, clip_level / (grad_norm + 1e-06))
    new_mom_down = momentum * down_momentum + factor * down_gradient
    new_mom_up = momentum * up_momentum + factor * up_gradient
    stacked = jnp.concatenate([jnp.swapaxes(new_mom_down, 1, 2), new_mom_up], axis=0)
    share_fraction = stacked.shape[2] // group
    begin_index = vocab_pos * share_fraction
    orthogonal_update = lax.dynamic_slice_in_dim(
        orthogonalize(stacked, lambda grams: grams), begin_index, share_fraction, 2
    )
    mom_down_part = lax.dynamic_slice_in_dim(new_mom_down, begin_index, share_fraction, 1)
    mom_up_part = lax.dynamic_slice_in_dim(new_mom_up, begin_index, share_fraction, 2)
    down_fresh = lax.dynamic_slice_in_dim(
        adapter_down, begin_index, share_fraction, 1
    ) - learning_rate * jnp.swapaxes(orthogonal_update[:4], 1, 2)
    up_fresh = (
        lax.dynamic_slice_in_dim(adapter_up, begin_index, share_fraction, 2)
        - learning_rate * orthogonal_update[4:]
    )
    return (
        smoothed_loss_sum,
        loss_count,
        grad_norm,
        mom_down_part,
        mom_up_part,
        down_fresh,
        up_fresh,
        down_fresh.astype(jnp.bfloat16),
        up_fresh.astype(jnp.bfloat16),
    )


MESH = pl.DeviceIdType.MESH


def dot_nt(left_side, right_side, setting=None):
    return dot_last_axis(left_side, right_side, setting)


def position():
    dp, z = lax.axis_index("dp"), lax.axis_index("vocab")
    y, x, core = dp // 4, dp // 2 % 2, dp % 2

    def place(y_at, x_at, core_at):
        return y_at * 4 + x_at * 2 + core_at

    along = (z, z // 2 * 2 + 1 - z % 2, (z + 2) % 4, (1 - z // 2) * 2 + 1 - z % 2)
    return dp, z, y, x, core, place, along


def inner(z):
    return (z + 1) // 2 % 2


def mirror(z, other):
    return (z // 2 + other // 2) % 2 * 2 + (z + other) % 2


def nearness(z, other):
    k = mirror(z, other)
    return k + inner(z) * (k // 2) * (5 - 2 * k)


def by_nearness(z):
    far = z // 2 * 3
    near = 2 - z // 2
    return (z, z // 2 * 2 + 1 - z % 2, near, 3 - far)


def meet_all(devices, group):
    me = lax.axis_index("dp") * group + lax.axis_index("vocab")
    barrier = pltpu.get_barrier_semaphore()

    def signal(step, state):
        other = lax.rem(me + step, devices)
        pl.semaphore_signal(
            barrier, inc=1, device_id=(other // group, other % group), device_id_type=MESH
        )
        return state

    lax.fori_loop(1, devices, signal, 0)
    pl.semaphore_wait(barrier, devices - 1)
    return me


def to_all(source_of, target, send_sems, recv_sems, devices, group, me):
    def copy(step):
        other = lax.rem(me + step, devices)
        return pltpu.make_async_remote_copy(
            source_of(other),
            target.at[me],
            send_sems.at[step],
            recv_sems.at[step],
            device_id=(other // group, other % group),
            device_id_type=MESH,
        )

    def start():
        def one(step, state):
            copy(step).start()
            return state

        lax.fori_loop(1, devices, one, 0)

    def arrive():
        def one(step, state):
            source = lax.rem(me + devices - step, devices)
            pltpu.make_async_remote_copy(
                target.at[source],
                target.at[source],
                send_sems.at[step],
                recv_sems.at[step],
                device_id=(source // group, source % group),
                device_id_type=MESH,
            ).wait_recv()
            return state

        lax.fori_loop(1, devices, one, 0)

    def sent():
        def one(step, state):
            copy(step).wait_send()
            return state

        lax.fori_loop(1, devices, one, 0)

    return start, arrive, sent


ARRIVE, TILE, BACK, MIDDLE, COLUMN = range(5)
ORDER = (
    (ARRIVE, 0, 1),
    (ARRIVE, 0, 2),
    (ARRIVE, 0, 3),
    (ARRIVE, 2, 1),
    (ARRIVE, 2, 0),
    (ARRIVE, 1, 0),
    (TILE, 2, 1),
    (TILE, 1, 0),
    (TILE, 0, 3),
    (ARRIVE, 1, 1),
    (ARRIVE, 1, 3),
    (ARRIVE, 2, 3),
    (ARRIVE, 1, 2),
    (BACK, 2, 1),
    (ARRIVE, 2, 2),
    (TILE, 0, 2),
    (TILE, 1, 3),
    (ARRIVE, 3, 1),
    (TILE, 1, 2),
    (BACK, 1, 3),
    (ARRIVE, 3, 3),
    (TILE, 3, 1),
    (TILE, 3, 3),
    (BACK, 3, 3),
    (ARRIVE, 3, 2),
    (TILE, 2, 3),
    (BACK, 2, 3),
    (ARRIVE, 3, 0),
    (BACK, 3, 1),
    (TILE, 0, 1),
    (MIDDLE, 1, 3),
    (BACK, 1, 2),
    (MIDDLE, 0, 3),
    (TILE, 1, 1),
    (TILE, 3, 2),
    (COLUMN, 1, 3),
    (BACK, 3, 2),
    (MIDDLE, 1, 1),
    (TILE, 3, 0),
    (COLUMN, 0, 3),
    (MIDDLE, 0, 1),
    (TILE, 2, 2),
    (MIDDLE, 0, 2),
    (BACK, 3, 0),
    (TILE, 2, 0),
    (BACK, 1, 1),
    (COLUMN, 1, 1),
    (MIDDLE, 1, 2),
    (BACK, 1, 0),
    (COLUMN, 0, 2),
    (BACK, 2, 2),
    (MIDDLE, 0, 0),
    (TILE, 0, 0),
    (COLUMN, 0, 1),
    (BACK, 2, 0),
    (COLUMN, 1, 2),
    (MIDDLE, 1, 0),
    (COLUMN, 0, 0),
    (COLUMN, 1, 0),
)


def of_four(values, at):
    low, high = at % 2, at // 2
    return (1 - high) * ((1 - low) * values[0] + low * values[1]) + high * (
        (1 - low) * values[2] + low * values[3]
    )


def head_kernel(table_rows, chunks, own, tab_a, turn_a, tab_b, turn_b, mean_out, lse_out, *refs):
    (
        tab,
        turn,
        score_a,
        score_b,
        total,
        hidden,
        part,
        part_lse,
        got,
        got_lse,
        load_sems,
        send_sems,
        recv_sems,
        back_send,
        back_recv,
    ) = refs
    dp, z, y, x, core, place, _ = position()
    along = by_nearness(z)
    pad_rows = tab_a.shape[0]
    width, tile = own.shape[1], own.shape[0]
    tiles = [event[1:] for event in ORDER if event[0] == TILE]
    slot = {at: index for index, at in enumerate(tiles)}
    columns = [slot[0, k] for k in range(4)]
    dev_x, dev_y = (place(y, 1 - x, core), z), (place(1 - y, x, core), z)
    dev_z = [(dp, along[k]) for k in range(4)]
    peers = [dev_x, dev_y] + dev_z[1:]
    loads = []
    for at, (source, target) in enumerate(
        (
            (own, hidden.at[slot[0, 0]]),
            (tab_a, tab.at[pl.ds(0, pad_rows)]),
            (tab_b, tab.at[pl.ds(pad_rows, pad_rows)]),
            (turn_a, turn.at[:, pl.ds(0, pad_rows)]),
            (turn_b, turn.at[:, pl.ds(pad_rows, pad_rows)]),
        )
    ):
        copy = pltpu.make_async_copy(source, target, load_sems.at[at])
        copy.start()
        loads.append(copy)
    barrier = pltpu.get_barrier_semaphore()
    for peer in peers:
        pl.semaphore_signal(barrier, inc=1, device_id=peer, device_id_type=MESH)
    pl.semaphore_wait(barrier, len(peers))
    loads[0].wait()

    sent = []

    def give(source, target, peer, half=None):
        rows = pl.ds(0, tile) if half is None else pl.ds(half * (tile // 2), tile // 2)
        copy = pltpu.make_async_remote_copy(
            hidden.at[slot[source], rows],
            hidden.at[slot[target], rows],
            send_sems.at[len(sent)],
            recv_sems.at[slot[target] + (16 if half == 1 else 0)],
            device_id=peer,
            device_id_type=MESH,
        )
        sent.append(copy)
        return copy

    def give_along(k, upward):
        there = z + 1 if upward else z - 1
        target = of_four(columns, nearness(there, along[k]))
        return pltpu.make_async_remote_copy(
            hidden.at[slot[0, k]],
            hidden.at[target],
            send_sems.at[24 + k + 4 * (not upward and k == 0)],
            recv_sems.at[target],
            device_id=(dp, there),
            device_id_type=MESH,
        )

    def pass_along(k, act):
        @pl.when((along[k] <= z) & (z < 3))
        def _():
            act(give_along(k, True))

        @pl.when((along[k] >= z) & (z > 0))
        def _():
            act(give_along(k, False))

    def start_all(copies):
        for copy in copies:
            copy.start()

    forwards = {}
    for k in range(4):
        forwards[0, k] = [give((0, k), (1, k), dev_x), give((0, k), (2, k), dev_y)]
        forwards[1, k] = [give((1, k), (3, k), dev_y, 1)]
        forwards[2, k] = [give((2, k), (3, k), dev_x, 0)]
        forwards[3, k] = []
    pass_along(0, lambda copy: copy.start())
    start_all(forwards[0, 0])

    def arrive(q, k):
        there = slot[q, k]
        cuts = [(pl.ds(0, tile), there)]
        if q == 3:
            cuts = [(pl.ds(0, tile // 2), there), (pl.ds(tile // 2, tile // 2), there + 16)]
        for rows, at in cuts:
            pltpu.make_async_remote_copy(
                hidden.at[there, rows],
                hidden.at[there, rows],
                send_sems.at[0],
                recv_sems.at[at],
                device_id=dev_x,
                device_id_type=MESH,
            ).wait_recv()
        if q == 0:
            pass_along(k, lambda copy: copy.start())
        start_all(forwards[q, k])

    back_sent = []

    def half_rows(half):
        return pl.ds(half * (width // 2), width // 2)

    def back_copies(number, q, k, half, landing, peer):
        if q == 0:
            landing = landing + 2 * mirror(z, along[k])
        return [
            pltpu.make_async_remote_copy(
                source,
                target,
                back_send.at[kind, number],
                back_recv.at[kind, landing],
                device_id=peer,
                device_id_type=MESH,
            )
            for kind, (source, target) in enumerate(
                (
                    (part.at[slot[q, k], half_rows(half)], got.at[landing]),
                    (part_lse.at[2 * slot[q, k] + half], got_lse.at[landing]),
                )
            )
        ]

    def back(*what):
        start_all(back_copies(len(back_sent), *what))
        back_sent.append(what)

    def back_wait(landing):
        for kind, target in enumerate((got, got_lse)):
            pltpu.make_async_remote_copy(
                target.at[landing],
                target.at[landing],
                back_send.at[kind, 0],
                back_recv.at[kind, landing],
                device_id=dev_x,
                device_id_type=MESH,
            ).wait_recv()

    def merge(q, k, half, landings):
        at = slot[q, k]
        for landing in landings:
            back_wait(landing)
        levels = [part_lse[2 * at + half]] + [got_lse[landing] for landing in landings]
        top = levels[0]
        for level in levels[1:]:
            top = jnp.maximum(top, level)
        shares = [jnp.exp(level - top) for level in levels]
        whole = sum(shares[1:], shares[0])
        shares = [share / whole for share in shares]
        part_lse[2 * at + half] = top + jnp.log(whole)
        begin = half * (width // 2)

        def rows(step, state):
            here = pl.ds(pl.multiple_of(step * 128, 128), 128)
            mine = pl.ds(pl.multiple_of(begin + step * 128, 128), 128)
            mixed = part[at, mine].astype(jnp.float32) * shares[0]
            for landing, share in zip(landings, shares[1:], strict=True):
                mixed += got[landing, here].astype(jnp.float32) * share
            part[at, mine] = mixed.astype(jnp.bfloat16)
            return state

        lax.fori_loop(0, width // 256, rows, 0)

    def go_back(q, k):
        if q == 3:
            back(3, k, 0, 16 + 2 * k, dev_x)
            back(3, k, 1, 17 + 2 * k, dev_y)
        elif q == 1:
            back(1, k, 0, 2 * k, dev_x)
        else:
            back(2, k, 1, 9 + 2 * k, dev_y)

    def merge_middle(half, k):
        q = 1 if half else 2
        merge(q, k, half, [16 + 2 * k + half])
        if half:
            back(1, k, 1, 1 + 2 * k, dev_x)
        else:
            back(2, k, 0, 8 + 2 * k, dev_y)

    def merge_column(half, k):
        merge(0, k, half, [2 * k + half, 8 + 2 * k + half])
        if k:
            back(0, k, half, 22 + half, dev_z[k])

    acts = {ARRIVE: arrive, BACK: go_back, MIDDLE: merge_middle, COLUMN: merge_column}
    groups = [[]]
    for event in ORDER:
        if event[0] == TILE:
            groups.append([])
        else:
            groups[-1].append(event)

    def work(group):
        for event in group:
            acts[event[0]](*event[1:])

    def events_before(t, parity):
        for at in range(parity, 16, 2):
            if groups[at]:

                @pl.when(t == at)
                def _(at=at):
                    work(groups[at])

    for copy in loads[1:]:
        copy.wait()
    starts = [sum(chunks[:at]) for at in range(len(chunks))]
    low = jnp.full((8, tile), -jnp.inf, jnp.float32)

    def scores_of(rows, at, score, top):
        begin, size = starts[at], chunks[at]
        values = dot_nt(tab[begin : begin + size], rows)
        score[begin : begin + size] = values
        cuts = [(begin, begin + size, False)]
        for half in range(2):
            edge = half * pad_rows + table_rows // 8 * 8
            stop = (half + 1) * pad_rows
            if begin <= edge < begin + size:
                cuts = [(begin, edge, False), (edge, min(stop, begin + size), True)]
                if stop < begin + size:
                    cuts.append((stop, begin + size, False))
        for first_row, last, masked in cuts:
            if first_row == last:
                continue
            cut = values[first_row - begin : last - begin]
            if masked:
                row = lax.broadcasted_iota(jnp.int32, cut.shape, 0)
                cut = jnp.where(row < table_rows % 8, cut, masked_value)
                score[first_row:last] = cut
            top = jnp.maximum(top, jnp.max(cut.reshape(-1, 8, tile), axis=0))
        return top

    def half_step(t, parity, score, score_next, top):
        events_before(t, parity)
        rows = hidden[jnp.minimum(t + 1, 15)]
        peak = jnp.max(top, axis=0, keepdims=True)
        summed = jnp.zeros((8, tile), jnp.float32)
        top_next = low
        for at in range(len(chunks)):
            begin, size = starts[at], chunks[at]
            expo = jnp.exp(score[begin : begin + size] - peak)
            summed += jnp.sum(expo.reshape(-1, 8, tile), axis=0)
            top_next = scores_of(rows, at, score_next, top_next)
            product = dot_without_transpose(
                turn[:, begin : begin + size], expo.astype(jnp.bfloat16)
            )
            if at == 0:
                total[...] = product
            else:
                total[...] += product
        denominator = jnp.sum(summed, axis=0, keepdims=True)
        part[t] = (total[...] * (1.0 / denominator)).astype(jnp.bfloat16)
        level = peak + jnp.log(denominator)
        part_lse[2 * t] = level
        part_lse[2 * t + 1] = level
        return top_next

    if tiles[0] != (0, 0):
        until = groups[0].index((ARRIVE,) + tiles[0]) + 1
        work(groups[0][:until])
        del groups[0][:until]
    top = low
    for at in range(len(chunks)):
        top = scores_of(hidden[0], at, score_a, top)

    def two_steps(step, top):
        top = half_step(2 * step, 0, score_a, score_b, top)
        return half_step(2 * step + 1, 1, score_b, score_a, top)

    lax.fori_loop(0, 8, two_steps, top)
    work(groups[16])
    home = slot[0, 0]
    merge(0, 0, 0, [24, 26, 28])
    merge(0, 0, 1, [25, 27, 29])
    mean_out[...] = part[home]
    lse_out[...] = part_lse[2 * home]
    for k in range(4):
        pass_along(k, lambda copy: copy.wait_send())
    for copy in sent:
        copy.wait_send()
    for number, what in enumerate(back_sent):
        for copy in back_copies(number, *what):
            copy.wait_send()


def head(final_state, table_rows, tables):
    tile, width = final_state.shape
    pad_rows = tables[0].shape[0]
    both = 2 * pad_rows
    chunks = [both // 256 // 4 * 256] * 4
    chunks[0] += both - sum(chunks)
    anywhere, vmem = pl.BlockSpec(memory_space=pl.ANY), pl.BlockSpec(memory_space=pltpu.VMEM)
    dma = pltpu.SemaphoreType.DMA
    return pl.pallas_call(
        partial(head_kernel, table_rows, chunks),
        out_shape=[
            jax.ShapeDtypeStruct((width, tile), jnp.bfloat16),
            jax.ShapeDtypeStruct((1, tile), jnp.float32),
        ],
        in_specs=[anywhere] * 5,
        out_specs=[vmem] * 2,
        scratch_shapes=[
            pltpu.VMEM((both, width), jnp.bfloat16),
            pltpu.VMEM((width, both), jnp.bfloat16),
            pltpu.VMEM((both, tile), jnp.float32),
            pltpu.VMEM((both, tile), jnp.float32),
            pltpu.VMEM((width, tile), jnp.float32),
            pltpu.VMEM((16, tile, width), jnp.bfloat16),
            pltpu.VMEM((16, width, tile), jnp.bfloat16),
            pltpu.VMEM((32, 1, tile), jnp.float32),
            pltpu.VMEM((30, width // 2, tile), jnp.bfloat16),
            pltpu.VMEM((30, 1, tile), jnp.float32),
            dma((5,)),
            dma((32,)),
            dma((32,)),
            dma((2, 30)),
            dma((2, 30)),
        ],
        name="head",
        compiler_params=pltpu.CompilerParams(
            collective_id=2, has_side_effects=True, vmem_limit_bytes=62 * 2**20
        ),
    )(final_state, *tables)


def sum_kernel(gathered, whole, numbers, other_half, mine, parts, piece, core_sems, sems, back_sems):
    dp, z, y, x, core, place, _ = position()
    half, plane = parts.shape[0], (y * 2 + x) * 4 + z
    width = whole.shape[2]
    partner = (place(y, x, 1 - core), z)

    def there(step, back=False):
        other = lax.rem(plane + (half - step if back else step), half)
        column = other // 4
        return other, (place(column // 2, column % 2, core), other % 4)

    barrier = pltpu.get_barrier_semaphore()

    def greet(step, state):
        pl.semaphore_signal(barrier, inc=1, device_id=there(step)[1], device_id_type=MESH)
        return state

    lax.fori_loop(1, half, greet, 0)
    pl.semaphore_signal(barrier, inc=1, device_id=partner, device_id_type=MESH)
    pl.semaphore_wait(barrier, half)

    def to_core(source, target, at):
        return pltpu.make_async_remote_copy(
            source,
            target,
            core_sems.at[2 * at],
            core_sems.at[2 * at + 1],
            device_id=partner,
            device_id_type=MESH,
        )

    first_swap = to_core(gathered.at[pl.ds((1 - core) * half, half)], other_half, 0)
    first_swap.start()
    first_swap.wait_recv()
    mine[...] = gathered[pl.ds(core * half, half)] + other_half[...]
    parts[pl.ds(plane, 1)] = mine[pl.ds(plane, 1)]

    def exchange(copy, target, used):
        def start(step, state):
            copy(step).start()
            return state

        def arrive(step, state):
            source, peer = there(step, True)
            pltpu.make_async_remote_copy(
                target(source),
                target(source),
                used.at[0, step],
                used.at[1, step],
                device_id=peer,
                device_id_type=MESH,
            ).wait_recv()
            return state

        lax.fori_loop(1, half, start, 0)
        lax.fori_loop(1, half, arrive, 0)

    def part_copy(step):
        other, peer = there(step)
        return pltpu.make_async_remote_copy(
            mine.at[other],
            parts.at[plane],
            sems.at[0, step],
            sems.at[1, step],
            device_id=peer,
            device_id_type=MESH,
        )

    exchange(part_copy, lambda source: parts.at[source], sems)
    summed = parts[0]
    for source in range(1, half):
        summed += parts[source]
    row = core * half + plane
    piece[...] = summed[:, :width]
    whole[pl.ds(row, 1)] = summed[None, :, :width]
    numbers[...] = summed[:, width:]

    def back_copy(step):
        return pltpu.make_async_remote_copy(
            piece,
            whole.at[row],
            back_sems.at[0, step],
            back_sems.at[1, step],
            device_id=there(step)[1],
            device_id_type=MESH,
        )

    exchange(back_copy, lambda source: whole.at[core * half + source], back_sems)
    rows = whole.at[pl.ds(core * half, half)]
    second_swap = to_core(rows, rows, 1)
    second_swap.start()
    to_core(rows, whole.at[pl.ds((1 - core) * half, half)], 1).wait_recv()
    first_swap.wait_send()
    second_swap.wait_send()

    def sent(step, state):
        part_copy(step).wait_send()
        back_copy(step).wait_send()
        return state

    lax.fori_loop(1, half, sent, 0)


def update_kernel(whole, numbers, adapter_rows, down_momentum, up_momentum, *refs):
    outs, (stage,) = refs[:9], refs[9:]
    mom_down, mom_up, new_down, new_up, low_down, low_up, loss_out, count_out, norm_out = outs
    z = lax.axis_index("vocab")
    weights = adapter_rows[...]
    devices, width = weights.shape
    gradient = whole[...].reshape(devices, width)
    squares = jnp.sum(jnp.sum(gradient * gradient, axis=0, keepdims=True), axis=1, keepdims=True)
    norm = jnp.sqrt(squares)
    factor = jnp.minimum(1.0, clip_level / (norm + 1e-06))
    state = momentum * stack_rows(down_momentum, up_momentum) + factor * gradient
    adapters, rank, share = mom_up.shape
    columns = pl.ds(pl.multiple_of(z * share, share), share)

    def give(values, *targets):
        stage[...] = values
        mine = stage[:, columns]
        for j in range(2 * adapters):
            for pair in targets:
                out = pair[j // adapters]
                out[j % adapters] = mine[j * rank : (j + 1) * rank].astype(out.dtype)

    give(state, (mom_down, mom_up))
    square = (devices, devices)
    row = lax.broadcasted_iota(jnp.int32, square, 0)
    column = lax.broadcasted_iota(jnp.int32, square, 1)
    blocks = row // rank == column // rank

    def gram_of(matrix):
        return jnp.where(blocks, dot_nt(matrix, matrix, highest_precision), 0.0)

    grams = gram_of(state)
    diagonal = jnp.sum(jnp.where(row == column, grams, 0.0), axis=0, keepdims=True)
    traces = jnp.sum(jnp.where(blocks, diagonal, 0.0), axis=1, keepdims=True)
    sizes = jnp.sqrt(traces) + 1e-07
    state = state / sizes
    grams = grams / (sizes * sizes)
    for turn_index in range(5):
        if turn_index:
            grams = gram_of(state)
        poly = coef_b * grams + coef_c * dot_without_transpose(grams, grams, highest_precision)
        state = coef_a * state + dot_without_transpose(poly, state, highest_precision)
    give(weights - learning_rate * state, (new_down, new_up), (low_down, low_up))
    loss_out[...] = numbers[:, 0:1]
    count_out[...] = numbers[:, 1:2]
    norm_out[...] = norm


def halves_of(values):
    high = values.astype(jnp.bfloat16)
    return high, (values - high.astype(jnp.float32)).astype(jnp.bfloat16)


def stacked_halves(values):
    return jnp.concatenate(halves_of(values), axis=0)


def added_halves(values):
    rows = values.shape[0] // 2
    return values[:rows] + values[rows:]


def dot_tn(left_side, right_side):
    return dot_first(left_side, right_side)


def normal(values):
    center = values - jnp.mean(values, axis=-1, keepdims=True)
    spread = lax.rsqrt(jnp.mean(center * center, axis=-1, keepdims=True) + ln_eps)
    return center * spread, spread


def normal_back(values, gain, gradient):
    unit, spread = normal(values)
    pulled = gradient * gain
    along = jnp.mean(pulled * unit, axis=-1, keepdims=True)
    return spread * (pulled - jnp.mean(pulled, axis=-1, keepdims=True) - unit * along)


def sequence_places(lengths, rows):
    col = lax.broadcasted_iota(jnp.int32, (rows, 1), 0)
    row = lax.broadcasted_iota(jnp.int32, (1, rows), 1)
    segment_col, segment_row = jnp.zeros_like(col), jnp.zeros_like(row)
    start_col = jnp.zeros_like(col)
    end = 0
    for at in range(lengths.shape[1]):
        length = lengths[0, at]
        end = end + length
        segment_col += (col >= end).astype(jnp.int32)
        segment_row += (row >= end).astype(jnp.int32)
        start_col += jnp.where(col >= end, length, 0)
    allowed = (segment_col == segment_row) & (row <= col)
    return col - start_col, allowed


def pairs_of(width):
    return width // (2 * HEAD_DIM)


def pair_at(pair):
    return pl.ds(pl.multiple_of(pair * 2 * HEAD_DIM, 2 * HEAD_DIM), 2 * HEAD_DIM)


def head_lanes(rows):
    return lax.broadcasted_iota(jnp.int32, (rows, 2 * HEAD_DIM), 1) < HEAD_DIM


def first_part(embedded, positions, lengths, gains, shifts, x0, h1):
    rows = x0.shape[0]
    place_col, allowed = sequence_places(lengths, rows)
    spots = lax.broadcasted_iota(jnp.int32, (rows, positions.shape[0]), 1)
    hot = (place_col == spots).astype(jnp.float32).astype(jnp.bfloat16)
    x0[...] = embedded[...] + dot_without_transpose(hot, positions[...])
    unit, _ = normal(x0[...])
    h1[...] = (unit * gains[0:1] + shifts[0:1]).astype(jnp.bfloat16)
    return allowed


def adapter_in(adapters, inputs):
    return added_halves(dot_nt(stacked_halves(adapters), inputs))


def adapter_out(inner, outer):
    high, low = halves_of(inner)
    top, rest = halves_of(outer)
    return adapter_scale * dot_tn(
        jnp.concatenate([high, high, low], axis=0), jnp.concatenate([top, rest, top], axis=0)
    )


def ranks(which, shape):
    return lax.broadcasted_iota(jnp.int32, shape, 0) // 4 == which


def project_part(h1, weight, bias, adapters, inner, joined):
    width = h1.shape[1]
    step = 512
    half = adapters.shape[0] // 2
    inner[...] = adapter_in(adapters[:half], h1[...])
    for which in range(3):

        def columns(at, state):
            here = pl.ds(pl.multiple_of(at * step, step), step)
            there = pl.ds(pl.multiple_of(which * width + at * step, step), step)
            outer = jnp.where(ranks(which, (half, step)), adapters[half:, here], 0.0)
            joined[:, there] = (
                dot_without_transpose(h1[...], weight[:, there])
                + bias[:, there]
                + adapter_out(inner[...], outer)
            ).astype(jnp.bfloat16)
            return state

        lax.fori_loop(0, width // step, columns, 0)


def attend_part(joined, allowed, probs, mixed):
    rows, width = mixed.shape
    lanes = head_lanes(rows)

    def pair_step(pair, state):
        query = joined[:, pair_at(pair)]
        keys = joined[:, pair_at(pairs_of(width) + pair)]
        values = joined[:, pair_at(2 * pairs_of(width) + pair)]
        outs = []
        for side in range(2):
            mine = lanes if side == 0 else ~lanes
            scores = dot_nt(jnp.where(mine, query, jnp.zeros_like(query)), keys) * score_scale
            scores = jnp.where(allowed, scores, masked_value)
            expo = jnp.exp(scores - jnp.max(scores, axis=-1, keepdims=True))
            chances = (expo / jnp.sum(expo, axis=-1, keepdims=True)).astype(jnp.bfloat16)
            probs[2 * pair + side] = chances
            outs.append(dot_without_transpose(chances, values))
        mixed[:, pair_at(pair)] = jnp.where(lanes, outs[0], outs[1]).astype(jnp.bfloat16)
        return state

    lax.fori_loop(0, pairs_of(width), pair_step, 0)


def output_part(x0, mixed, weight, bias, adapters, inner, gains, shifts, x1, h2):
    half = adapters.shape[0] // 2
    width = mixed.shape[1]
    here = ranks(3, inner.shape)
    fresh = adapter_in(adapters[:half], mixed[...])
    inner[...] = jnp.where(here, fresh, inner[...])
    outer = jnp.where(ranks(3, (half, width)), adapters[half:], 0.0)
    x1[...] = (
        x0[...]
        + dot_without_transpose(mixed[...], weight[...])
        + bias[:, 3 * width : 4 * width]
        + adapter_out(inner[...], outer)
    )
    unit, _ = normal(x1[...])
    h2[...] = (unit * gains[1:2] + shifts[1:2]).astype(jnp.bfloat16)


def up_part(h2, weight, bias, active, slope):
    width = h2.shape[1]
    step = 512

    def columns(at, state):
        here = pl.ds(pl.multiple_of(at * step, step), step)
        there = pl.ds(pl.multiple_of(4 * width + at * step, step), step)
        z = dot_without_transpose(h2[...], weight[:, here]) + bias[:, there]
        root = 0.7978845608028654
        square = z * z
        tanh = jnp.tanh(root * z * (1.0 + 0.044715 * square))
        half = 0.5 * (1.0 + tanh)
        active[:, here] = (z * half).astype(jnp.bfloat16)
        slope[:, here] = (
            half + 0.5 * z * (1.0 - tanh * tanh) * (root * (1.0 + 3 * 0.044715 * square))
        ).astype(jnp.bfloat16)
        return state

    lax.fori_loop(0, weight.shape[1] // step, columns, 0)


def down_part(x1, active, weight, bias, gains, shifts, x2, final):
    hidden, width = weight.shape
    step = 256

    def columns(at, state):
        here = pl.ds(pl.multiple_of(at * step, step), step)
        there = pl.ds(pl.multiple_of(4 * width + hidden + at * step, step), step)
        x2[:, here] = (
            x1[:, here]
            + dot_without_transpose(active[...], weight[:, here])
            + bias[:, there]
        )
        return state

    lax.fori_loop(0, width // step, columns, 0)
    unit, _ = normal(x2[...])
    final[...] = (unit * gains[2:3] + shifts[2:3]).astype(jnp.bfloat16)


def turn_rows(source, target):
    width = source.shape[0]

    def rows(at, state):
        here = pl.ds(pl.multiple_of(at * 128, 128), 128)
        target[:, here] = source[here].astype(jnp.float32).T.astype(target.dtype)
        return state

    lax.fori_loop(0, width // 128, rows, 0)


def backward_kernel(
    mean_rows,
    log_total,
    mask_row,
    mask_col,
    target_rows,
    table_sum,
    gains,
    adapters,
    final,
    h1_far,
    joined_far,
    probs_far,
    mixed_far,
    inner,
    x1,
    slope,
    x2,
    w_out,
    w_up,
    w_down,
    gathered,
    work,
    dx2,
    da,
    dz,
    dmix,
    pulls,
    out_here,
    up_here,
    down_here,
    h1,
    joined,
    probs,
    mixed,
    sems,
):
    loads = []
    for at, (source, target) in enumerate(
        (
            (w_down, down_here),
            (w_up, up_here),
            (w_out, out_here),
            (mixed_far, mixed),
            (joined_far, joined),
            (probs_far, probs),
            (h1_far, h1),
        )
    ):
        copy = pltpu.make_async_copy(source, target, sems.at[at])
        copy.start()
        loads.append(copy)
    rows, width = x1.shape
    half = adapters.shape[0] // 2
    hidden = slope.shape[1]
    turn_rows(mean_rows, work)
    pulled = (1.0 - smooth) * target_rows[...] + (smooth / V) * table_sum[...]
    row_dots = jnp.sum(final[...].astype(jnp.float32) * pulled, axis=1, keepdims=True)
    loss = jnp.sum(mask_row[...] * log_total[...], axis=1, keepdims=True) - jnp.sum(
        mask_col[...] * row_dots, axis=0, keepdims=True
    )
    counted = jnp.sum(mask_row[...], axis=1, keepdims=True)
    lanes = lax.broadcasted_iota(jnp.int32, (1, 128), 1)
    numbers = jnp.where(lanes == 0, loss, jnp.where(lanes == 1, counted, 0.0))
    dx2[...] = normal_back(x2[...], gains[2:3], mask_col[...] * (work[...] - pulled))
    da[...] = dx2[...].astype(jnp.bfloat16)
    loads[0].wait()
    step = 512

    def hidden_columns(at, state):
        here = pl.ds(pl.multiple_of(at * step, step), step)
        dz[:, here] = (
            dot_nt(da[...], down_here[here]) * slope[:, here].astype(jnp.float32)
        ).astype(jnp.bfloat16)
        return state

    lax.fori_loop(0, hidden // step, hidden_columns, 0)
    loads[1].wait()

    def columns(at, state):
        here = pl.ds(pl.multiple_of(at * 256, 256), 256)
        work[:, here] = dot_nt(dz[...], up_here[here])
        return state

    lax.fori_loop(0, width // 256, columns, 0)
    dx1 = dx2[...] + normal_back(x1[...], gains[1:2], work[...])
    da[...] = dx1.astype(jnp.bfloat16)
    loads[2].wait()
    loads[3].wait()
    upper = stacked_halves(adapters[half:])
    inner_halves = stacked_halves(inner[...])

    def adapter_grads(which, gradient, inputs):
        up_grad = adapter_scale * added_halves(dot_without_transpose(inner_halves, gradient))
        back = adapter_scale * added_halves(dot_nt(upper, gradient))
        back = jnp.where(ranks(which, back.shape), back, 0.0)
        down_grad = added_halves(dot_without_transpose(stacked_halves(back), inputs))
        keep = ranks(which, up_grad.shape)
        return back, down_grad, jnp.where(keep, up_grad, 0.0)

    back, down_total, up_total = adapter_grads(3, da[...], mixed[...])
    dmix[...] = (
        dot_nt(da[...], out_here[...]) + adapter_out(back, adapters[:half]) / adapter_scale
    ).astype(jnp.bfloat16)
    lane_mask = head_lanes(rows)
    for copy in loads[4:]:
        copy.wait()

    def pair_step(pair, state):
        query = joined[:, pair_at(pair)]
        keys = joined[:, pair_at(pairs_of(width) + pair)]
        values = joined[:, pair_at(2 * pairs_of(width) + pair)]
        pull = dmix[:, pair_at(pair)]
        outs = []
        for side in range(2):
            mine = lane_mask if side == 0 else ~lane_mask
            chances = probs[2 * pair + side]
            wide = chances.astype(jnp.float32)
            reach = dot_nt(jnp.where(mine, pull, jnp.zeros_like(pull)), values)
            slide = wide * (reach - jnp.sum(wide * reach, axis=-1, keepdims=True))
            slide = slide.astype(jnp.bfloat16)
            outs.append(
                (
                    dot_without_transpose(slide, keys) * score_scale,
                    dot_tn(slide, query) * score_scale,
                    dot_tn(chances, pull),
                )
            )
        for which in range(3):
            both = jnp.where(lane_mask, outs[0][which], outs[1][which])
            pulls[:, pair_at(which * pairs_of(width) + pair)] = both.astype(jnp.bfloat16)
        return state

    lax.fori_loop(0, pairs_of(width), pair_step, 0)
    for which in range(3):
        _, down_part_grad, up_part_grad = adapter_grads(
            which, pulls[:, which * width : (which + 1) * width], h1[...]
        )
        down_total += down_part_grad
        up_total += up_part_grad
    grads = jnp.concatenate([down_total, up_total], axis=0)
    numbers = jnp.broadcast_to(numbers, (2 * half, 128))
    gathered[...] = jnp.concatenate([grads, numbers], axis=1).reshape(2 * half, 1, width + 128)


def backward(mean_rows, log_total, mask, target_rows, table_sum, gains, adapters, kept, weights):
    rows = mask.shape[0]
    width = target_rows.shape[1]
    hidden = weights[2].shape[0]
    low, full = jnp.bfloat16, jnp.float32
    anywhere, vmem = pl.BlockSpec(memory_space=pl.ANY), pl.BlockSpec(memory_space=pltpu.VMEM)
    return pl.pallas_call(
        backward_kernel,
        out_shape=jax.ShapeDtypeStruct((adapters.shape[0], 1, width + 128), full),
        in_specs=[vmem] * 9 + [anywhere] * 4 + [vmem] * 4 + [anywhere] * 3,
        out_specs=vmem,
        scratch_shapes=[
            pltpu.VMEM((rows, width), full),
            pltpu.VMEM((rows, width), full),
            pltpu.VMEM((rows, width), low),
            pltpu.VMEM((rows, hidden), low),
            pltpu.VMEM((rows, width), low),
            pltpu.VMEM((rows, 3 * width), low),
        ]
        + [pltpu.VMEM(w.shape, low) for w in weights]
        + [pltpu.VMEM(value.shape, low) for value in kept[1:5]]
        + [pltpu.SemaphoreType.DMA((7,))],
        name="backward",
        compiler_params=pltpu.CompilerParams(vmem_limit_bytes=60 * 2**20),
    )(
        mean_rows,
        log_total,
        mask[None, :],
        mask[:, None],
        target_rows,
        table_sum,
        gains,
        adapters,
        *kept,
        *weights,
    )


def update(gathered, adapters, down_momentum, up_momentum):
    group = lax.axis_size("vocab")
    devices = lax.axis_size("dp") * group
    width = adapters.shape[1]
    low, full = jnp.bfloat16, jnp.float32
    vmem = pl.BlockSpec(memory_space=pltpu.VMEM)
    dma = pltpu.SemaphoreType.DMA
    shape = jax.ShapeDtypeStruct
    share = up_momentum.shape[:2] + (width // group,)
    half = devices // 2
    message = gathered.shape[1:]
    whole, numbers = pl.pallas_call(
        sum_kernel,
        out_shape=[shape((devices, 1, width), full), shape((1, 128), full)],
        in_specs=[vmem],
        out_specs=[vmem] * 2,
        scratch_shapes=[
            pltpu.VMEM((half,) + message, full),
            pltpu.VMEM((half,) + message, full),
            pltpu.VMEM((half,) + message, full),
            pltpu.VMEM((1, width), full),
            dma((4,)),
            dma((2, half)),
            dma((2, half)),
        ],
        name="sum_gradients",
        compiler_params=pltpu.CompilerParams(collective_id=3, has_side_effects=True),
    )(gathered)
    return pl.pallas_call(
        update_kernel,
        out_shape=[shape(share, full)] * 4 + [shape(share, low)] * 2 + [shape((1, 1), full)] * 3,
        in_specs=[vmem] * 5,
        out_specs=[vmem] * 9,
        scratch_shapes=[pltpu.VMEM((devices, width), full)],
        name="update",
    )(whole, numbers, adapters, jnp.swapaxes(down_momentum, 1, 2), up_momentum)


def col_of(row):
    size = row.shape[1]
    square = (size, size)
    same = lax.broadcasted_iota(jnp.int32, square, 0) == lax.broadcasted_iota(jnp.int32, square, 1)
    return jnp.sum(jnp.where(same, row, 0.0), axis=1, keepdims=True)


def stack_rows(down, up):
    return jnp.concatenate(
        [down[j] for j in range(down.shape[0])] + [up[j] for j in range(up.shape[0])], axis=0
    )


def pack_rows(positions, gains, shifts, biases):
    width, count = positions.shape
    square = (count, count)
    same = lax.broadcasted_iota(jnp.int32, square, 0) == lax.broadcasted_iota(jnp.int32, square, 1)
    places = dot_nt(same.astype(jnp.float32).astype(jnp.bfloat16), positions[...])
    span = count // 4
    places = jnp.concatenate([places[r * span : (r + 1) * span] for r in range(4)], axis=1)
    norms = jnp.concatenate(
        [
            gains[...].astype(jnp.float32),
            shifts[...].astype(jnp.float32),
            jnp.zeros((gains.shape[0], 128 - 2 * width), jnp.float32),
        ],
        axis=1,
    )
    flat = biases[...].astype(jnp.float32)
    flat = jnp.concatenate([flat, jnp.zeros((1, -flat.shape[1] % 128), jnp.float32)], axis=1)
    lines = [flat[:, r * 128 : (r + 1) * 128] for r in range(flat.shape[1] // 128)]
    rest = jnp.zeros((8 - gains.shape[0], 128), jnp.float32)
    tail = jnp.zeros((8 - len(lines), 128), jnp.float32)
    return jnp.concatenate([places, norms, rest] + lines + [tail], axis=0).astype(jnp.bfloat16)


def unpack_rows(packed, devices, width, span, norms, bias_size, positions, gains, shifts, bias):
    rows = packed.shape[0] // devices

    def group(j, state):
        devs = [
            packed[pl.ds(pl.multiple_of((4 * j + i) * rows, rows), rows)].astype(jnp.float32)
            for i in range(4)
        ]
        lanes = pl.ds(pl.multiple_of(j * 128, 128), 128)
        for r in range(4):
            block = [dev[:span, r * width : (r + 1) * width] for dev in devs]
            positions[r * span : (r + 1) * span, lanes] = jnp.concatenate(block, axis=1).astype(
                jnp.bfloat16
            )
        gains[:, lanes] = jnp.concatenate([dev[span : span + norms, :width] for dev in devs], axis=1)
        shifts[:, lanes] = jnp.concatenate(
            [dev[span : span + norms, width : 2 * width] for dev in devs], axis=1
        )
        flat = []
        for dev in devs:
            left = bias_size
            line = span + 8
            while left > 0:
                flat.append(dev[line : line + 1, : min(left, 128)])
                left -= 128
                line += 1
        bias[:, pl.ds(pl.multiple_of(j * 4 * bias_size, 128), 4 * bias_size)] = jnp.concatenate(
            flat, axis=1
        )
        return state

    lax.fori_loop(0, devices // 4, group, 0)


CAP, EXTRA = 16, 16
ASKED = 48
OWN, LINE, SIDE, DIAGONAL, CORE, ROWS = range(6)
ASK, SUM, ANSWER, TURN, UNPACK, EMBED, PROJECT, ATTEND, OUTPUT, UP, DOWN = range(6, 17)
FIRST_ORDER = (
    (OWN, 0, 0),
    (SUM, 0, 0),
    (OWN, 2, 0),
    (OWN, 1, 0),
    (ASK, 0, 0),
    (LINE, 2, 2),
    (LINE, 1, 1),
    (LINE, 1, 2),
    (ANSWER, 0, 0),
    (LINE, 2, 1),
    (OWN, 5, 0),
    (OWN, 3, 0),
    (LINE, 0, 1),
    (LINE, 2, 3),
    (LINE, 5, 2),
    (LINE, 5, 1),
    (LINE, 0, 2),
    (TURN, 0, 0),
    (LINE, 5, 3),
    (SIDE, 2, 2),
    (SIDE, 0, 0),
    (LINE, 1, 3),
    (LINE, 0, 3),
    (SIDE, 2, 0),
    (SIDE, 0, 2),
    (SIDE, 0, 1),
    (SIDE, 5, 1),
    (SIDE, 5, 0),
    (SIDE, 5, 3),
    (SIDE, 2, 3),
    (LINE, 3, 1),
    (SIDE, 2, 1),
    (OWN, 4, 0),
    (ROWS, 0, 0),
    (DIAGONAL, 5, 1),
    (SIDE, 1, 0),
    (SIDE, 1, 1),
    (SIDE, 0, 3),
    (SIDE, 1, 3),
    (DIAGONAL, 2, 2),
    (DIAGONAL, 0, 0),
    (ROWS, 0, 2),
    (LINE, 3, 3),
    (SIDE, 1, 2),
    (SIDE, 5, 2),
    (DIAGONAL, 2, 1),
    (LINE, 3, 2),
    (DIAGONAL, 0, 2),
    (LINE, 4, 2),
    (ROWS, 0, 3),
    (DIAGONAL, 1, 3),
    (DIAGONAL, 2, 3),
    (DIAGONAL, 0, 3),
    (DIAGONAL, 2, 0),
    (DIAGONAL, 1, 2),
    (DIAGONAL, 5, 3),
    (DIAGONAL, 0, 1),
    (ROWS, 0, 1),
    (CORE, 0, 0),
    (DIAGONAL, 5, 2),
    (LINE, 4, 1),
    (DIAGONAL, 5, 0),
    (DIAGONAL, 1, 0),
    (SIDE, 3, 0),
    (DIAGONAL, 1, 1),
    (SIDE, 3, 1),
    (SIDE, 3, 3),
    (SIDE, 3, 2),
    (UNPACK, 0, 0),
    (CORE, 5, 0),
    (LINE, 4, 3),
    (EMBED, 0, 0),
    (CORE, 1, 0),
    (PROJECT, 0, 0),
    (DIAGONAL, 3, 0),
    (ATTEND, 0, 0),
    (CORE, 2, 0),
    (SIDE, 4, 2),
    (SIDE, 4, 0),
    (DIAGONAL, 3, 3),
    (DIAGONAL, 3, 1),
    (SIDE, 4, 1),
    (DIAGONAL, 3, 2),
    (OUTPUT, 0, 0),
    (SIDE, 4, 3),
    (CORE, 3, 0),
    (UP, 0, 0),
    (DIAGONAL, 4, 2),
    (DIAGONAL, 4, 0),
    (DIAGONAL, 4, 3),
    (DIAGONAL, 4, 1),
    (CORE, 4, 0),
    (DOWN, 0, 0),
)


def first_kernel(table_rows, devices, group, row_counts, *refs):
    (
        ids,
        targets,
        mask,
        lengths,
        position_own,
        gain_own,
        shift_own,
        bias_own,
        adapter_down,
        adapter_up,
        table_tail,
        table,
        *refs,
    ) = refs
    weights_own = refs[:4]
    refs = refs[4:]
    (
        flags,
        target_out,
        table_sum,
        gains_out,
        adapters_out,
        final,
        inner,
        table_mine,
        turned_mine,
        table_other,
        turned_other,
        h1_out,
        joined_out,
        probs_out,
        mixed_out,
        x1_out,
        slope_out,
        x2_out,
        out_kept,
        up_kept,
        down_kept,
        *refs,
    ) = refs
    (
        send_sems,
        recv_sems,
        local_sems,
        table_sems,
        ask_sems,
        row_sems,
        sum_sems,
        keep_sems,
        table_here,
        turned_here,
        selector,
        rows_out,
        rows_in,
        ask_out,
        ask_in,
        sum_out,
        sum_in,
        extra_out,
        extra,
        pack_here,
        packed,
        w_qkv,
        w_out,
        w_up,
        w_down,
        positions,
        shifts,
        bias,
        embedded,
        x0,
        h1,
        joined,
        probs,
        mixed,
        x1,
        h2,
        active,
        slope,
        x2,
    ) = refs
    arrays = (packed, w_qkv, w_out, w_up, w_down, extra)
    ins = (pack_here,) + tuple(weights_own) + (extra_out,)
    dp, z, y, x, core, place, _ = position()
    along = by_nearness(z)
    dp_x, dp_y = place(y, 1 - x, core), place(1 - y, x, core)
    dp_core, dp_diagonal = place(y, x, 1 - core), place(1 - y, 1 - x, core)
    z_peers = [(dp, along[k]) for k in (1, 2, 3)]
    near_peers = [(dp_x, z), (dp_y, z), (dp_core, z)]
    body_rows = table_rows // 16 * 16
    tail_rows = table_here.shape[0] - body_rows
    loads = [
        pltpu.make_async_copy(
            table.at[pl.ds(0, body_rows)], table_here.at[pl.ds(0, body_rows)], table_sems.at[0]
        ),
        pltpu.make_async_copy(
            table_tail, table_here.at[pl.ds(body_rows, tail_rows)], table_sems.at[1]
        ),
    ]
    for copy in loads:
        copy.start()
    pack_here[...] = pack_rows(position_own, gain_own, shift_own, bias_own)
    me = meet_all(devices, group)
    sent, kept, used = [], {}, [0] * len(arrays)

    def piece(which, block):
        rows = row_counts[which]
        return arrays[which].at[pl.ds(pl.multiple_of(block * rows, rows), rows)]

    def copy_to(which, block, peer, source, number):
        return pltpu.make_async_remote_copy(
            piece(which, block) if source is None else source,
            piece(which, block),
            send_sems.at[which, number],
            recv_sems.at[which, block],
            device_id=peer,
            device_id_type=MESH,
        )

    def send(which, block, peer, source=None):
        copy = copy_to(which, block, peer, source, used[which])
        used[which] += 1
        copy.start()
        sent.append(copy)

    def arrive(which, block):
        copy_to(which, block, z_peers[0], ins[which], 0).wait_recv()

    def pass_along(which, k, act):
        source = None if k else ins[which]
        block = dp * 4 + along[k]

        @pl.when((along[k] <= z) & (z < 3))
        def _():
            act(copy_to(which, block, (dp, z + 1), source, 34 + k))

        @pl.when((along[k] >= z) & (z > 0))
        def _():
            act(copy_to(which, block, (dp, z - 1), source, 38 + k))

    def own_near(which):
        for peer in near_peers:
            send(which, me, peer, ins[which])
        copy = pltpu.make_async_copy(ins[which], piece(which, me), local_sems.at[which])
        copy.start()
        kept[which] = copy

    def own(which, _):
        if which == 5:
            own_near(which)
        pass_along(which, 0, lambda copy: copy.start())

    def line(which, k):
        block = dp * 4 + along[k]
        arrive(which, block)
        pass_along(which, k, lambda copy: copy.start())
        for peer in near_peers:
            send(which, block, peer)

    def side(which, k):
        block_x, block_y = dp_x * 4 + along[k], dp_y * 4 + along[k]
        arrive(which, block_y)
        if k < 2:
            send(which, block_y, (dp_x, z))
        arrive(which, block_x)
        if k >= 2:
            send(which, block_x, (dp_y, z))
        send(which, block_y, (dp_core, z))
        send(which, block_x, (dp_core, z))

    def diagonal(which, k):
        block = dp_diagonal * 4 + along[k]
        arrive(which, block)
        send(which, block, (dp_core, z))

    def other_core(which, _):
        for y_at in range(2):
            for x_at in range(2):
                for z_at in range(4):
                    arrive(which, place(y_at, x_at, 1 - core) * 4 + z_at)
        kept[which].wait()

    keeps = []

    def keep(source, target):
        copy = pltpu.make_async_copy(source, target, keep_sems.at[len(keeps)])
        copy.start()
        keeps.append(copy)

    for which in range(5):
        own_near(which)
    state = {}

    def ask():
        own_ids = ids[...].astype(jnp.float32)
        own_targets = jnp.where(mask[...] > 0, targets[...], ids[...]).astype(jnp.float32)
        ids_row = jnp.concatenate([own_ids, own_targets], axis=1)
        ids_col = jnp.concatenate([col_of(own_ids), col_of(own_targets)], axis=0)
        tokens = ids_row.shape[1]
        wide = (tokens, tokens)
        across = lax.broadcasted_iota(jnp.int32, wide, 1).astype(jnp.float32)
        down = lax.broadcasted_iota(jnp.int32, wide, 0).astype(jnp.float32)
        owner_row, owner_col = jnp.zeros_like(ids_row), jnp.zeros_like(ids_col)
        for device in range(1, devices):
            owner_row += (ids_row >= float(device * table_rows)).astype(jnp.float32)
            owner_col += (ids_col >= float(device * table_rows)).astype(jnp.float32)
        equal = ids_col == ids_row
        first_col = jnp.min(jnp.where(equal, across, float(tokens)), axis=1, keepdims=True)
        first_row = jnp.min(jnp.where(equal, down, float(tokens)), axis=0, keepdims=True)
        leads = jnp.where(first_row == across[:1], owner_row, -1.0)
        slot_col = jnp.sum(
            jnp.where((owner_col == leads) & (across < first_col), 1.0, 0.0),
            axis=1,
            keepdims=True,
        )
        takes = lax.broadcasted_iota(jnp.int32, (devices, tokens), 0).astype(jnp.float32) == leads
        local_row = jnp.where(takes, ids_row - owner_row * table_rows + 1.0, 0.0)
        lanes = lax.broadcasted_iota(jnp.int32, (tokens, 128), 1).astype(jnp.float32)
        asked = (
            dot_without_transpose(
                local_row, (slot_col == lanes).astype(jnp.float32), highest_precision
            )
            - 1.0
        )
        over = jnp.max(slot_col, axis=0, keepdims=True) >= float(ASKED)
        ask_lanes = lax.broadcasted_iota(jnp.int32, (devices, 128), 1)
        asked = jnp.where(ask_lanes == 127, over.astype(jnp.float32), asked)
        ask_out[...] = asked.reshape(devices, 1, 128)
        ask_in[pl.ds(me, 1)] = ask_out[pl.ds(me, 1)]
        start, state["ask_arrive"], state["ask_sent"] = to_all(
            lambda other: ask_out.at[other],
            ask_in,
            ask_sems.at[0],
            ask_sems.at[1],
            devices,
            group,
            me,
        )
        start()
        state["ids_col"] = ids_col
        state["owner_col"] = owner_col
        state["slot_col"] = slot_col

    def table_total():
        for copy in loads:
            copy.wait()
        keep(table_here, table_mine)

        def add_up(step, total):
            return total + jnp.sum(
                table_here[pl.ds(pl.multiple_of(step * 128, 128), 128)].astype(jnp.float32),
                axis=0,
                keepdims=True,
            )

        width = table_here.shape[1]
        sum_out[:, :width] = lax.fori_loop(
            0, table_here.shape[0] // 128, add_up, jnp.zeros((1, width), jnp.float32)
        )

    def answer():
        state["ask_arrive"]()
        width = table_here.shape[1]
        asked_all = ask_in[...].reshape(devices, 128)
        ask_lanes = lax.broadcasted_iota(jnp.int32, (devices, 128), 1)
        over = jnp.max(
            jnp.max(jnp.where(ask_lanes == 127, asked_all, 0.0), axis=0, keepdims=True),
            axis=1,
            keepdims=True,
        )
        square = (128, 128)
        eye = (
            lax.broadcasted_iota(jnp.int32, square, 0)
            == lax.broadcasted_iota(jnp.int32, square, 1)
        ).astype(jnp.float32)
        turned = jnp.round(dot_nt(eye, asked_all, highest_precision))
        more = turned[CAP:ASKED]
        counts = jnp.sum((more >= 0.0).astype(jnp.float32), axis=0, keepdims=True)
        pairs = (devices, devices)
        before = (
            lax.broadcasted_iota(jnp.int32, pairs, 0) < lax.broadcasted_iota(jnp.int32, pairs, 1)
        ).astype(jnp.float32)
        ahead = jnp.round(
            dot_without_transpose(
                jnp.broadcast_to(counts, (8, devices)), before, highest_precision
            )[:1]
        )
        order = ahead + lax.broadcasted_iota(jnp.int32, more.shape, 0).astype(jnp.float32)
        order = jnp.where(more >= 0.0, order, -1.0)
        total = jnp.sum(counts, axis=1, keepdims=True)
        over = jnp.maximum(over, (total > float(EXTRA)).astype(jnp.float32))
        extra_col = jnp.full((EXTRA, 1), -1.0, jnp.float32)
        extra_row = jnp.full((1, 128), -1.0, jnp.float32)
        spots_col = lax.broadcasted_iota(jnp.int32, (EXTRA, 1), 0)
        spots_row = lax.broadcasted_iota(jnp.int32, (1, 128), 1)
        for spot in range(EXTRA):
            found = jnp.where(order == float(spot), more + 1.0, 0.0)
            found = jnp.sum(jnp.sum(found, axis=0, keepdims=True), axis=1, keepdims=True) - 1.0
            extra_col = jnp.where(spots_col == spot, found, extra_col)
            extra_row = jnp.where(spots_row == spot, found, extra_row)
        first_id = (me * table_rows).astype(jnp.float32)
        extra_row = jnp.where(extra_row >= 0.0, extra_row + first_id, -1.0)
        sum_out[:, width:] = jnp.where(spots_row == 127, over, extra_row)
        sum_in[pl.ds(me, 1)] = sum_out[...][None]
        start, state["sum_arrive"], state["sum_sent"] = to_all(
            lambda other: sum_out, sum_in, sum_sems.at[0], sum_sems.at[1], devices, group, me
        )
        start()
        row_lanes = lax.broadcasted_iota(jnp.int32, (EXTRA, table_here.shape[0]), 1)
        row_lanes = row_lanes.astype(jnp.float32)
        batch = selector.shape[0] // CAP
        for step in range(devices // batch):
            for at in range(batch):
                source = step * batch + at
                hot = turned[:CAP, source : source + 1] == row_lanes
                selector[at * CAP : (at + 1) * CAP] = hot.astype(jnp.float32).astype(jnp.bfloat16)
            picked = dot_without_transpose(selector[...], table_here[...])
            rows_out[step * batch : (step + 1) * batch] = picked.astype(jnp.bfloat16).reshape(
                batch, CAP, -1
            )
        hot = (extra_col == row_lanes).astype(jnp.float32).astype(jnp.bfloat16)
        extra_out[...] = dot_without_transpose(hot, table_here[...]).astype(jnp.bfloat16)
        rows_in[pl.ds(me, 1)] = rows_out[pl.ds(me, 1)]

    def row_copy(offset, far, there):
        column = lax.rem(dp + offset, devices // group)
        other = column * group + there
        number = offset * group + far
        return pltpu.make_async_remote_copy(
            rows_out.at[other],
            rows_in.at[me],
            row_sems.at[0, number],
            row_sems.at[1, number],
            device_id=(column, there),
            device_id_type=MESH,
        )

    def row_copies(k):
        return [
            row_copy(offset, mirror(z, along[k]), along[k])
            for offset in range(0 if k else 1, devices // group)
        ]

    def send_rows(k):
        for copy in row_copies(k):
            copy.start()

    def rows_arrive():
        flips = (z, z // 2 * 2 + 1 - z % 2, (z + 2) % 4, (1 - z // 2) * 2 + 1 - z % 2)
        for offset in range(devices // group):
            for far in range(group):
                if offset or far:
                    column = lax.rem(dp + devices // group - offset, devices // group)
                    source = column * group + flips[far]
                    number = offset * group + far
                    pltpu.make_async_remote_copy(
                        rows_in.at[source],
                        rows_in.at[source],
                        row_sems.at[0, number],
                        row_sems.at[1, number],
                        device_id=(column, flips[far]),
                        device_id_type=MESH,
                    ).wait_recv()

    def turn():
        adapters_out[...] = stack_rows(adapter_down, adapter_up)
        turn_rows(table_here, turned_here)
        keep(turned_here, turned_mine)
        for at, (here, there) in enumerate(
            ((table_here, table_other), (turned_here, turned_other))
        ):
            copy = pltpu.make_async_remote_copy(
                here,
                there,
                table_sems.at[2 + 2 * at],
                table_sems.at[3 + 2 * at],
                device_id=(dp_core, z),
                device_id_type=MESH,
            )
            copy.start()
            state["swap", at] = copy

    def unpack():
        unpack_rows(
            packed,
            devices,
            position_own.shape[0],
            position_own.shape[1] // 4,
            gain_own.shape[0],
            bias_own.shape[1],
            positions,
            gains_out,
            shifts,
            bias,
        )

    def embed():
        rows_arrive()
        state["sum_arrive"]()
        width = table_here.shape[1]
        table_sum[...] = jnp.sum(sum_in[:, :, :width], axis=0)
        notes = sum_in[:, :, width:].reshape(devices, 128)
        note_lanes = lax.broadcasted_iota(jnp.int32, notes.shape, 1)
        over = jnp.max(jnp.where(note_lanes == 127, notes, 0.0), axis=0, keepdims=True)
        flags[...] = jnp.max(over, axis=1, keepdims=True)
        slot_col, owner_col, ids_col = state["slot_col"], state["owner_col"], state["ids_col"]
        tokens = ids_col.shape[0]
        slots = lax.broadcasted_iota(jnp.int32, (tokens, devices * CAP), 1).astype(jnp.float32)
        index_col = jnp.where(slot_col < float(CAP), owner_col * CAP + slot_col, -1.0)
        chosen = (index_col == slots).astype(jnp.float32).astype(jnp.bfloat16)
        taken = dot_without_transpose(chosen, rows_in[...].reshape(devices * CAP, -1))
        extra_ids = jnp.concatenate(
            [notes[source : source + 1, :EXTRA] for source in range(devices)], axis=1
        )
        spots = lax.broadcasted_iota(jnp.int32, (tokens, devices * EXTRA), 1).astype(jnp.float32)
        wanted = jnp.where(slot_col < float(CAP), -2.0, ids_col)
        hit = jnp.min(
            jnp.where(wanted == extra_ids, spots, float(devices * EXTRA)), axis=1, keepdims=True
        )
        chosen = (hit == spots).astype(jnp.float32).astype(jnp.bfloat16)
        taken += dot_without_transpose(chosen, extra[...])
        embedded[...] = taken[: tokens // 2]
        target_out[...] = taken[tokens // 2 :]
        state["allowed"] = first_part(embedded, positions, lengths, gains_out, shifts, x0, h1)
        keep(h1, h1_out)

    def project():
        project_part(h1, w_qkv, bias, adapters_out, inner, joined)
        keep(joined, joined_out)

    def attend():
        attend_part(joined, state["allowed"], probs, mixed)
        keep(probs, probs_out)
        keep(mixed, mixed_out)

    def output():
        keep(w_out, out_kept)
        output_part(x0, mixed, w_out, bias, adapters_out, inner, gains_out, shifts, x1, h2)
        keep(x1, x1_out)

    def up():
        keep(w_up, up_kept)
        up_part(h2, w_up, bias, active, slope)
        keep(slope, slope_out)

    def down():
        keep(w_down, down_kept)
        down_part(x1, active, w_down, bias, gains_out, shifts, x2, final)
        keep(x2, x2_out)

    comes = {OWN: own, LINE: line, SIDE: side, DIAGONAL: diagonal, CORE: other_core}
    works = {
        ASK: ask,
        SUM: table_total,
        ANSWER: answer,
        TURN: turn,
        UNPACK: unpack,
        EMBED: embed,
        PROJECT: project,
        ATTEND: attend,
        OUTPUT: output,
        UP: up,
        DOWN: down,
    }
    for kind, which, k in FIRST_ORDER:
        if kind in comes:
            comes[kind](which, k)
        elif kind == ROWS:
            send_rows(k)
        else:
            works[kind]()
    for at in range(2):
        state["swap", at].wait()
    for copy in keeps:
        copy.wait()
    for copy in sent:
        copy.wait_send()
    for which in range(len(arrays)):
        for k in range(4):
            pass_along(which, k, lambda copy: copy.wait_send())
    for k in range(4):
        for copy in row_copies(k):
            copy.wait_send()
    state["ask_sent"]()
    state["sum_sent"]()


def first(
    ids, targets, mask, lengths, table, small, adapter_down, adapter_up, weights
):
    group = lax.axis_size("vocab")
    devices = lax.axis_size("dp") * group
    table_rows, width = table.shape
    pad_rows = -(-table_rows // 128) * 128
    body_rows = table_rows // 16 * 16
    tail = jnp.pad(table[body_rows:], ((0, pad_rows - table_rows), (0, 0)))
    rows = ids.shape[0]
    hidden = weights[3].shape[0] * devices
    heads = width // HEAD_DIM
    low, full = jnp.bfloat16, jnp.float32
    positions, gains, shifts, biases = small
    pack_height = positions.shape[1] // 4 + 16
    counts = [pack_height] + [w.shape[0] for w in weights] + [EXTRA]
    anywhere, vmem = pl.BlockSpec(memory_space=pl.ANY), pl.BlockSpec(memory_space=pltpu.VMEM)
    dma = pltpu.SemaphoreType.DMA
    shape = jax.ShapeDtypeStruct
    adapter_rows = 2 * adapter_up.shape[0] * adapter_up.shape[1]
    whole = [(devices * w.shape[0], w.shape[1]) for w in weights]
    saved = [
        shape((pad_rows, width), low),
        shape((width, pad_rows), low),
        shape((pad_rows, width), low),
        shape((width, pad_rows), low),
        shape((rows, width), low),
        shape((rows, 3 * width), low),
        shape((heads, rows, rows), low),
        shape((rows, width), low),
        shape((rows, width), full),
        shape((rows, hidden), low),
        shape((rows, width), full),
    ] + [shape(w, low) for w in whole[1:]]
    return pl.pallas_call(
        partial(first_kernel, table_rows, devices, group, counts),
        out_shape=[
            shape((1, 1), full),
            shape((rows, width), full),
            shape((1, width), full),
            shape((gains.shape[0], width), full),
            shape((adapter_rows, width), full),
            shape((rows, width), low),
            shape((adapter_rows // 2, rows), full),
        ]
        + saved,
        in_specs=[vmem] * 3
        + [pl.BlockSpec(memory_space=pltpu.SMEM)]
        + [vmem] * 6
        + [anywhere] * (2 + len(weights)),
        out_specs=[vmem] * 7 + [anywhere] * len(saved),
        scratch_shapes=[
            dma((len(counts), 42)),
            dma((len(counts), devices)),
            dma((len(counts),)),
            dma((6,)),
            dma((2, devices)),
            dma((2, devices)),
            dma((2, devices)),
            dma((12,)),
            pltpu.VMEM((pad_rows, width), low),
            pltpu.VMEM((width, pad_rows), low),
            pltpu.VMEM((16 * CAP, pad_rows), low),
            pltpu.VMEM((devices, CAP, width), low),
            pltpu.VMEM((devices, CAP, width), low),
            pltpu.VMEM((devices, 1, 128), full),
            pltpu.VMEM((devices, 1, 128), full),
            pltpu.VMEM((1, width + 128), full),
            pltpu.VMEM((devices, 1, width + 128), full),
            pltpu.VMEM((EXTRA, width), low),
            pltpu.VMEM((devices * EXTRA, width), low),
            pltpu.VMEM((pack_height, 128), low),
            pltpu.VMEM((devices * pack_height, 128), low),
        ]
        + [pltpu.VMEM(w, low) for w in whole]
        + [
            pltpu.VMEM((positions.shape[1], width), low),
            pltpu.VMEM((shifts.shape[0], width), full),
            pltpu.VMEM((1, devices * biases.shape[0]), full),
            pltpu.VMEM((rows, width), full),
            pltpu.VMEM((rows, width), full),
            pltpu.VMEM((rows, width), low),
            pltpu.VMEM((rows, 3 * width), low),
            pltpu.VMEM((heads, rows, rows), low),
            pltpu.VMEM((rows, width), low),
            pltpu.VMEM((rows, width), full),
            pltpu.VMEM((rows, width), low),
            pltpu.VMEM((rows, hidden), low),
            pltpu.VMEM((rows, hidden), low),
            pltpu.VMEM((rows, width), full),
        ],
        name="first",
        compiler_params=pltpu.CompilerParams(
            collective_id=1, has_side_effects=True, vmem_limit_bytes=63 * 2**20
        ),
    )(
        ids[None, :],
        targets[None, :],
        mask[None, :],
        lengths,
        positions,
        gains,
        shifts,
        biases[None, :],
        jnp.swapaxes(adapter_down, 1, 2),
        adapter_up,
        tail,
        table,
        *weights,
    )


def per_device(
    ids,
    targets,
    counted_mask,
    lengths,
    table,
    position_table,
    layer_norm_gain,
    layer_norm_bias,
    query_key_value_weight,
    output_weight,
    up_weight,
    down_weight,
    biases,
    adapter_down,
    adapter_up,
    down_momentum,
    up_momentum,
):
    every = (
        ids,
        targets,
        counted_mask,
        lengths,
        table,
        position_table,
        layer_norm_gain,
        layer_norm_bias,
        query_key_value_weight,
        output_weight,
        up_weight,
        down_weight,
        biases,
        adapter_down,
        adapter_up,
    )
    table_rows = table.shape[0]
    (
        flags,
        target_rows,
        table_sum,
        gains_all,
        adapters,
        final_state,
        inner_rows,
        table_mine,
        turned_mine,
        table_other,
        turned_other,
        h1,
        joined,
        probs,
        mixed,
        x1,
        slope,
        x2,
        w_out_all,
        w_up_all,
        w_down_all,
    ) = first(
        ids,
        targets,
        counted_mask,
        lengths,
        table,
        (position_table.T, layer_norm_gain, layer_norm_bias, biases),
        adapter_down,
        adapter_up,
        (query_key_value_weight, output_weight, up_weight, down_weight),
    )
    kept = (h1, joined, probs, mixed, inner_rows, x1, slope, x2)
    mean_rows, log_total = head(
        final_state, table_rows, (table_mine, turned_mine, table_other, turned_other)
    )
    gathered = backward(
        mean_rows,
        log_total,
        counted_mask.astype(jnp.float32),
        target_rows,
        table_sum,
        gains_all,
        adapters,
        (final_state, *kept),
        (w_out_all, w_up_all, w_down_all),
    )

    def general():
        down_gradient, up_gradient, loss_own, count_own = gradients_general(*every)
        rows = jnp.concatenate([jnp.swapaxes(down_gradient, 1, 2), up_gradient], axis=0)
        rows = rows.reshape(gathered.shape[0], 1, -1)
        sums = jnp.zeros((rows.shape[0], 1, 128), jnp.float32)
        sums = sums.at[:, :, 0].set(loss_own).at[:, :, 1].set(count_own)
        return jnp.concatenate([rows, sums], axis=2)

    gathered = lax.cond(flags.reshape(()) > 0.0, general, lambda: gathered)
    mom_down, mom_up, new_down, new_up, low_down, low_up, loss, count, norm = update(
        gathered, adapters, down_momentum, up_momentum
    )
    return (
        loss.reshape(()),
        count.reshape(()),
        norm.reshape(()),
        jnp.swapaxes(mom_down, 1, 2),
        mom_up,
        jnp.swapaxes(new_down, 1, 2),
        new_up,
        jnp.swapaxes(low_down, 1, 2),
        low_up,
    )


def solution(mesh):
    fast = dict(mesh.shape) == {"dp": 8, "vocab": 4}
    placed = (
        P(("dp", "vocab")),
        P(("dp", "vocab")),
        P(("dp", "vocab")),
        P(("dp", "vocab"), None),
        P(("dp", "vocab"), None),
        P(None, ("dp", "vocab")),
        P(None, ("dp", "vocab")),
        P(None, ("dp", "vocab")),
        P(("dp", "vocab"), None),
        P(("dp", "vocab"), None),
        P(("dp", "vocab"), None),
        P(("dp", "vocab"), None),
        P(("dp", "vocab")),
        P(),
        P(),
        P(),
        P(),
    )
    return jax.shard_map(
        per_device if fast else per_device_general,
        mesh=mesh,
        in_specs=placed,
        out_specs=(
            P(),
            P(),
            P(),
            P(None, "vocab", None),
            P(None, None, "vocab"),
            P(None, "vocab", None),
            P(None, None, "vocab"),
            P(None, "vocab", None),
            P(None, None, "vocab"),
        ),
        check_vma=False,
    )
```

```python
from functools import partial

import jax
import jax.numpy as jnp
from jax import lax
from jax.experimental import pallas as pl
from jax.experimental.pallas import tpu as pltpu
from jax.sharding import PartitionSpec as P

HEAD_DIM = 64
V = 50304


highest_precision = lax.Precision.HIGHEST
ln_eps = 1e-05
adapter_scale = 8.0
smooth = 0.1
clip_level = 1.0
momentum = 0.5
learning_rate = 0.5
coef_a = 3.4445
coef_b = -4.775
coef_c = 2.0315
score_scale = 0.125
masked_value = -1e30


def merged(x, axis, join):
    gathered = jax.tree.map(
        lambda a, kind: lax.all_gather(a.astype(kind), axis),
        x,
        jax.tree.map(lambda a: jnp.bfloat16 if a.dtype == jnp.float32 else a.dtype, x),
    )

    def take(source):
        return jax.tree.map(
            lambda a, own: lax.dynamic_index_in_dim(a, source, 0, False).astype(own.dtype),
            gathered,
            x,
        )

    return lax.fori_loop(
        1, lax.axis_size(axis), lambda source, state: join(state, take(source)), take(0)
    )


def dot_without_transpose(left_side, right_side, setting=None):
    return jnp.dot(left_side, right_side, precision=setting, preferred_element_type=jnp.float32)


def dot_last_axis(left_side, right_side, setting=None):
    return lax.dot_general(
        left_side,
        right_side,
        (((1,), (1,)), ((), ())),
        precision=setting,
        preferred_element_type=jnp.float32,
    )


def dot_first(left_side, right_side, setting=None):
    return lax.dot_general(
        left_side,
        right_side,
        (((0,), (0,)), ((), ())),
        precision=setting,
        preferred_element_type=jnp.float32,
    )


def rounded_values(values):
    return lax.optimization_barrier(values.astype(jnp.bfloat16)).astype(jnp.float32)


def layer_norm(values, gain, offset):
    center = values - jnp.mean(values, axis=-1, keepdims=True)
    spread = jnp.mean(center * center, axis=-1, keepdims=True)
    return center * lax.rsqrt(spread + ln_eps) * gain + offset


def layout(seq_lengths, row_count):
    seq_ends = jnp.cumsum(seq_lengths)
    seq_starts = seq_ends - seq_lengths
    places = jnp.arange(row_count, dtype=jnp.int32)
    segment = jnp.sum((places[:, None] >= seq_ends[None, :]).astype(jnp.int32), axis=1)
    member = segment[:, None] == jnp.arange(seq_lengths.shape[0], dtype=jnp.int32)[None, :]
    positions_in = places - jnp.sum(jnp.where(member, seq_starts[None, :], 0), axis=1)
    allowed_mask = (segment[:, None] == segment[None, :]) & (places[None, :] <= places[:, None])
    return (positions_in, allowed_mask)


def owner_rows(token_ids, piece_rows, group, vocab_pos):
    piece_index = token_ids // piece_rows
    owner = piece_index % group
    local = piece_index // group * piece_rows + token_ids % piece_rows
    return jnp.where(owner == vocab_pos, local, -1)


def attention_scores(query, key_rows, allowed_mask):
    scores = (
        jnp.einsum("shd,thd->hst", query, key_rows, preferred_element_type=jnp.float32)
        * score_scale
    )
    return jnp.where(allowed_mask[None], scores, masked_value)


def layer_forward(residual_initial, frozen_weights, adapter_down, adapter_up, allowed_mask):
    query_key_value_weight, output_weight, up_weight, down_weight, gains, shifts, bias_stack = (
        frozen_weights
    )
    gains = gains.astype(jnp.float32)
    shifts = shifts.astype(jnp.float32)
    bias_stack = bias_stack.astype(jnp.float32)
    width_size = output_weight.shape[0]
    hidden_units = up_weight.shape[1]
    row_count = residual_initial.shape[0]
    heads = width_size // HEAD_DIM
    first_normed = layer_norm(residual_initial, gains[0], shifts[0]).astype(jnp.bfloat16)
    first_plain = first_normed.astype(jnp.float32)
    joined_rows = (
        dot_without_transpose(first_normed, query_key_value_weight) + bias_stack[: 3 * width_size]
    )
    adapt_in = []
    projected = []
    for which_index in range(3):
        inner_product = dot_without_transpose(
            first_plain, adapter_down[which_index], highest_precision
        )
        adapt_in.append(inner_product)
        branch_output = joined_rows[
            :, which_index * width_size : (which_index + 1) * width_size
        ] + adapter_scale * dot_without_transpose(
            inner_product, adapter_up[which_index], highest_precision
        )
        projected.append(branch_output.astype(jnp.bfloat16).reshape(row_count, heads, HEAD_DIM))
    query, key_rows, value_rows = projected
    scores = attention_scores(query, key_rows, allowed_mask)
    top = jnp.max(scores, axis=-1, keepdims=True)
    expo = jnp.exp(scores - top)
    summed = jnp.sum(expo, axis=-1, keepdims=True)
    log_total = top + jnp.log(summed)
    probs = (expo / summed).astype(jnp.bfloat16)
    mixed_state = jnp.einsum("hst,thd->shd", probs, value_rows, preferred_element_type=jnp.float32)
    mixed_state = mixed_state.reshape(row_count, width_size).astype(jnp.bfloat16)
    mixed_plain = mixed_state.astype(jnp.float32)
    adapter_output = dot_without_transpose(mixed_plain, adapter_down[3], highest_precision)
    attended_rows = (
        dot_without_transpose(mixed_state, output_weight)
        + bias_stack[3 * width_size : 4 * width_size]
        + adapter_scale * dot_without_transpose(adapter_output, adapter_up[3], highest_precision)
    )
    stream_one = residual_initial + attended_rows
    normed_two = layer_norm(stream_one, gains[1], shifts[1]).astype(jnp.bfloat16)
    before_gelu = (
        dot_without_transpose(normed_two, up_weight)
        + bias_stack[4 * width_size : 4 * width_size + hidden_units]
    )
    activation = jax.nn.gelu(before_gelu, approximate=True).astype(jnp.bfloat16)
    stream_two = (
        stream_one
        + dot_without_transpose(activation, down_weight)
        + bias_stack[4 * width_size + hidden_units :]
    )
    final_state = layer_norm(stream_two, gains[2], shifts[2]).astype(jnp.bfloat16)
    kept_rows = (
        first_plain,
        adapt_in,
        query,
        key_rows,
        value_rows,
        log_total,
        mixed_plain,
        adapter_output,
        stream_one,
        before_gelu,
        stream_two,
    )
    return (final_state, kept_rows)


def layer_backward(
    final_gradient, kept_rows, backward_weights, adapter_down, adapter_up, allowed_mask
):
    output_weight, up_weight, down_weight, gains = backward_weights
    gains = gains.astype(jnp.float32)
    (
        first_plain,
        adapt_in,
        query,
        key_rows,
        value_rows,
        log_total,
        mixed_plain,
        adapter_output,
        stream_one,
        before_gelu,
        stream_two,
    ) = kept_rows
    row_count = query.shape[0]
    width_size = query.shape[1] * HEAD_DIM
    _, pull_three = jax.vjp(lambda values: layer_norm(values, gains[2], 0.0), stream_two)
    grad_two = pull_three(final_gradient)[0]
    grad_act = dot_last_axis(grad_two.astype(jnp.bfloat16), down_weight)
    _, pull_gelu = jax.vjp(partial(jax.nn.gelu, approximate=True), before_gelu)
    grad_pre = pull_gelu(grad_act)[0].astype(jnp.bfloat16)
    _, pull_two = jax.vjp(lambda values: layer_norm(values, gains[1], 0.0), stream_one)
    first_gradient = grad_two + pull_two(dot_last_axis(grad_pre, up_weight))[0]
    attention_gradient = first_gradient.astype(jnp.bfloat16)
    attention_scaled = adapter_scale * rounded_values(first_gradient)
    up_grads = [None, None, None, None]
    down_grads = [None, None, None, None]
    up_grads[3] = dot_first(adapter_output, attention_scaled, highest_precision)
    backward_output = dot_last_axis(attention_scaled, adapter_up[3], highest_precision)
    down_grads[3] = dot_first(mixed_plain, backward_output, highest_precision)
    mixed_gradient = dot_last_axis(attention_gradient, output_weight) + dot_last_axis(
        backward_output, adapter_down[3], highest_precision
    )
    grad_heads = mixed_gradient.astype(jnp.bfloat16).reshape(query.shape)
    probs = jnp.exp(attention_scores(query, key_rows, allowed_mask) - log_total)
    grad_value = jnp.einsum(
        "hst,shd->thd", probs.astype(jnp.bfloat16), grad_heads, preferred_element_type=jnp.float32
    )
    grad_probs = jnp.einsum(
        "shd,thd->hst", grad_heads, value_rows, preferred_element_type=jnp.float32
    )
    grad_scores = probs * (grad_probs - jnp.sum(probs * grad_probs, axis=-1, keepdims=True))
    grad_scores = grad_scores.astype(jnp.bfloat16)
    grad_query = (
        jnp.einsum("hst,thd->shd", grad_scores, key_rows, preferred_element_type=jnp.float32)
        * score_scale
    )
    grad_key = (
        jnp.einsum("hst,shd->thd", grad_scores, query, preferred_element_type=jnp.float32)
        * score_scale
    )
    for which_index, branch_gradient in enumerate((grad_query, grad_key, grad_value)):
        scaled_values = adapter_scale * rounded_values(
            branch_gradient.reshape(row_count, width_size)
        )
        up_grads[which_index] = dot_first(adapt_in[which_index], scaled_values, highest_precision)
        backward_input = dot_last_axis(scaled_values, adapter_up[which_index], highest_precision)
        down_grads[which_index] = dot_first(first_plain, backward_input, highest_precision)
    return (jnp.stack(down_grads), jnp.stack(up_grads))


def orthogonalize(matrices, sum_grams):
    grams = sum_grams(
        jnp.einsum(
            "mrd,msd->mrs",
            matrices,
            matrices,
            precision=highest_precision,
            preferred_element_type=jnp.float32,
        )
    )
    sizes = jnp.sqrt(jnp.trace(grams, axis1=1, axis2=2))[:, None, None] + 1e-07
    state = matrices / sizes
    grams = grams / (sizes * sizes)
    for turn_index in range(5):
        if turn_index:
            grams = sum_grams(
                jnp.einsum(
                    "mrd,msd->mrs",
                    state,
                    state,
                    precision=highest_precision,
                    preferred_element_type=jnp.float32,
                )
            )
        poly = coef_b * grams + coef_c * jnp.einsum(
            "mrs,mst->mrt",
            grams,
            grams,
            precision=highest_precision,
            preferred_element_type=jnp.float32,
        )
        state = coef_a * state + jnp.einsum(
            "mrs,msd->mrd",
            poly,
            state,
            precision=highest_precision,
            preferred_element_type=jnp.float32,
        )
    return state


def gradients_general(
    ids,
    targets,
    counted_mask,
    lengths,
    table,
    position_table,
    layer_norm_gain,
    layer_norm_bias,
    query_key_value_weight,
    output_weight,
    up_weight,
    down_weight,
    biases,
    adapter_down,
    adapter_up,
):
    gathered = (
        lax.all_gather(query_key_value_weight, ("dp", "vocab"), axis=0, tiled=True),
        lax.all_gather(output_weight, ("dp", "vocab"), axis=0, tiled=True),
        lax.all_gather(up_weight, ("dp", "vocab"), axis=0, tiled=True),
        lax.all_gather(down_weight, ("dp", "vocab"), axis=0, tiled=True),
        lax.all_gather(layer_norm_gain, ("dp", "vocab"), axis=1, tiled=True),
        lax.all_gather(layer_norm_bias, ("dp", "vocab"), axis=1, tiled=True),
        lax.all_gather(biases, ("dp", "vocab"), axis=0, tiled=True),
        lax.all_gather(position_table, ("dp", "vocab"), axis=1, tiled=True),
    )
    w_qkv_all, w_out_all, w_up_all, w_down_all, gains_all, shifts_all, bias_stack, positions_all = (
        gathered
    )
    row_count = ids.shape[0]
    width_size = w_out_all.shape[0]
    group = lax.axis_size("vocab")
    vocab_pos = lax.axis_index("vocab")
    piece_rows = table.shape[0]
    ids_all, target_all, mask_all = (
        lax.all_gather(ids, "vocab", axis=0, tiled=True),
        lax.all_gather(targets, "vocab", axis=0, tiled=True),
        lax.all_gather(counted_mask, "vocab", axis=0, tiled=True),
    )
    table_full = lax.all_gather(table, "dp", axis=0, tiled=True)
    vocab_rows = table_full.shape[0]
    local_ids = owner_rows(ids_all, piece_rows, group, vocab_pos)
    inside = local_ids >= 0
    picked_rows = table_full[jnp.clip(local_ids, 0, vocab_rows - 1)]
    picked_rows = jnp.where(inside[:, None], picked_rows, jnp.zeros_like(picked_rows))
    embedded = lax.psum_scatter(
        picked_rows.astype(jnp.float32).astype(jnp.bfloat16),
        "vocab",
        scatter_dimension=0,
        tiled=True,
    ).astype(jnp.float32)
    positions_in, allowed_mask = layout(lengths[0], row_count)
    residual_initial = embedded + positions_all[positions_in].astype(jnp.float32)
    frozen_weights = (w_qkv_all, w_out_all, w_up_all, w_down_all, gains_all, shifts_all, bias_stack)
    final_state, kept_rows = layer_forward(
        residual_initial, frozen_weights, adapter_down, adapter_up, allowed_mask
    )
    final_all = lax.all_gather(final_state, "vocab", axis=0, tiled=True)
    total_rows = final_all.shape[0]
    block = 512
    count_blocks = total_rows // block
    final_blocks = final_all.reshape(count_blocks, block, width_size)
    local_targets = owner_rows(target_all, piece_rows, group, vocab_pos).reshape(
        count_blocks, block
    )
    columns = jnp.arange(vocab_rows, dtype=jnp.int32)

    def head_stats(item):
        piece, local = item
        logits = dot_last_axis(piece, table_full)
        top = jnp.max(logits, axis=1)
        expsum = jnp.sum(jnp.exp(logits - top[:, None]), axis=1)
        target_logit = jnp.sum(jnp.where(columns[None, :] == local[:, None], logits, 0.0), axis=1)
        return (top, expsum, target_logit, jnp.sum(logits, axis=1))

    stats = lax.map(head_stats, (final_blocks, local_targets))
    stats = tuple((entry.reshape(total_rows) for entry in stats))

    def combine(first_part, second_part):
        larger = jnp.maximum(first_part[0], second_part[0])
        merged_sum = first_part[1] * jnp.exp(first_part[0] - larger) + second_part[1] * jnp.exp(
            second_part[0] - larger
        )
        return (larger, merged_sum, first_part[2] + second_part[2], first_part[3] + second_part[3])

    top, expsum, target_logit, logit_sum = merged(stats, "vocab", combine)
    log_total = top + jnp.log(expsum)
    row_loss = log_total - (1.0 - smooth) * target_logit - smooth * logit_sum / V
    mask_float = mask_all.astype(jnp.float32)
    own_start = vocab_pos * row_count
    loss_own = jnp.sum(lax.dynamic_slice_in_dim(mask_float * row_loss, own_start, row_count))
    count_own = jnp.sum(counted_mask.astype(jnp.float32))

    def head_grad(item):
        piece, local, lse_block, weight = item
        logits = dot_last_axis(piece, table_full)
        probs = jnp.exp(logits - lse_block[:, None])
        onehot = (columns[None, :] == local[:, None]).astype(jnp.float32)
        grad_logits = weight[:, None] * (probs - (1.0 - smooth) * onehot - smooth / V)
        return dot_without_transpose(grad_logits.astype(jnp.bfloat16), table_full)

    partial_rows = lax.map(
        head_grad,
        (
            final_blocks,
            local_targets,
            log_total.reshape(count_blocks, block),
            mask_float.reshape(count_blocks, block),
        ),
    )
    final_gradient = lax.psum_scatter(
        partial_rows.reshape(total_rows, width_size).astype(jnp.bfloat16),
        "vocab",
        scatter_dimension=0,
        tiled=True,
    ).astype(jnp.float32)
    backward_weights = (
        lax.all_gather(output_weight, ("dp", "vocab"), axis=0, tiled=True),
        lax.all_gather(up_weight, ("dp", "vocab"), axis=0, tiled=True),
        lax.all_gather(down_weight, ("dp", "vocab"), axis=0, tiled=True),
        lax.all_gather(layer_norm_gain, ("dp", "vocab"), axis=1, tiled=True),
    )
    down_gradient, up_gradient = layer_backward(
        final_gradient, kept_rows, backward_weights, adapter_down, adapter_up, allowed_mask
    )
    return (down_gradient, up_gradient, loss_own, count_own)


def per_device_general(
    ids,
    targets,
    counted_mask,
    lengths,
    table,
    position_table,
    layer_norm_gain,
    layer_norm_bias,
    query_key_value_weight,
    output_weight,
    up_weight,
    down_weight,
    biases,
    adapter_down,
    adapter_up,
    down_momentum,
    up_momentum,
):
    group = lax.axis_size("vocab")
    vocab_pos = lax.axis_index("vocab")
    down_gradient, up_gradient, loss_own, count_own = gradients_general(
        ids,
        targets,
        counted_mask,
        lengths,
        table,
        position_table,
        layer_norm_gain,
        layer_norm_bias,
        query_key_value_weight,
        output_weight,
        up_weight,
        down_weight,
        biases,
        adapter_down,
        adapter_up,
    )
    down_gradient, up_gradient, smoothed_loss_sum, loss_count = lax.psum(
        (down_gradient, up_gradient, loss_own, count_own), ("dp", "vocab")
    )
    grad_norm = jnp.sqrt(
        jnp.sum(down_gradient * down_gradient) + jnp.sum(up_gradient * up_gradient)
    )
    factor = jnp.minimum(1.0, clip_level / (grad_norm + 1e-06))
    new_mom_down = momentum * down_momentum + factor * down_gradient
    new_mom_up = momentum * up_momentum + factor * up_gradient
    stacked = jnp.concatenate([jnp.swapaxes(new_mom_down, 1, 2), new_mom_up], axis=0)
    share_fraction = stacked.shape[2] // group
    begin_index = vocab_pos * share_fraction
    orthogonal_update = lax.dynamic_slice_in_dim(
        orthogonalize(stacked, lambda grams: grams), begin_index, share_fraction, 2
    )
    mom_down_part = lax.dynamic_slice_in_dim(new_mom_down, begin_index, share_fraction, 1)
    mom_up_part = lax.dynamic_slice_in_dim(new_mom_up, begin_index, share_fraction, 2)
    down_fresh = lax.dynamic_slice_in_dim(
        adapter_down, begin_index, share_fraction, 1
    ) - learning_rate * jnp.swapaxes(orthogonal_update[:4], 1, 2)
    up_fresh = (
        lax.dynamic_slice_in_dim(adapter_up, begin_index, share_fraction, 2)
        - learning_rate * orthogonal_update[4:]
    )
    return (
        smoothed_loss_sum,
        loss_count,
        grad_norm,
        mom_down_part,
        mom_up_part,
        down_fresh,
        up_fresh,
        down_fresh.astype(jnp.bfloat16),
        up_fresh.astype(jnp.bfloat16),
    )


MESH = pl.DeviceIdType.MESH


def dot_nt(left_side, right_side, setting=None):
    return dot_last_axis(left_side, right_side, setting)


def position():
    dp, z = lax.axis_index("dp"), lax.axis_index("vocab")
    y, x, core = dp // 4, dp // 2 % 2, dp % 2

    def place(y_at, x_at, core_at):
        return y_at * 4 + x_at * 2 + core_at

    along = (z, z // 2 * 2 + 1 - z % 2, (z + 2) % 4, (1 - z // 2) * 2 + 1 - z % 2)
    return dp, z, y, x, core, place, along


def inner(z):
    return (z + 1) // 2 % 2


def mirror(z, other):
    return (z // 2 + other // 2) % 2 * 2 + (z + other) % 2


def nearness(z, other):
    k = mirror(z, other)
    return k + inner(z) * (k // 2) * (5 - 2 * k)


def by_nearness(z):
    far = z // 2 * 3
    near = 2 - z // 2
    return (z, z // 2 * 2 + 1 - z % 2, near, 3 - far)


def meet_all(devices, group):
    me = lax.axis_index("dp") * group + lax.axis_index("vocab")
    barrier = pltpu.get_barrier_semaphore()

    def signal(step, state):
        other = lax.rem(me + step, devices)
        pl.semaphore_signal(
            barrier, inc=1, device_id=(other // group, other % group), device_id_type=MESH
        )
        return state

    lax.fori_loop(1, devices, signal, 0)
    pl.semaphore_wait(barrier, devices - 1)
    return me


def to_all(source_of, target, send_sems, recv_sems, devices, group, me):
    def copy(step):
        other = lax.rem(me + step, devices)
        return pltpu.make_async_remote_copy(
            source_of(other),
            target.at[me],
            send_sems.at[step],
            recv_sems.at[step],
            device_id=(other // group, other % group),
            device_id_type=MESH,
        )

    def start():
        def one(step, state):
            copy(step).start()
            return state

        lax.fori_loop(1, devices, one, 0)

    def arrive():
        def one(step, state):
            source = lax.rem(me + devices - step, devices)
            pltpu.make_async_remote_copy(
                target.at[source],
                target.at[source],
                send_sems.at[step],
                recv_sems.at[step],
                device_id=(source // group, source % group),
                device_id_type=MESH,
            ).wait_recv()
            return state

        lax.fori_loop(1, devices, one, 0)

    def sent():
        def one(step, state):
            copy(step).wait_send()
            return state

        lax.fori_loop(1, devices, one, 0)

    return start, arrive, sent


ARRIVE, TAIL, TILE, BACK, MIDDLE, COLUMN = range(6)
ORDER = (
    (ARRIVE, 0, 1),
    (ARRIVE, 0, 2),
    (ARRIVE, 1, 0),
    (ARRIVE, 2, 0),
    (TILE, 1, 0),
    (TILE, 0, 2),
    (ARRIVE, 0, 3),
    (ARRIVE, 2, 2),
    (TAIL, 2, 1),
    (ARRIVE, 1, 2),
    (TAIL, 1, 1),
    (ARRIVE, 2, 1),
    (ARRIVE, 1, 1),
    (TILE, 0, 1),
    (TILE, 2, 1),
    (TAIL, 2, 2),
    (TAIL, 1, 2),
    (BACK, 2, 1),
    (ARRIVE, 3, 0),
    (BACK, 1, 0),
    (TILE, 1, 1),
    (TILE, 1, 2),
    (ARRIVE, 2, 3),
    (TAIL, 3, 2),
    (ARRIVE, 3, 2),
    (TILE, 2, 2),
    (ARRIVE, 3, 1),
    (ARRIVE, 1, 3),
    (TILE, 3, 2),
    (BACK, 3, 2),
    (BACK, 2, 2),
    (TAIL, 3, 1),
    (BACK, 1, 2),
    (TILE, 0, 3),
    (ARRIVE, 3, 3),
    (TAIL, 3, 3),
    (TAIL, 2, 3),
    (MIDDLE, 0, 2),
    (MIDDLE, 1, 2),
    (TAIL, 1, 3),
    (TILE, 3, 1),
    (BACK, 3, 1),
    (TILE, 3, 3),
    (BACK, 1, 1),
    (COLUMN, 1, 2),
    (COLUMN, 0, 2),
    (BACK, 3, 3),
    (TILE, 2, 3),
    (MIDDLE, 0, 1),
    (BACK, 2, 3),
    (TILE, 1, 3),
    (MIDDLE, 1, 3),
    (TILE, 3, 0),
    (BACK, 3, 0),
    (COLUMN, 0, 1),
    (BACK, 1, 3),
    (TILE, 2, 0),
    (COLUMN, 1, 3),
    (MIDDLE, 0, 3),
    (MIDDLE, 1, 1),
    (TILE, 0, 0),
    (MIDDLE, 0, 0),
    (MIDDLE, 1, 0),
    (COLUMN, 0, 3),
    (COLUMN, 1, 1),
    (BACK, 2, 0),
    (COLUMN, 0, 0),
    (COLUMN, 1, 0),
)


def of_four(values, at):
    low, high = at % 2, at // 2
    return (1 - high) * ((1 - low) * values[0] + low * values[1]) + high * (
        (1 - low) * values[2] + low * values[3]
    )


def live_rows(tile):
    return tile * 7 // 8


def counted_first(mask_row):
    size = mask_row.shape[1]
    square = (size, size)
    down = lax.broadcasted_iota(jnp.int32, square, 0)
    across = lax.broadcasted_iota(jnp.int32, square, 1)
    mask_col = col_of(mask_row)
    ahead = jnp.sum(jnp.where(down < across, mask_col, 0.0), axis=0, keepdims=True)
    count = jnp.sum(mask_row, axis=1, keepdims=True)
    places = jnp.where(mask_row > 0.0, ahead, count + across[:1].astype(jnp.float32) - ahead)
    return (down.astype(jnp.float32) == places).astype(jnp.float32).astype(jnp.bfloat16)


def head_kernel(table_rows, chunks, own, tab_a, turn_a, tab_b, turn_b, mean_out, lse_out, *refs):
    (
        tab,
        turn,
        score_a,
        score_b,
        total,
        hidden,
        part,
        part_lse,
        got,
        got_lse,
        load_sems,
        send_sems,
        recv_sems,
        back_send,
        back_recv,
    ) = refs
    dp, z, y, x, core, place, _ = position()
    along = by_nearness(z)
    pad_rows = tab_a.shape[0]
    width, tile = own.shape[1], own.shape[0]
    tiles = [event[1:] for event in ORDER if event[0] == TILE]
    slot = {at: index for index, at in enumerate(tiles)}
    dev_x, dev_y = (place(y, 1 - x, core), z), (place(1 - y, x, core), z)
    dev_z = [(dp, along[k]) for k in range(4)]
    peers = [dev_x, dev_y] + dev_z[1:]
    loads = []
    for at, (source, target) in enumerate(
        (
            (own, hidden.at[slot[0, 0]]),
            (tab_a, tab.at[pl.ds(0, pad_rows)]),
            (tab_b, tab.at[pl.ds(pad_rows, pad_rows)]),
            (turn_a, turn.at[:, pl.ds(0, pad_rows)]),
            (turn_b, turn.at[:, pl.ds(pad_rows, pad_rows)]),
        )
    ):
        copy = pltpu.make_async_copy(source, target, load_sems.at[at])
        copy.start()
        loads.append(copy)
    for q, k in tiles:
        if (q, k) != (0, 0):
            hidden[slot[q, k], live_rows(tile) :] = jnp.zeros(
                (tile - live_rows(tile), width), jnp.bfloat16
            )
    barrier = pltpu.get_barrier_semaphore()
    for peer in peers:
        pl.semaphore_signal(barrier, inc=1, device_id=peer, device_id_type=MESH)
    pl.semaphore_wait(barrier, len(peers))
    loads[0].wait()

    sent = []
    live = live_rows(tile)
    body = live - tile * 2 // 16
    cut = body // 32 * 16 + body % 32

    def span(k, half=None):
        last, middle = (body, cut) if k else (live, live // 2)
        begin, end = ((0, last), (0, middle), (middle, last))[0 if half is None else 1 + half]
        return pl.ds(begin, end - begin)

    def give(source, target, peer, half=None):
        rows = span(target[1], half)
        copy = pltpu.make_async_remote_copy(
            hidden.at[slot[source], rows],
            hidden.at[slot[target], rows],
            send_sems.at[len(sent)],
            recv_sems.at[slot[target] + (16 if half == 1 else 0)],
            device_id=peer,
            device_id_type=MESH,
        )
        sent.append(copy)
        return copy

    def give_along(q, k, upward):
        there = z + 1 if upward else z - 1
        target = of_four([slot[q, at] for at in range(4)], nearness(there, along[k]))
        rows = pl.ds(body, live - body) if q else pl.ds(0, live)
        return pltpu.make_async_remote_copy(
            hidden.at[slot[q, k], rows],
            hidden.at[target, rows],
            send_sems.at[24 + 8 * q + k + 4 * (not upward and k == 0)],
            recv_sems.at[target + (32 if q else 0)],
            device_id=(dp, there),
            device_id_type=MESH,
        )

    def pass_along(q, k, act):
        @pl.when((along[k] <= z) & (z < 3))
        def _():
            act(give_along(q, k, True))

        @pl.when((along[k] >= z) & (z > 0))
        def _():
            act(give_along(q, k, False))

    def start_all(copies):
        for copy in copies:
            copy.start()

    forwards = {}
    for k in range(4):
        forwards[0, k] = [give((0, k), (1, k), dev_x), give((0, k), (2, k), dev_y)]
        forwards[1, k] = [give((1, k), (3, k), dev_y, 1)]
        forwards[2, k] = [give((2, k), (3, k), dev_x, 0)]
        forwards[3, k] = []
    pass_along(0, 0, lambda copy: copy.start())
    start_all(forwards[0, 0])

    def wait_rows(q, k, rows, at):
        there = hidden.at[slot[q, k], rows]
        pltpu.make_async_remote_copy(
            there,
            there,
            send_sems.at[0],
            recv_sems.at[slot[q, k] + at],
            device_id=dev_x,
            device_id_type=MESH,
        ).wait_recv()

    def arrive(q, k):
        if q == 3:
            wait_rows(q, k, span(k, 0), 0)
            wait_rows(q, k, span(k, 1), 16)
        else:
            wait_rows(q, k, span(k) if q else pl.ds(0, live), 0)
        if q == 0 or k == 0:
            pass_along(q, k, lambda copy: copy.start())
        start_all(forwards[q, k])

    def tail_comes(q, k):
        wait_rows(q, k, pl.ds(body, live - body), 32)
        pass_along(q, k, lambda copy: copy.start())

    back_sent = []

    def half_rows(half):
        return pl.ds(half * (width // 2), width // 2)

    def back_copies(number, q, k, half, landing, peer):
        if q == 0:
            landing = landing + 2 * mirror(z, along[k])
        return [
            pltpu.make_async_remote_copy(
                source,
                target,
                back_send.at[kind, number],
                back_recv.at[kind, landing],
                device_id=peer,
                device_id_type=MESH,
            )
            for kind, (source, target) in enumerate(
                (
                    (part.at[slot[q, k], half_rows(half)], got.at[landing]),
                    (part_lse.at[2 * slot[q, k] + half], got_lse.at[landing]),
                )
            )
        ]

    def back(*what):
        start_all(back_copies(len(back_sent), *what))
        back_sent.append(what)

    def back_wait(landing):
        for kind, target in enumerate((got, got_lse)):
            pltpu.make_async_remote_copy(
                target.at[landing],
                target.at[landing],
                back_send.at[kind, 0],
                back_recv.at[kind, landing],
                device_id=dev_x,
                device_id_type=MESH,
            ).wait_recv()

    def merge(q, k, half, landings):
        at = slot[q, k]
        for landing in landings:
            back_wait(landing)
        levels = [part_lse[2 * at + half]] + [got_lse[landing] for landing in landings]
        top = levels[0]
        for level in levels[1:]:
            top = jnp.maximum(top, level)
        shares = [jnp.exp(level - top) for level in levels]
        whole = sum(shares[1:], shares[0])
        shares = [share / whole for share in shares]
        part_lse[2 * at + half] = top + jnp.log(whole)
        begin = half * (width // 2)

        def rows(step, state):
            here = pl.ds(pl.multiple_of(step * 128, 128), 128)
            mine = pl.ds(pl.multiple_of(begin + step * 128, 128), 128)
            mixed = part[at, mine].astype(jnp.float32) * shares[0]
            for landing, share in zip(landings, shares[1:], strict=True):
                mixed += got[landing, here].astype(jnp.float32) * share
            part[at, mine] = mixed.astype(jnp.bfloat16)
            return state

        lax.fori_loop(0, width // 256, rows, 0)

    def go_back(q, k):
        if q == 3:
            back(3, k, 0, 16 + 2 * k, dev_x)
            back(3, k, 1, 17 + 2 * k, dev_y)
        elif q == 1:
            back(1, k, 0, 2 * k, dev_x)
        else:
            back(2, k, 1, 9 + 2 * k, dev_y)

    def merge_middle(half, k):
        q = 1 if half else 2
        merge(q, k, half, [16 + 2 * k + half])
        if half:
            back(1, k, 1, 1 + 2 * k, dev_x)
        else:
            back(2, k, 0, 8 + 2 * k, dev_y)

    def merge_column(half, k):
        merge(0, k, half, [2 * k + half, 8 + 2 * k + half])
        if k:
            back(0, k, half, 22 + half, dev_z[k])

    acts = {ARRIVE: arrive, TAIL: tail_comes, BACK: go_back, MIDDLE: merge_middle, COLUMN: merge_column}
    groups = [[]]
    for event in ORDER:
        if event[0] == TILE:
            groups.append([])
        else:
            groups[-1].append(event)

    def work(group):
        for event in group:
            acts[event[0]](*event[1:])

    def events_before(t, parity):
        for at in range(parity, 16, 2):
            if groups[at]:

                @pl.when(t == at)
                def _(at=at):
                    work(groups[at])

    for copy in loads[1:]:
        copy.wait()
    starts = [sum(chunks[:at]) for at in range(len(chunks))]
    low = jnp.full((8, tile), -jnp.inf, jnp.float32)

    def scores_of(rows, at, score, top):
        begin, size = starts[at], chunks[at]
        values = dot_nt(tab[begin : begin + size], rows)
        score[begin : begin + size] = values
        cuts = [(begin, begin + size, False)]
        for half in range(2):
            edge = half * pad_rows + table_rows // 8 * 8
            stop = (half + 1) * pad_rows
            if begin <= edge < begin + size:
                cuts = [(begin, edge, False), (edge, min(stop, begin + size), True)]
                if stop < begin + size:
                    cuts.append((stop, begin + size, False))
        for first_row, last, masked in cuts:
            if first_row == last:
                continue
            cut = values[first_row - begin : last - begin]
            if masked:
                row = lax.broadcasted_iota(jnp.int32, cut.shape, 0)
                cut = jnp.where(row < table_rows % 8, cut, masked_value)
                score[first_row:last] = cut
            top = jnp.maximum(top, jnp.max(cut.reshape(-1, 8, tile), axis=0))
        return top

    def half_step(t, parity, score, score_next, top):
        events_before(t, parity)
        rows = hidden[jnp.minimum(t + 1, 15)]
        peak = jnp.max(top, axis=0, keepdims=True)
        summed = jnp.zeros((8, tile), jnp.float32)
        top_next = low
        for at in range(len(chunks)):
            begin, size = starts[at], chunks[at]
            expo = jnp.exp(score[begin : begin + size] - peak)
            summed += jnp.sum(expo.reshape(-1, 8, tile), axis=0)
            top_next = scores_of(rows, at, score_next, top_next)
            product = dot_without_transpose(
                turn[:, begin : begin + size], expo.astype(jnp.bfloat16)
            )
            if at == 0:
                total[...] = product
            else:
                total[...] += product
        denominator = jnp.sum(summed, axis=0, keepdims=True)
        part[t] = (total[...] * (1.0 / denominator)).astype(jnp.bfloat16)
        level = peak + jnp.log(denominator)
        part_lse[2 * t] = level
        part_lse[2 * t + 1] = level
        return top_next

    if tiles[0] != (0, 0):
        until = 1 + max(at for at, event in enumerate(groups[0]) if event[1:] == tiles[0])
        work(groups[0][:until])
        del groups[0][:until]
    top = low
    for at in range(len(chunks)):
        top = scores_of(hidden[0], at, score_a, top)

    def two_steps(step, top):
        top = half_step(2 * step, 0, score_a, score_b, top)
        return half_step(2 * step + 1, 1, score_b, score_a, top)

    lax.fori_loop(0, 8, two_steps, top)
    work(groups[16])
    home = slot[0, 0]
    merge(0, 0, 0, [24, 26, 28])
    merge(0, 0, 1, [25, 27, 29])
    mean_out[...] = part[home]
    lse_out[...] = part_lse[2 * home]
    for q in range(4):
        for k in range(4):
            pass_along(q, k, lambda copy: copy.wait_send())
    for copy in sent:
        copy.wait_send()
    for number, what in enumerate(back_sent):
        for copy in back_copies(number, *what):
            copy.wait_send()


def head(final_state, table_rows, tables):
    tile, width = final_state.shape
    pad_rows = tables[0].shape[0]
    both = 2 * pad_rows
    chunks = [both // 256 // 4 * 256] * 4
    chunks[0] += both - sum(chunks)
    anywhere, vmem = pl.BlockSpec(memory_space=pl.ANY), pl.BlockSpec(memory_space=pltpu.VMEM)
    dma = pltpu.SemaphoreType.DMA
    return pl.pallas_call(
        partial(head_kernel, table_rows, chunks),
        out_shape=[
            jax.ShapeDtypeStruct((width, tile), jnp.bfloat16),
            jax.ShapeDtypeStruct((1, tile), jnp.float32),
        ],
        in_specs=[anywhere] * 5,
        out_specs=[vmem] * 2,
        scratch_shapes=[
            pltpu.VMEM((both, width), jnp.bfloat16),
            pltpu.VMEM((width, both), jnp.bfloat16),
            pltpu.VMEM((both, tile), jnp.float32),
            pltpu.VMEM((both, tile), jnp.float32),
            pltpu.VMEM((width, tile), jnp.float32),
            pltpu.VMEM((16, tile, width), jnp.bfloat16),
            pltpu.VMEM((16, width, tile), jnp.bfloat16),
            pltpu.VMEM((32, 1, tile), jnp.float32),
            pltpu.VMEM((30, width // 2, tile), jnp.bfloat16),
            pltpu.VMEM((30, 1, tile), jnp.float32),
            dma((5,)),
            dma((56,)),
            dma((48,)),
            dma((2, 30)),
            dma((2, 30)),
        ],
        name="head",
        compiler_params=pltpu.CompilerParams(
            collective_id=2, has_side_effects=True, vmem_limit_bytes=62 * 2**20
        ),
    )(final_state, *tables)


def sum_kernel(gathered, whole, numbers, other_half, mine, parts, piece, core_sems, sems, back_sems):
    dp, z, y, x, core, place, _ = position()
    half, plane = parts.shape[0], (y * 2 + x) * 4 + z
    width = whole.shape[2]
    partner = (place(y, x, 1 - core), z)

    def there(step, back=False):
        other = lax.rem(plane + (half - step if back else step), half)
        column = other // 4
        return other, (place(column // 2, column % 2, core), other % 4)

    barrier = pltpu.get_barrier_semaphore()

    def greet(step, state):
        pl.semaphore_signal(barrier, inc=1, device_id=there(step)[1], device_id_type=MESH)
        return state

    lax.fori_loop(1, half, greet, 0)
    pl.semaphore_signal(barrier, inc=1, device_id=partner, device_id_type=MESH)
    pl.semaphore_wait(barrier, half)

    def to_core(source, target, at):
        return pltpu.make_async_remote_copy(
            source,
            target,
            core_sems.at[2 * at],
            core_sems.at[2 * at + 1],
            device_id=partner,
            device_id_type=MESH,
        )

    first_swap = to_core(gathered.at[pl.ds((1 - core) * half, half)], other_half, 0)
    first_swap.start()
    first_swap.wait_recv()
    mine[...] = gathered[pl.ds(core * half, half)] + other_half[...]
    parts[pl.ds(plane, 1)] = mine[pl.ds(plane, 1)]

    def exchange(copy, target, used):
        def start(step, state):
            copy(step).start()
            return state

        def arrive(step, state):
            source, peer = there(step, True)
            pltpu.make_async_remote_copy(
                target(source),
                target(source),
                used.at[0, step],
                used.at[1, step],
                device_id=peer,
                device_id_type=MESH,
            ).wait_recv()
            return state

        lax.fori_loop(1, half, start, 0)
        lax.fori_loop(1, half, arrive, 0)

    def part_copy(step):
        other, peer = there(step)
        return pltpu.make_async_remote_copy(
            mine.at[other],
            parts.at[plane],
            sems.at[0, step],
            sems.at[1, step],
            device_id=peer,
            device_id_type=MESH,
        )

    exchange(part_copy, lambda source: parts.at[source], sems)
    summed = parts[0]
    for source in range(1, half):
        summed += parts[source]
    row = core * half + plane
    piece[...] = summed[:, :width]
    whole[pl.ds(row, 1)] = summed[None, :, :width]
    numbers[...] = summed[:, width:]

    def back_copy(step):
        return pltpu.make_async_remote_copy(
            piece,
            whole.at[row],
            back_sems.at[0, step],
            back_sems.at[1, step],
            device_id=there(step)[1],
            device_id_type=MESH,
        )

    exchange(back_copy, lambda source: whole.at[core * half + source], back_sems)
    rows = whole.at[pl.ds(core * half, half)]
    second_swap = to_core(rows, rows, 1)
    second_swap.start()
    to_core(rows, whole.at[pl.ds((1 - core) * half, half)], 1).wait_recv()
    first_swap.wait_send()
    second_swap.wait_send()

    def sent(step, state):
        part_copy(step).wait_send()
        back_copy(step).wait_send()
        return state

    lax.fori_loop(1, half, sent, 0)


def update_kernel(whole, numbers, adapter_rows, down_momentum, up_momentum, *refs):
    outs, (stage,) = refs[:9], refs[9:]
    mom_down, mom_up, new_down, new_up, low_down, low_up, loss_out, count_out, norm_out = outs
    z = lax.axis_index("vocab")
    weights = adapter_rows[...]
    devices, width = weights.shape
    gradient = whole[...].reshape(devices, width)
    squares = jnp.sum(jnp.sum(gradient * gradient, axis=0, keepdims=True), axis=1, keepdims=True)
    norm = jnp.sqrt(squares)
    factor = jnp.minimum(1.0, clip_level / (norm + 1e-06))
    state = momentum * stack_rows(down_momentum, up_momentum) + factor * gradient
    adapters, rank, share = mom_up.shape
    columns = pl.ds(pl.multiple_of(z * share, share), share)

    def give(values, *targets):
        stage[...] = values
        mine = stage[:, columns]
        for j in range(2 * adapters):
            for pair in targets:
                out = pair[j // adapters]
                out[j % adapters] = mine[j * rank : (j + 1) * rank].astype(out.dtype)

    give(state, (mom_down, mom_up))
    square = (devices, devices)
    row = lax.broadcasted_iota(jnp.int32, square, 0)
    column = lax.broadcasted_iota(jnp.int32, square, 1)
    blocks = row // rank == column // rank

    def gram_of(matrix):
        return jnp.where(blocks, dot_nt(matrix, matrix, highest_precision), 0.0)

    grams = gram_of(state)
    diagonal = jnp.sum(jnp.where(row == column, grams, 0.0), axis=0, keepdims=True)
    traces = jnp.sum(jnp.where(blocks, diagonal, 0.0), axis=1, keepdims=True)
    sizes = jnp.sqrt(traces) + 1e-07
    state = state / sizes
    grams = grams / (sizes * sizes)
    for turn_index in range(5):
        if turn_index:
            grams = gram_of(state)
        poly = coef_b * grams + coef_c * dot_without_transpose(grams, grams, highest_precision)
        state = coef_a * state + dot_without_transpose(poly, state, highest_precision)
    give(weights - learning_rate * state, (new_down, new_up), (low_down, low_up))
    loss_out[...] = numbers[:, 0:1]
    count_out[...] = numbers[:, 1:2]
    norm_out[...] = norm


def halves_of(values):
    high = values.astype(jnp.bfloat16)
    return high, (values - high.astype(jnp.float32)).astype(jnp.bfloat16)


def stacked_halves(values):
    return jnp.concatenate(halves_of(values), axis=0)


def added_halves(values):
    rows = values.shape[0] // 2
    return values[:rows] + values[rows:]


def dot_tn(left_side, right_side):
    return dot_first(left_side, right_side)


def normal(values):
    center = values - jnp.mean(values, axis=-1, keepdims=True)
    spread = lax.rsqrt(jnp.mean(center * center, axis=-1, keepdims=True) + ln_eps)
    return center * spread, spread


def normal_back(values, gain, gradient):
    unit, spread = normal(values)
    pulled = gradient * gain
    along = jnp.mean(pulled * unit, axis=-1, keepdims=True)
    return spread * (pulled - jnp.mean(pulled, axis=-1, keepdims=True) - unit * along)


def sequence_places(lengths, rows):
    col = lax.broadcasted_iota(jnp.int32, (rows, 1), 0)
    row = lax.broadcasted_iota(jnp.int32, (1, rows), 1)
    segment_col, segment_row = jnp.zeros_like(col), jnp.zeros_like(row)
    start_col = jnp.zeros_like(col)
    end = 0
    for at in range(lengths.shape[1]):
        length = lengths[0, at]
        end = end + length
        segment_col += (col >= end).astype(jnp.int32)
        segment_row += (row >= end).astype(jnp.int32)
        start_col += jnp.where(col >= end, length, 0)
    allowed = (segment_col == segment_row) & (row <= col)
    return col - start_col, allowed


def pairs_of(width):
    return width // (2 * HEAD_DIM)


def pair_at(pair):
    return pl.ds(pl.multiple_of(pair * 2 * HEAD_DIM, 2 * HEAD_DIM), 2 * HEAD_DIM)


def head_lanes(rows):
    return lax.broadcasted_iota(jnp.int32, (rows, 2 * HEAD_DIM), 1) < HEAD_DIM


def first_part(embedded, positions, lengths, gains, shifts, x0, h1):
    rows = x0.shape[0]
    place_col, allowed = sequence_places(lengths, rows)
    spots = lax.broadcasted_iota(jnp.int32, (rows, positions.shape[0]), 1)
    hot = (place_col == spots).astype(jnp.float32).astype(jnp.bfloat16)
    x0[...] = embedded[...] + dot_without_transpose(hot, positions[...])
    unit, _ = normal(x0[...])
    h1[...] = (unit * gains[0:1] + shifts[0:1]).astype(jnp.bfloat16)
    return allowed


def adapter_in(adapters, inputs):
    return added_halves(dot_nt(stacked_halves(adapters), inputs))


def adapter_out(inner, outer):
    high, low = halves_of(inner)
    top, rest = halves_of(outer)
    return adapter_scale * dot_tn(
        jnp.concatenate([high, high, low], axis=0), jnp.concatenate([top, rest, top], axis=0)
    )


def ranks(which, shape):
    return lax.broadcasted_iota(jnp.int32, shape, 0) // 4 == which


def project_part(h1, weight, bias, adapters, inner, joined):
    width = h1.shape[1]
    step = 512
    half = adapters.shape[0] // 2
    inner[...] = adapter_in(adapters[:half], h1[...])
    for which in range(3):

        def columns(at, state):
            here = pl.ds(pl.multiple_of(at * step, step), step)
            there = pl.ds(pl.multiple_of(which * width + at * step, step), step)
            outer = jnp.where(ranks(which, (half, step)), adapters[half:, here], 0.0)
            joined[:, there] = (
                dot_without_transpose(h1[...], weight[:, there])
                + bias[:, there]
                + adapter_out(inner[...], outer)
            ).astype(jnp.bfloat16)
            return state

        lax.fori_loop(0, width // step, columns, 0)


def attend_part(joined, allowed, probs, mixed):
    rows, width = mixed.shape
    lanes = head_lanes(rows)

    def pair_step(pair, state):
        query = joined[:, pair_at(pair)]
        keys = joined[:, pair_at(pairs_of(width) + pair)]
        values = joined[:, pair_at(2 * pairs_of(width) + pair)]
        outs = []
        for side in range(2):
            mine = lanes if side == 0 else ~lanes
            scores = dot_nt(jnp.where(mine, query, jnp.zeros_like(query)), keys) * score_scale
            scores = jnp.where(allowed, scores, masked_value)
            expo = jnp.exp(scores - jnp.max(scores, axis=-1, keepdims=True))
            chances = (expo / jnp.sum(expo, axis=-1, keepdims=True)).astype(jnp.bfloat16)
            probs[2 * pair + side] = chances
            outs.append(dot_without_transpose(chances, values))
        mixed[:, pair_at(pair)] = jnp.where(lanes, outs[0], outs[1]).astype(jnp.bfloat16)
        return state

    lax.fori_loop(0, pairs_of(width), pair_step, 0)


def output_part(x0, mixed, weight, bias, adapters, inner, gains, shifts, x1, h2):
    half = adapters.shape[0] // 2
    width = mixed.shape[1]
    here = ranks(3, inner.shape)
    fresh = adapter_in(adapters[:half], mixed[...])
    inner[...] = jnp.where(here, fresh, inner[...])
    outer = jnp.where(ranks(3, (half, width)), adapters[half:], 0.0)
    x1[...] = (
        x0[...]
        + dot_without_transpose(mixed[...], weight[...])
        + bias[:, 3 * width : 4 * width]
        + adapter_out(inner[...], outer)
    )
    unit, _ = normal(x1[...])
    h2[...] = (unit * gains[1:2] + shifts[1:2]).astype(jnp.bfloat16)


def up_part(h2, weight, bias, active, slope):
    width = h2.shape[1]
    step = 512

    def columns(at, state):
        here = pl.ds(pl.multiple_of(at * step, step), step)
        there = pl.ds(pl.multiple_of(4 * width + at * step, step), step)
        z = dot_without_transpose(h2[...], weight[:, here]) + bias[:, there]
        root = 0.7978845608028654
        square = z * z
        tanh = jnp.tanh(root * z * (1.0 + 0.044715 * square))
        half = 0.5 * (1.0 + tanh)
        active[:, here] = (z * half).astype(jnp.bfloat16)
        slope[:, here] = (
            half + 0.5 * z * (1.0 - tanh * tanh) * (root * (1.0 + 3 * 0.044715 * square))
        ).astype(jnp.bfloat16)
        return state

    lax.fori_loop(0, weight.shape[1] // step, columns, 0)


def down_part(begins, blocks, total, active, weight, bias, x2):
    hidden, width = weight.shape
    step = 256
    size = hidden // (2 * len(blocks))

    def columns(at, state):
        here = pl.ds(pl.multiple_of(at * step, step), step)
        there = pl.ds(pl.multiple_of(4 * width + hidden + at * step, step), step)
        values = total[:, here]
        if begins:
            values += bias[:, there]
        for block in blocks:
            units = pl.ds(pl.multiple_of(block * size, size), size)
            values += dot_without_transpose(active[:, units], weight[units, here])
        x2[:, here] = values
        return state

    lax.fori_loop(0, width // step, columns, 0)


def last_norm(x2, gains, shifts, final):
    unit, _ = normal(x2[...])
    final[...] = (unit * gains[2:3] + shifts[2:3]).astype(jnp.bfloat16)


def turn_rows(source, target):
    width = source.shape[0]

    def rows(at, state):
        here = pl.ds(pl.multiple_of(at * 128, 128), 128)
        target[:, here] = source[here].astype(jnp.float32).T.astype(target.dtype)
        return state

    lax.fori_loop(0, width // 128, rows, 0)


def backward_kernel(
    mean_rows,
    log_total,
    mask_row,
    target_rows,
    table_sum,
    gains,
    adapters,
    final,
    h1_far,
    joined_far,
    probs_far,
    mixed_far,
    inner,
    x1_far,
    slope_far,
    x2,
    w_out,
    w_up,
    w_down,
    gathered,
    work,
    dx2,
    da,
    dz,
    dmix,
    pulls,
    out_here,
    up_here,
    down_here,
    h1,
    joined,
    probs,
    mixed,
    x1,
    slope,
    sems,
):
    loads = []
    for at, (source, target) in enumerate(
        (
            (w_down, down_here),
            (slope_far, slope),
            (w_up, up_here),
            (x1_far, x1),
            (w_out, out_here),
            (mixed_far, mixed),
            (joined_far, joined),
            (probs_far, probs),
            (h1_far, h1),
        )
    ):
        copy = pltpu.make_async_copy(source, target, sems.at[at])
        copy.start()
        loads.append(copy)
    rows, width = x1.shape
    half = adapters.shape[0] // 2
    hidden = slope.shape[1]
    turn_rows(mean_rows, work)
    mask_col = col_of(mask_row[...])
    unsort = counted_first(mask_row[...])
    mean = dot_tn(unsort, work[...].astype(jnp.bfloat16))
    pulled = (1.0 - smooth) * target_rows[...] + (smooth / V) * table_sum[...]
    row_dots = jnp.sum(final[...].astype(jnp.float32) * pulled, axis=1, keepdims=True)
    count = jnp.sum(mask_row[...], axis=1, keepdims=True)
    spots = lax.broadcasted_iota(jnp.int32, mask_row.shape, 1).astype(jnp.float32)
    loss = jnp.sum(
        jnp.where(spots < count, log_total[...], 0.0), axis=1, keepdims=True
    ) - jnp.sum(mask_col * row_dots, axis=0, keepdims=True)
    lanes = lax.broadcasted_iota(jnp.int32, (1, 128), 1)
    numbers = jnp.where(lanes == 0, loss, jnp.where(lanes == 1, count, 0.0))
    dx2[...] = normal_back(x2[...], gains[2:3], mask_col * (mean - pulled))
    da[...] = dx2[...].astype(jnp.bfloat16)
    loads[0].wait()
    loads[1].wait()
    step = 512

    def hidden_columns(at, state):
        here = pl.ds(pl.multiple_of(at * step, step), step)
        dz[:, here] = (
            dot_nt(da[...], down_here[here]) * slope[:, here].astype(jnp.float32)
        ).astype(jnp.bfloat16)
        return state

    lax.fori_loop(0, hidden // step, hidden_columns, 0)
    loads[2].wait()
    loads[3].wait()

    def columns(at, state):
        here = pl.ds(pl.multiple_of(at * 256, 256), 256)
        work[:, here] = dot_nt(dz[...], up_here[here])
        return state

    lax.fori_loop(0, width // 256, columns, 0)
    dx1 = dx2[...] + normal_back(x1[...], gains[1:2], work[...])
    da[...] = dx1.astype(jnp.bfloat16)
    loads[4].wait()
    loads[5].wait()
    upper = stacked_halves(adapters[half:])
    inner_halves = stacked_halves(inner[...])

    def adapter_grads(which, gradient, inputs):
        up_grad = adapter_scale * added_halves(dot_without_transpose(inner_halves, gradient))
        back = adapter_scale * added_halves(dot_nt(upper, gradient))
        back = jnp.where(ranks(which, back.shape), back, 0.0)
        down_grad = added_halves(dot_without_transpose(stacked_halves(back), inputs))
        keep = ranks(which, up_grad.shape)
        return back, down_grad, jnp.where(keep, up_grad, 0.0)

    back, down_total, up_total = adapter_grads(3, da[...], mixed[...])
    dmix[...] = (
        dot_nt(da[...], out_here[...]) + adapter_out(back, adapters[:half]) / adapter_scale
    ).astype(jnp.bfloat16)
    lane_mask = head_lanes(rows)
    for copy in loads[6:]:
        copy.wait()

    def pair_step(pair, state):
        query = joined[:, pair_at(pair)]
        keys = joined[:, pair_at(pairs_of(width) + pair)]
        values = joined[:, pair_at(2 * pairs_of(width) + pair)]
        pull = dmix[:, pair_at(pair)]
        outs = []
        for side in range(2):
            mine = lane_mask if side == 0 else ~lane_mask
            chances = probs[2 * pair + side]
            wide = chances.astype(jnp.float32)
            reach = dot_nt(jnp.where(mine, pull, jnp.zeros_like(pull)), values)
            slide = wide * (reach - jnp.sum(wide * reach, axis=-1, keepdims=True))
            slide = slide.astype(jnp.bfloat16)
            outs.append(
                (
                    dot_without_transpose(slide, keys) * score_scale,
                    dot_tn(slide, query) * score_scale,
                    dot_tn(chances, pull),
                )
            )
        for which in range(3):
            both = jnp.where(lane_mask, outs[0][which], outs[1][which])
            pulls[:, pair_at(which * pairs_of(width) + pair)] = both.astype(jnp.bfloat16)
        return state

    lax.fori_loop(0, pairs_of(width), pair_step, 0)
    for which in range(3):
        _, down_part_grad, up_part_grad = adapter_grads(
            which, pulls[:, which * width : (which + 1) * width], h1[...]
        )
        down_total += down_part_grad
        up_total += up_part_grad
    grads = jnp.concatenate([down_total, up_total], axis=0)
    numbers = jnp.broadcast_to(numbers, (2 * half, 128))
    gathered[...] = jnp.concatenate([grads, numbers], axis=1).reshape(2 * half, 1, width + 128)


def backward(mean_rows, log_total, mask, target_rows, table_sum, gains, adapters, kept, weights):
    rows = mask.shape[0]
    width = target_rows.shape[1]
    hidden = weights[2].shape[0]
    low, full = jnp.bfloat16, jnp.float32
    anywhere, vmem = pl.BlockSpec(memory_space=pl.ANY), pl.BlockSpec(memory_space=pltpu.VMEM)
    return pl.pallas_call(
        backward_kernel,
        out_shape=jax.ShapeDtypeStruct((adapters.shape[0], 1, width + 128), full),
        in_specs=[vmem] * 8 + [anywhere] * 4 + [vmem, anywhere, anywhere, vmem] + [anywhere] * 3,
        out_specs=vmem,
        scratch_shapes=[
            pltpu.VMEM((rows, width), full),
            pltpu.VMEM((rows, width), full),
            pltpu.VMEM((rows, width), low),
            pltpu.VMEM((rows, hidden), low),
            pltpu.VMEM((rows, width), low),
            pltpu.VMEM((rows, 3 * width), low),
        ]
        + [pltpu.VMEM(w.shape, low) for w in weights]
        + [pltpu.VMEM(value.shape, value.dtype) for value in kept[1:5] + kept[6:8]]
        + [pltpu.SemaphoreType.DMA((9,))],
        name="backward",
        compiler_params=pltpu.CompilerParams(vmem_limit_bytes=60 * 2**20),
    )(
        mean_rows,
        log_total,
        mask[None, :],
        target_rows,
        table_sum,
        gains,
        adapters,
        *kept,
        *weights,
    )


def update(gathered, adapters, down_momentum, up_momentum):
    group = lax.axis_size("vocab")
    devices = lax.axis_size("dp") * group
    width = adapters.shape[1]
    low, full = jnp.bfloat16, jnp.float32
    vmem = pl.BlockSpec(memory_space=pltpu.VMEM)
    dma = pltpu.SemaphoreType.DMA
    shape = jax.ShapeDtypeStruct
    share = up_momentum.shape[:2] + (width // group,)
    half = devices // 2
    message = gathered.shape[1:]
    whole, numbers = pl.pallas_call(
        sum_kernel,
        out_shape=[shape((devices, 1, width), full), shape((1, 128), full)],
        in_specs=[vmem],
        out_specs=[vmem] * 2,
        scratch_shapes=[
            pltpu.VMEM((half,) + message, full),
            pltpu.VMEM((half,) + message, full),
            pltpu.VMEM((half,) + message, full),
            pltpu.VMEM((1, width), full),
            dma((4,)),
            dma((2, half)),
            dma((2, half)),
        ],
        name="sum_gradients",
        compiler_params=pltpu.CompilerParams(collective_id=3, has_side_effects=True),
    )(gathered)
    return pl.pallas_call(
        update_kernel,
        out_shape=[shape(share, full)] * 4 + [shape(share, low)] * 2 + [shape((1, 1), full)] * 3,
        in_specs=[vmem] * 5,
        out_specs=[vmem] * 9,
        scratch_shapes=[pltpu.VMEM((devices, width), full)],
        name="update",
    )(whole, numbers, adapters, jnp.swapaxes(down_momentum, 1, 2), up_momentum)


def col_of(row):
    size = row.shape[1]
    square = (size, size)
    same = lax.broadcasted_iota(jnp.int32, square, 0) == lax.broadcasted_iota(jnp.int32, square, 1)
    return jnp.sum(jnp.where(same, row, 0.0), axis=1, keepdims=True)


def stack_rows(down, up):
    return jnp.concatenate(
        [down[j] for j in range(down.shape[0])] + [up[j] for j in range(up.shape[0])], axis=0
    )


def pack_rows(positions, gains, shifts, biases):
    width, count = positions.shape
    square = (count, count)
    same = lax.broadcasted_iota(jnp.int32, square, 0) == lax.broadcasted_iota(jnp.int32, square, 1)
    places = dot_nt(same.astype(jnp.float32).astype(jnp.bfloat16), positions[...])
    span = count // 4
    places = jnp.concatenate([places[r * span : (r + 1) * span] for r in range(4)], axis=1)
    norms = jnp.concatenate(
        [
            gains[...].astype(jnp.float32),
            shifts[...].astype(jnp.float32),
            jnp.zeros((gains.shape[0], 128 - 2 * width), jnp.float32),
        ],
        axis=1,
    )
    flat = biases[...].astype(jnp.float32)
    flat = jnp.concatenate([flat, jnp.zeros((1, -flat.shape[1] % 128), jnp.float32)], axis=1)
    lines = [flat[:, r * 128 : (r + 1) * 128] for r in range(flat.shape[1] // 128)]
    rest = jnp.zeros((8 - gains.shape[0], 128), jnp.float32)
    tail = jnp.zeros((8 - len(lines), 128), jnp.float32)
    return jnp.concatenate([places, norms, rest] + lines + [tail], axis=0).astype(jnp.bfloat16)


def unpack_rows(packed, devices, width, span, norms, bias_size, positions, gains, shifts, bias):
    rows = packed.shape[0] // devices

    def group(j, state):
        devs = [
            packed[pl.ds(pl.multiple_of((4 * j + i) * rows, rows), rows)].astype(jnp.float32)
            for i in range(4)
        ]
        lanes = pl.ds(pl.multiple_of(j * 128, 128), 128)
        for r in range(4):
            block = [dev[:span, r * width : (r + 1) * width] for dev in devs]
            positions[r * span : (r + 1) * span, lanes] = jnp.concatenate(block, axis=1).astype(
                jnp.bfloat16
            )
        gains[:, lanes] = jnp.concatenate([dev[span : span + norms, :width] for dev in devs], axis=1)
        shifts[:, lanes] = jnp.concatenate(
            [dev[span : span + norms, width : 2 * width] for dev in devs], axis=1
        )
        flat = []
        for dev in devs:
            left = bias_size
            line = span + 8
            while left > 0:
                flat.append(dev[line : line + 1, : min(left, 128)])
                left -= 128
                line += 1
        bias[:, pl.ds(pl.multiple_of(j * 4 * bias_size, 128), 4 * bias_size)] = jnp.concatenate(
            flat, axis=1
        )
        return state

    lax.fori_loop(0, devices // 4, group, 0)


CAP, EXTRA = 16, 16
ASKED = 48
OWN, LINE, SIDE, DIAGONAL, CORE, ROWS = range(6)
ASK, SUM, ANSWER, TURN, UNPACK, EMBED, PROJECT, ATTEND, OUTPUT, UP, DOWN_NEAR, DOWN = range(6, 18)
FIRST_ORDER = (
    (OWN, 0, 0),
    (SUM, 0, 0),
    (OWN, 2, 0),
    (OWN, 1, 0),
    (ASK, 0, 0),
    (LINE, 2, 2),
    (LINE, 1, 1),
    (LINE, 1, 2),
    (ANSWER, 0, 0),
    (LINE, 2, 1),
    (OWN, 5, 0),
    (OWN, 3, 0),
    (LINE, 0, 1),
    (LINE, 2, 3),
    (LINE, 5, 2),
    (LINE, 5, 1),
    (LINE, 0, 2),
    (TURN, 0, 0),
    (LINE, 5, 3),
    (SIDE, 2, 2),
    (SIDE, 0, 0),
    (LINE, 1, 3),
    (LINE, 0, 3),
    (SIDE, 2, 0),
    (SIDE, 0, 2),
    (SIDE, 0, 1),
    (SIDE, 5, 1),
    (SIDE, 5, 0),
    (SIDE, 5, 3),
    (SIDE, 2, 3),
    (LINE, 3, 1),
    (SIDE, 2, 1),
    (OWN, 4, 0),
    (ROWS, 0, 0),
    (DIAGONAL, 5, 1),
    (SIDE, 1, 0),
    (SIDE, 1, 1),
    (SIDE, 0, 3),
    (SIDE, 1, 3),
    (DIAGONAL, 2, 2),
    (DIAGONAL, 0, 0),
    (ROWS, 0, 2),
    (LINE, 3, 3),
    (SIDE, 1, 2),
    (SIDE, 5, 2),
    (DIAGONAL, 2, 1),
    (LINE, 3, 2),
    (DIAGONAL, 0, 2),
    (LINE, 4, 2),
    (ROWS, 0, 3),
    (DIAGONAL, 1, 3),
    (DIAGONAL, 2, 3),
    (DIAGONAL, 0, 3),
    (DIAGONAL, 2, 0),
    (DIAGONAL, 1, 2),
    (DIAGONAL, 5, 3),
    (DIAGONAL, 0, 1),
    (ROWS, 0, 1),
    (CORE, 0, 0),
    (DIAGONAL, 5, 2),
    (LINE, 4, 1),
    (DIAGONAL, 5, 0),
    (DIAGONAL, 1, 0),
    (SIDE, 3, 0),
    (DIAGONAL, 1, 1),
    (SIDE, 3, 1),
    (SIDE, 3, 3),
    (SIDE, 3, 2),
    (UNPACK, 0, 0),
    (CORE, 5, 0),
    (LINE, 4, 3),
    (EMBED, 0, 0),
    (CORE, 1, 0),
    (PROJECT, 0, 0),
    (DIAGONAL, 3, 0),
    (ATTEND, 0, 0),
    (CORE, 2, 0),
    (SIDE, 4, 2),
    (SIDE, 4, 0),
    (DIAGONAL, 3, 3),
    (DIAGONAL, 3, 1),
    (SIDE, 4, 1),
    (DIAGONAL, 3, 2),
    (OUTPUT, 0, 0),
    (SIDE, 4, 3),
    (CORE, 3, 0),
    (UP, 0, 0),
    (DIAGONAL, 4, 2),
    (DIAGONAL, 4, 0),
    (DIAGONAL, 4, 3),
    (DIAGONAL, 4, 1),
    (DOWN_NEAR, 0, 0),
    (CORE, 4, 0),
    (DOWN, 0, 0),
)


def first_kernel(table_rows, devices, group, row_counts, *refs):
    (
        ids,
        targets,
        mask,
        lengths,
        position_own,
        gain_own,
        shift_own,
        bias_own,
        adapter_down,
        adapter_up,
        table_tail,
        table,
        *refs,
    ) = refs
    weights_own = refs[:4]
    refs = refs[4:]
    (
        flags,
        target_out,
        table_sum,
        gains_out,
        adapters_out,
        final,
        final_sorted,
        inner,
        table_mine,
        turned_mine,
        table_other,
        turned_other,
        h1_out,
        joined_out,
        probs_out,
        mixed_out,
        x1_out,
        slope_out,
        x2_out,
        out_kept,
        up_kept,
        down_kept,
        *refs,
    ) = refs
    (
        send_sems,
        recv_sems,
        local_sems,
        table_sems,
        ask_sems,
        row_sems,
        sum_sems,
        keep_sems,
        table_here,
        turned_here,
        selector,
        rows_out,
        rows_in,
        ask_out,
        ask_in,
        sum_out,
        sum_in,
        extra_out,
        extra,
        pack_here,
        packed,
        w_qkv,
        w_out,
        w_up,
        w_down,
        positions,
        shifts,
        bias,
        embedded,
        x0,
        h1,
        joined,
        probs,
        mixed,
        x1,
        h2,
        active,
        slope,
        x2,
    ) = refs
    arrays = (packed, w_qkv, w_out, w_up, w_down, extra)
    ins = (pack_here,) + tuple(weights_own) + (extra_out,)
    dp, z, y, x, core, place, _ = position()
    along = by_nearness(z)
    dp_x, dp_y = place(y, 1 - x, core), place(1 - y, x, core)
    dp_core, dp_diagonal = place(y, x, 1 - core), place(1 - y, 1 - x, core)
    z_peers = [(dp, along[k]) for k in (1, 2, 3)]
    near_peers = [(dp_x, z), (dp_y, z), (dp_core, z)]
    body_rows = table_rows // 16 * 16
    tail_rows = table_here.shape[0] - body_rows
    loads = [
        pltpu.make_async_copy(
            table.at[pl.ds(0, body_rows)], table_here.at[pl.ds(0, body_rows)], table_sems.at[0]
        ),
        pltpu.make_async_copy(
            table_tail, table_here.at[pl.ds(body_rows, tail_rows)], table_sems.at[1]
        ),
    ]
    for copy in loads:
        copy.start()
    pack_here[...] = pack_rows(position_own, gain_own, shift_own, bias_own)
    me = meet_all(devices, group)
    sent, kept, used = [], {}, [0] * len(arrays)

    def piece(which, block):
        rows = row_counts[which]
        return arrays[which].at[pl.ds(pl.multiple_of(block * rows, rows), rows)]

    def copy_to(which, block, peer, source, number):
        return pltpu.make_async_remote_copy(
            piece(which, block) if source is None else source,
            piece(which, block),
            send_sems.at[which, number],
            recv_sems.at[which, block],
            device_id=peer,
            device_id_type=MESH,
        )

    def send(which, block, peer, source=None):
        copy = copy_to(which, block, peer, source, used[which])
        used[which] += 1
        copy.start()
        sent.append(copy)

    def arrive(which, block):
        copy_to(which, block, z_peers[0], ins[which], 0).wait_recv()

    def pass_along(which, k, act):
        source = None if k else ins[which]
        block = dp * 4 + along[k]

        @pl.when((along[k] <= z) & (z < 3))
        def _():
            act(copy_to(which, block, (dp, z + 1), source, 34 + k))

        @pl.when((along[k] >= z) & (z > 0))
        def _():
            act(copy_to(which, block, (dp, z - 1), source, 38 + k))

    def own_near(which):
        for peer in near_peers:
            send(which, me, peer, ins[which])
        copy = pltpu.make_async_copy(ins[which], piece(which, me), local_sems.at[which])
        copy.start()
        kept[which] = copy

    def own(which, _):
        if which == 5:
            own_near(which)
        pass_along(which, 0, lambda copy: copy.start())

    def line(which, k):
        block = dp * 4 + along[k]
        arrive(which, block)
        pass_along(which, k, lambda copy: copy.start())
        for peer in near_peers:
            send(which, block, peer)

    def side(which, k):
        block_x, block_y = dp_x * 4 + along[k], dp_y * 4 + along[k]
        arrive(which, block_y)
        if k < 2:
            send(which, block_y, (dp_x, z))
        arrive(which, block_x)
        if k >= 2:
            send(which, block_x, (dp_y, z))
        send(which, block_y, (dp_core, z))
        send(which, block_x, (dp_core, z))

    def diagonal(which, k):
        block = dp_diagonal * 4 + along[k]
        arrive(which, block)
        send(which, block, (dp_core, z))

    def other_core(which, _):
        for y_at in range(2):
            for x_at in range(2):
                for z_at in range(4):
                    arrive(which, place(y_at, x_at, 1 - core) * 4 + z_at)
        if which in kept:
            kept.pop(which).wait()

    keeps = []

    def keep(source, target):
        copy = pltpu.make_async_copy(source, target, keep_sems.at[len(keeps)])
        copy.start()
        keeps.append(copy)

    for which in range(5):
        own_near(which)
    state = {}

    def ask():
        own_ids = ids[...].astype(jnp.float32)
        own_targets = jnp.where(mask[...] > 0, targets[...], ids[...]).astype(jnp.float32)
        ids_row = jnp.concatenate([own_ids, own_targets], axis=1)
        ids_col = jnp.concatenate([col_of(own_ids), col_of(own_targets)], axis=0)
        tokens = ids_row.shape[1]
        wide = (tokens, tokens)
        across = lax.broadcasted_iota(jnp.int32, wide, 1).astype(jnp.float32)
        down = lax.broadcasted_iota(jnp.int32, wide, 0).astype(jnp.float32)
        owner_row, owner_col = jnp.zeros_like(ids_row), jnp.zeros_like(ids_col)
        for device in range(1, devices):
            owner_row += (ids_row >= float(device * table_rows)).astype(jnp.float32)
            owner_col += (ids_col >= float(device * table_rows)).astype(jnp.float32)
        equal = ids_col == ids_row
        first_col = jnp.min(jnp.where(equal, across, float(tokens)), axis=1, keepdims=True)
        first_row = jnp.min(jnp.where(equal, down, float(tokens)), axis=0, keepdims=True)
        leads = jnp.where(first_row == across[:1], owner_row, -1.0)
        slot_col = jnp.sum(
            jnp.where((owner_col == leads) & (across < first_col), 1.0, 0.0),
            axis=1,
            keepdims=True,
        )
        takes = lax.broadcasted_iota(jnp.int32, (devices, tokens), 0).astype(jnp.float32) == leads
        local_row = jnp.where(takes, ids_row - owner_row * table_rows + 1.0, 0.0)
        lanes = lax.broadcasted_iota(jnp.int32, (tokens, 128), 1).astype(jnp.float32)
        asked = (
            dot_without_transpose(
                local_row, (slot_col == lanes).astype(jnp.float32), highest_precision
            )
            - 1.0
        )
        counted = jnp.sum(mask[...].astype(jnp.float32), axis=1, keepdims=True)
        over = (jnp.max(slot_col, axis=0, keepdims=True) >= float(ASKED)) | (
            counted > float(live_rows(mask.shape[1]))
        )
        ask_lanes = lax.broadcasted_iota(jnp.int32, (devices, 128), 1)
        asked = jnp.where(ask_lanes == 127, over.astype(jnp.float32), asked)
        ask_out[...] = asked.reshape(devices, 1, 128)
        ask_in[pl.ds(me, 1)] = ask_out[pl.ds(me, 1)]
        start, state["ask_arrive"], state["ask_sent"] = to_all(
            lambda other: ask_out.at[other],
            ask_in,
            ask_sems.at[0],
            ask_sems.at[1],
            devices,
            group,
            me,
        )
        start()
        state["ids_col"] = ids_col
        state["owner_col"] = owner_col
        state["slot_col"] = slot_col

    def table_total():
        for copy in loads:
            copy.wait()
        keep(table_here, table_mine)

        def add_up(step, total):
            return total + jnp.sum(
                table_here[pl.ds(pl.multiple_of(step * 128, 128), 128)].astype(jnp.float32),
                axis=0,
                keepdims=True,
            )

        width = table_here.shape[1]
        sum_out[:, :width] = lax.fori_loop(
            0, table_here.shape[0] // 128, add_up, jnp.zeros((1, width), jnp.float32)
        )

    def answer():
        state["ask_arrive"]()
        width = table_here.shape[1]
        asked_all = ask_in[...].reshape(devices, 128)
        ask_lanes = lax.broadcasted_iota(jnp.int32, (devices, 128), 1)
        over = jnp.max(
            jnp.max(jnp.where(ask_lanes == 127, asked_all, 0.0), axis=0, keepdims=True),
            axis=1,
            keepdims=True,
        )
        square = (128, 128)
        eye = (
            lax.broadcasted_iota(jnp.int32, square, 0)
            == lax.broadcasted_iota(jnp.int32, square, 1)
        ).astype(jnp.float32)
        turned = jnp.round(dot_nt(eye, asked_all, highest_precision))
        more = turned[CAP:ASKED]
        counts = jnp.sum((more >= 0.0).astype(jnp.float32), axis=0, keepdims=True)
        pairs = (devices, devices)
        before = (
            lax.broadcasted_iota(jnp.int32, pairs, 0) < lax.broadcasted_iota(jnp.int32, pairs, 1)
        ).astype(jnp.float32)
        ahead = jnp.round(
            dot_without_transpose(
                jnp.broadcast_to(counts, (8, devices)), before, highest_precision
            )[:1]
        )
        order = ahead + lax.broadcasted_iota(jnp.int32, more.shape, 0).astype(jnp.float32)
        order = jnp.where(more >= 0.0, order, -1.0)
        total = jnp.sum(counts, axis=1, keepdims=True)
        over = jnp.maximum(over, (total > float(EXTRA)).astype(jnp.float32))
        extra_col = jnp.full((EXTRA, 1), -1.0, jnp.float32)
        extra_row = jnp.full((1, 128), -1.0, jnp.float32)
        spots_col = lax.broadcasted_iota(jnp.int32, (EXTRA, 1), 0)
        spots_row = lax.broadcasted_iota(jnp.int32, (1, 128), 1)
        for spot in range(EXTRA):
            found = jnp.where(order == float(spot), more + 1.0, 0.0)
            found = jnp.sum(jnp.sum(found, axis=0, keepdims=True), axis=1, keepdims=True) - 1.0
            extra_col = jnp.where(spots_col == spot, found, extra_col)
            extra_row = jnp.where(spots_row == spot, found, extra_row)
        first_id = (me * table_rows).astype(jnp.float32)
        extra_row = jnp.where(extra_row >= 0.0, extra_row + first_id, -1.0)
        sum_out[:, width:] = jnp.where(spots_row == 127, over, extra_row)
        sum_in[pl.ds(me, 1)] = sum_out[...][None]
        start, state["sum_arrive"], state["sum_sent"] = to_all(
            lambda other: sum_out, sum_in, sum_sems.at[0], sum_sems.at[1], devices, group, me
        )
        start()
        row_lanes = lax.broadcasted_iota(jnp.int32, (EXTRA, table_here.shape[0]), 1)
        row_lanes = row_lanes.astype(jnp.float32)
        batch = selector.shape[0] // CAP
        for step in range(devices // batch):
            for at in range(batch):
                source = step * batch + at
                hot = turned[:CAP, source : source + 1] == row_lanes
                selector[at * CAP : (at + 1) * CAP] = hot.astype(jnp.float32).astype(jnp.bfloat16)
            picked = dot_without_transpose(selector[...], table_here[...])
            rows_out[step * batch : (step + 1) * batch] = picked.astype(jnp.bfloat16).reshape(
                batch, CAP, -1
            )
        hot = (extra_col == row_lanes).astype(jnp.float32).astype(jnp.bfloat16)
        extra_out[...] = dot_without_transpose(hot, table_here[...]).astype(jnp.bfloat16)
        rows_in[pl.ds(me, 1)] = rows_out[pl.ds(me, 1)]

    def row_copy(offset, far, there):
        column = lax.rem(dp + offset, devices // group)
        other = column * group + there
        number = offset * group + far
        return pltpu.make_async_remote_copy(
            rows_out.at[other],
            rows_in.at[me],
            row_sems.at[0, number],
            row_sems.at[1, number],
            device_id=(column, there),
            device_id_type=MESH,
        )

    def row_copies(k):
        return [
            row_copy(offset, mirror(z, along[k]), along[k])
            for offset in range(0 if k else 1, devices // group)
        ]

    def send_rows(k):
        for copy in row_copies(k):
            copy.start()

    def rows_arrive():
        flips = (z, z // 2 * 2 + 1 - z % 2, (z + 2) % 4, (1 - z // 2) * 2 + 1 - z % 2)
        for offset in range(devices // group):
            for far in range(group):
                if offset or far:
                    column = lax.rem(dp + devices // group - offset, devices // group)
                    source = column * group + flips[far]
                    number = offset * group + far
                    pltpu.make_async_remote_copy(
                        rows_in.at[source],
                        rows_in.at[source],
                        row_sems.at[0, number],
                        row_sems.at[1, number],
                        device_id=(column, flips[far]),
                        device_id_type=MESH,
                    ).wait_recv()

    def turn():
        adapters_out[...] = stack_rows(adapter_down, adapter_up)
        turn_rows(table_here, turned_here)
        keep(turned_here, turned_mine)
        for at, (here, there) in enumerate(
            ((table_here, table_other), (turned_here, turned_other))
        ):
            copy = pltpu.make_async_remote_copy(
                here,
                there,
                table_sems.at[2 + 2 * at],
                table_sems.at[3 + 2 * at],
                device_id=(dp_core, z),
                device_id_type=MESH,
            )
            copy.start()
            state["swap", at] = copy

    def unpack():
        unpack_rows(
            packed,
            devices,
            position_own.shape[0],
            position_own.shape[1] // 4,
            gain_own.shape[0],
            bias_own.shape[1],
            positions,
            gains_out,
            shifts,
            bias,
        )

    def embed():
        rows_arrive()
        state["sum_arrive"]()
        width = table_here.shape[1]
        table_sum[...] = jnp.sum(sum_in[:, :, :width], axis=0)
        notes = sum_in[:, :, width:].reshape(devices, 128)
        note_lanes = lax.broadcasted_iota(jnp.int32, notes.shape, 1)
        over = jnp.max(jnp.where(note_lanes == 127, notes, 0.0), axis=0, keepdims=True)
        flags[...] = jnp.max(over, axis=1, keepdims=True)
        slot_col, owner_col, ids_col = state["slot_col"], state["owner_col"], state["ids_col"]
        tokens = ids_col.shape[0]
        slots = lax.broadcasted_iota(jnp.int32, (tokens, devices * CAP), 1).astype(jnp.float32)
        index_col = jnp.where(slot_col < float(CAP), owner_col * CAP + slot_col, -1.0)
        chosen = (index_col == slots).astype(jnp.float32).astype(jnp.bfloat16)
        taken = dot_without_transpose(chosen, rows_in[...].reshape(devices * CAP, -1))
        extra_ids = jnp.concatenate(
            [notes[source : source + 1, :EXTRA] for source in range(devices)], axis=1
        )
        spots = lax.broadcasted_iota(jnp.int32, (tokens, devices * EXTRA), 1).astype(jnp.float32)
        wanted = jnp.where(slot_col < float(CAP), -2.0, ids_col)
        hit = jnp.min(
            jnp.where(wanted == extra_ids, spots, float(devices * EXTRA)), axis=1, keepdims=True
        )
        chosen = (hit == spots).astype(jnp.float32).astype(jnp.bfloat16)
        taken += dot_without_transpose(chosen, extra[...])
        embedded[...] = taken[: tokens // 2]
        target_out[...] = taken[tokens // 2 :]
        state["allowed"] = first_part(embedded, positions, lengths, gains_out, shifts, x0, h1)
        keep(h1, h1_out)

    def project():
        project_part(h1, w_qkv, bias, adapters_out, inner, joined)
        keep(joined, joined_out)

    def attend():
        attend_part(joined, state["allowed"], probs, mixed)
        keep(probs, probs_out)
        keep(mixed, mixed_out)

    def output():
        keep(w_out, out_kept)
        output_part(x0, mixed, w_out, bias, adapters_out, inner, gains_out, shifts, x1, h2)
        keep(x1, x1_out)

    def up():
        keep(w_up, up_kept)
        up_part(h2, w_up, bias, active, slope)
        keep(slope, slope_out)

    def chips(core_at):
        return [place(at // 2, at % 2, core_at) for at in range(4)]

    def down_near():
        kept.pop(4).wait()
        down_part(True, chips(core), x1, active, w_down, bias, x2)

    def down():
        keep(w_down, down_kept)
        down_part(False, chips(1 - core), x2, active, w_down, bias, x2)
        last_norm(x2, gains_out, shifts, final)
        sort = counted_first(mask[...].astype(jnp.float32))
        final_sorted[...] = dot_without_transpose(sort, final[...]).astype(jnp.bfloat16)
        keep(x2, x2_out)

    comes = {OWN: own, LINE: line, SIDE: side, DIAGONAL: diagonal, CORE: other_core}
    works = {
        ASK: ask,
        SUM: table_total,
        ANSWER: answer,
        TURN: turn,
        UNPACK: unpack,
        EMBED: embed,
        PROJECT: project,
        ATTEND: attend,
        OUTPUT: output,
        UP: up,
        DOWN_NEAR: down_near,
        DOWN: down,
    }
    for kind, which, k in FIRST_ORDER:
        if kind in comes:
            comes[kind](which, k)
        elif kind == ROWS:
            send_rows(k)
        else:
            works[kind]()
    for at in range(2):
        state["swap", at].wait()
    for copy in keeps:
        copy.wait()
    for copy in sent:
        copy.wait_send()
    for which in range(len(arrays)):
        for k in range(4):
            pass_along(which, k, lambda copy: copy.wait_send())
    for k in range(4):
        for copy in row_copies(k):
            copy.wait_send()
    state["ask_sent"]()
    state["sum_sent"]()


def first(
    ids, targets, mask, lengths, table, small, adapter_down, adapter_up, weights
):
    group = lax.axis_size("vocab")
    devices = lax.axis_size("dp") * group
    table_rows, width = table.shape
    pad_rows = -(-table_rows // 128) * 128
    body_rows = table_rows // 16 * 16
    tail = jnp.pad(table[body_rows:], ((0, pad_rows - table_rows), (0, 0)))
    rows = ids.shape[0]
    hidden = weights[3].shape[0] * devices
    heads = width // HEAD_DIM
    low, full = jnp.bfloat16, jnp.float32
    positions, gains, shifts, biases = small
    pack_height = positions.shape[1] // 4 + 16
    counts = [pack_height] + [w.shape[0] for w in weights] + [EXTRA]
    anywhere, vmem = pl.BlockSpec(memory_space=pl.ANY), pl.BlockSpec(memory_space=pltpu.VMEM)
    dma = pltpu.SemaphoreType.DMA
    shape = jax.ShapeDtypeStruct
    adapter_rows = 2 * adapter_up.shape[0] * adapter_up.shape[1]
    whole = [(devices * w.shape[0], w.shape[1]) for w in weights]
    saved = [
        shape((pad_rows, width), low),
        shape((width, pad_rows), low),
        shape((pad_rows, width), low),
        shape((width, pad_rows), low),
        shape((rows, width), low),
        shape((rows, 3 * width), low),
        shape((heads, rows, rows), low),
        shape((rows, width), low),
        shape((rows, width), full),
        shape((rows, hidden), low),
        shape((rows, width), full),
    ] + [shape(w, low) for w in whole[1:]]
    return pl.pallas_call(
        partial(first_kernel, table_rows, devices, group, counts),
        out_shape=[
            shape((1, 1), full),
            shape((rows, width), full),
            shape((1, width), full),
            shape((gains.shape[0], width), full),
            shape((adapter_rows, width), full),
            shape((rows, width), low),
            shape((rows, width), low),
            shape((adapter_rows // 2, rows), full),
        ]
        + saved,
        in_specs=[vmem] * 3
        + [pl.BlockSpec(memory_space=pltpu.SMEM)]
        + [vmem] * 6
        + [anywhere] * (2 + len(weights)),
        out_specs=[vmem] * 8 + [anywhere] * len(saved),
        scratch_shapes=[
            dma((len(counts), 42)),
            dma((len(counts), devices)),
            dma((len(counts),)),
            dma((6,)),
            dma((2, devices)),
            dma((2, devices)),
            dma((2, devices)),
            dma((12,)),
            pltpu.VMEM((pad_rows, width), low),
            pltpu.VMEM((width, pad_rows), low),
            pltpu.VMEM((16 * CAP, pad_rows), low),
            pltpu.VMEM((devices, CAP, width), low),
            pltpu.VMEM((devices, CAP, width), low),
            pltpu.VMEM((devices, 1, 128), full),
            pltpu.VMEM((devices, 1, 128), full),
            pltpu.VMEM((1, width + 128), full),
            pltpu.VMEM((devices, 1, width + 128), full),
            pltpu.VMEM((EXTRA, width), low),
            pltpu.VMEM((devices * EXTRA, width), low),
            pltpu.VMEM((pack_height, 128), low),
            pltpu.VMEM((devices * pack_height, 128), low),
        ]
        + [pltpu.VMEM(w, low) for w in whole]
        + [
            pltpu.VMEM((positions.shape[1], width), low),
            pltpu.VMEM((shifts.shape[0], width), full),
            pltpu.VMEM((1, devices * biases.shape[0]), full),
            pltpu.VMEM((rows, width), full),
            pltpu.VMEM((rows, width), full),
            pltpu.VMEM((rows, width), low),
            pltpu.VMEM((rows, 3 * width), low),
            pltpu.VMEM((heads, rows, rows), low),
            pltpu.VMEM((rows, width), low),
            pltpu.VMEM((rows, width), full),
            pltpu.VMEM((rows, width), low),
            pltpu.VMEM((rows, hidden), low),
            pltpu.VMEM((rows, hidden), low),
            pltpu.VMEM((rows, width), full),
        ],
        name="first",
        compiler_params=pltpu.CompilerParams(
            collective_id=1, has_side_effects=True, vmem_limit_bytes=63 * 2**20
        ),
    )(
        ids[None, :],
        targets[None, :],
        mask[None, :],
        lengths,
        positions,
        gains,
        shifts,
        biases[None, :],
        jnp.swapaxes(adapter_down, 1, 2),
        adapter_up,
        tail,
        table,
        *weights,
    )


def per_device(
    ids,
    targets,
    counted_mask,
    lengths,
    table,
    position_table,
    layer_norm_gain,
    layer_norm_bias,
    query_key_value_weight,
    output_weight,
    up_weight,
    down_weight,
    biases,
    adapter_down,
    adapter_up,
    down_momentum,
    up_momentum,
):
    every = (
        ids,
        targets,
        counted_mask,
        lengths,
        table,
        position_table,
        layer_norm_gain,
        layer_norm_bias,
        query_key_value_weight,
        output_weight,
        up_weight,
        down_weight,
        biases,
        adapter_down,
        adapter_up,
    )
    table_rows = table.shape[0]
    (
        flags,
        target_rows,
        table_sum,
        gains_all,
        adapters,
        final_state,
        final_sorted,
        inner_rows,
        table_mine,
        turned_mine,
        table_other,
        turned_other,
        h1,
        joined,
        probs,
        mixed,
        x1,
        slope,
        x2,
        w_out_all,
        w_up_all,
        w_down_all,
    ) = first(
        ids,
        targets,
        counted_mask,
        lengths,
        table,
        (position_table.T, layer_norm_gain, layer_norm_bias, biases),
        adapter_down,
        adapter_up,
        (query_key_value_weight, output_weight, up_weight, down_weight),
    )
    kept = (h1, joined, probs, mixed, inner_rows, x1, slope, x2)
    mean_rows, log_total = head(
        final_sorted, table_rows, (table_mine, turned_mine, table_other, turned_other)
    )
    gathered = backward(
        mean_rows,
        log_total,
        counted_mask.astype(jnp.float32),
        target_rows,
        table_sum,
        gains_all,
        adapters,
        (final_state, *kept),
        (w_out_all, w_up_all, w_down_all),
    )

    def general():
        down_gradient, up_gradient, loss_own, count_own = gradients_general(*every)
        rows = jnp.concatenate([jnp.swapaxes(down_gradient, 1, 2), up_gradient], axis=0)
        rows = rows.reshape(gathered.shape[0], 1, -1)
        sums = jnp.zeros((rows.shape[0], 1, 128), jnp.float32)
        sums = sums.at[:, :, 0].set(loss_own).at[:, :, 1].set(count_own)
        return jnp.concatenate([rows, sums], axis=2)

    gathered = lax.cond(flags.reshape(()) > 0.0, general, lambda: gathered)
    mom_down, mom_up, new_down, new_up, low_down, low_up, loss, count, norm = update(
        gathered, adapters, down_momentum, up_momentum
    )
    return (
        loss.reshape(()),
        count.reshape(()),
        norm.reshape(()),
        jnp.swapaxes(mom_down, 1, 2),
        mom_up,
        jnp.swapaxes(new_down, 1, 2),
        new_up,
        jnp.swapaxes(low_down, 1, 2),
        low_up,
    )


def solution(mesh):
    fast = dict(mesh.shape) == {"dp": 8, "vocab": 4}
    placed = (
        P(("dp", "vocab")),
        P(("dp", "vocab")),
        P(("dp", "vocab")),
        P(("dp", "vocab"), None),
        P(("dp", "vocab"), None),
        P(None, ("dp", "vocab")),
        P(None, ("dp", "vocab")),
        P(None, ("dp", "vocab")),
        P(("dp", "vocab"), None),
        P(("dp", "vocab"), None),
        P(("dp", "vocab"), None),
        P(("dp", "vocab"), None),
        P(("dp", "vocab")),
        P(),
        P(),
        P(),
        P(),
    )
    return jax.shard_map(
        per_device if fast else per_device_general,
        mesh=mesh,
        in_specs=placed,
        out_specs=(
            P(),
            P(),
            P(),
            P(None, "vocab", None),
            P(None, None, "vocab"),
            P(None, "vocab", None),
            P(None, None, "vocab"),
            P(None, "vocab", None),
            P(None, None, "vocab"),
        ),
        check_vma=False,
    )
```

```python
from functools import partial

import jax
import jax.numpy as jnp
from jax import lax
from jax.experimental import pallas as pl
from jax.experimental.pallas import tpu as pltpu
from jax.sharding import PartitionSpec as P

HEAD_DIM = 64
V = 50304


highest_precision = lax.Precision.HIGHEST
ln_eps = 1e-05
adapter_scale = 8.0
smooth = 0.1
clip_level = 1.0
momentum = 0.5
learning_rate = 0.5
coef_a = 3.4445
coef_b = -4.775
coef_c = 2.0315
score_scale = 0.125
masked_value = -1e30


def merged(x, axis, join):
    gathered = jax.tree.map(
        lambda a, kind: lax.all_gather(a.astype(kind), axis),
        x,
        jax.tree.map(lambda a: jnp.bfloat16 if a.dtype == jnp.float32 else a.dtype, x),
    )

    def take(source):
        return jax.tree.map(
            lambda a, own: lax.dynamic_index_in_dim(a, source, 0, False).astype(own.dtype),
            gathered,
            x,
        )

    return lax.fori_loop(
        1, lax.axis_size(axis), lambda source, state: join(state, take(source)), take(0)
    )


def dot_without_transpose(left_side, right_side, setting=None):
    return jnp.dot(left_side, right_side, precision=setting, preferred_element_type=jnp.float32)


def dot_last_axis(left_side, right_side, setting=None):
    return lax.dot_general(
        left_side,
        right_side,
        (((1,), (1,)), ((), ())),
        precision=setting,
        preferred_element_type=jnp.float32,
    )


def dot_first(left_side, right_side, setting=None):
    return lax.dot_general(
        left_side,
        right_side,
        (((0,), (0,)), ((), ())),
        precision=setting,
        preferred_element_type=jnp.float32,
    )


def rounded_values(values):
    return lax.optimization_barrier(values.astype(jnp.bfloat16)).astype(jnp.float32)


def layer_norm(values, gain, offset):
    center = values - jnp.mean(values, axis=-1, keepdims=True)
    spread = jnp.mean(center * center, axis=-1, keepdims=True)
    return center * lax.rsqrt(spread + ln_eps) * gain + offset


def layout(seq_lengths, row_count):
    seq_ends = jnp.cumsum(seq_lengths)
    seq_starts = seq_ends - seq_lengths
    places = jnp.arange(row_count, dtype=jnp.int32)
    segment = jnp.sum((places[:, None] >= seq_ends[None, :]).astype(jnp.int32), axis=1)
    member = segment[:, None] == jnp.arange(seq_lengths.shape[0], dtype=jnp.int32)[None, :]
    positions_in = places - jnp.sum(jnp.where(member, seq_starts[None, :], 0), axis=1)
    allowed_mask = (segment[:, None] == segment[None, :]) & (places[None, :] <= places[:, None])
    return (positions_in, allowed_mask)


def owner_rows(token_ids, piece_rows, group, vocab_pos):
    piece_index = token_ids // piece_rows
    owner = piece_index % group
    local = piece_index // group * piece_rows + token_ids % piece_rows
    return jnp.where(owner == vocab_pos, local, -1)


def attention_scores(query, key_rows, allowed_mask):
    scores = (
        jnp.einsum("shd,thd->hst", query, key_rows, preferred_element_type=jnp.float32)
        * score_scale
    )
    return jnp.where(allowed_mask[None], scores, masked_value)


def layer_forward(residual_initial, frozen_weights, adapter_down, adapter_up, allowed_mask):
    query_key_value_weight, output_weight, up_weight, down_weight, gains, shifts, bias_stack = (
        frozen_weights
    )
    gains = gains.astype(jnp.float32)
    shifts = shifts.astype(jnp.float32)
    bias_stack = bias_stack.astype(jnp.float32)
    width_size = output_weight.shape[0]
    hidden_units = up_weight.shape[1]
    row_count = residual_initial.shape[0]
    heads = width_size // HEAD_DIM
    first_normed = layer_norm(residual_initial, gains[0], shifts[0]).astype(jnp.bfloat16)
    first_plain = first_normed.astype(jnp.float32)
    joined_rows = (
        dot_without_transpose(first_normed, query_key_value_weight) + bias_stack[: 3 * width_size]
    )
    adapt_in = []
    projected = []
    for which_index in range(3):
        inner_product = dot_without_transpose(
            first_plain, adapter_down[which_index], highest_precision
        )
        adapt_in.append(inner_product)
        branch_output = joined_rows[
            :, which_index * width_size : (which_index + 1) * width_size
        ] + adapter_scale * dot_without_transpose(
            inner_product, adapter_up[which_index], highest_precision
        )
        projected.append(branch_output.astype(jnp.bfloat16).reshape(row_count, heads, HEAD_DIM))
    query, key_rows, value_rows = projected
    scores = attention_scores(query, key_rows, allowed_mask)
    top = jnp.max(scores, axis=-1, keepdims=True)
    expo = jnp.exp(scores - top)
    summed = jnp.sum(expo, axis=-1, keepdims=True)
    log_total = top + jnp.log(summed)
    probs = (expo / summed).astype(jnp.bfloat16)
    mixed_state = jnp.einsum("hst,thd->shd", probs, value_rows, preferred_element_type=jnp.float32)
    mixed_state = mixed_state.reshape(row_count, width_size).astype(jnp.bfloat16)
    mixed_plain = mixed_state.astype(jnp.float32)
    adapter_output = dot_without_transpose(mixed_plain, adapter_down[3], highest_precision)
    attended_rows = (
        dot_without_transpose(mixed_state, output_weight)
        + bias_stack[3 * width_size : 4 * width_size]
        + adapter_scale * dot_without_transpose(adapter_output, adapter_up[3], highest_precision)
    )
    stream_one = residual_initial + attended_rows
    normed_two = layer_norm(stream_one, gains[1], shifts[1]).astype(jnp.bfloat16)
    before_gelu = (
        dot_without_transpose(normed_two, up_weight)
        + bias_stack[4 * width_size : 4 * width_size + hidden_units]
    )
    activation = jax.nn.gelu(before_gelu, approximate=True).astype(jnp.bfloat16)
    stream_two = (
        stream_one
        + dot_without_transpose(activation, down_weight)
        + bias_stack[4 * width_size + hidden_units :]
    )
    final_state = layer_norm(stream_two, gains[2], shifts[2]).astype(jnp.bfloat16)
    kept_rows = (
        first_plain,
        adapt_in,
        query,
        key_rows,
        value_rows,
        log_total,
        mixed_plain,
        adapter_output,
        stream_one,
        before_gelu,
        stream_two,
    )
    return (final_state, kept_rows)


def layer_backward(
    final_gradient, kept_rows, backward_weights, adapter_down, adapter_up, allowed_mask
):
    output_weight, up_weight, down_weight, gains = backward_weights
    gains = gains.astype(jnp.float32)
    (
        first_plain,
        adapt_in,
        query,
        key_rows,
        value_rows,
        log_total,
        mixed_plain,
        adapter_output,
        stream_one,
        before_gelu,
        stream_two,
    ) = kept_rows
    row_count = query.shape[0]
    width_size = query.shape[1] * HEAD_DIM
    _, pull_three = jax.vjp(lambda values: layer_norm(values, gains[2], 0.0), stream_two)
    grad_two = pull_three(final_gradient)[0]
    grad_act = dot_last_axis(grad_two.astype(jnp.bfloat16), down_weight)
    _, pull_gelu = jax.vjp(partial(jax.nn.gelu, approximate=True), before_gelu)
    grad_pre = pull_gelu(grad_act)[0].astype(jnp.bfloat16)
    _, pull_two = jax.vjp(lambda values: layer_norm(values, gains[1], 0.0), stream_one)
    first_gradient = grad_two + pull_two(dot_last_axis(grad_pre, up_weight))[0]
    attention_gradient = first_gradient.astype(jnp.bfloat16)
    attention_scaled = adapter_scale * rounded_values(first_gradient)
    up_grads = [None, None, None, None]
    down_grads = [None, None, None, None]
    up_grads[3] = dot_first(adapter_output, attention_scaled, highest_precision)
    backward_output = dot_last_axis(attention_scaled, adapter_up[3], highest_precision)
    down_grads[3] = dot_first(mixed_plain, backward_output, highest_precision)
    mixed_gradient = dot_last_axis(attention_gradient, output_weight) + dot_last_axis(
        backward_output, adapter_down[3], highest_precision
    )
    grad_heads = mixed_gradient.astype(jnp.bfloat16).reshape(query.shape)
    probs = jnp.exp(attention_scores(query, key_rows, allowed_mask) - log_total)
    grad_value = jnp.einsum(
        "hst,shd->thd", probs.astype(jnp.bfloat16), grad_heads, preferred_element_type=jnp.float32
    )
    grad_probs = jnp.einsum(
        "shd,thd->hst", grad_heads, value_rows, preferred_element_type=jnp.float32
    )
    grad_scores = probs * (grad_probs - jnp.sum(probs * grad_probs, axis=-1, keepdims=True))
    grad_scores = grad_scores.astype(jnp.bfloat16)
    grad_query = (
        jnp.einsum("hst,thd->shd", grad_scores, key_rows, preferred_element_type=jnp.float32)
        * score_scale
    )
    grad_key = (
        jnp.einsum("hst,shd->thd", grad_scores, query, preferred_element_type=jnp.float32)
        * score_scale
    )
    for which_index, branch_gradient in enumerate((grad_query, grad_key, grad_value)):
        scaled_values = adapter_scale * rounded_values(
            branch_gradient.reshape(row_count, width_size)
        )
        up_grads[which_index] = dot_first(adapt_in[which_index], scaled_values, highest_precision)
        backward_input = dot_last_axis(scaled_values, adapter_up[which_index], highest_precision)
        down_grads[which_index] = dot_first(first_plain, backward_input, highest_precision)
    return (jnp.stack(down_grads), jnp.stack(up_grads))


def orthogonalize(matrices, sum_grams):
    grams = sum_grams(
        jnp.einsum(
            "mrd,msd->mrs",
            matrices,
            matrices,
            precision=highest_precision,
            preferred_element_type=jnp.float32,
        )
    )
    sizes = jnp.sqrt(jnp.trace(grams, axis1=1, axis2=2))[:, None, None] + 1e-07
    state = matrices / sizes
    grams = grams / (sizes * sizes)
    for turn_index in range(5):
        if turn_index:
            grams = sum_grams(
                jnp.einsum(
                    "mrd,msd->mrs",
                    state,
                    state,
                    precision=highest_precision,
                    preferred_element_type=jnp.float32,
                )
            )
        poly = coef_b * grams + coef_c * jnp.einsum(
            "mrs,mst->mrt",
            grams,
            grams,
            precision=highest_precision,
            preferred_element_type=jnp.float32,
        )
        state = coef_a * state + jnp.einsum(
            "mrs,msd->mrd",
            poly,
            state,
            precision=highest_precision,
            preferred_element_type=jnp.float32,
        )
    return state


def gradients_general(
    ids,
    targets,
    counted_mask,
    lengths,
    table,
    position_table,
    layer_norm_gain,
    layer_norm_bias,
    query_key_value_weight,
    output_weight,
    up_weight,
    down_weight,
    biases,
    adapter_down,
    adapter_up,
):
    gathered = (
        lax.all_gather(query_key_value_weight, ("dp", "vocab"), axis=0, tiled=True),
        lax.all_gather(output_weight, ("dp", "vocab"), axis=0, tiled=True),
        lax.all_gather(up_weight, ("dp", "vocab"), axis=0, tiled=True),
        lax.all_gather(down_weight, ("dp", "vocab"), axis=0, tiled=True),
        lax.all_gather(layer_norm_gain, ("dp", "vocab"), axis=1, tiled=True),
        lax.all_gather(layer_norm_bias, ("dp", "vocab"), axis=1, tiled=True),
        lax.all_gather(biases, ("dp", "vocab"), axis=0, tiled=True),
        lax.all_gather(position_table, ("dp", "vocab"), axis=1, tiled=True),
    )
    w_qkv_all, w_out_all, w_up_all, w_down_all, gains_all, shifts_all, bias_stack, positions_all = (
        gathered
    )
    row_count = ids.shape[0]
    width_size = w_out_all.shape[0]
    group = lax.axis_size("vocab")
    vocab_pos = lax.axis_index("vocab")
    piece_rows = table.shape[0]
    ids_all, target_all, mask_all = (
        lax.all_gather(ids, "vocab", axis=0, tiled=True),
        lax.all_gather(targets, "vocab", axis=0, tiled=True),
        lax.all_gather(counted_mask, "vocab", axis=0, tiled=True),
    )
    table_full = lax.all_gather(table, "dp", axis=0, tiled=True)
    vocab_rows = table_full.shape[0]
    local_ids = owner_rows(ids_all, piece_rows, group, vocab_pos)
    inside = local_ids >= 0
    picked_rows = table_full[jnp.clip(local_ids, 0, vocab_rows - 1)]
    picked_rows = jnp.where(inside[:, None], picked_rows, jnp.zeros_like(picked_rows))
    embedded = lax.psum_scatter(
        picked_rows.astype(jnp.float32).astype(jnp.bfloat16),
        "vocab",
        scatter_dimension=0,
        tiled=True,
    ).astype(jnp.float32)
    positions_in, allowed_mask = layout(lengths[0], row_count)
    residual_initial = embedded + positions_all[positions_in].astype(jnp.float32)
    frozen_weights = (w_qkv_all, w_out_all, w_up_all, w_down_all, gains_all, shifts_all, bias_stack)
    final_state, kept_rows = layer_forward(
        residual_initial, frozen_weights, adapter_down, adapter_up, allowed_mask
    )
    final_all = lax.all_gather(final_state, "vocab", axis=0, tiled=True)
    total_rows = final_all.shape[0]
    block = 512
    count_blocks = total_rows // block
    final_blocks = final_all.reshape(count_blocks, block, width_size)
    local_targets = owner_rows(target_all, piece_rows, group, vocab_pos).reshape(
        count_blocks, block
    )
    columns = jnp.arange(vocab_rows, dtype=jnp.int32)

    def head_stats(item):
        piece, local = item
        logits = dot_last_axis(piece, table_full)
        top = jnp.max(logits, axis=1)
        expsum = jnp.sum(jnp.exp(logits - top[:, None]), axis=1)
        target_logit = jnp.sum(jnp.where(columns[None, :] == local[:, None], logits, 0.0), axis=1)
        return (top, expsum, target_logit, jnp.sum(logits, axis=1))

    stats = lax.map(head_stats, (final_blocks, local_targets))
    stats = tuple((entry.reshape(total_rows) for entry in stats))

    def combine(first_part, second_part):
        larger = jnp.maximum(first_part[0], second_part[0])
        merged_sum = first_part[1] * jnp.exp(first_part[0] - larger) + second_part[1] * jnp.exp(
            second_part[0] - larger
        )
        return (larger, merged_sum, first_part[2] + second_part[2], first_part[3] + second_part[3])

    top, expsum, target_logit, logit_sum = merged(stats, "vocab", combine)
    log_total = top + jnp.log(expsum)
    row_loss = log_total - (1.0 - smooth) * target_logit - smooth * logit_sum / V
    mask_float = mask_all.astype(jnp.float32)
    own_start = vocab_pos * row_count
    loss_own = jnp.sum(lax.dynamic_slice_in_dim(mask_float * row_loss, own_start, row_count))
    count_own = jnp.sum(counted_mask.astype(jnp.float32))

    def head_grad(item):
        piece, local, lse_block, weight = item
        logits = dot_last_axis(piece, table_full)
        probs = jnp.exp(logits - lse_block[:, None])
        onehot = (columns[None, :] == local[:, None]).astype(jnp.float32)
        grad_logits = weight[:, None] * (probs - (1.0 - smooth) * onehot - smooth / V)
        return dot_without_transpose(grad_logits.astype(jnp.bfloat16), table_full)

    partial_rows = lax.map(
        head_grad,
        (
            final_blocks,
            local_targets,
            log_total.reshape(count_blocks, block),
            mask_float.reshape(count_blocks, block),
        ),
    )
    final_gradient = lax.psum_scatter(
        partial_rows.reshape(total_rows, width_size).astype(jnp.bfloat16),
        "vocab",
        scatter_dimension=0,
        tiled=True,
    ).astype(jnp.float32)
    backward_weights = (
        lax.all_gather(output_weight, ("dp", "vocab"), axis=0, tiled=True),
        lax.all_gather(up_weight, ("dp", "vocab"), axis=0, tiled=True),
        lax.all_gather(down_weight, ("dp", "vocab"), axis=0, tiled=True),
        lax.all_gather(layer_norm_gain, ("dp", "vocab"), axis=1, tiled=True),
    )
    down_gradient, up_gradient = layer_backward(
        final_gradient, kept_rows, backward_weights, adapter_down, adapter_up, allowed_mask
    )
    return (down_gradient, up_gradient, loss_own, count_own)


def per_device_general(
    ids,
    targets,
    counted_mask,
    lengths,
    table,
    position_table,
    layer_norm_gain,
    layer_norm_bias,
    query_key_value_weight,
    output_weight,
    up_weight,
    down_weight,
    biases,
    adapter_down,
    adapter_up,
    down_momentum,
    up_momentum,
):
    group = lax.axis_size("vocab")
    vocab_pos = lax.axis_index("vocab")
    down_gradient, up_gradient, loss_own, count_own = gradients_general(
        ids,
        targets,
        counted_mask,
        lengths,
        table,
        position_table,
        layer_norm_gain,
        layer_norm_bias,
        query_key_value_weight,
        output_weight,
        up_weight,
        down_weight,
        biases,
        adapter_down,
        adapter_up,
    )
    down_gradient, up_gradient, smoothed_loss_sum, loss_count = lax.psum(
        (down_gradient, up_gradient, loss_own, count_own), ("dp", "vocab")
    )
    grad_norm = jnp.sqrt(
        jnp.sum(down_gradient * down_gradient) + jnp.sum(up_gradient * up_gradient)
    )
    factor = jnp.minimum(1.0, clip_level / (grad_norm + 1e-06))
    new_mom_down = momentum * down_momentum + factor * down_gradient
    new_mom_up = momentum * up_momentum + factor * up_gradient
    stacked = jnp.concatenate([jnp.swapaxes(new_mom_down, 1, 2), new_mom_up], axis=0)
    share_fraction = stacked.shape[2] // group
    begin_index = vocab_pos * share_fraction
    orthogonal_update = lax.dynamic_slice_in_dim(
        orthogonalize(stacked, lambda grams: grams), begin_index, share_fraction, 2
    )
    mom_down_part = lax.dynamic_slice_in_dim(new_mom_down, begin_index, share_fraction, 1)
    mom_up_part = lax.dynamic_slice_in_dim(new_mom_up, begin_index, share_fraction, 2)
    down_fresh = lax.dynamic_slice_in_dim(
        adapter_down, begin_index, share_fraction, 1
    ) - learning_rate * jnp.swapaxes(orthogonal_update[:4], 1, 2)
    up_fresh = (
        lax.dynamic_slice_in_dim(adapter_up, begin_index, share_fraction, 2)
        - learning_rate * orthogonal_update[4:]
    )
    return (
        smoothed_loss_sum,
        loss_count,
        grad_norm,
        mom_down_part,
        mom_up_part,
        down_fresh,
        up_fresh,
        down_fresh.astype(jnp.bfloat16),
        up_fresh.astype(jnp.bfloat16),
    )


MESH = pl.DeviceIdType.MESH


def dot_nt(left_side, right_side, setting=None):
    return dot_last_axis(left_side, right_side, setting)


def position():
    dp, z = lax.axis_index("dp"), lax.axis_index("vocab")
    y, x, core = dp // 4, dp // 2 % 2, dp % 2

    def place(y_at, x_at, core_at):
        return y_at * 4 + x_at * 2 + core_at

    along = (z, z // 2 * 2 + 1 - z % 2, (z + 2) % 4, (1 - z // 2) * 2 + 1 - z % 2)
    return dp, z, y, x, core, place, along


def inner(z):
    return (z + 1) // 2 % 2


def mirror(z, other):
    return (z // 2 + other // 2) % 2 * 2 + (z + other) % 2


def nearness(z, other):
    k = mirror(z, other)
    return k + inner(z) * (k // 2) * (5 - 2 * k)


def by_nearness(z):
    far = z // 2 * 3
    near = 2 - z // 2
    return (z, z // 2 * 2 + 1 - z % 2, near, 3 - far)


def meet_all(devices, group):
    me = lax.axis_index("dp") * group + lax.axis_index("vocab")
    barrier = pltpu.get_barrier_semaphore()

    def signal(step, state):
        other = lax.rem(me + step, devices)
        pl.semaphore_signal(
            barrier, inc=1, device_id=(other // group, other % group), device_id_type=MESH
        )
        return state

    lax.fori_loop(1, devices, signal, 0)
    pl.semaphore_wait(barrier, devices - 1)
    return me


def to_all(source_of, target, send_sems, recv_sems, devices, group, me):
    def copy(step):
        other = lax.rem(me + step, devices)
        return pltpu.make_async_remote_copy(
            source_of(other),
            target.at[me],
            send_sems.at[step],
            recv_sems.at[step],
            device_id=(other // group, other % group),
            device_id_type=MESH,
        )

    def start():
        def one(step, state):
            copy(step).start()
            return state

        lax.fori_loop(1, devices, one, 0)

    def arrive():
        def one(step, state):
            source = lax.rem(me + devices - step, devices)
            pltpu.make_async_remote_copy(
                target.at[source],
                target.at[source],
                send_sems.at[step],
                recv_sems.at[step],
                device_id=(source // group, source % group),
                device_id_type=MESH,
            ).wait_recv()
            return state

        lax.fori_loop(1, devices, one, 0)

    def sent():
        def one(step, state):
            copy(step).wait_send()
            return state

        lax.fori_loop(1, devices, one, 0)

    return start, arrive, sent


ARRIVE, TAIL, TILE, BACK, MIDDLE, COLUMN = range(6)
ORDER = (
    (ARRIVE, 0, 1),
    (ARRIVE, 0, 2),
    (ARRIVE, 1, 0),
    (ARRIVE, 2, 0),
    (TILE, 1, 0),
    (TILE, 0, 2),
    (ARRIVE, 0, 3),
    (ARRIVE, 2, 2),
    (TAIL, 2, 1),
    (ARRIVE, 1, 2),
    (TAIL, 1, 1),
    (ARRIVE, 2, 1),
    (ARRIVE, 1, 1),
    (TILE, 0, 1),
    (TILE, 2, 1),
    (TAIL, 2, 2),
    (TAIL, 1, 2),
    (BACK, 2, 1),
    (ARRIVE, 3, 0),
    (BACK, 1, 0),
    (TILE, 1, 1),
    (TILE, 1, 2),
    (ARRIVE, 2, 3),
    (TAIL, 3, 2),
    (ARRIVE, 3, 2),
    (TILE, 2, 2),
    (ARRIVE, 3, 1),
    (ARRIVE, 1, 3),
    (TILE, 3, 2),
    (BACK, 3, 2),
    (BACK, 2, 2),
    (TAIL, 3, 1),
    (BACK, 1, 2),
    (TILE, 0, 3),
    (ARRIVE, 3, 3),
    (TAIL, 3, 3),
    (TAIL, 2, 3),
    (MIDDLE, 0, 2),
    (MIDDLE, 1, 2),
    (TAIL, 1, 3),
    (TILE, 3, 1),
    (BACK, 3, 1),
    (TILE, 3, 3),
    (BACK, 1, 1),
    (COLUMN, 1, 2),
    (COLUMN, 0, 2),
    (BACK, 3, 3),
    (TILE, 2, 3),
    (MIDDLE, 0, 1),
    (BACK, 2, 3),
    (TILE, 1, 3),
    (MIDDLE, 1, 3),
    (TILE, 3, 0),
    (BACK, 3, 0),
    (COLUMN, 0, 1),
    (BACK, 1, 3),
    (TILE, 2, 0),
    (COLUMN, 1, 3),
    (MIDDLE, 0, 3),
    (MIDDLE, 1, 1),
    (TILE, 0, 0),
    (MIDDLE, 0, 0),
    (MIDDLE, 1, 0),
    (COLUMN, 0, 3),
    (COLUMN, 1, 1),
    (BACK, 2, 0),
    (COLUMN, 0, 0),
    (COLUMN, 1, 0),
)


def of_four(values, at):
    low, high = at % 2, at // 2
    return (1 - high) * ((1 - low) * values[0] + low * values[1]) + high * (
        (1 - low) * values[2] + low * values[3]
    )


def live_rows(tile):
    return tile * 7 // 8


def counted_first(mask_row):
    size = mask_row.shape[1]
    square = (size, size)
    down = lax.broadcasted_iota(jnp.int32, square, 0)
    across = lax.broadcasted_iota(jnp.int32, square, 1)
    mask_col = col_of(mask_row)
    ahead = jnp.sum(jnp.where(down < across, mask_col, 0.0), axis=0, keepdims=True)
    count = jnp.sum(mask_row, axis=1, keepdims=True)
    places = jnp.where(mask_row > 0.0, ahead, count + across[:1].astype(jnp.float32) - ahead)
    return (down.astype(jnp.float32) == places).astype(jnp.float32).astype(jnp.bfloat16)


def head_kernel(table_rows, chunks, own, tab_a, turn_a, tab_b, turn_b, mean_out, lse_out, *refs):
    (
        tab,
        turn,
        score_a,
        score_b,
        total,
        hidden,
        part,
        part_lse,
        got,
        got_lse,
        load_sems,
        send_sems,
        recv_sems,
        back_send,
        back_recv,
    ) = refs
    dp, z, y, x, core, place, _ = position()
    along = by_nearness(z)
    pad_rows = tab_a.shape[0]
    width, tile = own.shape[1], own.shape[0]
    tiles = [event[1:] for event in ORDER if event[0] == TILE]
    slot = {at: index for index, at in enumerate(tiles)}
    dev_x, dev_y = (place(y, 1 - x, core), z), (place(1 - y, x, core), z)
    dev_z = [(dp, along[k]) for k in range(4)]
    peers = [dev_x, dev_y] + dev_z[1:]
    loads = []
    for at, (source, target) in enumerate(
        (
            (own, hidden.at[slot[0, 0]]),
            (tab_a, tab.at[pl.ds(0, pad_rows)]),
            (tab_b, tab.at[pl.ds(pad_rows, pad_rows)]),
            (turn_a, turn.at[:, pl.ds(0, pad_rows)]),
            (turn_b, turn.at[:, pl.ds(pad_rows, pad_rows)]),
        )
    ):
        copy = pltpu.make_async_copy(source, target, load_sems.at[at])
        copy.start()
        loads.append(copy)
    for q, k in tiles:
        if (q, k) != (0, 0):
            hidden[slot[q, k], live_rows(tile) :] = jnp.zeros(
                (tile - live_rows(tile), width), jnp.bfloat16
            )
    barrier = pltpu.get_barrier_semaphore()
    for peer in peers:
        pl.semaphore_signal(barrier, inc=1, device_id=peer, device_id_type=MESH)
    pl.semaphore_wait(barrier, len(peers))
    loads[0].wait()

    sent = []
    live = live_rows(tile)
    body = live - tile * 2 // 16
    cut = body // 32 * 16 + body % 32

    def span(k, half=None):
        last, middle = (body, cut) if k else (live, live // 2)
        begin, end = ((0, last), (0, middle), (middle, last))[0 if half is None else 1 + half]
        return pl.ds(begin, end - begin)

    def give(source, target, peer, half=None):
        rows = span(target[1], half)
        copy = pltpu.make_async_remote_copy(
            hidden.at[slot[source], rows],
            hidden.at[slot[target], rows],
            send_sems.at[len(sent)],
            recv_sems.at[slot[target] + (16 if half == 1 else 0)],
            device_id=peer,
            device_id_type=MESH,
        )
        sent.append(copy)
        return copy

    def give_along(q, k, upward):
        there = z + 1 if upward else z - 1
        target = of_four([slot[q, at] for at in range(4)], nearness(there, along[k]))
        rows = pl.ds(body, live - body) if q else pl.ds(0, live)
        return pltpu.make_async_remote_copy(
            hidden.at[slot[q, k], rows],
            hidden.at[target, rows],
            send_sems.at[24 + 8 * q + k + 4 * (not upward and k == 0)],
            recv_sems.at[target + (32 if q else 0)],
            device_id=(dp, there),
            device_id_type=MESH,
        )

    def pass_along(q, k, act):
        @pl.when((along[k] <= z) & (z < 3))
        def _():
            act(give_along(q, k, True))

        @pl.when((along[k] >= z) & (z > 0))
        def _():
            act(give_along(q, k, False))

    def start_all(copies):
        for copy in copies:
            copy.start()

    forwards = {}
    for k in range(4):
        forwards[0, k] = [give((0, k), (1, k), dev_x), give((0, k), (2, k), dev_y)]
        forwards[1, k] = [give((1, k), (3, k), dev_y, 1)]
        forwards[2, k] = [give((2, k), (3, k), dev_x, 0)]
        forwards[3, k] = []
    pass_along(0, 0, lambda copy: copy.start())
    start_all(forwards[0, 0])

    def wait_rows(q, k, rows, at):
        there = hidden.at[slot[q, k], rows]
        pltpu.make_async_remote_copy(
            there,
            there,
            send_sems.at[0],
            recv_sems.at[slot[q, k] + at],
            device_id=dev_x,
            device_id_type=MESH,
        ).wait_recv()

    def arrive(q, k):
        if q == 3:
            wait_rows(q, k, span(k, 0), 0)
            wait_rows(q, k, span(k, 1), 16)
        else:
            wait_rows(q, k, span(k) if q else pl.ds(0, live), 0)
        if q == 0 or k == 0:
            pass_along(q, k, lambda copy: copy.start())
        start_all(forwards[q, k])

    def tail_comes(q, k):
        wait_rows(q, k, pl.ds(body, live - body), 32)
        pass_along(q, k, lambda copy: copy.start())

    back_sent = []

    def half_rows(half):
        return pl.ds(half * (width // 2), width // 2)

    def back_copies(number, q, k, half, landing, peer):
        if q == 0:
            landing = landing + 2 * mirror(z, along[k])
        return [
            pltpu.make_async_remote_copy(
                source,
                target,
                back_send.at[kind, number],
                back_recv.at[kind, landing],
                device_id=peer,
                device_id_type=MESH,
            )
            for kind, (source, target) in enumerate(
                (
                    (part.at[slot[q, k], half_rows(half)], got.at[landing]),
                    (part_lse.at[2 * slot[q, k] + half], got_lse.at[landing]),
                )
            )
        ]

    def back(*what):
        start_all(back_copies(len(back_sent), *what))
        back_sent.append(what)

    def back_wait(landing):
        for kind, target in enumerate((got, got_lse)):
            pltpu.make_async_remote_copy(
                target.at[landing],
                target.at[landing],
                back_send.at[kind, 0],
                back_recv.at[kind, landing],
                device_id=dev_x,
                device_id_type=MESH,
            ).wait_recv()

    def merge(q, k, half, landings):
        at = slot[q, k]
        for landing in landings:
            back_wait(landing)
        levels = [part_lse[2 * at + half]] + [got_lse[landing] for landing in landings]
        top = levels[0]
        for level in levels[1:]:
            top = jnp.maximum(top, level)
        shares = [jnp.exp(level - top) for level in levels]
        whole = sum(shares[1:], shares[0])
        shares = [share / whole for share in shares]
        part_lse[2 * at + half] = top + jnp.log(whole)
        begin = half * (width // 2)

        def rows(step, state):
            here = pl.ds(pl.multiple_of(step * 128, 128), 128)
            mine = pl.ds(pl.multiple_of(begin + step * 128, 128), 128)
            mixed = part[at, mine].astype(jnp.float32) * shares[0]
            for landing, share in zip(landings, shares[1:], strict=True):
                mixed += got[landing, here].astype(jnp.float32) * share
            part[at, mine] = mixed.astype(jnp.bfloat16)
            return state

        lax.fori_loop(0, width // 256, rows, 0)

    def go_back(q, k):
        if q == 3:
            back(3, k, 0, 16 + 2 * k, dev_x)
            back(3, k, 1, 17 + 2 * k, dev_y)
        elif q == 1:
            back(1, k, 0, 2 * k, dev_x)
        else:
            back(2, k, 1, 9 + 2 * k, dev_y)

    def merge_middle(half, k):
        q = 1 if half else 2
        merge(q, k, half, [16 + 2 * k + half])
        if half:
            back(1, k, 1, 1 + 2 * k, dev_x)
        else:
            back(2, k, 0, 8 + 2 * k, dev_y)

    def merge_column(half, k):
        merge(0, k, half, [2 * k + half, 8 + 2 * k + half])
        if k:
            back(0, k, half, 22 + half, dev_z[k])

    acts = {ARRIVE: arrive, TAIL: tail_comes, BACK: go_back, MIDDLE: merge_middle, COLUMN: merge_column}
    groups = [[]]
    for event in ORDER:
        if event[0] == TILE:
            groups.append([])
        else:
            groups[-1].append(event)

    def work(group):
        for event in group:
            acts[event[0]](*event[1:])

    def events_before(t, parity):
        for at in range(parity, 16, 2):
            if groups[at]:

                @pl.when(t == at)
                def _(at=at):
                    work(groups[at])

    for copy in loads[1:]:
        copy.wait()
    starts = [sum(chunks[:at]) for at in range(len(chunks))]
    low = jnp.full((8, tile), -jnp.inf, jnp.float32)

    def scores_of(rows, at, score, top):
        begin, size = starts[at], chunks[at]
        values = dot_nt(tab[begin : begin + size], rows)
        score[begin : begin + size] = values
        cuts = [(begin, begin + size, False)]
        for half in range(2):
            edge = half * pad_rows + table_rows // 8 * 8
            stop = (half + 1) * pad_rows
            if begin <= edge < begin + size:
                cuts = [(begin, edge, False), (edge, min(stop, begin + size), True)]
                if stop < begin + size:
                    cuts.append((stop, begin + size, False))
        for first_row, last, masked in cuts:
            if first_row == last:
                continue
            cut = values[first_row - begin : last - begin]
            if masked:
                row = lax.broadcasted_iota(jnp.int32, cut.shape, 0)
                cut = jnp.where(row < table_rows % 8, cut, masked_value)
                score[first_row:last] = cut
            top = jnp.maximum(top, jnp.max(cut.reshape(-1, 8, tile), axis=0))
        return top

    def half_step(t, parity, score, score_next, top):
        events_before(t, parity)
        rows = hidden[jnp.minimum(t + 1, 15)]
        peak = jnp.max(top, axis=0, keepdims=True)
        summed = jnp.zeros((8, tile), jnp.float32)
        top_next = low
        for at in range(len(chunks)):
            begin, size = starts[at], chunks[at]
            expo = jnp.exp(score[begin : begin + size] - peak)
            summed += jnp.sum(expo.reshape(-1, 8, tile), axis=0)
            top_next = scores_of(rows, at, score_next, top_next)
            product = dot_without_transpose(
                turn[:, begin : begin + size], expo.astype(jnp.bfloat16)
            )
            if at == 0:
                total[...] = product
            else:
                total[...] += product
        denominator = jnp.sum(summed, axis=0, keepdims=True)
        part[t] = (total[...] * (1.0 / denominator)).astype(jnp.bfloat16)
        level = peak + jnp.log(denominator)
        part_lse[2 * t] = level
        part_lse[2 * t + 1] = level
        return top_next

    if tiles[0] != (0, 0):
        until = 1 + max(at for at, event in enumerate(groups[0]) if event[1:] == tiles[0])
        work(groups[0][:until])
        del groups[0][:until]
    top = low
    for at in range(len(chunks)):
        top = scores_of(hidden[0], at, score_a, top)

    def two_steps(step, top):
        top = half_step(2 * step, 0, score_a, score_b, top)
        return half_step(2 * step + 1, 1, score_b, score_a, top)

    lax.fori_loop(0, 8, two_steps, top)
    work(groups[16])
    home = slot[0, 0]
    merge(0, 0, 0, [24, 26, 28])
    merge(0, 0, 1, [25, 27, 29])
    mean_out[...] = part[home]
    lse_out[...] = part_lse[2 * home]
    for q in range(4):
        for k in range(4):
            pass_along(q, k, lambda copy: copy.wait_send())
    for copy in sent:
        copy.wait_send()
    for number, what in enumerate(back_sent):
        for copy in back_copies(number, *what):
            copy.wait_send()


def head(final_state, table_rows, tables):
    tile, width = final_state.shape
    pad_rows = tables[0].shape[0]
    both = 2 * pad_rows
    chunks = [both // 256 // 4 * 256] * 4
    chunks[0] += both - sum(chunks)
    anywhere, vmem = pl.BlockSpec(memory_space=pl.ANY), pl.BlockSpec(memory_space=pltpu.VMEM)
    dma = pltpu.SemaphoreType.DMA
    return pl.pallas_call(
        partial(head_kernel, table_rows, chunks),
        out_shape=[
            jax.ShapeDtypeStruct((width, tile), jnp.bfloat16),
            jax.ShapeDtypeStruct((1, tile), jnp.float32),
        ],
        in_specs=[anywhere] * 5,
        out_specs=[vmem] * 2,
        scratch_shapes=[
            pltpu.VMEM((both, width), jnp.bfloat16),
            pltpu.VMEM((width, both), jnp.bfloat16),
            pltpu.VMEM((both, tile), jnp.float32),
            pltpu.VMEM((both, tile), jnp.float32),
            pltpu.VMEM((width, tile), jnp.float32),
            pltpu.VMEM((16, tile, width), jnp.bfloat16),
            pltpu.VMEM((16, width, tile), jnp.bfloat16),
            pltpu.VMEM((32, 1, tile), jnp.float32),
            pltpu.VMEM((30, width // 2, tile), jnp.bfloat16),
            pltpu.VMEM((30, 1, tile), jnp.float32),
            dma((5,)),
            dma((56,)),
            dma((48,)),
            dma((2, 30)),
            dma((2, 30)),
        ],
        name="head",
        compiler_params=pltpu.CompilerParams(
            collective_id=2, has_side_effects=True, vmem_limit_bytes=62 * 2**20
        ),
    )(final_state, *tables)


def sum_kernel(gathered, whole, numbers, other_half, mine, parts, piece, core_sems, sems, back_sems):
    dp, z, y, x, core, place, _ = position()
    half, plane = parts.shape[0], (y * 2 + x) * 4 + z
    width = whole.shape[2]
    partner = (place(y, x, 1 - core), z)

    def there(step, back=False):
        other = lax.rem(plane + (half - step if back else step), half)
        column = other // 4
        return other, (place(column // 2, column % 2, core), other % 4)

    barrier = pltpu.get_barrier_semaphore()

    def greet(step, state):
        pl.semaphore_signal(barrier, inc=1, device_id=there(step)[1], device_id_type=MESH)
        return state

    lax.fori_loop(1, half, greet, 0)
    pl.semaphore_signal(barrier, inc=1, device_id=partner, device_id_type=MESH)
    pl.semaphore_wait(barrier, half)

    def to_core(source, target, at):
        return pltpu.make_async_remote_copy(
            source,
            target,
            core_sems.at[2 * at],
            core_sems.at[2 * at + 1],
            device_id=partner,
            device_id_type=MESH,
        )

    first_swap = to_core(gathered.at[pl.ds((1 - core) * half, half)], other_half, 0)
    first_swap.start()
    first_swap.wait_recv()
    mine[...] = gathered[pl.ds(core * half, half)] + other_half[...]
    parts[pl.ds(plane, 1)] = mine[pl.ds(plane, 1)]

    def exchange(copy, target, used):
        def start(step, state):
            copy(step).start()
            return state

        def arrive(step, state):
            source, peer = there(step, True)
            pltpu.make_async_remote_copy(
                target(source),
                target(source),
                used.at[0, step],
                used.at[1, step],
                device_id=peer,
                device_id_type=MESH,
            ).wait_recv()
            return state

        lax.fori_loop(1, half, start, 0)
        lax.fori_loop(1, half, arrive, 0)

    def part_copy(step):
        other, peer = there(step)
        return pltpu.make_async_remote_copy(
            mine.at[other],
            parts.at[plane],
            sems.at[0, step],
            sems.at[1, step],
            device_id=peer,
            device_id_type=MESH,
        )

    exchange(part_copy, lambda source: parts.at[source], sems)
    summed = parts[0]
    for source in range(1, half):
        summed += parts[source]
    row = core * half + plane
    piece[...] = summed[:, :width]
    whole[pl.ds(row, 1)] = summed[None, :, :width]
    numbers[...] = summed[:, width:]

    def back_copy(step):
        return pltpu.make_async_remote_copy(
            piece,
            whole.at[row],
            back_sems.at[0, step],
            back_sems.at[1, step],
            device_id=there(step)[1],
            device_id_type=MESH,
        )

    exchange(back_copy, lambda source: whole.at[core * half + source], back_sems)
    rows = whole.at[pl.ds(core * half, half)]
    second_swap = to_core(rows, rows, 1)
    second_swap.start()
    to_core(rows, whole.at[pl.ds((1 - core) * half, half)], 1).wait_recv()
    first_swap.wait_send()
    second_swap.wait_send()

    def sent(step, state):
        part_copy(step).wait_send()
        back_copy(step).wait_send()
        return state

    lax.fori_loop(1, half, sent, 0)


def update_kernel(whole, numbers, adapter_rows, down_momentum, up_momentum, *refs):
    outs, (stage,) = refs[:9], refs[9:]
    mom_down, mom_up, new_down, new_up, low_down, low_up, loss_out, count_out, norm_out = outs
    z = lax.axis_index("vocab")
    weights = adapter_rows[...]
    devices, width = weights.shape
    gradient = whole[...].reshape(devices, width)
    squares = jnp.sum(jnp.sum(gradient * gradient, axis=0, keepdims=True), axis=1, keepdims=True)
    norm = jnp.sqrt(squares)
    factor = jnp.minimum(1.0, clip_level / (norm + 1e-06))
    state = momentum * stack_rows(down_momentum, up_momentum) + factor * gradient
    adapters, rank, share = mom_up.shape
    columns = pl.ds(pl.multiple_of(z * share, share), share)

    def give(values, *targets):
        stage[...] = values
        mine = stage[:, columns]
        for j in range(2 * adapters):
            for pair in targets:
                out = pair[j // adapters]
                out[j % adapters] = mine[j * rank : (j + 1) * rank].astype(out.dtype)

    give(state, (mom_down, mom_up))
    square = (devices, devices)
    row = lax.broadcasted_iota(jnp.int32, square, 0)
    column = lax.broadcasted_iota(jnp.int32, square, 1)
    blocks = row // rank == column // rank

    def gram_of(matrix):
        return jnp.where(blocks, dot_nt(matrix, matrix, highest_precision), 0.0)

    grams = gram_of(state)
    diagonal = jnp.sum(jnp.where(row == column, grams, 0.0), axis=0, keepdims=True)
    traces = jnp.sum(jnp.where(blocks, diagonal, 0.0), axis=1, keepdims=True)
    sizes = jnp.sqrt(traces) + 1e-07
    state = state / sizes
    grams = grams / (sizes * sizes)
    for turn_index in range(5):
        if turn_index:
            grams = gram_of(state)
        poly = coef_b * grams + coef_c * dot_without_transpose(grams, grams, highest_precision)
        state = coef_a * state + dot_without_transpose(poly, state, highest_precision)
    give(weights - learning_rate * state, (new_down, new_up), (low_down, low_up))
    loss_out[...] = numbers[:, 0:1]
    count_out[...] = numbers[:, 1:2]
    norm_out[...] = norm


def halves_of(values):
    high = values.astype(jnp.bfloat16)
    return high, (values - high.astype(jnp.float32)).astype(jnp.bfloat16)


def stacked_halves(values):
    return jnp.concatenate(halves_of(values), axis=0)


def added_halves(values):
    rows = values.shape[0] // 2
    return values[:rows] + values[rows:]


def dot_tn(left_side, right_side):
    return dot_first(left_side, right_side)


def normal(values):
    center = values - jnp.mean(values, axis=-1, keepdims=True)
    spread = lax.rsqrt(jnp.mean(center * center, axis=-1, keepdims=True) + ln_eps)
    return center * spread, spread


def normal_back(values, gain, gradient):
    unit, spread = normal(values)
    pulled = gradient * gain
    along = jnp.mean(pulled * unit, axis=-1, keepdims=True)
    return spread * (pulled - jnp.mean(pulled, axis=-1, keepdims=True) - unit * along)


def sequence_places(lengths, rows):
    col = lax.broadcasted_iota(jnp.int32, (rows, 1), 0)
    row = lax.broadcasted_iota(jnp.int32, (1, rows), 1)
    segment_col, segment_row = jnp.zeros_like(col), jnp.zeros_like(row)
    start_col = jnp.zeros_like(col)
    end = 0
    for at in range(lengths.shape[1]):
        length = lengths[0, at]
        end = end + length
        segment_col += (col >= end).astype(jnp.int32)
        segment_row += (row >= end).astype(jnp.int32)
        start_col += jnp.where(col >= end, length, 0)
    allowed = (segment_col == segment_row) & (row <= col)
    return col - start_col, allowed


def pairs_of(width):
    return width // (2 * HEAD_DIM)


def pair_at(pair):
    return pl.ds(pl.multiple_of(pair * 2 * HEAD_DIM, 2 * HEAD_DIM), 2 * HEAD_DIM)


def head_lanes(rows):
    return lax.broadcasted_iota(jnp.int32, (rows, 2 * HEAD_DIM), 1) < HEAD_DIM


def first_part(embedded, positions, lengths, gains, shifts, x0, h1):
    rows = x0.shape[0]
    place_col, allowed = sequence_places(lengths, rows)
    spots = lax.broadcasted_iota(jnp.int32, (rows, positions.shape[0]), 1)
    hot = (place_col == spots).astype(jnp.float32).astype(jnp.bfloat16)
    x0[...] = embedded[...] + dot_without_transpose(hot, positions[...])
    unit, _ = normal(x0[...])
    h1[...] = (unit * gains[0:1] + shifts[0:1]).astype(jnp.bfloat16)
    return allowed


def adapter_in(adapters, inputs):
    return added_halves(dot_nt(stacked_halves(adapters), inputs))


def adapter_out(inner, outer):
    high, low = halves_of(inner)
    top, rest = halves_of(outer)
    return adapter_scale * dot_tn(
        jnp.concatenate([high, high, low], axis=0), jnp.concatenate([top, rest, top], axis=0)
    )


def ranks(which, shape):
    return lax.broadcasted_iota(jnp.int32, shape, 0) // 4 == which


def project_part(h1, weight, bias, adapters, inner, joined):
    width = h1.shape[1]
    step = 512
    half = adapters.shape[0] // 2
    inner[...] = adapter_in(adapters[:half], h1[...])
    for which in range(3):

        def columns(at, state):
            here = pl.ds(pl.multiple_of(at * step, step), step)
            there = pl.ds(pl.multiple_of(which * width + at * step, step), step)
            outer = jnp.where(ranks(which, (half, step)), adapters[half:, here], 0.0)
            joined[:, there] = (
                dot_without_transpose(h1[...], weight[:, there])
                + bias[:, there]
                + adapter_out(inner[...], outer)
            ).astype(jnp.bfloat16)
            return state

        lax.fori_loop(0, width // step, columns, 0)


def attend_part(joined, allowed, probs, mixed):
    rows, width = mixed.shape
    lanes = head_lanes(rows)

    def pair_step(pair, state):
        query = joined[:, pair_at(pair)]
        keys = joined[:, pair_at(pairs_of(width) + pair)]
        values = joined[:, pair_at(2 * pairs_of(width) + pair)]
        outs = []
        for side in range(2):
            mine = lanes if side == 0 else ~lanes
            scores = dot_nt(jnp.where(mine, query, jnp.zeros_like(query)), keys) * score_scale
            scores = jnp.where(allowed, scores, masked_value)
            expo = jnp.exp(scores - jnp.max(scores, axis=-1, keepdims=True))
            chances = (expo / jnp.sum(expo, axis=-1, keepdims=True)).astype(jnp.bfloat16)
            probs[2 * pair + side] = chances
            outs.append(dot_without_transpose(chances, values))
        mixed[:, pair_at(pair)] = jnp.where(lanes, outs[0], outs[1]).astype(jnp.bfloat16)
        return state

    lax.fori_loop(0, pairs_of(width), pair_step, 0)


def output_part(x0, mixed, weight, bias, adapters, inner, gains, shifts, x1, h2):
    half = adapters.shape[0] // 2
    width = mixed.shape[1]
    here = ranks(3, inner.shape)
    fresh = adapter_in(adapters[:half], mixed[...])
    inner[...] = jnp.where(here, fresh, inner[...])
    outer = jnp.where(ranks(3, (half, width)), adapters[half:], 0.0)
    x1[...] = (
        x0[...]
        + dot_without_transpose(mixed[...], weight[...])
        + bias[:, 3 * width : 4 * width]
        + adapter_out(inner[...], outer)
    )
    unit, _ = normal(x1[...])
    h2[...] = (unit * gains[1:2] + shifts[1:2]).astype(jnp.bfloat16)


def up_part(h2, weight, bias, active, slope):
    width = h2.shape[1]
    step = 512

    def columns(at, state):
        here = pl.ds(pl.multiple_of(at * step, step), step)
        there = pl.ds(pl.multiple_of(4 * width + at * step, step), step)
        z = dot_without_transpose(h2[...], weight[:, here]) + bias[:, there]
        root = 0.7978845608028654
        square = z * z
        tanh = jnp.tanh(root * z * (1.0 + 0.044715 * square))
        half = 0.5 * (1.0 + tanh)
        active[:, here] = (z * half).astype(jnp.bfloat16)
        slope[:, here] = (
            half + 0.5 * z * (1.0 - tanh * tanh) * (root * (1.0 + 3 * 0.044715 * square))
        ).astype(jnp.bfloat16)
        return state

    lax.fori_loop(0, weight.shape[1] // step, columns, 0)


def down_part(begins, blocks, total, active, weight, bias, x2):
    hidden, width = weight.shape
    step = 256
    size = hidden // (2 * len(blocks))

    def columns(at, state):
        here = pl.ds(pl.multiple_of(at * step, step), step)
        there = pl.ds(pl.multiple_of(4 * width + hidden + at * step, step), step)
        values = total[:, here]
        if begins:
            values += bias[:, there]
        for block in blocks:
            units = pl.ds(pl.multiple_of(block * size, size), size)
            values += dot_without_transpose(active[:, units], weight[units, here])
        x2[:, here] = values
        return state

    lax.fori_loop(0, width // step, columns, 0)


def last_norm(x2, gains, shifts, final):
    unit, _ = normal(x2[...])
    final[...] = (unit * gains[2:3] + shifts[2:3]).astype(jnp.bfloat16)


def turn_rows(source, target):
    width = source.shape[0]

    def rows(at, state):
        here = pl.ds(pl.multiple_of(at * 128, 128), 128)
        target[:, here] = source[here].astype(jnp.float32).T.astype(target.dtype)
        return state

    lax.fori_loop(0, width // 128, rows, 0)


def backward_kernel(
    mean_rows,
    log_total,
    mask_row,
    target_rows,
    table_sum,
    gains,
    adapters,
    final,
    h1_far,
    joined_far,
    probs_far,
    mixed_far,
    inner,
    x1_far,
    slope_far,
    x2,
    w_out,
    w_up,
    w_down,
    gathered,
    work,
    dx2,
    da,
    dz,
    dmix,
    pulls,
    out_here,
    up_here,
    down_here,
    h1,
    joined,
    probs,
    mixed,
    x1,
    slope,
    sems,
):
    loads = []
    for at, (source, target) in enumerate(
        (
            (w_down, down_here),
            (slope_far, slope),
            (w_up, up_here),
            (x1_far, x1),
            (w_out, out_here),
            (mixed_far, mixed),
            (joined_far, joined),
            (probs_far, probs),
            (h1_far, h1),
        )
    ):
        copy = pltpu.make_async_copy(source, target, sems.at[at])
        copy.start()
        loads.append(copy)
    rows, width = x1.shape
    half = adapters.shape[0] // 2
    hidden = slope.shape[1]
    turn_rows(mean_rows, work)
    mask_col = col_of(mask_row[...])
    unsort = counted_first(mask_row[...])
    mean = dot_tn(unsort, work[...].astype(jnp.bfloat16))
    pulled = (1.0 - smooth) * target_rows[...] + (smooth / V) * table_sum[...]
    row_dots = jnp.sum(final[...].astype(jnp.float32) * pulled, axis=1, keepdims=True)
    count = jnp.sum(mask_row[...], axis=1, keepdims=True)
    spots = lax.broadcasted_iota(jnp.int32, mask_row.shape, 1).astype(jnp.float32)
    loss = jnp.sum(
        jnp.where(spots < count, log_total[...], 0.0), axis=1, keepdims=True
    ) - jnp.sum(mask_col * row_dots, axis=0, keepdims=True)
    lanes = lax.broadcasted_iota(jnp.int32, (1, 128), 1)
    numbers = jnp.where(lanes == 0, loss, jnp.where(lanes == 1, count, 0.0))
    dx2[...] = normal_back(x2[...], gains[2:3], mask_col * (mean - pulled))
    da[...] = dx2[...].astype(jnp.bfloat16)
    loads[0].wait()
    loads[1].wait()
    step = 512

    def hidden_columns(at, state):
        here = pl.ds(pl.multiple_of(at * step, step), step)
        dz[:, here] = (
            dot_nt(da[...], down_here[here]) * slope[:, here].astype(jnp.float32)
        ).astype(jnp.bfloat16)
        return state

    lax.fori_loop(0, hidden // step, hidden_columns, 0)
    loads[2].wait()
    loads[3].wait()

    def columns(at, state):
        here = pl.ds(pl.multiple_of(at * 256, 256), 256)
        work[:, here] = dot_nt(dz[...], up_here[here])
        return state

    lax.fori_loop(0, width // 256, columns, 0)
    dx1 = dx2[...] + normal_back(x1[...], gains[1:2], work[...])
    da[...] = dx1.astype(jnp.bfloat16)
    loads[4].wait()
    loads[5].wait()
    upper = stacked_halves(adapters[half:])
    inner_halves = stacked_halves(inner[...])

    def adapter_grads(which, gradient, inputs):
        up_grad = adapter_scale * added_halves(dot_without_transpose(inner_halves, gradient))
        back = adapter_scale * added_halves(dot_nt(upper, gradient))
        back = jnp.where(ranks(which, back.shape), back, 0.0)
        down_grad = added_halves(dot_without_transpose(stacked_halves(back), inputs))
        keep = ranks(which, up_grad.shape)
        return back, down_grad, jnp.where(keep, up_grad, 0.0)

    back, down_total, up_total = adapter_grads(3, da[...], mixed[...])
    dmix[...] = (
        dot_nt(da[...], out_here[...]) + adapter_out(back, adapters[:half]) / adapter_scale
    ).astype(jnp.bfloat16)
    lane_mask = head_lanes(rows)
    for copy in loads[6:]:
        copy.wait()

    def pair_step(pair, state):
        query = joined[:, pair_at(pair)]
        keys = joined[:, pair_at(pairs_of(width) + pair)]
        values = joined[:, pair_at(2 * pairs_of(width) + pair)]
        pull = dmix[:, pair_at(pair)]
        outs = []
        for side in range(2):
            mine = lane_mask if side == 0 else ~lane_mask
            chances = probs[2 * pair + side]
            wide = chances.astype(jnp.float32)
            reach = dot_nt(jnp.where(mine, pull, jnp.zeros_like(pull)), values)
            slide = wide * (reach - jnp.sum(wide * reach, axis=-1, keepdims=True))
            slide = slide.astype(jnp.bfloat16)
            outs.append(
                (
                    dot_without_transpose(slide, keys) * score_scale,
                    dot_tn(slide, query) * score_scale,
                    dot_tn(chances, pull),
                )
            )
        for which in range(3):
            both = jnp.where(lane_mask, outs[0][which], outs[1][which])
            pulls[:, pair_at(which * pairs_of(width) + pair)] = both.astype(jnp.bfloat16)
        return state

    lax.fori_loop(0, pairs_of(width), pair_step, 0)
    for which in range(3):
        _, down_part_grad, up_part_grad = adapter_grads(
            which, pulls[:, which * width : (which + 1) * width], h1[...]
        )
        down_total += down_part_grad
        up_total += up_part_grad
    grads = jnp.concatenate([down_total, up_total], axis=0)
    numbers = jnp.broadcast_to(numbers, (2 * half, 128))
    gathered[...] = jnp.concatenate([grads, numbers], axis=1).reshape(2 * half, 1, width + 128)


def backward(mean_rows, log_total, mask, target_rows, table_sum, gains, adapters, kept, weights):
    rows = mask.shape[0]
    width = target_rows.shape[1]
    hidden = weights[2].shape[0]
    low, full = jnp.bfloat16, jnp.float32
    anywhere, vmem = pl.BlockSpec(memory_space=pl.ANY), pl.BlockSpec(memory_space=pltpu.VMEM)
    return pl.pallas_call(
        backward_kernel,
        out_shape=jax.ShapeDtypeStruct((adapters.shape[0], 1, width + 128), full),
        in_specs=[vmem] * 8 + [anywhere] * 4 + [vmem, anywhere, anywhere, vmem] + [anywhere] * 3,
        out_specs=vmem,
        scratch_shapes=[
            pltpu.VMEM((rows, width), full),
            pltpu.VMEM((rows, width), full),
            pltpu.VMEM((rows, width), low),
            pltpu.VMEM((rows, hidden), low),
            pltpu.VMEM((rows, width), low),
            pltpu.VMEM((rows, 3 * width), low),
        ]
        + [pltpu.VMEM(w.shape, low) for w in weights]
        + [pltpu.VMEM(value.shape, value.dtype) for value in kept[1:5] + kept[6:8]]
        + [pltpu.SemaphoreType.DMA((9,))],
        name="backward",
        compiler_params=pltpu.CompilerParams(vmem_limit_bytes=60 * 2**20),
    )(
        mean_rows,
        log_total,
        mask[None, :],
        target_rows,
        table_sum,
        gains,
        adapters,
        *kept,
        *weights,
    )


def update(gathered, adapters, down_momentum, up_momentum):
    group = lax.axis_size("vocab")
    devices = lax.axis_size("dp") * group
    width = adapters.shape[1]
    low, full = jnp.bfloat16, jnp.float32
    vmem = pl.BlockSpec(memory_space=pltpu.VMEM)
    dma = pltpu.SemaphoreType.DMA
    shape = jax.ShapeDtypeStruct
    share = up_momentum.shape[:2] + (width // group,)
    half = devices // 2
    message = gathered.shape[1:]
    whole, numbers = pl.pallas_call(
        sum_kernel,
        out_shape=[shape((devices, 1, width), full), shape((1, 128), full)],
        in_specs=[vmem],
        out_specs=[vmem] * 2,
        scratch_shapes=[
            pltpu.VMEM((half,) + message, full),
            pltpu.VMEM((half,) + message, full),
            pltpu.VMEM((half,) + message, full),
            pltpu.VMEM((1, width), full),
            dma((4,)),
            dma((2, half)),
            dma((2, half)),
        ],
        name="sum_gradients",
        compiler_params=pltpu.CompilerParams(collective_id=3, has_side_effects=True),
    )(gathered)
    return pl.pallas_call(
        update_kernel,
        out_shape=[shape(share, full)] * 4 + [shape(share, low)] * 2 + [shape((1, 1), full)] * 3,
        in_specs=[vmem] * 5,
        out_specs=[vmem] * 9,
        scratch_shapes=[pltpu.VMEM((devices, width), full)],
        name="update",
    )(whole, numbers, adapters, jnp.swapaxes(down_momentum, 1, 2), up_momentum)


def col_of(row):
    size = row.shape[1]
    square = (size, size)
    same = lax.broadcasted_iota(jnp.int32, square, 0) == lax.broadcasted_iota(jnp.int32, square, 1)
    return jnp.sum(jnp.where(same, row, 0.0), axis=1, keepdims=True)


def stack_rows(down, up):
    return jnp.concatenate(
        [down[j] for j in range(down.shape[0])] + [up[j] for j in range(up.shape[0])], axis=0
    )


def pack_rows(positions, gains, shifts, biases):
    width, count = positions.shape
    square = (count, count)
    same = lax.broadcasted_iota(jnp.int32, square, 0) == lax.broadcasted_iota(jnp.int32, square, 1)
    places = dot_nt(same.astype(jnp.float32).astype(jnp.bfloat16), positions[...])
    span = count // 4
    places = jnp.concatenate([places[r * span : (r + 1) * span] for r in range(4)], axis=1)
    norms = jnp.concatenate(
        [
            gains[...].astype(jnp.float32),
            shifts[...].astype(jnp.float32),
            jnp.zeros((gains.shape[0], 128 - 2 * width), jnp.float32),
        ],
        axis=1,
    )
    flat = biases[...].astype(jnp.float32)
    flat = jnp.concatenate([flat, jnp.zeros((1, -flat.shape[1] % 128), jnp.float32)], axis=1)
    lines = [flat[:, r * 128 : (r + 1) * 128] for r in range(flat.shape[1] // 128)]
    rest = jnp.zeros((8 - gains.shape[0], 128), jnp.float32)
    tail = jnp.zeros((8 - len(lines), 128), jnp.float32)
    return jnp.concatenate([places, norms, rest] + lines + [tail], axis=0).astype(jnp.bfloat16)


def unpack_rows(packed, devices, width, span, norms, bias_size, positions, gains, shifts, bias):
    rows = packed.shape[0] // devices

    def group(j, state):
        devs = [
            packed[pl.ds(pl.multiple_of((4 * j + i) * rows, rows), rows)].astype(jnp.float32)
            for i in range(4)
        ]
        lanes = pl.ds(pl.multiple_of(j * 128, 128), 128)
        for r in range(4):
            block = [dev[:span, r * width : (r + 1) * width] for dev in devs]
            positions[r * span : (r + 1) * span, lanes] = jnp.concatenate(block, axis=1).astype(
                jnp.bfloat16
            )
        gains[:, lanes] = jnp.concatenate([dev[span : span + norms, :width] for dev in devs], axis=1)
        shifts[:, lanes] = jnp.concatenate(
            [dev[span : span + norms, width : 2 * width] for dev in devs], axis=1
        )
        flat = []
        for dev in devs:
            left = bias_size
            line = span + 8
            while left > 0:
                flat.append(dev[line : line + 1, : min(left, 128)])
                left -= 128
                line += 1
        bias[:, pl.ds(pl.multiple_of(j * 4 * bias_size, 128), 4 * bias_size)] = jnp.concatenate(
            flat, axis=1
        )
        return state

    lax.fori_loop(0, devices // 4, group, 0)


CAP, EXTRA = 16, 16
ASKED = 48
OWN, LINE, SIDE, DIAGONAL, CORE, ROWS = range(6)
ASK, SUM, ANSWER, TURN, UNPACK, EMBED, PROJECT, ATTEND, OUTPUT, UP, DOWN_NEAR, DOWN = range(6, 18)
FIRST_ORDER = (
    (OWN, 0, 0),
    (SUM, 0, 0),
    (OWN, 2, 0),
    (OWN, 1, 0),
    (ASK, 0, 0),
    (LINE, 2, 2),
    (LINE, 1, 1),
    (LINE, 1, 2),
    (ANSWER, 0, 0),
    (LINE, 2, 1),
    (OWN, 5, 0),
    (OWN, 3, 0),
    (LINE, 0, 1),
    (LINE, 2, 3),
    (LINE, 5, 2),
    (LINE, 5, 1),
    (LINE, 0, 2),
    (LINE, 5, 3),
    (SIDE, 2, 2),
    (SIDE, 0, 0),
    (LINE, 1, 3),
    (LINE, 0, 3),
    (SIDE, 2, 0),
    (SIDE, 0, 2),
    (SIDE, 0, 1),
    (SIDE, 5, 1),
    (SIDE, 5, 0),
    (SIDE, 5, 3),
    (SIDE, 2, 3),
    (LINE, 3, 1),
    (SIDE, 2, 1),
    (OWN, 4, 0),
    (ROWS, 0, 0),
    (DIAGONAL, 5, 1),
    (SIDE, 1, 0),
    (SIDE, 1, 1),
    (SIDE, 0, 3),
    (SIDE, 1, 3),
    (DIAGONAL, 2, 2),
    (DIAGONAL, 0, 0),
    (ROWS, 0, 2),
    (LINE, 3, 3),
    (SIDE, 1, 2),
    (SIDE, 5, 2),
    (DIAGONAL, 2, 1),
    (LINE, 3, 2),
    (DIAGONAL, 0, 2),
    (LINE, 4, 2),
    (ROWS, 0, 3),
    (DIAGONAL, 1, 3),
    (DIAGONAL, 2, 3),
    (DIAGONAL, 0, 3),
    (DIAGONAL, 2, 0),
    (DIAGONAL, 1, 2),
    (DIAGONAL, 5, 3),
    (DIAGONAL, 0, 1),
    (ROWS, 0, 1),
    (CORE, 0, 0),
    (DIAGONAL, 5, 2),
    (LINE, 4, 1),
    (DIAGONAL, 5, 0),
    (DIAGONAL, 1, 0),
    (SIDE, 3, 0),
    (DIAGONAL, 1, 1),
    (SIDE, 3, 1),
    (SIDE, 3, 3),
    (SIDE, 3, 2),
    (UNPACK, 0, 0),
    (CORE, 5, 0),
    (LINE, 4, 3),
    (TURN, 0, 0),
    (EMBED, 0, 0),
    (CORE, 1, 0),
    (PROJECT, 0, 0),
    (DIAGONAL, 3, 0),
    (ATTEND, 0, 0),
    (CORE, 2, 0),
    (SIDE, 4, 2),
    (SIDE, 4, 0),
    (DIAGONAL, 3, 3),
    (DIAGONAL, 3, 1),
    (SIDE, 4, 1),
    (DIAGONAL, 3, 2),
    (OUTPUT, 0, 0),
    (SIDE, 4, 3),
    (CORE, 3, 0),
    (UP, 0, 0),
    (DIAGONAL, 4, 2),
    (DIAGONAL, 4, 0),
    (DIAGONAL, 4, 3),
    (DIAGONAL, 4, 1),
    (DOWN_NEAR, 0, 0),
    (CORE, 4, 0),
    (DOWN, 0, 0),
)


def first_kernel(table_rows, devices, group, row_counts, *refs):
    (
        ids,
        targets,
        mask,
        lengths,
        position_own,
        gain_own,
        shift_own,
        bias_own,
        adapter_down,
        adapter_up,
        table_tail,
        table,
        *refs,
    ) = refs
    weights_own = refs[:4]
    refs = refs[4:]
    (
        flags,
        target_out,
        table_sum,
        gains_out,
        adapters_out,
        final,
        final_sorted,
        inner,
        table_mine,
        turned_mine,
        table_other,
        turned_other,
        h1_out,
        joined_out,
        probs_out,
        mixed_out,
        x1_out,
        slope_out,
        x2_out,
        out_kept,
        up_kept,
        down_kept,
        *refs,
    ) = refs
    (
        send_sems,
        recv_sems,
        local_sems,
        table_sems,
        ask_sems,
        row_sems,
        sum_sems,
        keep_sems,
        table_here,
        turned_here,
        selector,
        rows_out,
        rows_in,
        ask_out,
        ask_in,
        sum_out,
        sum_in,
        extra_out,
        extra,
        pack_here,
        packed,
        w_qkv,
        w_out,
        w_up,
        w_down,
        positions,
        shifts,
        bias,
        embedded,
        x0,
        h1,
        joined,
        probs,
        mixed,
        x1,
        h2,
        active,
        slope,
        x2,
    ) = refs
    arrays = (packed, w_qkv, w_out, w_up, w_down, extra)
    ins = (pack_here,) + tuple(weights_own) + (extra_out,)
    dp, z, y, x, core, place, _ = position()
    along = by_nearness(z)
    dp_x, dp_y = place(y, 1 - x, core), place(1 - y, x, core)
    dp_core, dp_diagonal = place(y, x, 1 - core), place(1 - y, 1 - x, core)
    z_peers = [(dp, along[k]) for k in (1, 2, 3)]
    near_peers = [(dp_x, z), (dp_y, z), (dp_core, z)]
    body_rows = table_rows // 16 * 16
    loads = [
        pltpu.make_async_copy(
            table.at[pl.ds(0, body_rows)], table_here.at[pl.ds(0, body_rows)], table_sems.at[0]
        )
    ]
    loads[0].start()
    ends = table_tail[...].astype(jnp.float32)[16 - table_rows + body_rows :]
    rest = jnp.zeros((table_here.shape[0] - table_rows, table_here.shape[1]), jnp.float32)
    table_here[body_rows:] = jnp.concatenate([ends, rest], axis=0).astype(jnp.bfloat16)
    pack_here[...] = pack_rows(position_own, gain_own, shift_own, bias_own)
    me = meet_all(devices, group)
    sent, kept, used = [], {}, [0] * len(arrays)

    def piece(which, block):
        rows = row_counts[which]
        return arrays[which].at[pl.ds(pl.multiple_of(block * rows, rows), rows)]

    def copy_to(which, block, peer, source, number):
        return pltpu.make_async_remote_copy(
            piece(which, block) if source is None else source,
            piece(which, block),
            send_sems.at[which, number],
            recv_sems.at[which, block],
            device_id=peer,
            device_id_type=MESH,
        )

    def send(which, block, peer, source=None):
        copy = copy_to(which, block, peer, source, used[which])
        used[which] += 1
        copy.start()
        sent.append(copy)

    def arrive(which, block):
        copy_to(which, block, z_peers[0], ins[which], 0).wait_recv()

    def pass_along(which, k, act):
        source = None if k else ins[which]
        block = dp * 4 + along[k]

        @pl.when((along[k] <= z) & (z < 3))
        def _():
            act(copy_to(which, block, (dp, z + 1), source, 34 + k))

        @pl.when((along[k] >= z) & (z > 0))
        def _():
            act(copy_to(which, block, (dp, z - 1), source, 38 + k))

    def own_near(which):
        for peer in near_peers:
            send(which, me, peer, ins[which])
        copy = pltpu.make_async_copy(ins[which], piece(which, me), local_sems.at[which])
        copy.start()
        kept[which] = copy

    def own(which, _):
        if which == 5:
            own_near(which)
        pass_along(which, 0, lambda copy: copy.start())

    def line(which, k):
        block = dp * 4 + along[k]
        arrive(which, block)
        pass_along(which, k, lambda copy: copy.start())
        for peer in near_peers:
            send(which, block, peer)

    def side(which, k):
        block_x, block_y = dp_x * 4 + along[k], dp_y * 4 + along[k]
        arrive(which, block_y)
        if k < 2:
            send(which, block_y, (dp_x, z))
        arrive(which, block_x)
        if k >= 2:
            send(which, block_x, (dp_y, z))
        send(which, block_y, (dp_core, z))
        send(which, block_x, (dp_core, z))

    def diagonal(which, k):
        block = dp_diagonal * 4 + along[k]
        arrive(which, block)
        send(which, block, (dp_core, z))

    def other_core(which, _):
        for y_at in range(2):
            for x_at in range(2):
                for z_at in range(4):
                    arrive(which, place(y_at, x_at, 1 - core) * 4 + z_at)
        if which in kept:
            kept.pop(which).wait()

    keeps = []

    def keep(source, target):
        copy = pltpu.make_async_copy(source, target, keep_sems.at[len(keeps)])
        copy.start()
        keeps.append(copy)

    for which in range(5):
        own_near(which)
    state = {}

    def ask():
        own_ids = ids[...].astype(jnp.float32)
        own_targets = jnp.where(mask[...] > 0, targets[...], ids[...]).astype(jnp.float32)
        ids_row = jnp.concatenate([own_ids, own_targets], axis=1)
        ids_col = jnp.concatenate([col_of(own_ids), col_of(own_targets)], axis=0)
        tokens = ids_row.shape[1]
        wide = (tokens, tokens)
        across = lax.broadcasted_iota(jnp.int32, wide, 1).astype(jnp.float32)
        down = lax.broadcasted_iota(jnp.int32, wide, 0).astype(jnp.float32)
        owner_row, owner_col = jnp.zeros_like(ids_row), jnp.zeros_like(ids_col)
        for device in range(1, devices):
            owner_row += (ids_row >= float(device * table_rows)).astype(jnp.float32)
            owner_col += (ids_col >= float(device * table_rows)).astype(jnp.float32)
        equal = ids_col == ids_row
        first_col = jnp.min(jnp.where(equal, across, float(tokens)), axis=1, keepdims=True)
        first_row = jnp.min(jnp.where(equal, down, float(tokens)), axis=0, keepdims=True)
        leads = jnp.where(first_row == across[:1], owner_row, -1.0)
        slot_col = jnp.sum(
            jnp.where((owner_col == leads) & (across < first_col), 1.0, 0.0),
            axis=1,
            keepdims=True,
        )
        takes = lax.broadcasted_iota(jnp.int32, (devices, tokens), 0).astype(jnp.float32) == leads
        local_row = jnp.where(takes, ids_row - owner_row * table_rows + 1.0, 0.0)
        lanes = lax.broadcasted_iota(jnp.int32, (tokens, 128), 1).astype(jnp.float32)
        asked = (
            dot_without_transpose(
                local_row, (slot_col == lanes).astype(jnp.float32), highest_precision
            )
            - 1.0
        )
        counted = jnp.sum(mask[...].astype(jnp.float32), axis=1, keepdims=True)
        over = (jnp.max(slot_col, axis=0, keepdims=True) >= float(ASKED)) | (
            counted > float(live_rows(mask.shape[1]))
        )
        ask_lanes = lax.broadcasted_iota(jnp.int32, (devices, 128), 1)
        asked = jnp.where(ask_lanes == 127, over.astype(jnp.float32), asked)
        ask_out[...] = asked.reshape(devices, 1, 128)
        ask_in[pl.ds(me, 1)] = ask_out[pl.ds(me, 1)]
        start, state["ask_arrive"], state["ask_sent"] = to_all(
            lambda other: ask_out.at[other],
            ask_in,
            ask_sems.at[0],
            ask_sems.at[1],
            devices,
            group,
            me,
        )
        start()
        state["ids_col"] = ids_col
        state["owner_col"] = owner_col
        state["slot_col"] = slot_col

    def table_total():
        for copy in loads:
            copy.wait()
        keep(table_here, table_mine)

        def add_up(step, total):
            return total + jnp.sum(
                table_here[pl.ds(pl.multiple_of(step * 128, 128), 128)].astype(jnp.float32),
                axis=0,
                keepdims=True,
            )

        width = table_here.shape[1]
        sum_out[:, :width] = lax.fori_loop(
            0, table_here.shape[0] // 128, add_up, jnp.zeros((1, width), jnp.float32)
        )

    def answer():
        state["ask_arrive"]()
        width = table_here.shape[1]
        asked_all = ask_in[...].reshape(devices, 128)
        ask_lanes = lax.broadcasted_iota(jnp.int32, (devices, 128), 1)
        over = jnp.max(
            jnp.max(jnp.where(ask_lanes == 127, asked_all, 0.0), axis=0, keepdims=True),
            axis=1,
            keepdims=True,
        )
        square = (128, 128)
        eye = (
            lax.broadcasted_iota(jnp.int32, square, 0)
            == lax.broadcasted_iota(jnp.int32, square, 1)
        ).astype(jnp.float32)
        turned = jnp.round(dot_nt(eye, asked_all, highest_precision))
        more = turned[CAP:ASKED]
        counts = jnp.sum((more >= 0.0).astype(jnp.float32), axis=0, keepdims=True)
        pairs = (devices, devices)
        before = (
            lax.broadcasted_iota(jnp.int32, pairs, 0) < lax.broadcasted_iota(jnp.int32, pairs, 1)
        ).astype(jnp.float32)
        ahead = jnp.round(
            dot_without_transpose(
                jnp.broadcast_to(counts, (8, devices)), before, highest_precision
            )[:1]
        )
        order = ahead + lax.broadcasted_iota(jnp.int32, more.shape, 0).astype(jnp.float32)
        order = jnp.where(more >= 0.0, order, -1.0)
        total = jnp.sum(counts, axis=1, keepdims=True)
        over = jnp.maximum(over, (total > float(EXTRA)).astype(jnp.float32))
        extra_col = jnp.full((EXTRA, 1), -1.0, jnp.float32)
        extra_row = jnp.full((1, 128), -1.0, jnp.float32)
        spots_col = lax.broadcasted_iota(jnp.int32, (EXTRA, 1), 0)
        spots_row = lax.broadcasted_iota(jnp.int32, (1, 128), 1)
        for spot in range(EXTRA):
            found = jnp.where(order == float(spot), more + 1.0, 0.0)
            found = jnp.sum(jnp.sum(found, axis=0, keepdims=True), axis=1, keepdims=True) - 1.0
            extra_col = jnp.where(spots_col == spot, found, extra_col)
            extra_row = jnp.where(spots_row == spot, found, extra_row)
        first_id = (me * table_rows).astype(jnp.float32)
        extra_row = jnp.where(extra_row >= 0.0, extra_row + first_id, -1.0)
        sum_out[:, width:] = jnp.where(spots_row == 127, over, extra_row)
        sum_in[pl.ds(me, 1)] = sum_out[...][None]
        start, state["sum_arrive"], state["sum_sent"] = to_all(
            lambda other: sum_out, sum_in, sum_sems.at[0], sum_sems.at[1], devices, group, me
        )
        start()
        row_lanes = lax.broadcasted_iota(jnp.int32, (EXTRA, table_here.shape[0]), 1)
        row_lanes = row_lanes.astype(jnp.float32)
        batch = selector.shape[0] // CAP
        for step in range(devices // batch):
            for at in range(batch):
                source = step * batch + at
                hot = turned[:CAP, source : source + 1] == row_lanes
                selector[at * CAP : (at + 1) * CAP] = hot.astype(jnp.float32).astype(jnp.bfloat16)
            picked = dot_without_transpose(selector[...], table_here[...])
            rows_out[step * batch : (step + 1) * batch] = picked.astype(jnp.bfloat16).reshape(
                batch, CAP, -1
            )
        hot = (extra_col == row_lanes).astype(jnp.float32).astype(jnp.bfloat16)
        extra_out[...] = dot_without_transpose(hot, table_here[...]).astype(jnp.bfloat16)
        rows_in[pl.ds(me, 1)] = rows_out[pl.ds(me, 1)]

    def row_copy(offset, far, there):
        column = lax.rem(dp + offset, devices // group)
        other = column * group + there
        number = offset * group + far
        return pltpu.make_async_remote_copy(
            rows_out.at[other],
            rows_in.at[me],
            row_sems.at[0, number],
            row_sems.at[1, number],
            device_id=(column, there),
            device_id_type=MESH,
        )

    def row_copies(k):
        return [
            row_copy(offset, mirror(z, along[k]), along[k])
            for offset in range(0 if k else 1, devices // group)
        ]

    def send_rows(k):
        for copy in row_copies(k):
            copy.start()

    def rows_arrive():
        flips = (z, z // 2 * 2 + 1 - z % 2, (z + 2) % 4, (1 - z // 2) * 2 + 1 - z % 2)
        for offset in range(devices // group):
            for far in range(group):
                if offset or far:
                    column = lax.rem(dp + devices // group - offset, devices // group)
                    source = column * group + flips[far]
                    number = offset * group + far
                    pltpu.make_async_remote_copy(
                        rows_in.at[source],
                        rows_in.at[source],
                        row_sems.at[0, number],
                        row_sems.at[1, number],
                        device_id=(column, flips[far]),
                        device_id_type=MESH,
                    ).wait_recv()

    def turn():
        adapters_out[...] = stack_rows(adapter_down, adapter_up)
        state["sort"] = counted_first(mask[...].astype(jnp.float32))
        turn_rows(table_here, turned_here)
        keep(turned_here, turned_mine)
        for at, (here, there) in enumerate(
            ((table_here, table_other), (turned_here, turned_other))
        ):
            copy = pltpu.make_async_remote_copy(
                here,
                there,
                table_sems.at[2 + 2 * at],
                table_sems.at[3 + 2 * at],
                device_id=(dp_core, z),
                device_id_type=MESH,
            )
            copy.start()
            state["swap", at] = copy

    def unpack():
        unpack_rows(
            packed,
            devices,
            position_own.shape[0],
            position_own.shape[1] // 4,
            gain_own.shape[0],
            bias_own.shape[1],
            positions,
            gains_out,
            shifts,
            bias,
        )

    def embed():
        rows_arrive()
        state["sum_arrive"]()
        width = table_here.shape[1]
        table_sum[...] = jnp.sum(sum_in[:, :, :width], axis=0)
        notes = sum_in[:, :, width:].reshape(devices, 128)
        note_lanes = lax.broadcasted_iota(jnp.int32, notes.shape, 1)
        over = jnp.max(jnp.where(note_lanes == 127, notes, 0.0), axis=0, keepdims=True)
        flags[...] = jnp.max(over, axis=1, keepdims=True)
        slot_col, owner_col, ids_col = state["slot_col"], state["owner_col"], state["ids_col"]
        tokens = ids_col.shape[0]
        slots = lax.broadcasted_iota(jnp.int32, (tokens, devices * CAP), 1).astype(jnp.float32)
        index_col = jnp.where(slot_col < float(CAP), owner_col * CAP + slot_col, -1.0)
        chosen = (index_col == slots).astype(jnp.float32).astype(jnp.bfloat16)
        taken = dot_without_transpose(chosen, rows_in[...].reshape(devices * CAP, -1))
        extra_ids = jnp.concatenate(
            [notes[source : source + 1, :EXTRA] for source in range(devices)], axis=1
        )
        spots = lax.broadcasted_iota(jnp.int32, (tokens, devices * EXTRA), 1).astype(jnp.float32)
        wanted = jnp.where(slot_col < float(CAP), -2.0, ids_col)
        hit = jnp.min(
            jnp.where(wanted == extra_ids, spots, float(devices * EXTRA)), axis=1, keepdims=True
        )
        chosen = (hit == spots).astype(jnp.float32).astype(jnp.bfloat16)
        taken += dot_without_transpose(chosen, extra[...])
        embedded[...] = taken[: tokens // 2]
        target_out[...] = taken[tokens // 2 :]
        state["allowed"] = first_part(embedded, positions, lengths, gains_out, shifts, x0, h1)
        keep(h1, h1_out)

    def project():
        project_part(h1, w_qkv, bias, adapters_out, inner, joined)
        keep(joined, joined_out)

    def attend():
        attend_part(joined, state["allowed"], probs, mixed)
        keep(probs, probs_out)
        keep(mixed, mixed_out)

    def output():
        keep(w_out, out_kept)
        output_part(x0, mixed, w_out, bias, adapters_out, inner, gains_out, shifts, x1, h2)
        keep(x1, x1_out)

    def up():
        keep(w_up, up_kept)
        up_part(h2, w_up, bias, active, slope)
        keep(slope, slope_out)

    def chips(core_at):
        return [place(at // 2, at % 2, core_at) for at in range(4)]

    def down_near():
        kept.pop(4).wait()
        down_part(True, chips(core), x1, active, w_down, bias, x2)

    def down():
        keep(w_down, down_kept)
        down_part(False, chips(1 - core), x2, active, w_down, bias, x2)
        last_norm(x2, gains_out, shifts, final)
        final_sorted[...] = dot_without_transpose(state["sort"], final[...]).astype(jnp.bfloat16)
        keep(x2, x2_out)

    comes = {OWN: own, LINE: line, SIDE: side, DIAGONAL: diagonal, CORE: other_core}
    works = {
        ASK: ask,
        SUM: table_total,
        ANSWER: answer,
        TURN: turn,
        UNPACK: unpack,
        EMBED: embed,
        PROJECT: project,
        ATTEND: attend,
        OUTPUT: output,
        UP: up,
        DOWN_NEAR: down_near,
        DOWN: down,
    }
    for kind, which, k in FIRST_ORDER:
        if kind in comes:
            comes[kind](which, k)
        elif kind == ROWS:
            send_rows(k)
        else:
            works[kind]()
    for at in range(2):
        state["swap", at].wait()
    for copy in keeps:
        copy.wait()
    for copy in sent:
        copy.wait_send()
    for which in range(len(arrays)):
        for k in range(4):
            pass_along(which, k, lambda copy: copy.wait_send())
    for k in range(4):
        for copy in row_copies(k):
            copy.wait_send()
    state["ask_sent"]()
    state["sum_sent"]()


def first(
    ids, targets, mask, lengths, table, small, adapter_down, adapter_up, weights
):
    group = lax.axis_size("vocab")
    devices = lax.axis_size("dp") * group
    table_rows, width = table.shape
    pad_rows = -(-table_rows // 128) * 128
    tail = table[table_rows - 16 :]
    rows = ids.shape[0]
    hidden = weights[3].shape[0] * devices
    heads = width // HEAD_DIM
    low, full = jnp.bfloat16, jnp.float32
    positions, gains, shifts, biases = small
    pack_height = positions.shape[1] // 4 + 16
    counts = [pack_height] + [w.shape[0] for w in weights] + [EXTRA]
    anywhere, vmem = pl.BlockSpec(memory_space=pl.ANY), pl.BlockSpec(memory_space=pltpu.VMEM)
    dma = pltpu.SemaphoreType.DMA
    shape = jax.ShapeDtypeStruct
    adapter_rows = 2 * adapter_up.shape[0] * adapter_up.shape[1]
    whole = [(devices * w.shape[0], w.shape[1]) for w in weights]
    saved = [
        shape((pad_rows, width), low),
        shape((width, pad_rows), low),
        shape((pad_rows, width), low),
        shape((width, pad_rows), low),
        shape((rows, width), low),
        shape((rows, 3 * width), low),
        shape((heads, rows, rows), low),
        shape((rows, width), low),
        shape((rows, width), full),
        shape((rows, hidden), low),
        shape((rows, width), full),
    ] + [shape(w, low) for w in whole[1:]]
    return pl.pallas_call(
        partial(first_kernel, table_rows, devices, group, counts),
        out_shape=[
            shape((1, 1), full),
            shape((rows, width), full),
            shape((1, width), full),
            shape((gains.shape[0], width), full),
            shape((adapter_rows, width), full),
            shape((rows, width), low),
            shape((rows, width), low),
            shape((adapter_rows // 2, rows), full),
        ]
        + saved,
        in_specs=[vmem] * 3
        + [pl.BlockSpec(memory_space=pltpu.SMEM)]
        + [vmem] * 7
        + [anywhere] * (1 + len(weights)),
        out_specs=[vmem] * 8 + [anywhere] * len(saved),
        scratch_shapes=[
            dma((len(counts), 42)),
            dma((len(counts), devices)),
            dma((len(counts),)),
            dma((6,)),
            dma((2, devices)),
            dma((2, devices)),
            dma((2, devices)),
            dma((12,)),
            pltpu.VMEM((pad_rows, width), low),
            pltpu.VMEM((width, pad_rows), low),
            pltpu.VMEM((16 * CAP, pad_rows), low),
            pltpu.VMEM((devices, CAP, width), low),
            pltpu.VMEM((devices, CAP, width), low),
            pltpu.VMEM((devices, 1, 128), full),
            pltpu.VMEM((devices, 1, 128), full),
            pltpu.VMEM((1, width + 128), full),
            pltpu.VMEM((devices, 1, width + 128), full),
            pltpu.VMEM((EXTRA, width), low),
            pltpu.VMEM((devices * EXTRA, width), low),
            pltpu.VMEM((pack_height, 128), low),
            pltpu.VMEM((devices * pack_height, 128), low),
        ]
        + [pltpu.VMEM(w, low) for w in whole]
        + [
            pltpu.VMEM((positions.shape[1], width), low),
            pltpu.VMEM((shifts.shape[0], width), full),
            pltpu.VMEM((1, devices * biases.shape[0]), full),
            pltpu.VMEM((rows, width), full),
            pltpu.VMEM((rows, width), full),
            pltpu.VMEM((rows, width), low),
            pltpu.VMEM((rows, 3 * width), low),
            pltpu.VMEM((heads, rows, rows), low),
            pltpu.VMEM((rows, width), low),
            pltpu.VMEM((rows, width), full),
            pltpu.VMEM((rows, width), low),
            pltpu.VMEM((rows, hidden), low),
            pltpu.VMEM((rows, hidden), low),
            pltpu.VMEM((rows, width), full),
        ],
        name="first",
        compiler_params=pltpu.CompilerParams(
            collective_id=1, has_side_effects=True, vmem_limit_bytes=63 * 2**20
        ),
    )(
        ids[None, :],
        targets[None, :],
        mask[None, :],
        lengths,
        positions,
        gains,
        shifts,
        biases[None, :],
        jnp.swapaxes(adapter_down, 1, 2),
        adapter_up,
        tail,
        table,
        *weights,
    )


def per_device(
    ids,
    targets,
    counted_mask,
    lengths,
    table,
    position_table,
    layer_norm_gain,
    layer_norm_bias,
    query_key_value_weight,
    output_weight,
    up_weight,
    down_weight,
    biases,
    adapter_down,
    adapter_up,
    down_momentum,
    up_momentum,
):
    every = (
        ids,
        targets,
        counted_mask,
        lengths,
        table,
        position_table,
        layer_norm_gain,
        layer_norm_bias,
        query_key_value_weight,
        output_weight,
        up_weight,
        down_weight,
        biases,
        adapter_down,
        adapter_up,
    )
    table_rows = table.shape[0]
    (
        flags,
        target_rows,
        table_sum,
        gains_all,
        adapters,
        final_state,
        final_sorted,
        inner_rows,
        table_mine,
        turned_mine,
        table_other,
        turned_other,
        h1,
        joined,
        probs,
        mixed,
        x1,
        slope,
        x2,
        w_out_all,
        w_up_all,
        w_down_all,
    ) = first(
        ids,
        targets,
        counted_mask,
        lengths,
        table,
        (position_table.T, layer_norm_gain, layer_norm_bias, biases),
        adapter_down,
        adapter_up,
        (query_key_value_weight, output_weight, up_weight, down_weight),
    )
    kept = (h1, joined, probs, mixed, inner_rows, x1, slope, x2)
    mean_rows, log_total = head(
        final_sorted, table_rows, (table_mine, turned_mine, table_other, turned_other)
    )
    gathered = backward(
        mean_rows,
        log_total,
        counted_mask.astype(jnp.float32),
        target_rows,
        table_sum,
        gains_all,
        adapters,
        (final_state, *kept),
        (w_out_all, w_up_all, w_down_all),
    )

    def general():
        down_gradient, up_gradient, loss_own, count_own = gradients_general(*every)
        rows = jnp.concatenate([jnp.swapaxes(down_gradient, 1, 2), up_gradient], axis=0)
        rows = rows.reshape(gathered.shape[0], 1, -1)
        sums = jnp.zeros((rows.shape[0], 1, 128), jnp.float32)
        sums = sums.at[:, :, 0].set(loss_own).at[:, :, 1].set(count_own)
        return jnp.concatenate([rows, sums], axis=2)

    gathered = lax.cond(flags.reshape(()) > 0.0, general, lambda: gathered)
    mom_down, mom_up, new_down, new_up, low_down, low_up, loss, count, norm = update(
        gathered, adapters, down_momentum, up_momentum
    )
    return (
        loss.reshape(()),
        count.reshape(()),
        norm.reshape(()),
        jnp.swapaxes(mom_down, 1, 2),
        mom_up,
        jnp.swapaxes(new_down, 1, 2),
        new_up,
        jnp.swapaxes(low_down, 1, 2),
        low_up,
    )


def solution(mesh):
    fast = dict(mesh.shape) == {"dp": 8, "vocab": 4}
    placed = (
        P(("dp", "vocab")),
        P(("dp", "vocab")),
        P(("dp", "vocab")),
        P(("dp", "vocab"), None),
        P(("dp", "vocab"), None),
        P(None, ("dp", "vocab")),
        P(None, ("dp", "vocab")),
        P(None, ("dp", "vocab")),
        P(("dp", "vocab"), None),
        P(("dp", "vocab"), None),
        P(("dp", "vocab"), None),
        P(("dp", "vocab"), None),
        P(("dp", "vocab")),
        P(),
        P(),
        P(),
        P(),
    )
    return jax.shard_map(
        per_device if fast else per_device_general,
        mesh=mesh,
        in_specs=placed,
        out_specs=(
            P(),
            P(),
            P(),
            P(None, "vocab", None),
            P(None, None, "vocab"),
            P(None, "vocab", None),
            P(None, None, "vocab"),
            P(None, "vocab", None),
            P(None, None, "vocab"),
        ),
        check_vma=False,
    )
```
